256 devices in a mesh: dp: 8 (over z), ctx: 32 (over x, y, core).
Axes of the slice: x: 4, y: 4, z: 8, core: 2. Of those that a mesh axis runs over, the one named last changes fastest.
Arguments:
- queries: bfloat16 [8, 8192, 512], P('dp', 'ctx'), may hold values from -11 to 11
- key_rows: bfloat16 [8, 8192, 512], P('dp', 'ctx'), may hold values from -11 to 11
- value_rows: bfloat16 [8, 8192, 512], P('dp', 'ctx'), may hold values from -6 to 6
- segment_ids: int32 [8, 8192], P('dp', 'ctx'), may hold values from 0 to 3, never falling along the last dimension, each value on 1 to 4096 neighbouring positions
- w_out: bfloat16 [512, 512], replicated, may hold values from -0.25 to 0.25
- d_out: bfloat16 [8, 8192, 512], P('dp', 'ctx'), may hold values from -6 to 6
Outputs:
- layer_out: bfloat16 [8, 8192, 512], P('dp', 'ctx')
- d_queries: bfloat16 [8, 8192, 512], P('dp', 'ctx')
- d_key_rows: bfloat16 [8, 8192, 512], P('dp', 'ctx')
- d_value_rows: bfloat16 [8, 8192, 512], P('dp', 'ctx')
- d_w_out: bfloat16 [512, 512], P('ctx')
The draws below stay inside these ranges and needn't reach their ends.
Inputs may be any that keep to these rules, and one draw needn't show every extreme that they name: `segment_ids`: never falls along a sequence; each of the 4 documents of a sequence holds 1 to 4096 tokens, one exactly 4096.
All inputs are finite; a program needn't handle non-finite values.
Results may differ from the reference program's by a relative error of at most 0.04.
Values may be sent and summed in bfloat16 or wider, within the bound.
No kernel may reach another device: no remote copies, remote signals or barrier semaphores. Data moves between devices by JAX's collectives and lax.ppermute only.
A program may use at most 192 MiB of HBM per device.

```python
import math
from functools import reduce
import jax
import jax.numpy as jnp
import numpy as np
from jax import lax

HEADS = 8
HEAD_DIM = 64
D = 512
BLOCK = 64
LEVELS = 4
SEGS = 4
LENGTH = 8192
BATCH = 8


def draw_queries(key, part):
    key = jax.random.fold_in(key, 3)
    base = jnp.clip(jax.random.normal(key, (BATCH, LENGTH, D), jnp.float32), -6.0, 6.0)
    return base.astype(jnp.bfloat16)


def draw_key_rows(key, part):
    key = jax.random.fold_in(key, 4)
    base = jnp.clip(jax.random.normal(key, (BATCH, LENGTH, D), jnp.float32), -6.0, 6.0)
    return base.astype(jnp.bfloat16)


def shard_levels(stream_key, shape, cuts, smallest, largest):
    loudness = 1.0
    for dim, parts in cuts:
        heights = jax.random.uniform(jax.random.fold_in(jax.random.fold_in(stream_key, 6), dim), (parts,), jnp.float32, smallest / len(cuts), largest / len(cuts))
        loudness = loudness * jnp.repeat(jnp.exp(heights), shape[dim] // parts).reshape((-1,) + (1,) * (len(shape) - 1 - dim))
    return loudness


def length_profile(number_of, total, most, skew):
    weights = [(1 << 20) // math.isqrt(standing ** skew) + 1 for standing in range(2, number_of + 1)]
    surplus, counts = total - most - (number_of - 1), [1] * (number_of - 1)
    while surplus > 0:
        candidates = [i for i in range(number_of - 1) if counts[i] < most]
        whole, remaining = sum([weights[i] for i in candidates]), surplus
        for i in candidates:
            addition = min(most - counts[i], max(1, remaining * weights[i] // whole), surplus)
            counts[i] = counts[i] + addition
            surplus = surplus - addition
    return np.array([most] + counts)


def uneven_parts(own_key, number_of, total, most, skew):
    if number_of == 2:
        one = jax.random.randint(own_key, (), max(1, total - most), min(most, total - 1) + 1)
        return jnp.stack([one, total - one])
    lengths = jnp.asarray(length_profile(number_of, total, most, skew), jnp.int32)
    couples = (number_of - 1) // 2
    donor, sink = lengths[1:1 + 2 * couples:2], lengths[2:2 + 2 * couples:2]
    slack = jnp.minimum(donor - 1, most - sink)
    shifted = jax.random.randint(jax.random.fold_in(own_key, 1), (couples,), 0, 1 << 20) % (slack + 1)
    lengths = lengths.at[1:1 + 2 * couples:2].set(donor - shifted).at[2:2 + 2 * couples:2].set(sink + shifted)
    return lengths[jax.random.permutation(jax.random.fold_in(own_key, 2), number_of)]


def centred(own_key, extent, spread, reach, split=(), held_as=jnp.bfloat16):
    factor_of = shard_levels(own_key, extent, split, -0.22, 0.18) if split else 1.0
    result = jax.random.normal(own_key, extent, jnp.float32) * spread * factor_of
    return jnp.minimum(jnp.maximum(result, -reach), reach).astype(held_as)


def setup_inputs(seed: int = 0) -> dict:
    key_of = jax.random.split(jax.random.key(seed), 7)
    queries = draw_queries(jax.random.fold_in(key_of[6], 71), 0)
    key_rows = draw_key_rows(jax.random.fold_in(key_of[6], 71), 0)
    value_rows = centred(key_of[2], (BATCH, LENGTH, D), 1.0, 6.0, ((0, 8), (1, 32)))
    segment_ids = jax.vmap(lambda own: jnp.searchsorted(jnp.cumsum(uneven_parts(own, SEGS, LENGTH, LENGTH // 2, 0)), jnp.arange(LENGTH), side="right"))(jax.random.split(key_of[3], BATCH)).reshape((BATCH, LENGTH)).astype(jnp.int32)
    w_out = centred(key_of[4], (D, D), D ** -0.5, 0.25)
    d_out = centred(key_of[5], (BATCH, LENGTH, D), 1.0, 6.0, ((0, 8), (1, 32)))
    return dict(queries=queries, key_rows=key_rows, value_rows=value_rows, segment_ids=segment_ids, w_out=w_out, d_out=d_out)


NEGATIVE = -1e30
HIGHEST = lax.Precision.HIGHEST


def coarse_of(tokens, factor, average):
    if factor == 1:
        return tokens
    grouped = tokens.reshape(tokens.shape[0], tokens.shape[1] // factor, factor, tokens.shape[2])
    summed = jnp.sum(grouped.astype(jnp.float32), axis=2)
    if average:
        summed = summed / factor
    return summed.astype(jnp.bfloat16)


def level_mask(query_pos, key_pos, query_seg, key_seg, degree, total_rows):
    inside = (key_pos >= 0) & (key_pos < total_rows)
    allowed = jnp.broadcast_to(inside[:, None, :], (query_pos.shape[0], query_pos.shape[1], key_pos.shape[1]))
    if degree > 0:
        half_block = BLOCK // 2
        far_apart = jnp.abs(query_pos[:, :, None] // half_block - key_pos[:, None, :] // half_block) >= 2
        allowed = allowed & far_apart
    same_doc = query_seg[:, :, :, None] == key_seg[:, :, None, :]
    return same_doc & allowed[None]


def split_heads(blocks):
    return blocks.reshape(blocks.shape[:3] + (HEADS, blocks.shape[3] // HEADS)).astype(jnp.float32)


def attend_ref(query_blocks, key_window, value_window, pair_mask, weight_count):
    score_scale = HEAD_DIM ** -0.5
    scores = jnp.einsum("sbqhe,sbkhe->sbhqk", split_heads(query_blocks), split_heads(key_window), precision=HIGHEST) * score_scale
    keep_mask = pair_mask[:, :, None]
    masked = jnp.where(keep_mask, scores, NEGATIVE)
    peak_score = jnp.max(masked, axis=-1)
    probabilities = jnp.where(keep_mask, jnp.exp(masked - peak_score[..., None]), 0.0).astype(jnp.bfloat16)
    numerator = jnp.einsum("sbhqk,sbkhe->sbqhe", probabilities.astype(jnp.float32), split_heads(value_window), precision=HIGHEST)
    denominator = jnp.sum(probabilities.astype(jnp.float32), axis=-1) * weight_count
    return peak_score, numerator, denominator, probabilities


def attend_back_ref(query_blocks, key_window, value_window, probabilities, grad_coarse, delta_coarse, weight_count):
    score_scale = HEAD_DIM ** -0.5
    grad_float = grad_coarse.astype(jnp.float32)
    product = jnp.einsum("sbqhe,sbkhe->sbhqk", grad_float, split_heads(value_window), precision=HIGHEST)
    dscore = (probabilities.astype(jnp.float32) * (product - delta_coarse[..., None] * weight_count)).astype(jnp.bfloat16).astype(jnp.float32)
    grad_query = jnp.einsum("sbhqk,sbkhe->sbqhe", dscore, split_heads(key_window), precision=HIGHEST) * score_scale
    grad_key = jnp.einsum("sbhqk,sbqhe->sbkhe", dscore, split_heads(query_blocks), precision=HIGHEST) * score_scale
    grad_value = jnp.einsum("sbhqk,sbqhe->sbkhe", probabilities.astype(jnp.float32), grad_float, precision=HIGHEST)
    return grad_query, grad_key, grad_value


def merge_heads(blocks):
    return blocks.reshape(blocks.shape[:3] + (blocks.shape[3] * blocks.shape[4],))


def combine_levels(peak_list, numerator_list, denominator_list):
    factors = [2 ** degree for degree in range(len(peak_list))]
    wide_peaks = [jnp.repeat(peak_score, factor, axis=1) for peak_score, factor in zip(peak_list, factors)]
    top_peak = reduce(jnp.maximum, wide_peaks)
    weights = [jnp.exp(wide_peak - top_peak) for wide_peak in wide_peaks]
    normalizer = reduce(jnp.add, [weight * jnp.repeat(part_sum, factor, axis=1) for weight, part_sum, factor in zip(weights, denominator_list, factors)])
    numerator = reduce(jnp.add, [weight[..., None] * jnp.repeat(part_sum, factor, axis=1) for weight, part_sum, factor in zip(weights, numerator_list, factors)])
    attended = (numerator / normalizer[..., None]).astype(jnp.bfloat16)
    shares = [weight / normalizer for weight in weights]
    return attended.reshape(attended.shape[0], attended.shape[1], -1), shares


def restrict(level_share, grad_heads, delta_rows, factor):
    seq_count, row_count, head_count, head_size = grad_heads.shape
    grad_coarse = jnp.sum((level_share[..., None] * grad_heads).reshape(seq_count, row_count // factor, factor, head_count, head_size), axis=2).astype(jnp.bfloat16)
    delta_coarse = jnp.sum((level_share * delta_rows).reshape(seq_count, row_count // factor, factor, head_count), axis=2)
    return grad_coarse, delta_coarse


def level_inputs(queries, key_rows, value_rows, segment_ids, degree):
    factor = 2 ** degree
    return (coarse_of(queries, factor, True), coarse_of(key_rows, factor, True), coarse_of(value_rows, factor, False), segment_ids[:, factor - 1::factor])


def padded_level(level_data):
    key_pad = jnp.pad(level_data[1], ((0, 0), (BLOCK, BLOCK), (0, 0)))
    value_pad = jnp.pad(level_data[2], ((0, 0), (BLOCK, BLOCK), (0, 0)))
    seg_pad = jnp.pad(level_data[3], ((0, 0), (BLOCK, BLOCK)), constant_values=-1)
    return key_pad, value_pad, seg_pad


def block_view(level_data, padded, degree, block_index):
    total_rows = level_data[0].shape[1]
    row_start = (block_index * BLOCK).astype(jnp.int32)
    query_blocks = lax.dynamic_slice_in_dim(level_data[0], row_start, BLOCK, 1)[:, None]
    query_seg = lax.dynamic_slice_in_dim(level_data[3], row_start, BLOCK, 1)[:, None]
    key_window = lax.dynamic_slice_in_dim(padded[0], row_start, 3 * BLOCK, 1)[:, None]
    value_window = lax.dynamic_slice_in_dim(padded[1], row_start, 3 * BLOCK, 1)[:, None]
    key_seg = lax.dynamic_slice_in_dim(padded[2], row_start, 3 * BLOCK, 1)[:, None]
    query_pos = (row_start + jnp.arange(BLOCK, dtype=jnp.int32))[None]
    key_pos = (row_start - BLOCK + jnp.arange(3 * BLOCK, dtype=jnp.int32))[None]
    pair_mask = level_mask(query_pos, key_pos, query_seg, key_seg, degree, total_rows)
    return query_blocks, key_window, value_window, pair_mask, row_start


def level_forward(level_data, degree):
    padded = padded_level(level_data)
    seq_count, total_rows, model_width = level_data[0].shape
    block_count = total_rows // BLOCK

    def one_block(block_index):
        query_blocks, key_window, value_window, pair_mask, row_start = block_view(level_data, padded, degree, block_index)
        peak_score, numerator, denominator, probabilities = attend_ref(query_blocks, key_window, value_window, pair_mask, float(2 ** degree))
        return peak_score[:, 0], numerator[:, 0], denominator[:, 0]

    peaks, numerators, denominators = lax.map(one_block, jnp.arange(block_count, dtype=jnp.int32))
    peak_rows = jnp.swapaxes(jnp.moveaxis(peaks, 0, 1), 2, 3).reshape(seq_count, total_rows, HEADS)
    denominator_rows = jnp.swapaxes(jnp.moveaxis(denominators, 0, 1), 2, 3).reshape(seq_count, total_rows, HEADS)
    numerator_rows = jnp.moveaxis(numerators, 0, 1).reshape(seq_count, total_rows, HEADS, model_width // HEADS)
    return peak_rows, numerator_rows, denominator_rows


def level_backward(level_data, degree, grad_coarse, delta_coarse):
    padded = padded_level(level_data)
    seq_count, total_rows, model_width = level_data[0].shape
    block_count = total_rows // BLOCK

    def one_block(carry, block_index):
        key_grad, value_grad = carry
        query_blocks, key_window, value_window, pair_mask, row_start = block_view(level_data, padded, degree, block_index)
        probabilities = attend_ref(query_blocks, key_window, value_window, pair_mask, float(2 ** degree))[3]
        grad_block = lax.dynamic_slice_in_dim(grad_coarse, row_start, BLOCK, 1)[:, None]
        delta_block = jnp.swapaxes(lax.dynamic_slice_in_dim(delta_coarse, row_start, BLOCK, 1), 1, 2)[:, None]
        grad_query, grad_key, grad_value = attend_back_ref(query_blocks, key_window, value_window, probabilities, grad_block, delta_block, float(2 ** degree))
        key_grad = lax.dynamic_update_slice_in_dim(key_grad, lax.dynamic_slice_in_dim(key_grad, row_start, 3 * BLOCK, 1) + merge_heads(grad_key)[:, 0], row_start, 1)
        value_grad = lax.dynamic_update_slice_in_dim(value_grad, lax.dynamic_slice_in_dim(value_grad, row_start, 3 * BLOCK, 1) + merge_heads(grad_value)[:, 0], row_start, 1)
        return (key_grad, value_grad), merge_heads(grad_query)[:, 0]

    start_grads = (jnp.zeros((seq_count, total_rows + 2 * BLOCK, model_width), jnp.float32), jnp.zeros((seq_count, total_rows + 2 * BLOCK, model_width), jnp.float32))
    final_grads, query_parts = lax.scan(one_block, start_grads, jnp.arange(block_count, dtype=jnp.int32))
    query_grad = jnp.moveaxis(query_parts, 0, 1).reshape(seq_count, total_rows, model_width)
    return query_grad, final_grads[0][:, BLOCK:-BLOCK], final_grads[1][:, BLOCK:-BLOCK]


def reference(queries, key_rows, value_rows, segment_ids, w_out, d_out):
    seq_count, row_count, model_width = queries.shape
    level_list = [level_inputs(queries, key_rows, value_rows, segment_ids, degree) for degree in range(LEVELS + 1)]
    forward_parts = [level_forward(level_list[degree], degree) for degree in range(LEVELS + 1)]
    attended, shares = combine_levels([part[0] for part in forward_parts], [part[1] for part in forward_parts], [part[2] for part in forward_parts])
    layer_out = jnp.einsum("snd,df->snf", attended.astype(jnp.float32), w_out.astype(jnp.float32), precision=HIGHEST).astype(jnp.bfloat16)
    grad_att = jnp.einsum("snf,df->snd", d_out.astype(jnp.float32), w_out.astype(jnp.float32), precision=HIGHEST)
    grad_heads = grad_att.reshape(seq_count, row_count, HEADS, model_width // HEADS)
    delta_rows = jnp.sum(grad_heads * attended.reshape(grad_heads.shape).astype(jnp.float32), axis=-1)
    d_w_out = jnp.einsum("snd,snf->df", attended.astype(jnp.float32), d_out.astype(jnp.float32), precision=HIGHEST).astype(jnp.bfloat16)
    query_total = jnp.zeros((seq_count, row_count, model_width), jnp.float32)
    key_total = jnp.zeros((seq_count, row_count, model_width), jnp.float32)
    value_total = jnp.zeros((seq_count, row_count, model_width), jnp.float32)
    for degree in range(LEVELS + 1):
        factor = 2 ** degree
        grad_coarse, delta_coarse = restrict(shares[degree], grad_heads, delta_rows, factor)
        query_grad, key_grad, value_grad = level_backward(level_list[degree], degree, grad_coarse, delta_coarse)
        query_total = query_total + jnp.repeat(query_grad, factor, axis=1) / factor
        key_total = key_total + jnp.repeat(key_grad, factor, axis=1) / factor
        value_total = value_total + jnp.repeat(value_grad, factor, axis=1)
    return (layer_out, query_total.astype(jnp.bfloat16), key_total.astype(jnp.bfloat16), value_total.astype(jnp.bfloat16), d_w_out)
```

```python
import functools

import jax
import jax.numpy as jnp
import numpy as np
from jax import lax
from jax.experimental import pallas as pl
from jax.experimental.pallas import tpu as pltpu
from jax.sharding import PartitionSpec as P

HEAD_DIM = 64
BLOCK = 64
HALF = 32
LEVELS = 4
ROWS = 256
WIDTH = 512
PAIRS = 4
LANES = 128
DOCS = 4
NEGATIVE = -1e30
BLOCKED = -2e30
SCALE = HEAD_DIM**-0.5
PACK = 2 * WIDTH + LANES
COARSE = 240
OFFSET = {1: 0, 2: 128, 3: 192, 4: 224}
COUNT = {0: 256, 1: 128, 2: 64, 3: 32, 4: 16}
F32 = jnp.float32
BF16 = jnp.bfloat16


def level_tables():
    total = np.zeros((COARSE, ROWS), np.float32)
    mean = np.zeros((COARSE, ROWS), np.float32)
    last = np.zeros((COARSE, ROWS), np.float32)
    for level in range(1, LEVELS + 1):
        factor = 2**level
        for row in range(COUNT[level]):
            at = OFFSET[level] + row
            total[at, row * factor : (row + 1) * factor] = 1
            mean[at, row * factor : (row + 1) * factor] = 1 / factor
            last[at, (row + 1) * factor - 1] = 1
    return total, mean, last


def position_tables():
    query = np.zeros((128 + 128 + 64, LANES), np.float32)
    key = np.zeros((256 + 256 + 128, LANES), np.float32)
    for row in range(128):
        query[row, 8 + row // BLOCK] = 1
        query[128 + row, 8 + row // HALF] = 1
    for row in range(64):
        query[256 + row, 8 + row // HALF] = 1
    for row in range(256):
        for place in range(2):
            if row // BLOCK - place not in (0, 1, 2):
                key[row, 8 + place] = BLOCKED
        for place in range(4):
            there, here = row // HALF - 2, place
            near = abs(there // 2 - here // 2) <= 1 and abs(there - here) >= 2
            if not near:
                key[256 + row, 8 + place] = BLOCKED
    for row in range(128):
        for place in range(2):
            there = (-2, -1, 2, 3)[row // HALF]
            if abs(there - place) < 2:
                key[512 + row, 8 + place] = BLOCKED
    return query, key


def dot(a, b, a_dim=1, b_dim=0):
    return lax.dot_general(a, b, (((a_dim,), (b_dim,)), ((), ())), preferred_element_type=F32)


def split(x):
    high = x.astype(BF16)
    return high, (x - high.astype(F32)).astype(BF16)


def head_lanes(rows):
    lane = lax.broadcasted_iota(jnp.int32, (rows, LANES), 1)
    return lane < HEAD_DIM


def stacked(x):
    first = head_lanes(x.shape[0]).astype(F32).astype(BF16)
    return jnp.concatenate([x * first, x * (1 - first)], axis=0)


def unstacked(x, rows):
    return jnp.where(head_lanes(rows), x[:rows], x[rows:])


def coarsen_kernel(seg, k, v, total, mean, last, up, down, far3, far4, own1, doc0, qdoc):
    sub = lax.broadcasted_iota(jnp.int32, (LANES, ROWS), 0)
    marks = jnp.where(seg[...] == sub, 1.0, 0.0).T.astype(BF16)
    coarse_marks = dot(last[...], marks).astype(BF16)
    key_c = dot(mean[...], k[...]).astype(BF16)
    value_c = dot(total[...], v[...]).astype(BF16)

    def key_side(x):
        lane = lax.broadcasted_iota(jnp.int32, x.shape, 1)
        return jnp.where(lane < DOCS, (1.0 - x.astype(F32)) * BLOCKED, 0.0).astype(BF16)

    doc_0 = key_side(marks)
    doc_c = key_side(coarse_marks)
    qdoc[0:ROWS] = marks
    qdoc[ROWS : ROWS + COARSE] = coarse_marks
    doc0[...] = doc_0

    def put(ref, at, keys, values, docs):
        rows = keys.shape[0]
        ref[at : at + rows, 0:WIDTH] = keys
        ref[at : at + rows, WIDTH : 2 * WIDTH] = values
        ref[at : at + rows, 2 * WIDTH :] = docs

    def rows_of(level, start, stop):
        if level == 0:
            return k[start:stop], v[start:stop], doc_0[start:stop]
        at = OFFSET[level]
        return tuple(x[at + start : at + stop] for x in (key_c, value_c, doc_c))

    for level in range(3):
        put(up, BLOCK * level, *rows_of(level, COUNT[level] - BLOCK, COUNT[level]))
        put(down, BLOCK * level, *rows_of(level, 0, BLOCK))
    put(own1, 0, *rows_of(1, 0, COUNT[1]))
    put(far3, 0, *rows_of(3, 0, COUNT[3]))
    put(far4, 0, *rows_of(4, 0, COUNT[4]))


class Window:
    def __init__(self, level, start, rows, position=None):
        self.level, self.start, self.rows, self.position = level, start, rows, position


GROUPS = (
    Window(0, 0, 128, (0, 0)),
    Window(0, 128, 128, (0, 0)),
    Window(1, 0, 128, (128, 256)),
    Window(2, 0, 64, (256, 512)),
    Window(3, 0, 32),
    Window(4, 0, 16),
)
KEYS = (256, 256, 256, 128, 96, 96)
P_AT = (0, 256, 512, 768, 896, 960)
P_ROWS = 992
COARSE_AT = {0: 0, 1: 256, 2: 384, 3: 448, 4: 480}
ALL_ROWS = 496


def window_parts(index, k, v, doc0, own1, low, high, far3, far4, part):
    lanes = (slice(0, WIDTH), slice(WIDTH, 2 * WIDTH), slice(2 * WIDTH, PACK))[part]
    fine = (k, v, doc0)[part]

    def rim(ref, level):
        return ref[BLOCK * level : BLOCK * (level + 1), lanes]

    if index == 0:
        return [rim(low, 0), fine[0:192]]
    if index == 1:
        return [fine[64:256], rim(high, 0)]
    if index == 2:
        return [rim(low, 1), own1[:, lanes], rim(high, 1)]
    if index == 3:
        return [rim(low, 2), rim(high, 2)]
    return [ref[:, lanes] for ref in (far3 if index == 4 else far4)]


def forward_kernel(n3, n4, *refs):
    (q, k, v, doc0, qdoc, own1, low, high), refs = refs[:8], refs[8:]
    far3, refs = refs[:n3], refs[n3:]
    far4, refs = refs[:n4], refs[n4:]
    (w, d_out, total, mean, spread, pos_q, pos_k), refs = refs[:7], refs[7:]
    layer_out, d_w, p_out, g_out, d_side, q_out, kw_out, vw_out = refs
    sources = (k, v, doc0, own1, low, high, far3, far4)
    q_coarse = dot(mean[...], q[...]).astype(BF16)
    key_docs = []
    for index, group in enumerate(GROUPS):
        docs = jnp.concatenate(window_parts(index, *sources, 2), axis=0)
        if group.position is not None:
            at = group.position[1]
            docs = docs + pos_k[at : at + KEYS[index]]
        key_docs.append(docs)
    query_docs = []
    for group in GROUPS:
        at = COARSE_AT[group.level] + group.start
        docs = qdoc[at : at + group.rows]
        if group.position is not None:
            docs = docs + pos_q[group.position[0] : group.position[0] + group.rows]
        query_docs.append(jnp.concatenate([docs, docs], axis=0))
    for index in range(len(GROUPS)):
        at = sum(KEYS[:index])
        kw_out[at : at + KEYS[index]] = jnp.concatenate(window_parts(index, *sources, 0), axis=0)
        vw_out[at : at + KEYS[index]] = jnp.concatenate(window_parts(index, *sources, 1), axis=0)
    grad_att = dot(d_out[...], w[...], 1, 1)
    lane = lax.broadcasted_iota(jnp.int32, (LANES, LANES), 1) // HEAD_DIM
    sub = lax.broadcasted_iota(jnp.int32, (LANES, LANES), 0) // HEAD_DIM
    same_head = jnp.where(lane == sub, 1.0, 0.0).astype(BF16)
    result = jnp.zeros((ROWS, WIDTH), F32)
    for pair in range(PAIRS):
        cols = slice(pair * LANES, (pair + 1) * LANES)
        q_all = jnp.concatenate([q[:, cols], q_coarse[:, cols]], axis=0) * SCALE
        q_all = q_all.astype(BF16)
        q_out[:, cols] = q_all
        parts = []
        for index, group in enumerate(GROUPS):
            at = COARSE_AT[group.level] + group.start
            rows, key_at = group.rows, sum(KEYS[:index])
            queries = jnp.concatenate(
                [stacked(q_all[at : at + rows]), query_docs[index]], axis=1
            )
            keys = jnp.concatenate(
                [kw_out[key_at : key_at + KEYS[index], cols], key_docs[index]], axis=1
            )
            scores = dot(queries, keys, 1, 1)
            peak = jnp.maximum(jnp.max(scores, axis=1, keepdims=True), NEGATIVE)
            peak = peak.astype(BF16).astype(F32)
            p = jnp.exp(scores - peak).astype(BF16)
            p_out[pair, P_AT[index] : P_AT[index] + 2 * rows, 0 : KEYS[index]] = p
            ones = jnp.ones((KEYS[index], LANES), BF16)
            values = jnp.concatenate([vw_out[key_at : key_at + KEYS[index], cols], ones], axis=1)
            both = dot(p, values)
            both = jnp.where(
                jnp.concatenate([head_lanes(rows)] * 2, axis=1), both[:rows], both[rows:]
            )
            wide_peak = jnp.where(head_lanes(rows), peak[:rows], peak[rows:])
            parts.append((both[:, :LANES], both[:, LANES:], wide_peak))
        fine = [jnp.concatenate([a, b], axis=0) for a, b in zip(parts[0], parts[1])]
        levels = [tuple(fine)]
        for level in range(1, LEVELS + 1):
            packed = jnp.concatenate([x.astype(BF16) for x in parts[level + 1]], axis=1)
            at = OFFSET[level]
            wide = dot(spread[:, LANES * (level - 1) : LANES * (level - 1) + COUNT[level]], packed)
            levels.append(tuple(wide[:, LANES * i : LANES * (i + 1)] for i in range(3)))
        top = functools.reduce(jnp.maximum, [x[2] for x in levels])
        weights = [jnp.exp(x[2] - top) for x in levels]
        norm = functools.reduce(
            jnp.add, [wt * x[1] * float(2**i) for i, (wt, x) in enumerate(zip(weights, levels))]
        )
        numer = functools.reduce(jnp.add, [wt * x[0] for wt, x in zip(weights, levels)])
        inverse = 1.0 / norm
        attended = (numer * inverse).astype(BF16)
        result = result + dot(attended, w[cols, :])
        d_w[cols, :] = dot(attended, d_out[...], 0, 0)
        grad = grad_att[:, cols]
        high_part, low_part = split(grad * attended.astype(F32))
        delta = dot(high_part, same_head) + dot(low_part, same_head)
        for level in range(LEVELS + 1):
            share = weights[level] * inverse
            at, rows = COARSE_AT[level], COUNT[level]
            if level == 0:
                grad_c, delta_c = (share * grad), share * delta
            else:
                d_high, d_low = split(share * delta)
                packed = jnp.concatenate([(share * grad).astype(BF16), d_high, d_low], axis=1)
                summed = dot(total[OFFSET[level] : OFFSET[level] + rows], packed)
                grad_c = summed[:, :LANES]
                delta_c = summed[:, LANES : 2 * LANES] + summed[:, 2 * LANES :]
            g_out[at : at + rows, cols] = grad_c.astype(BF16)
            d_high, d_low = split(delta_c * -float(2**level))
            quarter = lax.broadcasted_iota(jnp.int32, (rows, LANES), 1) % HEAD_DIM < HALF
            d_side[at : at + rows, cols] = jnp.where(
                quarter, d_high.astype(F32), d_low.astype(F32)
            ).astype(BF16)
    layer_out[...] = result.astype(BF16)


def backward_kernel(n3, n4, *refs):
    (p_in, g_in, d_side, q_in, kw, vw, spread_mean, spread_total), refs = refs[:8], refs[8:]
    d_q, own_k, own_v, to_low, to_high = refs[:5]
    to3, to4 = refs[5 : 5 + n3], refs[5 + n3 :]
    for pair in range(PAIRS):
        cols = slice(pair * LANES, (pair + 1) * LANES)
        value_cols = slice(WIDTH + pair * LANES, WIDTH + (pair + 1) * LANES)
        grads_q, grads_k, grads_v = [], [], []
        for index, group in enumerate(GROUPS):
            at = COARSE_AT[group.level] + group.start
            rows, keys, key_at = group.rows, KEYS[index], sum(KEYS[:index])
            grad = stacked(g_in[at : at + rows, cols])
            side = stacked(d_side[at : at + rows, cols])
            lane = lax.broadcasted_iota(jnp.int32, (keys, LANES), 1)
            ones = jnp.where(lane % HALF == 0, 1.0, 0.0).astype(BF16)
            values = jnp.concatenate([vw[key_at : key_at + keys, cols], ones], axis=1)
            product = dot(jnp.concatenate([grad, side], axis=1), values, 1, 1)
            p = p_in[pair, P_AT[index] : P_AT[index] + 2 * rows, 0:keys]
            ds = (p.astype(F32) * product).astype(BF16)
            grad_q = dot(ds, kw[key_at : key_at + keys, cols])
            grads_q.append(unstacked(grad_q, rows) * SCALE)
            grads_k.append(dot(ds, stacked(q_in[at : at + rows, cols]), 0, 0))
            grads_v.append(dot(p, grad, 0, 0))
        coarse = jnp.concatenate([x.astype(BF16) for x in grads_q[2:]], axis=0)
        d_q[:, cols] = (
            jnp.concatenate(grads_q[:2], axis=0) + dot(spread_mean[...], coarse)
        ).astype(BF16)
        for grads, own, out_cols, table in (
            (grads_k, own_k, cols, spread_mean),
            (grads_v, own_v, value_cols, spread_total),
        ):
            a, b, c, d, e, f = grads
            middle = jnp.concatenate([a[64:128], a[128:256] + b[0:128], b[128:192]], axis=0)
            spread = dot(table[:, 0 : COUNT[1]], c[64:192].astype(BF16))
            own[:, cols] = middle + spread
            to_low[:, out_cols] = jnp.concatenate([a[:64], c[:64], d[:64]], axis=0).astype(BF16)
            to_high[:, out_cols] = jnp.concatenate([b[192:], c[192:], d[64:]], axis=0).astype(BF16)
            for at, ref in enumerate(to3):
                rows = 96 // n3
                ref[:, out_cols] = e[at * rows : (at + 1) * rows].astype(BF16)
            for at, ref in enumerate(to4):
                rows = 96 // n4
                ref[:, out_cols] = f[at * rows : (at + 1) * rows].astype(BF16)


def gather_kernel(n3, n4, *refs):
    (own_k, own_v, low, high, spread_mean, spread_total), refs = refs[:6], refs[6:]
    from3, from4, (d_k, d_v) = refs[:n3], refs[n3 : n3 + n4], refs[n3 + n4 :]
    for own, out, lanes, table in (
        (own_k, d_k, slice(0, WIDTH), spread_mean),
        (own_v, d_v, slice(WIDTH, 2 * WIDTH), spread_total),
    ):

        def rim(ref, level):
            return ref[BLOCK * level : BLOCK * (level + 1), lanes].astype(F32)

        def summed(parts):
            return functools.reduce(jnp.add, [ref[:, lanes].astype(F32) for ref in parts])

        coarse = jnp.concatenate(
            [
                rim(high, 1),
                rim(low, 1),
                rim(low, 2) + rim(high, 2),
                summed(from3),
                summed(from4),
            ],
            axis=0,
        ).astype(BF16)
        whole = own[...] + dot(table[...], coarse)
        out[0:64] = (whole[0:64] + rim(high, 0)).astype(BF16)
        out[64:192] = whole[64:192].astype(BF16)
        out[192:256] = (whole[192:256] + rim(low, 0)).astype(BF16)


def vmem(count):
    return [pl.BlockSpec(memory_space=pltpu.VMEM)] * count


def call(kernel, name, outs, args):
    return pl.pallas_call(
        kernel,
        name=name,
        out_shape=[jax.ShapeDtypeStruct(shape, dtype) for shape, dtype in outs],
        in_specs=vmem(len(args)),
        out_specs=vmem(len(outs)),
        compiler_params=pltpu.CompilerParams(vmem_limit_bytes=48 * 1024 * 1024),
    )(*args)


def moved(x, route, back=False):
    count = lax.axis_size("ctx")
    pairs = [(i, route(i) % count) for i in range(count)]
    if back:
        pairs = [(b, a) for a, b in pairs]
    return lax.ppermute(x, "ctx", pairs)


ROUTES_3 = (
    lambda i: i + 2,
    lambda i: i - 2,
    lambda i: i - 3 if i % 2 else i + 3,
)


def routes_4():
    def route(shift, swap):
        def go(i):
            pair, side = i // 2, i % 2
            if shift == 0:
                pair = pair + (-3 if pair % 2 else 3)
            else:
                pair = pair + shift
            return 2 * pair + (side ^ swap)

        return go

    return [(route(shift, swap), swap) for shift in (2, -2, 0) for swap in (0, 1)]


def body(queries, key_rows, value_rows, segment_ids, w_out, d_out):
    q, k, v, grad_out = queries[0], key_rows[0], value_rows[0], d_out[0]
    total, mean, last = level_tables()
    pos_q, pos_k = (jnp.asarray(x, BF16) for x in position_tables())
    spread_padded = np.zeros((ROWS, LEVELS * LANES), np.float32)
    for level in range(1, LEVELS + 1):
        at = LANES * (level - 1)
        spread_padded[:, at : at + COUNT[level]] = total[
            OFFSET[level] : OFFSET[level] + COUNT[level]
        ].T
    spread_padded = jnp.asarray(spread_padded, BF16)
    spread_mean = jnp.asarray(mean.T, BF16)
    spread_total = jnp.asarray(total.T, BF16)
    total, mean, last = (jnp.asarray(x, BF16) for x in (total, mean, last))
    up, down, far3, far4, own1, doc0, qdoc = call(
        coarsen_kernel,
        "coarsen",
        [
            ((192, PACK), BF16),
            ((192, PACK), BF16),
            ((32, PACK), BF16),
            ((16, PACK), BF16),
            ((128, PACK), BF16),
            ((ROWS, LANES), BF16),
            ((ALL_ROWS, LANES), BF16),
        ],
        [segment_ids, k, v, total, mean, last],
    )
    low = moved(up, lambda i: i + 1)
    high = moved(down, lambda i: i - 1)
    got3 = [moved(far3, route) for route in ROUTES_3]
    got4 = [moved(far4, route) for route, _ in routes_4()]
    n3, n4 = len(got3), len(got4)
    layer_out, d_w, p, g, d_side, q_all, kw, vw = call(
        functools.partial(forward_kernel, n3, n4),
        "forward",
        [
            ((ROWS, WIDTH), BF16),
            ((WIDTH, WIDTH), F32),
            ((PAIRS, P_ROWS, 256), BF16),
            ((ALL_ROWS, WIDTH), BF16),
            ((ALL_ROWS, WIDTH), BF16),
            ((ALL_ROWS, WIDTH), BF16),
            ((sum(KEYS), WIDTH), BF16),
            ((sum(KEYS), WIDTH), BF16),
        ],
        [q, k, v, doc0, qdoc, own1, low, high, *got3, *got4]
        + [w_out, grad_out, total, mean, spread_padded, pos_q, pos_k],
    )
    d_w = lax.psum_scatter(d_w, "ctx", scatter_dimension=0, tiled=True)
    d_w = lax.psum(d_w, "dp").astype(BF16)
    outs = call(
        functools.partial(backward_kernel, n3, n4),
        "backward",
        [
            ((ROWS, WIDTH), BF16),
            ((ROWS, WIDTH), F32),
            ((ROWS, WIDTH), F32),
            ((192, 2 * WIDTH), BF16),
            ((192, 2 * WIDTH), BF16),
        ]
        + [((32, 2 * WIDTH), BF16)] * n3
        + [((16, 2 * WIDTH), BF16)] * n4,
        [p, g, d_side, q_all, kw, vw, spread_mean, spread_total],
    )
    d_q, own_k, own_v, to_low, to_high = outs[:5]
    low_back = moved(to_low, lambda i: i - 1)
    high_back = moved(to_high, lambda i: i + 1)
    back3 = [moved(x, route, back=True) for x, route in zip(outs[5 : 5 + n3], ROUTES_3)]
    back4 = [moved(x, route, back=True) for x, (route, _) in zip(outs[5 + n3 :], routes_4())]
    d_k, d_v = call(
        functools.partial(gather_kernel, n3, n4),
        "combine",
        [((ROWS, WIDTH), BF16)] * 2,
        [own_k, own_v, low_back, high_back, spread_mean, spread_total, *back3, *back4],
    )
    return layer_out[None], d_q[None], d_k[None], d_v[None], d_w


def solution(mesh):
    tokens = P("dp", "ctx", None)
    return jax.shard_map(
        body,
        mesh=mesh,
        in_specs=(tokens, tokens, tokens, P("dp", "ctx"), P(), tokens),
        out_specs=(tokens, tokens, tokens, tokens, P("ctx", None)),
        check_vma=False,
    )
```

```python
import functools

import jax
import jax.numpy as jnp
from jax import lax
from jax.experimental import pallas as pl
from jax.experimental.pallas import tpu as pltpu
from jax.sharding import PartitionSpec as P

HEAD_DIM = 64
BLOCK = 64
HALF = 32
LEVELS = 4
ROWS = 256
WIDTH = 512
PAIRS = 4
LANES = 128
DOCS = 4
NEGATIVE = -1e30
BLOCKED = -2e30
SCALE = HEAD_DIM**-0.5
PACK = 2 * WIDTH + LANES
COUNT = (256, 128, 64, 32, 16)
AT = (0, 256, 384, 448, 480)
ALL_ROWS = 496
F32 = jnp.float32
BF16 = jnp.bfloat16

GROUPS = (
    (0, 0, 128, 256),
    (0, 128, 128, 256),
    (1, 0, 128, 256),
    (2, 0, 64, 128),
    (3, 0, 32, 96),
    (4, 0, 16, 96),
)
NEAR = (0, 1, 2, 3)
FAR = (4, 5)
P_AT = {0: 0, 1: 256, 2: 512, 3: 768, 4: 0, 5: 64}
P_NEAR, P_FAR = 896, 96


def iota(shape, dim):
    return lax.broadcasted_iota(jnp.int32, shape, dim)


def gather_table(level, value=1.0):
    shape = (COUNT[level], ROWS)
    return jnp.where(iota(shape, 1) // 2**level == iota(shape, 0), value, 0.0).astype(BF16)


def spread_table(level, value=1.0):
    shape = (ROWS, COUNT[level])
    return jnp.where(iota(shape, 0) // 2**level == iota(shape, 1), value, 0.0).astype(BF16)


def last_table(level):
    shape = (COUNT[level], ROWS)
    last = iota(shape, 0) * 2**level + (2**level - 1)
    return jnp.where(iota(shape, 1) == last, 1.0, 0.0).astype(BF16)


def query_place(index):
    level, _, rows, _ = GROUPS[index]
    size = BLOCK if level == 0 else HALF
    shape = (rows, LANES)
    return jnp.where(iota(shape, 0) // size + 8 == iota(shape, 1), 1.0, 0.0).astype(BF16)


def key_place(index):
    level, _, _, keys = GROUPS[index]
    shape = (keys, LANES)
    row, place = iota(shape, 0), iota(shape, 1) - 8
    if level == 0:
        apart = row // BLOCK - place
        blocked = (apart < 0) | (apart > 2)
        places = 2
    elif level == 1:
        there, here = row // HALF, place + 2
        block_apart = jnp.abs(there // 2 - (place + 2) // 2)
        blocked = (block_apart > 1) | (jnp.abs(there - here) < 2)
        places = 4
    else:
        blocked = row // HALF == place + 1
        places = 2
    blocked = blocked & (place >= 0) & (place < places)
    return jnp.where(blocked, BLOCKED, 0.0).astype(BF16)


def dot(a, b, a_dim=1, b_dim=0):
    return lax.dot_general(a, b, (((a_dim,), (b_dim,)), ((), ())), preferred_element_type=F32)


def split(x):
    high = x.astype(BF16)
    return high, (x - high.astype(F32)).astype(BF16)


def head_lanes(rows, width=LANES):
    return iota((rows, width), 1) % LANES < HEAD_DIM


def stacked(x):
    first = head_lanes(x.shape[0]).astype(F32).astype(BF16)
    return jnp.concatenate([x * first, x * (1 - first)], axis=0)


def unstacked(x, rows):
    return jnp.where(head_lanes(rows, x.shape[1]), x[:rows], x[rows:])


def lanes_of(pair, part=0):
    return slice(part * WIDTH + pair * LANES, part * WIDTH + (pair + 1) * LANES)


DOC_LANES = slice(2 * WIDTH, PACK)


def near_window(index, own0, own1, low, high, lanes):
    def rim(ref, level):
        return ref[BLOCK * level : BLOCK * (level + 1), lanes]

    if index == 0:
        parts = [rim(low, 0), own0[0:192, lanes]]
    elif index == 1:
        parts = [own0[64:256, lanes], rim(high, 0)]
    elif index == 2:
        parts = [rim(low, 1), own1[:, lanes], rim(high, 1)]
    else:
        parts = [rim(low, 2), rim(high, 2)]
    return jnp.concatenate(parts, axis=0)


def far_window(refs, lanes):
    return jnp.concatenate([ref[:, lanes] for ref in refs], axis=0)


def fetch(sources, targets, sems):
    copies = [
        pltpu.make_async_copy(source, target, sems.at[i])
        for i, (source, target) in enumerate(zip(sources, targets))
    ]
    for copy in copies:
        copy.start()
    return copies


def coarsen_kernel(seg, k_hbm, v_hbm, up, down, far3, far4, own0, own1, qdoc, k, v, sems):
    copies = fetch((k_hbm, v_hbm), (k, v), sems)
    marks = jnp.where(seg[...] == iota((LANES, ROWS), 0), 1.0, 0.0).T.astype(BF16)

    def key_side(x):
        doc = iota(x.shape, 1) < DOCS
        return jnp.where(doc, (1.0 - x.astype(F32)) * BLOCKED, 0.0).astype(BF16)

    for copy in copies:
        copy.wait()
    levels = [(k[...], v[...], key_side(marks))]
    qdoc[0:ROWS] = marks
    for level in range(1, LEVELS + 1):
        marks_c = dot(last_table(level), marks).astype(BF16)
        qdoc[AT[level] : AT[level] + COUNT[level]] = marks_c
        keys = dot(gather_table(level, 0.5**level), levels[0][0]).astype(BF16)
        values = dot(gather_table(level), levels[0][1]).astype(BF16)
        levels.append((keys, values, key_side(marks_c)))

    def put(ref, at, level, start, stop):
        for part, lanes in zip(
            levels[level], (slice(0, WIDTH), slice(WIDTH, 2 * WIDTH), DOC_LANES)
        ):
            ref[at : at + stop - start, lanes] = part[start:stop]

    for level in range(3):
        put(up, BLOCK * level, level, COUNT[level] - BLOCK, COUNT[level])
        put(down, BLOCK * level, level, 0, BLOCK)
    put(far3, 0, 3, 0, COUNT[3])
    put(far4, 0, 4, 0, COUNT[4])
    put(own0, 0, 0, 0, COUNT[0])
    put(own1, 0, 1, 0, COUNT[1])


def prepare_kernel(q_hbm, d_hbm, w_hbm, q_out, grad_att, w, d_out, q, sems):
    copies = fetch((q_hbm, d_hbm, w_hbm), (q, d_out, w), sems)
    copies[0].wait()
    for level in range(LEVELS + 1):
        queries = q[...] if level == 0 else dot(gather_table(level, 0.5**level), q[...]).astype(BF16)
        q_out[AT[level] : AT[level] + COUNT[level]] = (queries * SCALE).astype(BF16)
    copies[1].wait()
    copies[2].wait()
    grad_att[...] = dot(d_out[...], w[...], 1, 1)


def attend(queries, query_docs, keys, key_docs, values):
    rows = queries.shape[0]
    scores = dot(
        jnp.concatenate([stacked(queries), query_docs], axis=1),
        jnp.concatenate([keys, key_docs], axis=1),
        1,
        1,
    )
    peak = jnp.maximum(jnp.max(scores, axis=1, keepdims=True), NEGATIVE)
    peak = peak.astype(BF16).astype(F32)
    p = jnp.exp(scores - peak).astype(BF16)
    ones = jnp.ones(values.shape, BF16)
    both = unstacked(dot(p, jnp.concatenate([values, ones], axis=1)), rows)
    wide_peak = jnp.where(head_lanes(rows), peak[:rows], peak[rows:])
    return p, jnp.concatenate([both, wide_peak], axis=1)


def docs_of(index, qdoc):
    level, start, rows, _ = GROUPS[index]
    docs = qdoc[AT[level] + start : AT[level] + start + rows]
    if index in NEAR:
        docs = docs + query_place(index)
    return jnp.concatenate([docs, docs], axis=0)


def near_kernel(q_all, qdoc, own0, own1, low, high, p_out, fine, coarse):
    for index in NEAR:
        level, start, rows, keys = GROUPS[index]
        at = AT[level] + start
        query_docs = docs_of(index, qdoc)
        key_docs = near_window(index, own0, own1, low, high, DOC_LANES) + key_place(index)
        for pair in range(PAIRS):
            window = [
                near_window(index, own0, own1, low, high, lanes_of(pair, part)) for part in (0, 1)
            ]
            p, stats = attend(
                q_all[at : at + rows, lanes_of(pair)], query_docs, window[0], key_docs, window[1]
            )
            p_out[pair, P_AT[index] : P_AT[index] + 2 * rows, 0:keys] = p
            if level == 0:
                fine[pair, at : at + rows] = stats
            else:
                coarse[pair, at - ROWS : at - ROWS + rows] = stats.astype(BF16)


def merge_kernel(n3, n4, q_all, qdoc, fine, coarse, grad_att, w, *refs):
    far = (refs[:n3], refs[n3 : n3 + n4])
    layer_out, attended_out, p_out, g_out, d_side = refs[n3 + n4 :]
    docs = [(docs_of(index, qdoc), far_window(ref, DOC_LANES)) for index, ref in zip(FAR, far)]
    shape = (LANES, LANES)
    same_head = jnp.where(iota(shape, 0) // HEAD_DIM == iota(shape, 1) // HEAD_DIM, 1.0, 0.0)
    same_head = same_head.astype(BF16)
    result = jnp.zeros((ROWS, WIDTH), F32)
    spreads = [None] + [spread_table(level) for level in range(1, LEVELS + 1)]
    gathers = [None] + [gather_table(level) for level in range(1, LEVELS + 1)]
    for pair in range(PAIRS):
        cols = lanes_of(pair)
        packed = [None, coarse[pair, 0:128], coarse[pair, 128:192]]
        for index, ref, (query_docs, key_docs) in zip(FAR, far, docs):
            level, _, rows, keys = GROUPS[index]
            p, stats = attend(
                q_all[AT[level] : AT[level] + rows, cols],
                query_docs,
                far_window(ref, lanes_of(pair)),
                key_docs,
                far_window(ref, lanes_of(pair, 1)),
            )
            p_out[pair, P_AT[index] : P_AT[index] + 2 * rows, 0:keys] = p
            packed.append(stats.astype(BF16))
        wide = [fine[pair]] + [
            dot(spreads[level], packed[level]) for level in range(1, LEVELS + 1)
        ]
        levels = [[x[:, LANES * i : LANES * (i + 1)] for i in range(3)] for x in wide]
        top = functools.reduce(jnp.maximum, [x[2] for x in levels])
        weights = [jnp.exp(x[2] - top) for x in levels]
        norm = functools.reduce(
            jnp.add, [wt * x[1] * float(2**i) for i, (wt, x) in enumerate(zip(weights, levels))]
        )
        numer = functools.reduce(jnp.add, [wt * x[0] for wt, x in zip(weights, levels)])
        inverse = 1.0 / norm
        attended = (numer * inverse).astype(BF16)
        attended_out[:, cols] = attended
        result = result + dot(attended, w[cols, :])
        grad = grad_att[:, cols]
        high_part, low_part = split(grad * attended.astype(F32))
        delta = dot(high_part, same_head) + dot(low_part, same_head)
        for level in range(LEVELS + 1):
            share = weights[level] * inverse
            at, rows = AT[level], COUNT[level]
            if level == 0:
                grad_c, delta_c = share * grad, share * delta
            else:
                d_high, d_low = split(share * delta)
                terms = jnp.concatenate([(share * grad).astype(BF16), d_high, d_low], axis=1)
                summed = dot(gathers[level], terms)
                grad_c = summed[:, :LANES]
                delta_c = summed[:, LANES : 2 * LANES] + summed[:, 2 * LANES :]
            g_out[at : at + rows, cols] = grad_c.astype(BF16)
            d_high, d_low = split(delta_c * -float(2**level))
            upper = iota((rows, LANES), 1) % HEAD_DIM < HALF
            d_side[at : at + rows, cols] = jnp.where(
                upper, d_high.astype(F32), d_low.astype(F32)
            ).astype(BF16)
    layer_out[...] = result.astype(BF16)


def attend_back(p, queries, grad, side, keys, values):
    rows = queries.shape[0]
    ones = jnp.where(iota(values.shape, 1) % HALF == 0, 1.0, 0.0).astype(BF16)
    grad = stacked(grad)
    product = dot(
        jnp.concatenate([grad, stacked(side)], axis=1),
        jnp.concatenate([values, ones], axis=1),
        1,
        1,
    )
    ds = (p.astype(F32) * product).astype(BF16)
    grad_q = unstacked(dot(ds, keys), rows) * SCALE
    return grad_q, dot(ds, stacked(queries), 0, 0), dot(p, grad, 0, 0)


def far_back_kernel(n3, n4, p_in, q_all, g_in, d_side, *refs):
    far = (refs[:n3], refs[n3 : n3 + n4])
    outs = refs[n3 + n4 :]
    d_q, to_far = outs[0], (outs[1 : 1 + n3], outs[1 + n3 :])
    for pair in range(PAIRS):
        cols = lanes_of(pair)
        for index, ref, to in zip(FAR, far, to_far):
            level, _, rows, keys = GROUPS[index]
            at = AT[level]
            grad_q, grad_k, grad_v = attend_back(
                p_in[pair, P_AT[index] : P_AT[index] + 2 * rows, 0:keys],
                q_all[at : at + rows, cols],
                g_in[at : at + rows, cols],
                d_side[at : at + rows, cols],
                far_window(ref, cols),
                far_window(ref, lanes_of(pair, 1)),
            )
            d_q[at - AT[3] : at - AT[3] + rows, cols] = grad_q.astype(BF16)
            size = keys // len(to)
            for i, out in enumerate(to):
                out[:, cols] = grad_k[i * size : (i + 1) * size].astype(BF16)
                out[:, lanes_of(pair, 1)] = grad_v[i * size : (i + 1) * size].astype(BF16)


def near_back_kernel(
    p_in, q_all, g_in, d_side, own0, own1, low, high, d_far, attended, d_out,
    d_q, own_k, own_v, to_low, to_high, d_w,
):
    spread = jnp.concatenate([spread_table(level, 0.5**level) for level in (1, 2, 3, 4)], axis=1)
    for pair in range(PAIRS):
        cols = lanes_of(pair)
        grads = []
        for index in NEAR:
            level, start, rows, keys = GROUPS[index]
            at = AT[level] + start
            grads.append(
                attend_back(
                    p_in[pair, P_AT[index] : P_AT[index] + 2 * rows, 0:keys],
                    q_all[at : at + rows, cols],
                    g_in[at : at + rows, cols],
                    d_side[at : at + rows, cols],
                    near_window(index, own0, own1, low, high, cols),
                    near_window(index, own0, own1, low, high, lanes_of(pair, 1)),
                )
            )
        coarse = [x[0].astype(BF16) for x in grads[2:]] + [d_far[:, cols]]
        whole = jnp.concatenate([x[0] for x in grads[:2]], axis=0)
        d_q[:, cols] = (whole + dot(spread, jnp.concatenate(coarse, axis=0))).astype(BF16)
        for part, own, value in ((0, own_k, 0.5), (1, own_v, 1.0)):
            a, b, c, d = (x[1 + part] for x in grads)
            lanes = lanes_of(pair, part)
            middle = jnp.concatenate([a[64:128], a[128:256] + b[0:128], b[128:192]], axis=0)
            own[:, cols] = middle + dot(spread_table(1, value), c[64:192].astype(BF16))
            to_low[:, lanes] = jnp.concatenate([a[:64], c[:64], d[:64]], axis=0).astype(BF16)
            to_high[:, lanes] = jnp.concatenate([b[192:], c[192:], d[64:]], axis=0).astype(BF16)
        d_w[cols, :] = dot(attended[:, cols], d_out[...], 0, 0).astype(BF16)


def combine_kernel(n3, n4, own_k, own_v, low, high, *refs):
    from3, from4, (d_k, d_v) = refs[:n3], refs[n3 : n3 + n4], refs[n3 + n4 :]
    for part, own, out in ((0, own_k, d_k), (1, own_v, d_v)):
        lanes = slice(part * WIDTH, (part + 1) * WIDTH)
        table = jnp.concatenate(
            [spread_table(level, 1.0 if part else 0.5**level) for level in (1, 2, 3, 4)], axis=1
        )

        def rim(ref, level):
            return ref[BLOCK * level : BLOCK * (level + 1), lanes].astype(F32)

        def summed(parts):
            return functools.reduce(jnp.add, [ref[:, lanes].astype(F32) for ref in parts])

        coarse = jnp.concatenate(
            [
                rim(high, 1),
                rim(low, 1),
                rim(low, 2) + rim(high, 2),
                summed(from3),
                summed(from4),
            ],
            axis=0,
        ).astype(BF16)
        whole = own[...] + dot(table, coarse)
        out[0:64] = (whole[0:64] + rim(high, 0)).astype(BF16)
        out[64:192] = whole[64:192].astype(BF16)
        out[192:256] = (whole[192:256] + rim(low, 0)).astype(BF16)


def call(kernel, name, outs, args, scratch=(), in_hbm=0):
    vmem, hbm = pl.BlockSpec(memory_space=pltpu.VMEM), pl.BlockSpec(memory_space=pl.ANY)
    return pl.pallas_call(
        kernel,
        name=name,
        out_shape=[jax.ShapeDtypeStruct(shape, dtype) for shape, dtype in outs],
        in_specs=[vmem] * (len(args) - in_hbm) + [hbm] * in_hbm,
        out_specs=[vmem] * len(outs),
        scratch_shapes=scratch,
        compiler_params=pltpu.CompilerParams(vmem_limit_bytes=48 * 1024 * 1024),
    )(*args)


def moved(x, route, back=False):
    count = lax.axis_size("ctx")
    pairs = [(i, route(i) % count) for i in range(count)]
    if back:
        pairs = [(b, a) for a, b in pairs]
    return lax.ppermute(x, "ctx", pairs)


ROUTES_3 = (
    lambda i: i + 2,
    lambda i: i - 2,
    lambda i: i - 3 if i % 2 else i + 3,
)


def route_4(shift, swap):
    def route(i):
        pair, side = i // 2, i % 2
        pair = pair + shift if shift else pair + (-3 if pair % 2 else 3)
        return 2 * pair + (side ^ swap)

    return route


ROUTES_4 = tuple(route_4(shift, swap) for shift in (2, -2, 0) for swap in (0, 1))


def body(queries, key_rows, value_rows, segment_ids, w_out, d_out):
    q, k, v, grad_out = queries[0], key_rows[0], value_rows[0], d_out[0]
    tokens, dma = (ROWS, WIDTH), pltpu.SemaphoreType.DMA
    up, down, far3, far4, own0, own1, qdoc = call(
        coarsen_kernel,
        "coarsen",
        [((192, PACK), BF16), ((192, PACK), BF16), ((32, PACK), BF16), ((16, PACK), BF16)]
        + [((ROWS, PACK), BF16), ((128, PACK), BF16), ((ALL_ROWS, LANES), BF16)],
        [segment_ids, k, v],
        [pltpu.VMEM(tokens, BF16), pltpu.VMEM(tokens, BF16), dma((2,))],
        in_hbm=2,
    )
    low = moved(up, lambda i: i + 1)
    high = moved(down, lambda i: i - 1)
    got = [moved(far3, route) for route in ROUTES_3] + [moved(far4, route) for route in ROUTES_4]
    n3, n4 = len(ROUTES_3), len(ROUTES_4)
    q_all, grad_att, w, grad_rows = call(
        prepare_kernel,
        "prepare",
        [((ALL_ROWS, WIDTH), BF16), (tokens, F32), ((WIDTH, WIDTH), BF16), (tokens, BF16)],
        [q, grad_out, w_out],
        [pltpu.VMEM(tokens, BF16), dma((3,))],
        in_hbm=3,
    )
    near = (own0, own1, low, high)
    p_near, fine, coarse = call(
        near_kernel,
        "near",
        [
            ((PAIRS, P_NEAR, 256), BF16),
            ((PAIRS, ROWS, 3 * LANES), F32),
            ((PAIRS, 192, 3 * LANES), BF16),
        ],
        [q_all, qdoc, *near],
    )
    layer_out, attended, p_far, g, d_side = call(
        functools.partial(merge_kernel, n3, n4),
        "merge",
        [(tokens, BF16), (tokens, BF16), ((PAIRS, P_FAR, LANES), BF16)]
        + [((ALL_ROWS, WIDTH), BF16)] * 2,
        [q_all, qdoc, fine, coarse, grad_att, w, *got],
    )
    d_far, *to_far = call(
        functools.partial(far_back_kernel, n3, n4),
        "far_back",
        [((48, WIDTH), BF16)]
        + [((32, 2 * WIDTH), BF16)] * n3
        + [((16, 2 * WIDTH), BF16)] * n4,
        [p_far, q_all, g, d_side, *got],
    )
    back = [moved(x, route, back=True) for x, route in zip(to_far, ROUTES_3 + ROUTES_4)]
    d_q, own_k, own_v, to_low, to_high, d_w = call(
        near_back_kernel,
        "near_back",
        [(tokens, BF16), (tokens, F32), (tokens, F32)]
        + [((192, 2 * WIDTH), BF16)] * 2
        + [((WIDTH, WIDTH), BF16)],
        [p_near, q_all, g, d_side, *near, d_far, attended, grad_rows],
    )
    low_back = moved(to_low, lambda i: i - 1)
    high_back = moved(to_high, lambda i: i + 1)
    count, dp_count = lax.axis_size("ctx"), lax.axis_size("dp")
    parts = d_w.reshape(count, WIDTH // count, WIDTH)
    parts = lax.all_to_all(parts, "ctx", 0, 0, tiled=True)
    mine = jnp.sum(parts.astype(F32), axis=0)
    copies = jnp.broadcast_to(mine[None], (dp_count,) + mine.shape)
    d_w = jnp.sum(lax.all_to_all(copies, "dp", 0, 0, tiled=True), axis=0).astype(BF16)
    d_k, d_v = call(
        functools.partial(combine_kernel, n3, n4),
        "combine",
        [(tokens, BF16)] * 2,
        [own_k, own_v, low_back, high_back, *back],
    )
    return layer_out[None], d_q[None], d_k[None], d_v[None], d_w


def solution(mesh):
    tokens = P("dp", "ctx", None)
    return jax.shard_map(
        body,
        mesh=mesh,
        in_specs=(tokens, tokens, tokens, P("dp", "ctx"), P(), tokens),
        out_specs=(tokens, tokens, tokens, tokens, P("ctx", None)),
        check_vma=False,
    )
```

```python
import functools

import jax
import jax.numpy as jnp
from jax import lax
from jax.experimental import pallas as pl
from jax.experimental.pallas import tpu as pltpu
from jax.sharding import PartitionSpec as P

HEAD_DIM = 64
BLOCK = 64
HALF = 32
LEVELS = 4
ROWS = 256
WIDTH = 512
PAIRS = 4
LANES = 128
DOCS = 4
NEGATIVE = -1e30
BLOCKED = -2e30
SCALE = HEAD_DIM**-0.5
PACK = 2 * WIDTH + LANES
COUNT = (256, 128, 64, 32, 16)
AT = (0, 256, 384, 448, 480)
ALL_ROWS = 496
F32 = jnp.float32
BF16 = jnp.bfloat16
VMEM_MIB = 20

GROUPS = (
    (0, 0, 128, 256),
    (0, 128, 128, 256),
    (1, 0, 128, 256),
    (2, 0, 64, 128),
    (3, 0, 32, 96),
    (4, 0, 16, 96),
)
NEAR = (0, 1, 2, 3)
FAR = (4, 5)
P_AT = {0: 0, 1: 256, 2: 512, 3: 768, 4: 0, 5: 64}
P_NEAR, P_FAR = 896, 96


def iota(shape, dim):
    return lax.broadcasted_iota(jnp.int32, shape, dim)


def gather_table(level, value=1.0):
    shape = (COUNT[level], ROWS)
    return jnp.where(iota(shape, 1) // 2**level == iota(shape, 0), value, 0.0).astype(BF16)


def spread_table(level, value=1.0):
    shape = (ROWS, COUNT[level])
    return jnp.where(iota(shape, 0) // 2**level == iota(shape, 1), value, 0.0).astype(BF16)


def last_table(level):
    shape = (COUNT[level], ROWS)
    last = iota(shape, 0) * 2**level + (2**level - 1)
    return jnp.where(iota(shape, 1) == last, 1.0, 0.0).astype(BF16)


def query_place(index):
    level, _, rows, _ = GROUPS[index]
    size = BLOCK if level == 0 else HALF
    shape = (rows, LANES)
    return jnp.where(iota(shape, 0) // size + 8 == iota(shape, 1), 1.0, 0.0).astype(BF16)


def key_place(index):
    level, _, _, keys = GROUPS[index]
    shape = (keys, LANES)
    row, place = iota(shape, 0), iota(shape, 1) - 8
    if level == 0:
        apart = row // BLOCK - place
        blocked = (apart < 0) | (apart > 2)
        places = 2
    elif level == 1:
        there, here = row // HALF, place + 2
        block_apart = jnp.abs(there // 2 - (place + 2) // 2)
        blocked = (block_apart > 1) | (jnp.abs(there - here) < 2)
        places = 4
    else:
        blocked = row // HALF == place + 1
        places = 2
    blocked = blocked & (place >= 0) & (place < places)
    return jnp.where(blocked, BLOCKED, 0.0).astype(BF16)


def dot(a, b, a_dim=1, b_dim=0):
    return lax.dot_general(a, b, (((a_dim,), (b_dim,)), ((), ())), preferred_element_type=F32)


def split(x):
    high = x.astype(BF16)
    return high, (x - high.astype(F32)).astype(BF16)


def head_lanes(rows, width=LANES):
    return iota((rows, width), 1) % LANES < HEAD_DIM


def stacked(x):
    first = head_lanes(x.shape[0]).astype(F32).astype(BF16)
    return jnp.concatenate([x * first, x * (1 - first)], axis=0)


def unstacked(x, rows):
    return jnp.where(head_lanes(rows, x.shape[1]), x[:rows], x[rows:])


def lanes_of(pair, part=0):
    return slice(part * WIDTH + pair * LANES, part * WIDTH + (pair + 1) * LANES)


DOC_LANES = slice(2 * WIDTH, PACK)


def near_window(index, own0, own1, low, high, lanes):
    def rim(ref, level):
        return ref[BLOCK * level : BLOCK * (level + 1), lanes]

    if index == 0:
        parts = [rim(low, 0), own0[0:192, lanes]]
    elif index == 1:
        parts = [own0[64:256, lanes], rim(high, 0)]
    elif index == 2:
        parts = [rim(low, 1), own1[:, lanes], rim(high, 1)]
    else:
        parts = [rim(low, 2), rim(high, 2)]
    return jnp.concatenate(parts, axis=0)


def far_window(refs, lanes):
    return jnp.concatenate([ref[:, lanes] for ref in refs], axis=0)


def fetch(sources, targets, sems):
    copies = [
        pltpu.make_async_copy(source, target, sems.at[i])
        for i, (source, target) in enumerate(zip(sources, targets))
    ]
    for copy in copies:
        copy.start()
    return copies


def coarsen_kernel(
    seg_hbm, k_hbm, v_hbm, up, down, far3, far4, own0, own1, qdoc, seg, k, v, sems
):
    copies = fetch((seg_hbm, k_hbm, v_hbm), (seg, k, v), sems)
    copies[0].wait()
    marks = jnp.where(seg[...] == iota((LANES, ROWS), 0), 1.0, 0.0).T.astype(BF16)

    def key_side(x):
        doc = iota(x.shape, 1) < DOCS
        return jnp.where(doc, (1.0 - x.astype(F32)) * BLOCKED, 0.0).astype(BF16)

    copies[1].wait()
    copies[2].wait()
    levels = [(k[...], v[...], key_side(marks))]
    qdoc[0:ROWS] = marks
    for level in range(1, LEVELS + 1):
        marks_c = dot(last_table(level), marks).astype(BF16)
        qdoc[AT[level] : AT[level] + COUNT[level]] = marks_c
        keys = dot(gather_table(level, 0.5**level), levels[0][0]).astype(BF16)
        values = dot(gather_table(level), levels[0][1]).astype(BF16)
        levels.append((keys, values, key_side(marks_c)))

    def put(ref, at, level, start, stop):
        for part, lanes in zip(
            levels[level], (slice(0, WIDTH), slice(WIDTH, 2 * WIDTH), DOC_LANES)
        ):
            ref[at : at + stop - start, lanes] = part[start:stop]

    for level in range(3):
        put(up, BLOCK * level, level, COUNT[level] - BLOCK, COUNT[level])
        put(down, BLOCK * level, level, 0, BLOCK)
    put(far3, 0, 3, 0, COUNT[3])
    put(far4, 0, 4, 0, COUNT[4])
    put(own0, 0, 0, 0, COUNT[0])
    put(own1, 0, 1, 0, COUNT[1])


def prepare_kernel(
    far3_in, far4_in, q_hbm, d_hbm, w_hbm, far3, far4, q_out, grad_att, w, d_out, q, sems
):
    copies = fetch((q_hbm, d_hbm, w_hbm), (q, d_out, w), sems)
    far3[...] = far3_in[...]
    far4[...] = far4_in[...]
    copies[0].wait()
    for level in range(LEVELS + 1):
        queries = q[...] if level == 0 else dot(gather_table(level, 0.5**level), q[...]).astype(BF16)
        q_out[AT[level] : AT[level] + COUNT[level]] = (queries * SCALE).astype(BF16)
    copies[1].wait()
    copies[2].wait()
    grad_att[...] = dot(d_out[...], w[...], 1, 1)


def attend(queries, query_docs, keys, key_docs, values):
    rows = queries.shape[0]
    scores = dot(
        jnp.concatenate([stacked(queries), query_docs], axis=1),
        jnp.concatenate([keys, key_docs], axis=1),
        1,
        1,
    )
    peak = jnp.maximum(jnp.max(scores, axis=1, keepdims=True), NEGATIVE)
    peak = peak.astype(BF16).astype(F32)
    p = jnp.exp(scores - peak).astype(BF16)
    ones = jnp.ones(values.shape, BF16)
    both = unstacked(dot(p, jnp.concatenate([values, ones], axis=1)), rows)
    wide_peak = jnp.where(head_lanes(rows), peak[:rows], peak[rows:])
    return p, jnp.concatenate([both, wide_peak], axis=1)


def docs_of(index, qdoc):
    level, start, rows, _ = GROUPS[index]
    docs = qdoc[AT[level] + start : AT[level] + start + rows]
    if index in NEAR:
        docs = docs + query_place(index)
    return jnp.concatenate([docs, docs], axis=0)


def near_kernel(q_all, qdoc, own0, own1, low, high, p_out, fine, coarse):
    for index in NEAR:
        level, start, rows, keys = GROUPS[index]
        at = AT[level] + start
        query_docs = docs_of(index, qdoc)
        key_docs = near_window(index, own0, own1, low, high, DOC_LANES) + key_place(index)
        for pair in range(PAIRS):
            window = [
                near_window(index, own0, own1, low, high, lanes_of(pair, part)) for part in (0, 1)
            ]
            p, stats = attend(
                q_all[at : at + rows, lanes_of(pair)], query_docs, window[0], key_docs, window[1]
            )
            p_out[pair, P_AT[index] : P_AT[index] + 2 * rows, 0:keys] = p
            if level == 0:
                fine[pair, at : at + rows] = stats
            else:
                coarse[pair, at - ROWS : at - ROWS + rows] = stats.astype(BF16)


def far_refs(refs):
    below, above, four_a, four_b, four_c, partner = refs
    return (
        (below, above, partner.at[0:32]),
        (four_a, four_b, four_c, partner.at[32:80]),
    )


def block_at(block):
    x, y, core = block // 8, block // 2 % 4, block % 2
    return 16 * (16 * core + 4 * y + x)


def merge_kernel(q_all, qdoc, fine, coarse, grad_att, d_out, *refs):
    far = far_refs(refs[:6])
    attended_out, d_w, p_out, g_out, d_side = refs[6:]
    docs = [(docs_of(index, qdoc), far_window(ref, DOC_LANES)) for index, ref in zip(FAR, far)]
    shape = (LANES, LANES)
    same_head = jnp.where(iota(shape, 0) // HEAD_DIM == iota(shape, 1) // HEAD_DIM, 1.0, 0.0)
    same_head = same_head.astype(BF16)
    spreads = [None] + [spread_table(level) for level in range(1, LEVELS + 1)]
    gathers = [None] + [gather_table(level) for level in range(1, LEVELS + 1)]
    for pair in range(PAIRS):
        cols = lanes_of(pair)
        packed = [None, coarse[pair, 0:128], coarse[pair, 128:192]]
        for index, ref, (query_docs, key_docs) in zip(FAR, far, docs):
            level, _, rows, keys = GROUPS[index]
            p, stats = attend(
                q_all[AT[level] : AT[level] + rows, cols],
                query_docs,
                far_window(ref, lanes_of(pair)),
                key_docs,
                far_window(ref, lanes_of(pair, 1)),
            )
            p_out[pair, P_AT[index] : P_AT[index] + 2 * rows, 0:keys] = p
            packed.append(stats.astype(BF16))
        wide = [fine[pair]] + [
            dot(spreads[level], packed[level]) for level in range(1, LEVELS + 1)
        ]
        levels = [[x[:, LANES * i : LANES * (i + 1)] for i in range(3)] for x in wide]
        top = functools.reduce(jnp.maximum, [x[2] for x in levels])
        weights = [jnp.exp(x[2] - top) for x in levels]
        norm = functools.reduce(
            jnp.add, [wt * x[1] * float(2**i) for i, (wt, x) in enumerate(zip(weights, levels))]
        )
        numer = functools.reduce(jnp.add, [wt * x[0] for wt, x in zip(weights, levels)])
        inverse = 1.0 / norm
        attended = (numer * inverse).astype(BF16)
        grad_w = dot(attended, d_out[...], 0, 0)
        for block in range(8):
            at = block_at(8 * pair + block)
            d_w[at : at + 16] = grad_w[16 * block : 16 * (block + 1)]
        attended_out[:, cols] = attended
        grad = grad_att[:, cols]
        high_part, low_part = split(grad * attended.astype(F32))
        delta = dot(high_part, same_head) + dot(low_part, same_head)
        for level in range(LEVELS + 1):
            share = weights[level] * inverse
            at, rows = AT[level], COUNT[level]
            if level == 0:
                grad_c, delta_c = share * grad, share * delta
            else:
                d_high, d_low = split(share * delta)
                terms = jnp.concatenate([(share * grad).astype(BF16), d_high, d_low], axis=1)
                summed = dot(gathers[level], terms)
                grad_c = summed[:, :LANES]
                delta_c = summed[:, LANES : 2 * LANES] + summed[:, 2 * LANES :]
            g_out[at : at + rows, cols] = grad_c.astype(BF16)
            d_high, d_low = split(delta_c * -float(2**level))
            upper = iota((rows, LANES), 1) % HEAD_DIM < HALF
            d_side[at : at + rows, cols] = jnp.where(
                upper, d_high.astype(F32), d_low.astype(F32)
            ).astype(BF16)


def attend_back(p, queries, grad, side, keys, values):
    rows = queries.shape[0]
    ones = jnp.where(iota(values.shape, 1) % HALF == 0, 1.0, 0.0).astype(BF16)
    grad = stacked(grad)
    product = dot(
        jnp.concatenate([grad, stacked(side)], axis=1),
        jnp.concatenate([values, ones], axis=1),
        1,
        1,
    )
    ds = (p.astype(F32) * product).astype(BF16)
    grad_q = unstacked(dot(ds, keys), rows) * SCALE
    return grad_q, dot(ds, stacked(queries), 0, 0), dot(p, grad, 0, 0)


def far_back_kernel(p_in, q_all, g_in, d_side, *refs):
    far = far_refs(refs[:6])
    d_q, to_3, to_4, to_partner = refs[6:]
    to_far = (
        (to_3.at[0], to_3.at[1], to_partner.at[0:32]),
        (to_4.at[0], to_4.at[1], to_4.at[2], to_partner.at[32:80]),
    )
    for pair in range(PAIRS):
        cols = lanes_of(pair)
        for index, ref, to in zip(FAR, far, to_far):
            level, _, rows, keys = GROUPS[index]
            at = AT[level]
            grad_q, grad_k, grad_v = attend_back(
                p_in[pair, P_AT[index] : P_AT[index] + 2 * rows, 0:keys],
                q_all[at : at + rows, cols],
                g_in[at : at + rows, cols],
                d_side[at : at + rows, cols],
                far_window(ref, cols),
                far_window(ref, lanes_of(pair, 1)),
            )
            d_q[at - AT[3] : at - AT[3] + rows, cols] = grad_q.astype(BF16)
            start = 0
            for out in to:
                stop = start + out.shape[0]
                out[:, cols] = grad_k[start:stop].astype(BF16)
                out[:, lanes_of(pair, 1)] = grad_v[start:stop].astype(BF16)
                start = stop


NEAR_PARTS = ((0,), (1, 2), (3,))


def near_back(pairs, p_in, q_all, g_in, d_side, own0, own1, low, high, d_far):
    spread = jnp.concatenate([spread_table(level, 0.5**level) for level in (1, 2, 3, 4)], axis=1)
    for pair in pairs:
        cols = lanes_of(pair)
        grads = []
        for index in NEAR:
            level, start, rows, keys = GROUPS[index]
            at = AT[level] + start
            grads.append(
                attend_back(
                    p_in[pair, P_AT[index] : P_AT[index] + 2 * rows, 0:keys],
                    q_all[at : at + rows, cols],
                    g_in[at : at + rows, cols],
                    d_side[at : at + rows, cols],
                    near_window(index, own0, own1, low, high, cols),
                    near_window(index, own0, own1, low, high, lanes_of(pair, 1)),
                )
            )
        coarse = [x[0].astype(BF16) for x in grads[2:]] + [d_far[:, cols]]
        whole = jnp.concatenate([x[0] for x in grads[:2]], axis=0)
        d_q = (whole + dot(spread, jnp.concatenate(coarse, axis=0))).astype(BF16)
        own, to_low, to_high = [], [], []
        for part, value in ((0, 0.5), (1, 1.0)):
            a, b, c, d = (x[1 + part] for x in grads)
            middle = jnp.concatenate([a[64:128], a[128:256] + b[0:128], b[128:192]], axis=0)
            own.append(middle + dot(spread_table(1, value), c[64:192].astype(BF16)))
            to_low.append(jnp.concatenate([a[:64], c[:64], d[:64]], axis=0).astype(BF16))
            to_high.append(jnp.concatenate([b[192:], c[192:], d[64:]], axis=0).astype(BF16))
        yield pair, d_q, own, to_low, to_high


def near_back_first_kernel(pairs, attended, w, *refs):
    inputs, outs = refs[:9], refs[9:]
    layer_out = None
    if attended is not None:
        layer_out, result, sem = outs[-3:]
        result[...] = dot(attended[...], w[...]).astype(BF16)
        copy = pltpu.make_async_copy(result, layer_out, sem)
        copy.start()
    d_q, own_k, own_v, to_low, to_high = outs[:5]
    for pair, dq, own, low, high in near_back(pairs, *inputs):
        at = slice((pair - pairs[0]) * LANES, (pair - pairs[0] + 1) * LANES)
        d_q[:, at], own_k[:, at], own_v[:, at] = dq, own[0], own[1]
        for part in range(2):
            to_low[part, :, at], to_high[part, :, at] = low[part], high[part]
    if attended is not None:
        copy.wait()


def near_back_a_kernel(attended, w, *refs):
    near_back_first_kernel(NEAR_PARTS[0], attended, w, *refs)


def near_back_b_kernel(*refs):
    near_back_first_kernel(NEAR_PARTS[1], None, None, *refs[:9], *refs[-5:])


def near_back_c_kernel(*refs):
    inputs, earlier = refs[:9], (refs[9:12], refs[12:15])
    d_q_hbm, own_k, own_v, to_low, to_high, d_q, sems = refs[-7:]
    for pairs, (dq, low, high) in zip(NEAR_PARTS, earlier):
        cols = slice(pairs[0] * LANES, (pairs[-1] + 1) * LANES)
        d_q[:, cols] = dq[...]
        for part in range(2):
            lanes = slice(part * WIDTH + cols.start, part * WIDTH + cols.stop)
            to_low[:, lanes], to_high[:, lanes] = low[part], high[part]
    last = NEAR_PARTS[2][0] * LANES
    before = pltpu.make_async_copy(d_q.at[:, 0:last], d_q_hbm.at[:, 0:last], sems.at[0])
    before.start()
    for pair, dq, own, low, high in near_back(NEAR_PARTS[2], *inputs):
        d_q[:, lanes_of(pair)] = dq
        own_k[...], own_v[...] = own[0], own[1]
        after = pltpu.make_async_copy(
            d_q.at[:, lanes_of(pair)], d_q_hbm.at[:, lanes_of(pair)], sems.at[1]
        )
        after.start()
        for part in range(2):
            to_low[:, lanes_of(pair, part)] = low[part]
            to_high[:, lanes_of(pair, part)] = high[part]
    before.wait()
    after.wait()


def combine_kernel(*refs):
    own, (low, high), from3, from4 = (refs[0:3], refs[3:6]), refs[6:8], refs[8:10], refs[10:13]
    d_k_hbm, d_v_hbm, d_k, d_v, sems = refs[13:]
    copies = []
    for part, out, out_hbm in ((0, d_k, d_k_hbm), (1, d_v, d_v_hbm)):
        lanes = slice(part * WIDTH, (part + 1) * WIDTH)
        table = jnp.concatenate(
            [spread_table(level, 1.0 if part else 0.5**level) for level in (1, 2, 3, 4)], axis=1
        )

        def rim(ref, level):
            return ref[BLOCK * level : BLOCK * (level + 1), lanes].astype(F32)

        def summed(parts):
            return functools.reduce(jnp.add, [ref[:, lanes].astype(F32) for ref in parts])

        coarse = jnp.concatenate(
            [
                rim(high, 1),
                rim(low, 1),
                rim(low, 2) + rim(high, 2),
                summed(from3),
                summed(from4),
            ],
            axis=0,
        ).astype(BF16)
        whole = jnp.concatenate([x[...] for x in own[part]], axis=1) + dot(table, coarse)
        out[0:64] = (whole[0:64] + rim(high, 0)).astype(BF16)
        out[64:192] = whole[64:192].astype(BF16)
        out[192:256] = (whole[192:256] + rim(low, 0)).astype(BF16)
        copies.append(pltpu.make_async_copy(out, out_hbm, sems.at[part]))
        copies[-1].start()
    for copy in copies:
        copy.wait()


def call(
    kernel, name, outs, args, scratch=(), in_hbm=0, microseconds=1.0, to_hbm=()
):
    vmem, hbm = pl.BlockSpec(memory_space=pltpu.VMEM), pl.BlockSpec(memory_space=pl.ANY)
    return pl.pallas_call(
        kernel,
        name=name,
        out_shape=[jax.ShapeDtypeStruct(shape, dtype) for shape, dtype in outs],
        in_specs=[vmem] * (len(args) - in_hbm) + [hbm] * in_hbm,
        out_specs=[hbm if i in to_hbm else vmem for i in range(len(outs))],
        scratch_shapes=scratch,
        cost_estimate=pl.CostEstimate(
            flops=int(microseconds * 1e9), bytes_accessed=1 << 20, transcendentals=0
        ),
        compiler_params=pltpu.CompilerParams(vmem_limit_bytes=VMEM_MIB * 1024 * 1024),
    )(*args)


def moved(x, route):
    count = lax.axis_size("ctx")
    return lax.ppermute(x, "ctx", [(i, route(i) % count) for i in range(count)])


def partner(i):
    return i ^ 1


def third(i):
    return i - 6 if i // 2 % 2 else i + 6


ROUTES_3 = (lambda i: i + 2, lambda i: i - 2)
ROUTES_4 = (lambda i: i + 4, lambda i: i - 4, third)
BACK_3 = (lambda i: i - 2, lambda i: i + 2)
BACK_4 = (lambda i: i - 4, lambda i: i + 4, third)


def scattered(y, low, bits, after=None):
    side, count = lax.axis_index("ctx") >> low & (1 << bits) - 1, 1 << bits
    rows = y.shape[0] // count

    def part(index):
        return lax.dynamic_slice_in_dim(y, index * rows, rows)

    result = part(side)
    if after is not None:
        result, _ = lax.optimization_barrier((result, after))
    for step in range(1, count):
        message = part(side ^ step).astype(BF16)
        result = result + moved(message, lambda i, step=step: i ^ step << low).astype(F32)
    return result


def body(queries, key_rows, value_rows, segment_ids, w_out, d_out):
    q, k, v, grad_out = queries[0], key_rows[0], value_rows[0], d_out[0]
    tokens, dma = (ROWS, WIDTH), pltpu.SemaphoreType.DMA
    even = lax.axis_index("ctx") % 2 == 0
    up, down, far3, far4, own0, own1, qdoc = call(
        coarsen_kernel,
        "coarsen",
        [((192, PACK), BF16), ((192, PACK), BF16), ((32, PACK), BF16), ((16, PACK), BF16)]
        + [((ROWS, PACK), BF16), ((128, PACK), BF16), ((ALL_ROWS, LANES), BF16)],
        [segment_ids, k, v],
        [pltpu.VMEM((1, ROWS), jnp.int32)] + [pltpu.VMEM(tokens, BF16)] * 2 + [dma((3,))],
        in_hbm=3,
    )
    far3, far4, q_all, grad_att, w, grad_rows = call(
        prepare_kernel,
        "prepare",
        [((32, PACK), BF16), ((16, PACK), BF16)]
        + [((ALL_ROWS, WIDTH), BF16), (tokens, F32), ((WIDTH, WIDTH), BF16), (tokens, BF16)],
        [far3, far4, q, grad_out, w_out],
        [pltpu.VMEM(tokens, BF16), dma((3,))],
        in_hbm=3,
    )
    low = moved(up, lambda i: i + 1)
    high = moved(down, lambda i: i - 1)
    got3 = [moved(far3, route) for route in ROUTES_3]
    got4 = [moved(far4, route) for route in ROUTES_4]
    low, high, *got3 = lax.optimization_barrier((low, high, *got3))
    passed = jnp.concatenate([jnp.where(even, got3[0], got3[1]), *got4], axis=0)
    low, high, passed = lax.optimization_barrier((low, high, passed))
    far = (*got3, *got4, moved(passed, partner))
    near = (own0, own1, low, high)
    p_near, fine, coarse = call(
        near_kernel,
        "near",
        [
            ((PAIRS, P_NEAR, 256), BF16),
            ((PAIRS, ROWS, 3 * LANES), F32),
            ((PAIRS, 192, 3 * LANES), BF16),
        ],
        [q_all, qdoc, *near],
        microseconds=50,
    )
    attended, d_w, p_far, g, d_side = call(
        merge_kernel,
        "merge",
        [(tokens, BF16), ((WIDTH, WIDTH), F32), ((PAIRS, P_FAR, LANES), BF16)]
        + [((ALL_ROWS, WIDTH), BF16)] * 2,
        [q_all, qdoc, fine, coarse, grad_att, grad_rows, *far],
        microseconds=6,
    )
    d_far, to_3, to_4, to_partner = call(
        far_back_kernel,
        "far_back",
        [((48, WIDTH), BF16), ((2, 32, 2 * WIDTH), BF16)]
        + [((3, 16, 2 * WIDTH), BF16), ((80, 2 * WIDTH), BF16)],
        [p_far, q_all, g, d_side, *far],
    )
    d_w = scattered(d_w, 0, 1)
    from_partner = moved(to_partner, partner).astype(F32)
    swapped3, swapped4 = from_partner[:32], from_partner[32:].reshape(3, 16, 2 * WIDTH)
    mine = jnp.stack([jnp.where(even, swapped3, 0), jnp.where(even, 0, swapped3)])
    to_3 = (to_3.astype(F32) + mine).astype(BF16)
    to_4 = (to_4.astype(F32) + swapped4).astype(BF16)

    def part_outs(part):
        width = len(NEAR_PARTS[part]) * LANES
        return [((ROWS, width), BF16), ((ROWS, width), F32), ((ROWS, width), F32)] + [
            ((2, 192, width), BF16)
        ] * 2

    args = [p_near, q_all, g, d_side, *near, d_far]
    *part_a, layer_out = call(
        near_back_a_kernel,
        "near_back_a",
        part_outs(0) + [(tokens, BF16)],
        [attended, w, *args],
        [pltpu.VMEM(tokens, BF16), dma(())],
        microseconds=3,
        to_hbm=(5,),
    )
    part_b = call(
        near_back_b_kernel,
        "near_back_b",
        part_outs(1),
        [*args, part_a[0], to_3, d_w],
        in_hbm=3,
        microseconds=4,
    )
    back = [moved(to_3[i], route) for i, route in enumerate(BACK_3)]
    d_w = scattered(d_w, 1, 2, after=part_b[0])
    to_4, _ = lax.optimization_barrier((to_4, part_b[0]))
    d_q, own_k, own_v, to_low, to_high = call(
        near_back_c_kernel,
        "near_back_c",
        [(tokens, BF16), ((ROWS, LANES), F32), ((ROWS, LANES), F32)]
        + [((192, 2 * WIDTH), BF16)] * 2,
        [*args, part_a[0], *part_a[3:], part_b[0], *part_b[3:], to_4, d_w, *back],
        [pltpu.VMEM(tokens, BF16), dma((2,))],
        in_hbm=4,
        microseconds=2,
        to_hbm=(0,),
    )
    back += [moved(to_4[i], route) for i, route in enumerate(BACK_4)]
    d_w = scattered(d_w, 3, 2, after=to_low)
    low_back = moved(to_low, lambda i: i - 1)
    high_back = moved(to_high, lambda i: i + 1)
    dp_count = lax.axis_size("dp")
    copies = jnp.broadcast_to(d_w.astype(BF16)[None], (dp_count,) + d_w.shape)
    copies = lax.all_to_all(copies, "dp", 0, 0, tiled=True)
    d_w = jnp.sum(copies.astype(F32), axis=0).astype(BF16)
    d_k, d_v = call(
        combine_kernel,
        "combine",
        [(tokens, BF16)] * 2,
        [part_a[1], part_b[1], own_k, part_a[2], part_b[2], own_v, low_back, high_back, *back],
        [pltpu.VMEM(tokens, BF16)] * 2 + [dma((2,))],
        to_hbm=(0, 1),
    )
    return layer_out[None], d_q[None], d_k[None], d_v[None], d_w


def solution(mesh):
    tokens = P("dp", "ctx", None)
    return jax.shard_map(
        body,
        mesh=mesh,
        in_specs=(tokens, tokens, tokens, P("dp", "ctx"), P(), tokens),
        out_specs=(tokens, tokens, tokens, tokens, P("ctx", None)),
        check_vma=False,
    )
```

```python
import functools

import jax
import jax.numpy as jnp
from jax import lax
from jax.experimental import pallas as pl
from jax.experimental.pallas import tpu as pltpu
from jax.sharding import PartitionSpec as P

HEAD_DIM = 64
BLOCK = 64
HALF = 32
LEVELS = 4
ROWS = 256
WIDTH = 512
PAIRS = 4
LANES = 128
DOCS = 4
NEGATIVE = -1e30
BLOCKED = -2e30
SCALE = HEAD_DIM**-0.5
PACK = 2 * WIDTH + LANES
COUNT = (256, 128, 64, 32, 16)
AT = (0, 256, 384, 448, 480)
ALL_ROWS = 496
F32 = jnp.float32
BF16 = jnp.bfloat16
VMEM_MIB = 20

GROUPS = (
    (0, 0, 128, 256),
    (0, 128, 128, 256),
    (1, 0, 128, 256),
    (2, 0, 64, 128),
    (3, 0, 32, 96),
    (4, 0, 16, 96),
)
NEAR = (0, 1, 2, 3)
FAR = (4, 5)
P_AT = {0: 0, 1: 256, 2: 512, 3: 768, 4: 0, 5: 64}
P_NEAR, P_FAR = 896, 96


def iota(shape, dim):
    return lax.broadcasted_iota(jnp.int32, shape, dim)


def gather_table(level, value=1.0):
    shape = (COUNT[level], ROWS)
    return jnp.where(iota(shape, 1) // 2**level == iota(shape, 0), value, 0.0).astype(BF16)


def spread_table(level, value=1.0):
    shape = (ROWS, COUNT[level])
    return jnp.where(iota(shape, 0) // 2**level == iota(shape, 1), value, 0.0).astype(BF16)


def last_table(level):
    shape = (COUNT[level], ROWS)
    last = iota(shape, 0) * 2**level + (2**level - 1)
    return jnp.where(iota(shape, 1) == last, 1.0, 0.0).astype(BF16)


def query_place(index):
    level, _, rows, _ = GROUPS[index]
    size = BLOCK if level == 0 else HALF
    shape = (rows, LANES)
    return jnp.where(iota(shape, 0) // size + 8 == iota(shape, 1), 1.0, 0.0).astype(BF16)


def key_place(index):
    level, _, _, keys = GROUPS[index]
    shape = (keys, LANES)
    row, place = iota(shape, 0), iota(shape, 1) - 8
    if level == 0:
        apart = row // BLOCK - place
        blocked = (apart < 0) | (apart > 2)
        places = 2
    elif level == 1:
        there, here = row // HALF, place + 2
        block_apart = jnp.abs(there // 2 - (place + 2) // 2)
        blocked = (block_apart > 1) | (jnp.abs(there - here) < 2)
        places = 4
    else:
        blocked = row // HALF == place + 1
        places = 2
    blocked = blocked & (place >= 0) & (place < places)
    return jnp.where(blocked, BLOCKED, 0.0).astype(BF16)


def dot(a, b, a_dim=1, b_dim=0):
    return lax.dot_general(a, b, (((a_dim,), (b_dim,)), ((), ())), preferred_element_type=F32)


def split(x):
    high = x.astype(BF16)
    return high, (x - high.astype(F32)).astype(BF16)


def head_lanes(rows, width=LANES):
    return iota((rows, width), 1) % LANES < HEAD_DIM


def stacked(x):
    first = head_lanes(x.shape[0]).astype(F32).astype(BF16)
    return jnp.concatenate([x * first, x * (1 - first)], axis=0)


def unstacked(x, rows):
    return jnp.where(head_lanes(rows, x.shape[1]), x[:rows], x[rows:])


def lanes_of(pair, part=0):
    return slice(part * WIDTH + pair * LANES, part * WIDTH + (pair + 1) * LANES)


DOC_LANES = slice(2 * WIDTH, PACK)


def near_window(index, own0, own1, low, high, lanes):
    def rim(ref, level):
        return ref[BLOCK * level : BLOCK * (level + 1), lanes]

    if index == 0:
        parts = [rim(low, 0), own0[0:192, lanes]]
    elif index == 1:
        parts = [own0[64:256, lanes], rim(high, 0)]
    elif index == 2:
        parts = [rim(low, 1), own1[:, lanes], rim(high, 1)]
    else:
        parts = [rim(low, 2), rim(high, 2)]
    return jnp.concatenate(parts, axis=0)


def far_window(refs, lanes):
    return jnp.concatenate([ref[:, lanes] for ref in refs], axis=0)


def fetch(sources, targets, sems):
    copies = [
        pltpu.make_async_copy(source, target, sems.at[i])
        for i, (source, target) in enumerate(zip(sources, targets))
    ]
    for copy in copies:
        copy.start()
    return copies


def coarsen_kernel(
    seg_hbm, k_hbm, v_hbm, up, down, far3, far4, own0, own1, qdoc, seg, k, v, sems
):
    copies = fetch((seg_hbm, k_hbm, v_hbm), (seg, k, v), sems)
    copies[0].wait()
    marks = jnp.where(seg[...] == iota((LANES, ROWS), 0), 1.0, 0.0).T.astype(BF16)

    def key_side(x):
        doc = iota(x.shape, 1) < DOCS
        return jnp.where(doc, (1.0 - x.astype(F32)) * BLOCKED, 0.0).astype(BF16)

    copies[1].wait()
    copies[2].wait()
    levels = [(k[...], v[...], key_side(marks))]
    qdoc[0:ROWS] = marks
    for level in range(1, LEVELS + 1):
        marks_c = dot(last_table(level), marks).astype(BF16)
        qdoc[AT[level] : AT[level] + COUNT[level]] = marks_c
        keys = dot(gather_table(level, 0.5**level), levels[0][0]).astype(BF16)
        values = dot(gather_table(level), levels[0][1]).astype(BF16)
        levels.append((keys, values, key_side(marks_c)))

    def put(ref, at, level, start, stop):
        for part, lanes in zip(
            levels[level], (slice(0, WIDTH), slice(WIDTH, 2 * WIDTH), DOC_LANES)
        ):
            ref[at : at + stop - start, lanes] = part[start:stop]

    for level in range(3):
        put(up, BLOCK * level, level, COUNT[level] - BLOCK, COUNT[level])
        put(down, BLOCK * level, level, 0, BLOCK)
    put(far3, 0, 3, 0, COUNT[3])
    put(far4, 0, 4, 0, COUNT[4])
    put(own0, 0, 0, 0, COUNT[0])
    put(own1, 0, 1, 0, COUNT[1])


def prepare_kernel(
    far3_in, far4_in, q_hbm, d_hbm, w_hbm, far3, far4, q_out, grad_att, w, d_out, q, sems
):
    copies = fetch((q_hbm, d_hbm, w_hbm), (q, d_out, w), sems)
    far3[...] = far3_in[...]
    far4[...] = far4_in[...]
    copies[0].wait()
    for level in range(LEVELS + 1):
        queries = q[...] if level == 0 else dot(gather_table(level, 0.5**level), q[...]).astype(BF16)
        q_out[AT[level] : AT[level] + COUNT[level]] = (queries * SCALE).astype(BF16)
    copies[1].wait()
    copies[2].wait()
    grad_att[...] = dot(d_out[...], w[...], 1, 1)


def attend(queries, query_docs, keys, key_docs, values):
    rows = queries.shape[0]
    scores = dot(
        jnp.concatenate([stacked(queries), query_docs], axis=1),
        jnp.concatenate([keys, key_docs], axis=1),
        1,
        1,
    )
    peak = jnp.maximum(jnp.max(scores, axis=1, keepdims=True), NEGATIVE)
    peak = peak.astype(BF16).astype(F32)
    p = jnp.exp(scores - peak).astype(BF16)
    ones = jnp.ones(values.shape, BF16)
    both = unstacked(dot(p, jnp.concatenate([values, ones], axis=1)), rows)
    wide_peak = jnp.where(head_lanes(rows), peak[:rows], peak[rows:])
    return p, jnp.concatenate([both, wide_peak], axis=1)


def docs_of(index, qdoc):
    level, start, rows, _ = GROUPS[index]
    docs = qdoc[AT[level] + start : AT[level] + start + rows]
    if index in NEAR:
        docs = docs + query_place(index)
    return jnp.concatenate([docs, docs], axis=0)


def near_kernel(q_all, qdoc, own0, own1, low, high, p_out, fine, coarse):
    for index in NEAR:
        level, start, rows, keys = GROUPS[index]
        at = AT[level] + start
        query_docs = docs_of(index, qdoc)
        key_docs = near_window(index, own0, own1, low, high, DOC_LANES) + key_place(index)
        for pair in range(PAIRS):
            window = [
                near_window(index, own0, own1, low, high, lanes_of(pair, part)) for part in (0, 1)
            ]
            p, stats = attend(
                q_all[at : at + rows, lanes_of(pair)], query_docs, window[0], key_docs, window[1]
            )
            p_out[pair, P_AT[index] : P_AT[index] + 2 * rows, 0:keys] = p
            if level == 0:
                fine[pair, at : at + rows] = stats
            else:
                coarse[pair, at - ROWS : at - ROWS + rows] = stats.astype(BF16)


def far_refs(refs):
    below, above, four_a, four_b, four_c, partner = refs
    return (
        (below, above, partner.at[0:32]),
        (four_a, four_b, four_c, partner.at[32:80]),
    )


def block_at(block):
    x, y, core = block // 8, block // 2 % 4, block % 2
    return 16 * (16 * core + 4 * y + x)


def merge_kernel(q_all, qdoc, fine, coarse, grad_att, d_out, *refs):
    far = far_refs(refs[:6])
    attended_out, keep, give, p_out, g_out, d_side, d_w = refs[6:]
    docs = [(docs_of(index, qdoc), far_window(ref, DOC_LANES)) for index, ref in zip(FAR, far)]
    shape = (LANES, LANES)
    same_head = jnp.where(iota(shape, 0) // HEAD_DIM == iota(shape, 1) // HEAD_DIM, 1.0, 0.0)
    same_head = same_head.astype(BF16)
    spreads = [None] + [spread_table(level) for level in range(1, LEVELS + 1)]
    gathers = [None] + [gather_table(level) for level in range(1, LEVELS + 1)]
    for pair in range(PAIRS):
        cols = lanes_of(pair)
        packed = [None, coarse[pair, 0:128], coarse[pair, 128:192]]
        for index, ref, (query_docs, key_docs) in zip(FAR, far, docs):
            level, _, rows, keys = GROUPS[index]
            p, stats = attend(
                q_all[AT[level] : AT[level] + rows, cols],
                query_docs,
                far_window(ref, lanes_of(pair)),
                key_docs,
                far_window(ref, lanes_of(pair, 1)),
            )
            p_out[pair, P_AT[index] : P_AT[index] + 2 * rows, 0:keys] = p
            packed.append(stats.astype(BF16))
        wide = [fine[pair]] + [
            dot(spreads[level], packed[level]) for level in range(1, LEVELS + 1)
        ]
        levels = [[x[:, LANES * i : LANES * (i + 1)] for i in range(3)] for x in wide]
        top = functools.reduce(jnp.maximum, [x[2] for x in levels])
        weights = [jnp.exp(x[2] - top) for x in levels]
        norm = functools.reduce(
            jnp.add, [wt * x[1] * float(2**i) for i, (wt, x) in enumerate(zip(weights, levels))]
        )
        numer = functools.reduce(jnp.add, [wt * x[0] for wt, x in zip(weights, levels)])
        inverse = 1.0 / norm
        attended = (numer * inverse).astype(BF16)
        grad_w = dot(attended, d_out[...], 0, 0)
        for block in range(8):
            at = block_at(8 * pair + block)
            d_w[at : at + 16] = grad_w[16 * block : 16 * (block + 1)]
        attended_out[:, cols] = attended
        grad = grad_att[:, cols]
        high_part, low_part = split(grad * attended.astype(F32))
        delta = dot(high_part, same_head) + dot(low_part, same_head)
        for level in range(LEVELS + 1):
            share = weights[level] * inverse
            at, rows = AT[level], COUNT[level]
            if level == 0:
                grad_c, delta_c = share * grad, share * delta
            else:
                d_high, d_low = split(share * delta)
                terms = jnp.concatenate([(share * grad).astype(BF16), d_high, d_low], axis=1)
                summed = dot(gathers[level], terms)
                grad_c = summed[:, :LANES]
                delta_c = summed[:, LANES : 2 * LANES] + summed[:, 2 * LANES :]
            g_out[at : at + rows, cols] = grad_c.astype(BF16)
            d_high, d_low = split(delta_c * -float(2**level))
            upper = iota((rows, LANES), 1) % HEAD_DIM < HALF
            d_side[at : at + rows, cols] = jnp.where(
                upper, d_high.astype(F32), d_low.astype(F32)
            ).astype(BF16)
    core = lax.axis_index("ctx") % 2
    keep[...] = d_w[pl.ds(pl.multiple_of(core * 256, 256), 256)]
    give[...] = d_w[pl.ds(pl.multiple_of((1 - core) * 256, 256), 256)].astype(BF16)


def attend_back(p, queries, grad, side, keys, values):
    rows = queries.shape[0]
    ones = jnp.where(iota(values.shape, 1) % HALF == 0, 1.0, 0.0).astype(BF16)
    grad = stacked(grad)
    product = dot(
        jnp.concatenate([grad, stacked(side)], axis=1),
        jnp.concatenate([values, ones], axis=1),
        1,
        1,
    )
    ds = (p.astype(F32) * product).astype(BF16)
    grad_q = unstacked(dot(ds, keys), rows) * SCALE
    return grad_q, dot(ds, stacked(queries), 0, 0), dot(p, grad, 0, 0)


def far_back_kernel(p_in, q_all, g_in, d_side, *refs):
    far = far_refs(refs[:6])
    d_q, to_3, to_4, to_partner = refs[6:]
    to_far = (
        (to_3.at[0], to_3.at[1], to_partner.at[0:32]),
        (to_4.at[0], to_4.at[1], to_4.at[2], to_partner.at[32:80]),
    )
    for pair in range(PAIRS):
        cols = lanes_of(pair)
        for index, ref, to in zip(FAR, far, to_far):
            level, _, rows, keys = GROUPS[index]
            at = AT[level]
            grad_q, grad_k, grad_v = attend_back(
                p_in[pair, P_AT[index] : P_AT[index] + 2 * rows, 0:keys],
                q_all[at : at + rows, cols],
                g_in[at : at + rows, cols],
                d_side[at : at + rows, cols],
                far_window(ref, cols),
                far_window(ref, lanes_of(pair, 1)),
            )
            d_q[at - AT[3] : at - AT[3] + rows, cols] = grad_q.astype(BF16)
            start = 0
            for out in to:
                stop = start + out.shape[0]
                out[:, cols] = grad_k[start:stop].astype(BF16)
                out[:, lanes_of(pair, 1)] = grad_v[start:stop].astype(BF16)
                start = stop


NEAR_PARTS = ((0,), (1, 2), (3,))


def near_back(pairs, p_in, q_all, g_in, d_side, own0, own1, low, high, d_far):
    spread = jnp.concatenate([spread_table(level, 0.5**level) for level in (1, 2, 3, 4)], axis=1)
    for pair in pairs:
        cols = lanes_of(pair)
        grads = []
        for index in NEAR:
            level, start, rows, keys = GROUPS[index]
            at = AT[level] + start
            grads.append(
                attend_back(
                    p_in[pair, P_AT[index] : P_AT[index] + 2 * rows, 0:keys],
                    q_all[at : at + rows, cols],
                    g_in[at : at + rows, cols],
                    d_side[at : at + rows, cols],
                    near_window(index, own0, own1, low, high, cols),
                    near_window(index, own0, own1, low, high, lanes_of(pair, 1)),
                )
            )
        coarse = [x[0].astype(BF16) for x in grads[2:]] + [d_far[:, cols]]
        whole = jnp.concatenate([x[0] for x in grads[:2]], axis=0)
        d_q = (whole + dot(spread, jnp.concatenate(coarse, axis=0))).astype(BF16)
        own, to_low, to_high = [], [], []
        for part, value in ((0, 0.5), (1, 1.0)):
            a, b, c, d = (x[1 + part] for x in grads)
            middle = jnp.concatenate([a[64:128], a[128:256] + b[0:128], b[128:192]], axis=0)
            own.append(middle + dot(spread_table(1, value), c[64:192].astype(BF16)))
            to_low.append(jnp.concatenate([a[:64], c[:64], d[:64]], axis=0).astype(BF16))
            to_high.append(jnp.concatenate([b[192:], c[192:], d[64:]], axis=0).astype(BF16))
        yield pair, d_q, own, to_low, to_high


def near_back_first_kernel(pairs, attended, w, *refs):
    inputs, outs = refs[:9], refs[9:]
    layer_out = None
    if attended is not None:
        layer_out, result, sem = outs[-3:]
        result[...] = dot(attended[...], w[...]).astype(BF16)
        copy = pltpu.make_async_copy(result, layer_out, sem)
        copy.start()
    d_q, own_k, own_v, to_low, to_high = outs[:5]
    for pair, dq, own, low, high in near_back(pairs, *inputs):
        at = slice((pair - pairs[0]) * LANES, (pair - pairs[0] + 1) * LANES)
        d_q[:, at], own_k[:, at], own_v[:, at] = dq, own[0], own[1]
        for part in range(2):
            to_low[part, :, at], to_high[part, :, at] = low[part], high[part]
    if attended is not None:
        copy.wait()


def near_back_a_kernel(attended, w, *refs):
    near_back_first_kernel(NEAR_PARTS[0], attended, w, *refs)


def near_back_b_kernel(*refs):
    near_back_first_kernel(NEAR_PARTS[1], None, None, *refs[:9], *refs[-5:])


def near_back_c_kernel(*refs):
    inputs, earlier = refs[:9], (refs[9:12], refs[12:15])
    d_q_hbm, own_k, own_v, to_low, to_high, d_q, sems = refs[-7:]
    for pairs, (dq, low, high) in zip(NEAR_PARTS, earlier):
        cols = slice(pairs[0] * LANES, (pairs[-1] + 1) * LANES)
        d_q[:, cols] = dq[...]
        for part in range(2):
            lanes = slice(part * WIDTH + cols.start, part * WIDTH + cols.stop)
            to_low[:, lanes], to_high[:, lanes] = low[part], high[part]
    last = NEAR_PARTS[2][0] * LANES
    before = pltpu.make_async_copy(d_q.at[:, 0:last], d_q_hbm.at[:, 0:last], sems.at[0])
    before.start()
    for pair, dq, own, low, high in near_back(NEAR_PARTS[2], *inputs):
        d_q[:, lanes_of(pair)] = dq
        own_k[...], own_v[...] = own[0], own[1]
        after = pltpu.make_async_copy(
            d_q.at[:, lanes_of(pair)], d_q_hbm.at[:, lanes_of(pair)], sems.at[1]
        )
        after.start()
        for part in range(2):
            to_low[:, lanes_of(pair, part)] = low[part]
            to_high[:, lanes_of(pair, part)] = high[part]
    before.wait()
    after.wait()


def pass_on_kernel(below, above, four_a, four_b, four_c, out):
    even = lax.axis_index("ctx") % 2 == 0
    out[0:32] = jnp.where(even, below[...], above[...])
    for i, ref in enumerate((four_a, four_b, four_c)):
        out[32 + 16 * i : 48 + 16 * i] = ref[...]


def far_sum_kernel(to_3, to_4, swapped, *outs):
    even = lax.axis_index("ctx") % 2 == 0
    third = swapped[0:32].astype(F32)
    outs[0][...] = (to_3[0].astype(F32) + jnp.where(even, third, 0.0)).astype(BF16)
    outs[1][...] = (to_3[1].astype(F32) + jnp.where(even, 0.0, third)).astype(BF16)
    for i in range(3):
        part = swapped[32 + 16 * i : 48 + 16 * i].astype(F32)
        outs[2 + i][...] = (to_4[i].astype(F32) + part).astype(BF16)


def scatter_kernel(low, bits, count, keep, *refs):
    got, outs = refs[:count], refs[-(1 << bits) - 1 : -1]
    total = refs[-1]
    total[...] = functools.reduce(jnp.add, [x[...].astype(F32) for x in got], keep[...])
    side = (lax.axis_index("ctx") // (1 << low)) % (1 << bits)
    rows = total.shape[0] >> bits
    for step, out in enumerate(outs):
        flipped = side if step == 0 else side + step - 2 * sum(
            (side // (1 << bit) % 2) * (1 << bit) for bit in range(bits) if step >> bit & 1
        )
        part = total[pl.ds(pl.multiple_of(flipped * rows, rows), rows)]
        out[...] = part if step == 0 else part.astype(BF16)


def copies_kernel(keep, *refs):
    total = functools.reduce(jnp.add, [x[...].astype(F32) for x in refs[:3]], keep[...])
    for i in range(refs[-1].shape[0]):
        refs[-1][i] = total.astype(BF16)


def last_sum_kernel(parts, out):
    total = parts[0].astype(F32)
    for i in range(1, parts.shape[0]):
        total = total + parts[i].astype(F32)
    out[...] = total.astype(BF16)


def combine_kernel(*refs):
    own, (low, high), from3, from4 = (refs[0:3], refs[3:6]), refs[6:8], refs[8:10], refs[10:13]
    d_k_hbm, d_v_hbm, d_k, d_v, sems = refs[13:]
    copies = []
    for part, out, out_hbm in ((0, d_k, d_k_hbm), (1, d_v, d_v_hbm)):
        lanes = slice(part * WIDTH, (part + 1) * WIDTH)
        table = jnp.concatenate(
            [spread_table(level, 1.0 if part else 0.5**level) for level in (1, 2, 3, 4)], axis=1
        )

        def rim(ref, level):
            return ref[BLOCK * level : BLOCK * (level + 1), lanes].astype(F32)

        def summed(parts):
            return functools.reduce(jnp.add, [ref[:, lanes].astype(F32) for ref in parts])

        coarse = jnp.concatenate(
            [
                rim(high, 1),
                rim(low, 1),
                rim(low, 2) + rim(high, 2),
                summed(from3),
                summed(from4),
            ],
            axis=0,
        ).astype(BF16)
        whole = jnp.concatenate([x[...] for x in own[part]], axis=1) + dot(table, coarse)
        out[0:64] = (whole[0:64] + rim(high, 0)).astype(BF16)
        out[64:192] = whole[64:192].astype(BF16)
        out[192:256] = (whole[192:256] + rim(low, 0)).astype(BF16)
        copies.append(pltpu.make_async_copy(out, out_hbm, sems.at[part]))
        copies[-1].start()
    for copy in copies:
        copy.wait()


def call(
    kernel, name, outs, args, scratch=(), in_hbm=0, microseconds=1.0, to_hbm=()
):
    vmem, hbm = pl.BlockSpec(memory_space=pltpu.VMEM), pl.BlockSpec(memory_space=pl.ANY)
    return pl.pallas_call(
        kernel,
        name=name,
        out_shape=[jax.ShapeDtypeStruct(shape, dtype) for shape, dtype in outs],
        in_specs=[vmem] * (len(args) - in_hbm) + [hbm] * in_hbm,
        out_specs=[hbm if i in to_hbm else vmem for i in range(len(outs))],
        scratch_shapes=scratch,
        cost_estimate=pl.CostEstimate(
            flops=int(microseconds * 1e9), bytes_accessed=1 << 20, transcendentals=0
        ),
        compiler_params=pltpu.CompilerParams(vmem_limit_bytes=VMEM_MIB * 1024 * 1024),
    )(*args)


def moved(x, route):
    count = lax.axis_size("ctx")
    return lax.ppermute(x, "ctx", [(i, route(i) % count) for i in range(count)])


def partner(i):
    return i ^ 1


def third(i):
    return i - 6 if i // 2 % 2 else i + 6


ROUTES_3 = (lambda i: i + 2, lambda i: i - 2)
ROUTES_4 = (lambda i: i + 4, lambda i: i - 4, third)
BACK_3 = (lambda i: i - 2, lambda i: i + 2)
BACK_4 = (lambda i: i - 4, lambda i: i + 4, third)


def messages(parts, low):
    return [
        moved(part, lambda i, step=step: i ^ step << low) for step, part in enumerate(parts, 1)
    ]


def body(queries, key_rows, value_rows, segment_ids, w_out, d_out):
    q, k, v, grad_out = queries[0], key_rows[0], value_rows[0], d_out[0]
    tokens, dma = (ROWS, WIDTH), pltpu.SemaphoreType.DMA
    up, down, far3, far4, own0, own1, qdoc = call(
        coarsen_kernel,
        "coarsen",
        [((192, PACK), BF16), ((192, PACK), BF16), ((32, PACK), BF16), ((16, PACK), BF16)]
        + [((ROWS, PACK), BF16), ((128, PACK), BF16), ((ALL_ROWS, LANES), BF16)],
        [segment_ids, k, v],
        [pltpu.VMEM((1, ROWS), jnp.int32)] + [pltpu.VMEM(tokens, BF16)] * 2 + [dma((3,))],
        in_hbm=3,
    )
    far3, far4, q_all, grad_att, w, grad_rows = call(
        prepare_kernel,
        "prepare",
        [((32, PACK), BF16), ((16, PACK), BF16)]
        + [((ALL_ROWS, WIDTH), BF16), (tokens, F32), ((WIDTH, WIDTH), BF16), (tokens, BF16)],
        [far3, far4, q, grad_out, w_out],
        [pltpu.VMEM(tokens, BF16), dma((3,))],
        in_hbm=3,
    )
    low = moved(up, lambda i: i + 1)
    high = moved(down, lambda i: i - 1)
    got3 = [moved(far3, route) for route in ROUTES_3]
    got4 = [moved(far4, route) for route in ROUTES_4]
    low, high, *got3 = lax.optimization_barrier((low, high, *got3))
    passed = call(pass_on_kernel, "pass_on", [((80, PACK), BF16)], [*got3, *got4])[0]
    far = (*got3, *got4, moved(passed, partner))
    near = (own0, own1, low, high)
    p_near, fine, coarse = call(
        near_kernel,
        "near",
        [
            ((PAIRS, P_NEAR, 256), BF16),
            ((PAIRS, ROWS, 3 * LANES), F32),
            ((PAIRS, 192, 3 * LANES), BF16),
        ],
        [q_all, qdoc, *near],
        microseconds=50,
    )
    attended, keep, give, p_far, g, d_side = call(
        merge_kernel,
        "merge",
        [(tokens, BF16), ((256, WIDTH), F32), ((256, WIDTH), BF16)]
        + [((PAIRS, P_FAR, LANES), BF16)]
        + [((ALL_ROWS, WIDTH), BF16)] * 2,
        [q_all, qdoc, fine, coarse, grad_att, grad_rows, *far],
        [pltpu.VMEM((WIDTH, WIDTH), F32)],
        microseconds=6,
    )
    got_w = moved(give, partner)
    d_far, to_3, to_4, to_partner = call(
        far_back_kernel,
        "far_back",
        [((48, WIDTH), BF16), ((2, 32, 2 * WIDTH), BF16)]
        + [((3, 16, 2 * WIDTH), BF16), ((80, 2 * WIDTH), BF16)],
        [p_far, q_all, g, d_side, *far],
    )
    swapped = moved(to_partner, partner)

    def part_outs(part):
        width = len(NEAR_PARTS[part]) * LANES
        return [((ROWS, width), BF16), ((ROWS, width), F32), ((ROWS, width), F32)] + [
            ((2, 192, width), BF16)
        ] * 2

    args = [p_near, q_all, g, d_side, *near, d_far]
    *part_a, layer_out = call(
        near_back_a_kernel,
        "near_back_a",
        part_outs(0) + [(tokens, BF16)],
        [attended, w, *args],
        [pltpu.VMEM(tokens, BF16), dma(())],
        microseconds=3,
        to_hbm=(5,),
    )
    far_sums = call(
        far_sum_kernel,
        "far_sum",
        [((32, 2 * WIDTH), BF16)] * 2 + [((16, 2 * WIDTH), BF16)] * 3,
        [to_3, to_4, swapped],
    )
    keep, *parts = call(
        functools.partial(scatter_kernel, 1, 2, 1),
        "scatter_y",
        [((64, WIDTH), F32)] + [((64, WIDTH), BF16)] * 3,
        [keep, got_w],
        [pltpu.VMEM((256, WIDTH), F32)],
    )
    got_w = messages(parts, 1)
    back = [moved(x, route) for x, route in zip(far_sums[:2], BACK_3)]
    part_b = call(
        near_back_b_kernel,
        "near_back_b",
        part_outs(1),
        [*args, part_a[0], far_sums[0], keep],
        in_hbm=3,
        microseconds=4,
    )
    keep, *parts = call(
        functools.partial(scatter_kernel, 3, 2, 3),
        "scatter_x",
        [((16, WIDTH), F32)] + [((16, WIDTH), BF16)] * 3,
        [keep, *got_w, part_b[0]],
        [pltpu.VMEM((64, WIDTH), F32)],
        in_hbm=1,
    )
    got_w = messages(parts, 3)
    to_4, _ = lax.optimization_barrier((far_sums[2:], part_b[0]))
    back_4 = [moved(x, route) for x, route in zip(to_4, BACK_4)]
    d_q, own_k, own_v, to_low, to_high = call(
        near_back_c_kernel,
        "near_back_c",
        [(tokens, BF16), ((ROWS, LANES), F32), ((ROWS, LANES), F32)]
        + [((192, 2 * WIDTH), BF16)] * 2,
        [*args, part_a[0], *part_a[3:], part_b[0], *part_b[3:], to_4[0], keep, *back],
        [pltpu.VMEM(tokens, BF16), dma((2,))],
        in_hbm=4,
        microseconds=2,
        to_hbm=(0,),
    )
    low_back = moved(to_low, lambda i: i - 1)
    high_back = moved(to_high, lambda i: i + 1)
    copies = call(
        copies_kernel,
        "copies",
        [((lax.axis_size("dp"), 16, WIDTH), BF16)],
        [keep, *got_w, to_low],
        in_hbm=1,
    )[0]
    copies = lax.all_to_all(copies, "dp", 0, 0, tiled=True)
    d_w = call(last_sum_kernel, "last_sum", [((16, WIDTH), BF16)], [copies])[0]
    d_k, d_v = call(
        combine_kernel,
        "combine",
        [(tokens, BF16)] * 2,
        [part_a[1], part_b[1], own_k, part_a[2], part_b[2], own_v, low_back, high_back]
        + [*back, *back_4],
        [pltpu.VMEM(tokens, BF16)] * 2 + [dma((2,))],
        to_hbm=(0, 1),
    )
    return layer_out[None], d_q[None], d_k[None], d_v[None], d_w


def solution(mesh):
    tokens = P("dp", "ctx", None)
    return jax.shard_map(
        body,
        mesh=mesh,
        in_specs=(tokens, tokens, tokens, P("dp", "ctx"), P(), tokens),
        out_specs=(tokens, tokens, tokens, tokens, P("ctx", None)),
        check_vma=False,
    )
```

```python
import functools

import jax
import jax.numpy as jnp
from jax import lax
from jax.experimental import pallas as pl
from jax.experimental.pallas import tpu as pltpu
from jax.sharding import PartitionSpec as P

HEAD_DIM = 64
BLOCK = 64
HALF = 32
LEVELS = 4
ROWS = 256
WIDTH = 512
PAIRS = 4
LANES = 128
DOCS = 4
NEGATIVE = -1e30
BLOCKED = -2e30
SCALE = HEAD_DIM**-0.5
PACK = 2 * WIDTH + LANES
COUNT = (256, 128, 64, 32, 16)
AT = (0, 256, 384, 448, 480)
ALL_ROWS = 496
F32 = jnp.float32
BF16 = jnp.bfloat16
VMEM_MIB = 20

GROUPS = (
    (0, 0, 128, 256),
    (0, 128, 128, 256),
    (1, 0, 128, 256),
    (2, 0, 64, 128),
    (3, 0, 32, 96),
    (4, 0, 16, 96),
)
NEAR = (0, 1, 2, 3)
FAR = (4, 5)
P_AT = {0: 0, 1: 256, 2: 512, 3: 768, 4: 0, 5: 64}
P_NEAR, P_FAR = 896, 96


def iota(shape, dim):
    return lax.broadcasted_iota(jnp.int32, shape, dim)


def gather_table(level, value=1.0):
    shape = (COUNT[level], ROWS)
    return jnp.where(iota(shape, 1) // 2**level == iota(shape, 0), value, 0.0).astype(BF16)


def spread_table(level, value=1.0):
    shape = (ROWS, COUNT[level])
    return jnp.where(iota(shape, 0) // 2**level == iota(shape, 1), value, 0.0).astype(BF16)


def last_table(level):
    shape = (COUNT[level], ROWS)
    last = iota(shape, 0) * 2**level + (2**level - 1)
    return jnp.where(iota(shape, 1) == last, 1.0, 0.0).astype(BF16)


def query_place(index):
    level, _, rows, _ = GROUPS[index]
    size = BLOCK if level == 0 else HALF
    shape = (rows, LANES)
    return jnp.where(iota(shape, 0) // size + 8 == iota(shape, 1), 1.0, 0.0).astype(BF16)


def key_place(index):
    level, _, _, keys = GROUPS[index]
    shape = (keys, LANES)
    row, place = iota(shape, 0), iota(shape, 1) - 8
    if level == 0:
        apart = row // BLOCK - place
        blocked = (apart < 0) | (apart > 2)
        places = 2
    elif level == 1:
        there, here = row // HALF, place + 2
        block_apart = jnp.abs(there // 2 - (place + 2) // 2)
        blocked = (block_apart > 1) | (jnp.abs(there - here) < 2)
        places = 4
    else:
        blocked = row // HALF == place + 1
        places = 2
    blocked = blocked & (place >= 0) & (place < places)
    return jnp.where(blocked, BLOCKED, 0.0).astype(BF16)


def dot(a, b, a_dim=1, b_dim=0):
    return lax.dot_general(a, b, (((a_dim,), (b_dim,)), ((), ())), preferred_element_type=F32)


def split(x):
    high = x.astype(BF16)
    return high, (x - high.astype(F32)).astype(BF16)


def head_lanes(rows, width=LANES):
    return iota((rows, width), 1) % LANES < HEAD_DIM


def stacked(x):
    first = head_lanes(x.shape[0]).astype(F32).astype(BF16)
    return jnp.concatenate([x * first, x * (1 - first)], axis=0)


def unstacked(x, rows):
    return jnp.where(head_lanes(rows, x.shape[1]), x[:rows], x[rows:])


def lanes_of(pair, part=0):
    return slice(part * WIDTH + pair * LANES, part * WIDTH + (pair + 1) * LANES)


DOC_LANES = slice(2 * WIDTH, PACK)


def near_window(index, own0, own1, low, high, lanes):
    def rim(ref, level):
        return ref[BLOCK * level : BLOCK * (level + 1), lanes]

    if index == 0:
        parts = [rim(low, 0), own0[0:192, lanes]]
    elif index == 1:
        parts = [own0[64:256, lanes], rim(high, 0)]
    elif index == 2:
        parts = [rim(low, 1), own1[:, lanes], rim(high, 1)]
    else:
        parts = [rim(low, 2), rim(high, 2)]
    return jnp.concatenate(parts, axis=0)


def far_window(refs, lanes):
    return jnp.concatenate([ref[:, lanes] for ref in refs], axis=0)


def fetch(sources, targets, sems):
    copies = [
        pltpu.make_async_copy(source, target, sems.at[i])
        for i, (source, target) in enumerate(zip(sources, targets))
    ]
    for copy in copies:
        copy.start()
    return copies


def coarsen_kernel(
    seg_hbm, k_hbm, v_hbm, up, down, far, own0, own1, qdoc, seg, k, v, sems
):
    copies = fetch((seg_hbm, k_hbm, v_hbm), (seg, k, v), sems)
    copies[0].wait()
    marks = jnp.where(seg[...] == iota((LANES, ROWS), 0), 1.0, 0.0).T.astype(BF16)

    def key_side(x):
        doc = iota(x.shape, 1) < DOCS
        return jnp.where(doc, (1.0 - x.astype(F32)) * BLOCKED, 0.0).astype(BF16)

    copies[1].wait()
    copies[2].wait()
    levels = [(k[...], v[...], key_side(marks))]
    qdoc[0:ROWS] = marks
    for level in range(1, LEVELS + 1):
        marks_c = dot(last_table(level), marks).astype(BF16)
        qdoc[AT[level] : AT[level] + COUNT[level]] = marks_c
        keys = dot(gather_table(level, 0.5**level), levels[0][0]).astype(BF16)
        values = dot(gather_table(level), levels[0][1]).astype(BF16)
        levels.append((keys, values, key_side(marks_c)))

    def put(ref, at, level, start, stop):
        for part, lanes in zip(
            levels[level], (slice(0, WIDTH), slice(WIDTH, 2 * WIDTH), DOC_LANES)
        ):
            ref[at : at + stop - start, lanes] = part[start:stop]

    for level in range(3):
        put(up, BLOCK * level, level, COUNT[level] - BLOCK, COUNT[level])
        put(down, BLOCK * level, level, 0, BLOCK)
    put(far, 0, 3, 0, COUNT[3])
    put(far, COUNT[3], 4, 0, COUNT[4])
    put(own0, 0, 0, 0, COUNT[0])
    put(own1, 0, 1, 0, COUNT[1])


def core_index():
    return lax.axis_index("ctx") % 2


def prepare_kernel(
    far, far_partner, q_hbm, d_hbm, w_hbm, far3, far4, third, q_out, grad_att, w, d_out, q, sems
):
    copies = fetch((q_hbm, d_hbm, w_hbm), (q, d_out, w), sems)
    even = core_index() == 0
    for out, start, rows in ((far3, 0, 32), (far4, 32, 16)):
        own, other = far[start : start + rows], far_partner[start : start + rows]
        out[0:rows] = jnp.where(even, own, other)
        out[rows : 2 * rows] = jnp.where(even, other, own)
    third[...] = far[32:48]
    copies[0].wait()
    for level in range(LEVELS + 1):
        queries = q[...] if level == 0 else dot(gather_table(level, 0.5**level), q[...]).astype(BF16)
        q_out[AT[level] : AT[level] + COUNT[level]] = (queries * SCALE).astype(BF16)
    copies[1].wait()
    copies[2].wait()
    grad_att[...] = dot(d_out[...], w[...], 1, 1)


def attend(queries, query_docs, keys, key_docs, values):
    rows = queries.shape[0]
    scores = dot(
        jnp.concatenate([stacked(queries), query_docs], axis=1),
        jnp.concatenate([keys, key_docs], axis=1),
        1,
        1,
    )
    peak = jnp.maximum(jnp.max(scores, axis=1, keepdims=True), NEGATIVE)
    peak = peak.astype(BF16).astype(F32)
    p = jnp.exp(scores - peak).astype(BF16)
    ones = jnp.ones(values.shape, BF16)
    both = unstacked(dot(p, jnp.concatenate([values, ones], axis=1)), rows)
    wide_peak = jnp.where(head_lanes(rows), peak[:rows], peak[rows:])
    return p, jnp.concatenate([both, wide_peak], axis=1)


def docs_of(index, qdoc):
    level, start, rows, _ = GROUPS[index]
    docs = qdoc[AT[level] + start : AT[level] + start + rows]
    if index in NEAR:
        docs = docs + query_place(index)
    return jnp.concatenate([docs, docs], axis=0)


def near_kernel(q_all, qdoc, own0, own1, low, high, p_out, fine, coarse):
    for index in NEAR:
        level, start, rows, keys = GROUPS[index]
        at = AT[level] + start
        query_docs = docs_of(index, qdoc)
        key_docs = near_window(index, own0, own1, low, high, DOC_LANES) + key_place(index)
        for pair in range(PAIRS):
            window = [
                near_window(index, own0, own1, low, high, lanes_of(pair, part)) for part in (0, 1)
            ]
            p, stats = attend(
                q_all[at : at + rows, lanes_of(pair)], query_docs, window[0], key_docs, window[1]
            )
            p_out[pair, P_AT[index] : P_AT[index] + 2 * rows, 0:keys] = p
            if level == 0:
                fine[pair, at : at + rows] = stats
            else:
                coarse[pair, at - ROWS : at - ROWS + rows] = stats.astype(BF16)


def far_refs(refs):
    own3, got4, third, passed = refs
    return (
        (own3, passed.at[0:64]),
        (got4, passed.at[64:96], third, passed.at[96:112]),
    )


def block_at(block):
    x, y, core = block // 8, block // 2 % 4, block % 2
    return 16 * (16 * core + 4 * y + x)


def merge_kernel(q_all, qdoc, fine, coarse, grad_att, d_out, *refs):
    far = far_refs(refs[:4])
    attended_out, keep, give, p_out, g_out, d_side, d_w = refs[4:]
    docs = [(docs_of(index, qdoc), far_window(ref, DOC_LANES)) for index, ref in zip(FAR, far)]
    shape = (LANES, LANES)
    same_head = jnp.where(iota(shape, 0) // HEAD_DIM == iota(shape, 1) // HEAD_DIM, 1.0, 0.0)
    same_head = same_head.astype(BF16)
    spreads = [None] + [spread_table(level) for level in range(1, LEVELS + 1)]
    gathers = [None] + [gather_table(level) for level in range(1, LEVELS + 1)]
    for pair in range(PAIRS):
        cols = lanes_of(pair)
        packed = [None, coarse[pair, 0:128], coarse[pair, 128:192]]
        for index, ref, (query_docs, key_docs) in zip(FAR, far, docs):
            level, _, rows, keys = GROUPS[index]
            p, stats = attend(
                q_all[AT[level] : AT[level] + rows, cols],
                query_docs,
                far_window(ref, lanes_of(pair)),
                key_docs,
                far_window(ref, lanes_of(pair, 1)),
            )
            p_out[pair, P_AT[index] : P_AT[index] + 2 * rows, 0:keys] = p
            packed.append(stats.astype(BF16))
        wide = [fine[pair]] + [
            dot(spreads[level], packed[level]) for level in range(1, LEVELS + 1)
        ]
        levels = [[x[:, LANES * i : LANES * (i + 1)] for i in range(3)] for x in wide]
        top = functools.reduce(jnp.maximum, [x[2] for x in levels])
        weights = [jnp.exp(x[2] - top) for x in levels]
        norm = functools.reduce(
            jnp.add, [wt * x[1] * float(2**i) for i, (wt, x) in enumerate(zip(weights, levels))]
        )
        numer = functools.reduce(jnp.add, [wt * x[0] for wt, x in zip(weights, levels)])
        inverse = 1.0 / norm
        attended = (numer * inverse).astype(BF16)
        grad_w = dot(attended, d_out[...], 0, 0)
        for block in range(8):
            at = block_at(8 * pair + block)
            d_w[at : at + 16] = grad_w[16 * block : 16 * (block + 1)]
        attended_out[:, cols] = attended
        grad = grad_att[:, cols]
        high_part, low_part = split(grad * attended.astype(F32))
        delta = dot(high_part, same_head) + dot(low_part, same_head)
        for level in range(LEVELS + 1):
            share = weights[level] * inverse
            at, rows = AT[level], COUNT[level]
            if level == 0:
                grad_c, delta_c = share * grad, share * delta
            else:
                d_high, d_low = split(share * delta)
                terms = jnp.concatenate([(share * grad).astype(BF16), d_high, d_low], axis=1)
                summed = dot(gathers[level], terms)
                grad_c = summed[:, :LANES]
                delta_c = summed[:, LANES : 2 * LANES] + summed[:, 2 * LANES :]
            g_out[at : at + rows, cols] = grad_c.astype(BF16)
            d_high, d_low = split(delta_c * -float(2**level))
            upper = iota((rows, LANES), 1) % HEAD_DIM < HALF
            d_side[at : at + rows, cols] = jnp.where(
                upper, d_high.astype(F32), d_low.astype(F32)
            ).astype(BF16)
    core = core_index()
    keep[...] = d_w[pl.ds(pl.multiple_of(core * 256, 256), 256)]
    give[...] = d_w[pl.ds(pl.multiple_of((1 - core) * 256, 256), 256)].astype(BF16)


def attend_back(p, queries, grad, side, keys, values):
    rows = queries.shape[0]
    ones = jnp.where(iota(values.shape, 1) % HALF == 0, 1.0, 0.0).astype(BF16)
    grad = stacked(grad)
    product = dot(
        jnp.concatenate([grad, stacked(side)], axis=1),
        jnp.concatenate([values, ones], axis=1),
        1,
        1,
    )
    ds = (p.astype(F32) * product).astype(BF16)
    grad_q = unstacked(dot(ds, keys), rows) * SCALE
    return grad_q, dot(ds, stacked(queries), 0, 0), dot(p, grad, 0, 0)


def far_back_kernel(p_in, q_all, g_in, d_side, *refs):
    far = far_refs(refs[:4])
    d_q, to_3, to_4, to_third, to_partner = refs[4:]
    to_far = (
        (to_3, to_partner.at[0:64]),
        (to_4, to_partner.at[64:96], to_third, to_partner.at[96:112]),
    )
    for pair in range(PAIRS):
        cols = lanes_of(pair)
        for index, ref, to in zip(FAR, far, to_far):
            level, _, rows, keys = GROUPS[index]
            at = AT[level]
            grad_q, grad_k, grad_v = attend_back(
                p_in[pair, P_AT[index] : P_AT[index] + 2 * rows, 0:keys],
                q_all[at : at + rows, cols],
                g_in[at : at + rows, cols],
                d_side[at : at + rows, cols],
                far_window(ref, cols),
                far_window(ref, lanes_of(pair, 1)),
            )
            d_q[at - AT[3] : at - AT[3] + rows, cols] = grad_q.astype(BF16)
            start = 0
            for out in to:
                stop = start + out.shape[0]
                out[:, cols] = grad_k[start:stop].astype(BF16)
                out[:, lanes_of(pair, 1)] = grad_v[start:stop].astype(BF16)
                start = stop


NEAR_PARTS = ((0,), (1, 2), (3,))


def near_back(pairs, p_in, q_all, g_in, d_side, own0, own1, low, high, d_far):
    spread = jnp.concatenate([spread_table(level, 0.5**level) for level in (1, 2, 3, 4)], axis=1)
    for pair in pairs:
        cols = lanes_of(pair)
        grads = []
        for index in NEAR:
            level, start, rows, keys = GROUPS[index]
            at = AT[level] + start
            grads.append(
                attend_back(
                    p_in[pair, P_AT[index] : P_AT[index] + 2 * rows, 0:keys],
                    q_all[at : at + rows, cols],
                    g_in[at : at + rows, cols],
                    d_side[at : at + rows, cols],
                    near_window(index, own0, own1, low, high, cols),
                    near_window(index, own0, own1, low, high, lanes_of(pair, 1)),
                )
            )
        coarse = [x[0].astype(BF16) for x in grads[2:]] + [d_far[:, cols]]
        whole = jnp.concatenate([x[0] for x in grads[:2]], axis=0)
        d_q = (whole + dot(spread, jnp.concatenate(coarse, axis=0))).astype(BF16)
        own, to_low, to_high = [], [], []
        for part, value in ((0, 0.5), (1, 1.0)):
            a, b, c, d = (x[1 + part] for x in grads)
            middle = jnp.concatenate([a[64:128], a[128:256] + b[0:128], b[128:192]], axis=0)
            own.append(middle + dot(spread_table(1, value), c[64:192].astype(BF16)))
            to_low.append(jnp.concatenate([a[:64], c[:64], d[:64]], axis=0).astype(BF16))
            to_high.append(jnp.concatenate([b[192:], c[192:], d[64:]], axis=0).astype(BF16))
        yield pair, d_q, own, to_low, to_high


def near_back_first_kernel(pairs, attended, w, *refs):
    inputs, outs = refs[:9], refs[9:]
    layer_out = None
    if attended is not None:
        layer_out, result, sem = outs[-3:]
        result[...] = dot(attended[...], w[...]).astype(BF16)
        copy = pltpu.make_async_copy(result, layer_out, sem)
        copy.start()
    d_q, own_k, own_v, to_low, to_high = outs[:5]
    for pair, dq, own, low, high in near_back(pairs, *inputs):
        at = slice((pair - pairs[0]) * LANES, (pair - pairs[0] + 1) * LANES)
        d_q[:, at], own_k[:, at], own_v[:, at] = dq, own[0], own[1]
        for part in range(2):
            to_low[part, :, at], to_high[part, :, at] = low[part], high[part]
    if attended is not None:
        copy.wait()


def near_back_a_kernel(attended, w, *refs):
    near_back_first_kernel(NEAR_PARTS[0], attended, w, *refs[:9], *refs[-8:])


def near_back_b_kernel(*refs):
    near_back_first_kernel(NEAR_PARTS[1], None, None, *refs[:9], *refs[-5:])


def near_back_c_kernel(*refs):
    inputs, earlier = refs[:9], (refs[9:12], refs[12:15])
    d_q_hbm, own_k, own_v, to_low, to_high, d_q, sems = refs[-7:]
    for pairs, (dq, low, high) in zip(NEAR_PARTS, earlier):
        cols = slice(pairs[0] * LANES, (pairs[-1] + 1) * LANES)
        d_q[:, cols] = dq[...]
        for part in range(2):
            lanes = slice(part * WIDTH + cols.start, part * WIDTH + cols.stop)
            to_low[:, lanes], to_high[:, lanes] = low[part], high[part]
    last = NEAR_PARTS[2][0] * LANES
    before = pltpu.make_async_copy(d_q.at[:, 0:last], d_q_hbm.at[:, 0:last], sems.at[0])
    before.start()
    for pair, dq, own, low, high in near_back(NEAR_PARTS[2], *inputs):
        d_q[:, lanes_of(pair)] = dq
        own_k[...], own_v[...] = own[0], own[1]
        after = pltpu.make_async_copy(
            d_q.at[:, lanes_of(pair)], d_q_hbm.at[:, lanes_of(pair)], sems.at[1]
        )
        after.start()
        for part in range(2):
            to_low[:, lanes_of(pair, part)] = low[part]
            to_high[:, lanes_of(pair, part)] = high[part]
    before.wait()
    after.wait()


def pass_on_kernel(got3, got4, third, own3, out):
    out[0:64] = got3[...]
    out[64:96] = got4[...]
    out[96:112] = third[...]
    own3[...] = jnp.where(core_index() == 0, got3[0:32], got3[32:64])


def far_sum_kernel(to_3, to_4, to_third, swapped, sum3, sum4, sum_third):
    even = core_index() == 0
    own3 = to_3[...].astype(F32)
    sum3[0:32] = (swapped[0:32].astype(F32) + jnp.where(even, own3, 0.0)).astype(BF16)
    sum3[32:64] = (swapped[32:64].astype(F32) + jnp.where(even, 0.0, own3)).astype(BF16)
    sum4[...] = (swapped[64:96].astype(F32) + to_4[...].astype(F32)).astype(BF16)
    sum_third[...] = (swapped[96:112].astype(F32) + to_third[...].astype(F32)).astype(BF16)


def core_rows(ref, core, rows):
    return ref[pl.ds(pl.multiple_of(core * rows, rows), rows)]


def far_split_kernel(back3, back4, give):
    other = 1 - core_index()
    give[0:32] = core_rows(back3, other, 32)
    give[32:48] = core_rows(back4, other, 16)


def halve_kernel(divisor, keep, got, *refs):
    keep_out, give_out, total = refs[-3:]
    total[...] = keep[...] + got[...].astype(F32)
    side = lax.axis_index("ctx") // divisor % 2
    half = total.shape[0] // 2
    keep_out[...] = total[pl.ds(pl.multiple_of(side * half, half), half)]
    give_out[...] = total[pl.ds(pl.multiple_of((1 - side) * half, half), half)].astype(BF16)


def copies_kernel(keep, got, *refs):
    total = keep[...] + got[...].astype(F32)
    for i in range(refs[-1].shape[0]):
        refs[-1][i] = total.astype(BF16)


def last_sum_kernel(parts, out):
    total = parts[0].astype(F32)
    for i in range(1, parts.shape[0]):
        total = total + parts[i].astype(F32)
    out[...] = total.astype(BF16)


def combine_kernel(*refs):
    own, (low, high) = (refs[0:3], refs[3:6]), refs[6:8]
    back3, back4, third, swapped = refs[8:12]
    d_k_hbm, d_v_hbm, d_k, d_v, sems = refs[12:]
    core = core_index()
    far3 = core_rows(back3, core, 32).astype(F32) + swapped[0:32].astype(F32)
    far4 = core_rows(back4, core, 16).astype(F32) + swapped[32:48].astype(F32)
    far4 = far4 + third[...].astype(F32)
    copies = []
    for part, out, out_hbm in ((0, d_k, d_k_hbm), (1, d_v, d_v_hbm)):
        lanes = slice(part * WIDTH, (part + 1) * WIDTH)
        table = jnp.concatenate(
            [spread_table(level, 1.0 if part else 0.5**level) for level in (1, 2, 3, 4)], axis=1
        )

        def rim(ref, level):
            return ref[BLOCK * level : BLOCK * (level + 1), lanes].astype(F32)

        coarse = jnp.concatenate(
            [
                rim(high, 1),
                rim(low, 1),
                rim(low, 2) + rim(high, 2),
                far3[:, lanes],
                far4[:, lanes],
            ],
            axis=0,
        ).astype(BF16)
        whole = jnp.concatenate([x[...] for x in own[part]], axis=1) + dot(table, coarse)
        out[0:64] = (whole[0:64] + rim(high, 0)).astype(BF16)
        out[64:192] = whole[64:192].astype(BF16)
        out[192:256] = (whole[192:256] + rim(low, 0)).astype(BF16)
        copies.append(pltpu.make_async_copy(out, out_hbm, sems.at[part]))
        copies[-1].start()
    for copy in copies:
        copy.wait()


def call(
    kernel, name, outs, args, scratch=(), in_hbm=0, microseconds=1.0, to_hbm=()
):
    vmem, hbm = pl.BlockSpec(memory_space=pltpu.VMEM), pl.BlockSpec(memory_space=pl.ANY)
    return pl.pallas_call(
        kernel,
        name=name,
        out_shape=[jax.ShapeDtypeStruct(shape, dtype) for shape, dtype in outs],
        in_specs=[vmem] * (len(args) - in_hbm) + [hbm] * in_hbm,
        out_specs=[hbm if i in to_hbm else vmem for i in range(len(outs))],
        scratch_shapes=scratch,
        cost_estimate=pl.CostEstimate(
            flops=int(microseconds * 1e9), bytes_accessed=1 << 20, transcendentals=0
        ),
        compiler_params=pltpu.CompilerParams(vmem_limit_bytes=VMEM_MIB * 1024 * 1024),
    )(*args)


def moved(x, route):
    count = lax.axis_size("ctx")
    return lax.ppermute(x, "ctx", [(i, route(i) % count) for i in range(count)])


def partner(i):
    return i ^ 1


def third(i):
    return i - 6 if i // 2 % 2 else i + 6


def route_3(i):
    return i - 2 if i % 2 else i + 2


def route_4(i):
    return i - 4 if i % 2 else i + 4


def back_3(i):
    return i + 2 if i % 2 else i - 2


def back_4(i):
    return i + 4 if i % 2 else i - 4


def body(queries, key_rows, value_rows, segment_ids, w_out, d_out):
    q, k, v, grad_out = queries[0], key_rows[0], value_rows[0], d_out[0]
    tokens, dma = (ROWS, WIDTH), pltpu.SemaphoreType.DMA
    up, down, far, own0, own1, qdoc = call(
        coarsen_kernel,
        "coarsen",
        [((192, PACK), BF16), ((192, PACK), BF16), ((48, PACK), BF16)]
        + [((ROWS, PACK), BF16), ((128, PACK), BF16), ((ALL_ROWS, LANES), BF16)],
        [segment_ids, k, v],
        [pltpu.VMEM((1, ROWS), jnp.int32)] + [pltpu.VMEM(tokens, BF16)] * 2 + [dma((3,))],
        in_hbm=3,
    )
    far_partner = moved(far, partner)
    far3, far4, third_rows, q_all, grad_att, w, grad_rows = call(
        prepare_kernel,
        "prepare",
        [((64, PACK), BF16), ((32, PACK), BF16), ((16, PACK), BF16)]
        + [((ALL_ROWS, WIDTH), BF16), (tokens, F32), ((WIDTH, WIDTH), BF16), (tokens, BF16)],
        [far, far_partner, q, grad_out, w_out],
        [pltpu.VMEM(tokens, BF16), dma((3,))],
        in_hbm=3,
    )
    low = moved(up, lambda i: i + 1)
    high = moved(down, lambda i: i - 1)
    got3 = moved(far3, route_3)
    got4 = moved(far4, route_4)
    got_third = moved(third_rows, third)
    low, high, got3 = lax.optimization_barrier((low, high, got3))
    own3, passed = call(
        pass_on_kernel,
        "pass_on",
        [((32, PACK), BF16), ((112, PACK), BF16)],
        [got3, got4, got_third],
    )
    far = (own3, got4, got_third, moved(passed, partner))
    near = (own0, own1, low, high)
    p_near, fine, coarse = call(
        near_kernel,
        "near",
        [
            ((PAIRS, P_NEAR, 256), BF16),
            ((PAIRS, ROWS, 3 * LANES), F32),
            ((PAIRS, 192, 3 * LANES), BF16),
        ],
        [q_all, qdoc, *near],
        microseconds=50,
    )
    attended, keep, give, p_far, g, d_side = call(
        merge_kernel,
        "merge",
        [(tokens, BF16), ((256, WIDTH), F32), ((256, WIDTH), BF16)]
        + [((PAIRS, P_FAR, LANES), BF16)]
        + [((ALL_ROWS, WIDTH), BF16)] * 2,
        [q_all, qdoc, fine, coarse, grad_att, grad_rows, *far],
        [pltpu.VMEM((WIDTH, WIDTH), F32)],
        microseconds=6,
    )
    got_w = moved(give, partner)
    d_far, *to_far, to_partner = call(
        far_back_kernel,
        "far_back",
        [((48, WIDTH), BF16), ((32, 2 * WIDTH), BF16), ((32, 2 * WIDTH), BF16)]
        + [((16, 2 * WIDTH), BF16), ((112, 2 * WIDTH), BF16)],
        [p_far, q_all, g, d_side, *far],
    )
    swapped = moved(to_partner, partner)

    def halved(keep, got, divisor, route, after):
        rows = keep.shape[0] // 2
        keep, give = call(
            functools.partial(halve_kernel, divisor),
            "halve_" + str(rows),
            [((rows, WIDTH), F32), ((rows, WIDTH), BF16)],
            [keep, got, after],
            [pltpu.VMEM((2 * rows, WIDTH), F32)],
            in_hbm=1,
        )
        return keep, moved(give, route)

    keep, got_w = halved(keep, got_w, 4, lambda i: i ^ 6, d_far)

    def part_outs(part):
        width = len(NEAR_PARTS[part]) * LANES
        return [((ROWS, width), BF16), ((ROWS, width), F32), ((ROWS, width), F32)] + [
            ((2, 192, width), BF16)
        ] * 2

    args = [p_near, q_all, g, d_side, *near, d_far]
    *part_a, layer_out = call(
        near_back_a_kernel,
        "near_back_a",
        part_outs(0) + [(tokens, BF16)],
        [attended, w, *args, keep],
        [pltpu.VMEM(tokens, BF16), dma(())],
        in_hbm=1,
        microseconds=3,
        to_hbm=(5,),
    )
    sum3, sum4, sum_third = call(
        far_sum_kernel,
        "far_sum",
        [((64, 2 * WIDTH), BF16), ((32, 2 * WIDTH), BF16), ((16, 2 * WIDTH), BF16)],
        [*to_far, swapped],
    )
    back3 = moved(sum3, back_3)
    back4 = moved(sum4, back_4)
    back_third = moved(sum_third, third)
    keep, got_w = halved(keep, got_w, 2, lambda i: i ^ 2, part_a[0])
    part_b = call(
        near_back_b_kernel,
        "near_back_b",
        part_outs(1),
        [*args, part_a[0], sum3, keep],
        in_hbm=3,
        microseconds=4,
    )
    keep, got_w = halved(keep, got_w, 16, lambda i: i ^ 24, part_b[0])
    d_q, own_k, own_v, to_low, to_high = call(
        near_back_c_kernel,
        "near_back_c",
        [(tokens, BF16), ((ROWS, LANES), F32), ((ROWS, LANES), F32)]
        + [((192, 2 * WIDTH), BF16)] * 2,
        [*args, part_a[0], *part_a[3:], part_b[0], *part_b[3:], keep],
        [pltpu.VMEM(tokens, BF16), dma((2,))],
        in_hbm=1,
        microseconds=2,
        to_hbm=(0,),
    )
    low_back = moved(to_low, lambda i: i - 1)
    high_back = moved(to_high, lambda i: i + 1)
    give = call(far_split_kernel, "far_split", [((48, 2 * WIDTH), BF16)], [back3, back4])[0]
    swapped = moved(give, partner)
    keep, got_w = halved(keep, got_w, 8, lambda i: i ^ 8, to_low)
    copies = call(
        copies_kernel,
        "copies",
        [((lax.axis_size("dp"), 16, WIDTH), BF16)],
        [keep, got_w],
    )[0]
    copies = lax.all_to_all(copies, "dp", 0, 0, tiled=True)
    d_w = call(last_sum_kernel, "last_sum", [((16, WIDTH), BF16)], [copies])[0]
    d_k, d_v = call(
        combine_kernel,
        "combine",
        [(tokens, BF16)] * 2,
        [part_a[1], part_b[1], own_k, part_a[2], part_b[2], own_v, low_back, high_back]
        + [back3, back4, back_third, swapped],
        [pltpu.VMEM(tokens, BF16)] * 2 + [dma((2,))],
        to_hbm=(0, 1),
    )
    return layer_out[None], d_q[None], d_k[None], d_v[None], d_w


def solution(mesh):
    tokens = P("dp", "ctx", None)
    return jax.shard_map(
        body,
        mesh=mesh,
        in_specs=(tokens, tokens, tokens, P("dp", "ctx"), P(), tokens),
        out_specs=(tokens, tokens, tokens, tokens, P("ctx", None)),
        check_vma=False,
    )
```

```python
import functools

import jax
import jax.numpy as jnp
from jax import lax
from jax.experimental import pallas as pl
from jax.experimental.pallas import tpu as pltpu
from jax.sharding import PartitionSpec as P

HEAD_DIM = 64
BLOCK = 64
HALF = 32
LEVELS = 4
ROWS = 256
WIDTH = 512
PAIRS = 4
LANES = 128
DOCS = 4
NEGATIVE = -1e30
BLOCKED = -2e30
SCALE = HEAD_DIM**-0.5
PACK = 2 * WIDTH + LANES
COUNT = (256, 128, 64, 32, 16)
AT = (0, 256, 384, 448, 480)
ALL_ROWS = 496
F32 = jnp.float32
BF16 = jnp.bfloat16
VMEM_MIB = 20

GROUPS = (
    (0, 0, 128, 256),
    (0, 128, 128, 256),
    (1, 0, 128, 256),
    (2, 0, 64, 128),
    (3, 0, 32, 96),
    (4, 0, 16, 96),
)
NEAR = (0, 1, 2, 3)
FAR = (4, 5)
P_AT = {0: 0, 1: 256, 2: 512, 3: 768, 4: 0, 5: 64}
P_NEAR, P_FAR = 896, 96


def iota(shape, dim):
    return lax.broadcasted_iota(jnp.int32, shape, dim)


def gather_table(level, value=1.0):
    shape = (COUNT[level], ROWS)
    return jnp.where(iota(shape, 1) // 2**level == iota(shape, 0), value, 0.0).astype(BF16)


def spread_table(level, value=1.0):
    shape = (ROWS, COUNT[level])
    return jnp.where(iota(shape, 0) // 2**level == iota(shape, 1), value, 0.0).astype(BF16)


def last_table(level):
    shape = (COUNT[level], ROWS)
    last = iota(shape, 0) * 2**level + (2**level - 1)
    return jnp.where(iota(shape, 1) == last, 1.0, 0.0).astype(BF16)


def query_place(index):
    level, _, rows, _ = GROUPS[index]
    size = BLOCK if level == 0 else HALF
    shape = (rows, LANES)
    return jnp.where(iota(shape, 0) // size + 8 == iota(shape, 1), 1.0, 0.0).astype(BF16)


def key_place(index):
    level, _, _, keys = GROUPS[index]
    shape = (keys, LANES)
    row, place = iota(shape, 0), iota(shape, 1) - 8
    if level == 0:
        apart = row // BLOCK - place
        blocked = (apart < 0) | (apart > 2)
        places = 2
    elif level == 1:
        there, here = row // HALF, place + 2
        block_apart = jnp.abs(there // 2 - (place + 2) // 2)
        blocked = (block_apart > 1) | (jnp.abs(there - here) < 2)
        places = 4
    else:
        blocked = row // HALF == place + 1
        places = 2
    blocked = blocked & (place >= 0) & (place < places)
    return jnp.where(blocked, BLOCKED, 0.0).astype(BF16)


def dot(a, b, a_dim=1, b_dim=0):
    return lax.dot_general(a, b, (((a_dim,), (b_dim,)), ((), ())), preferred_element_type=F32)


def split(x):
    high = x.astype(BF16)
    return high, (x - high.astype(F32)).astype(BF16)


def head_lanes(rows, width=LANES):
    return iota((rows, width), 1) % LANES < HEAD_DIM


def stacked(x):
    first = head_lanes(x.shape[0]).astype(F32).astype(BF16)
    return jnp.concatenate([x * first, x * (1 - first)], axis=0)


def unstacked(x, rows):
    return jnp.where(head_lanes(rows, x.shape[1]), x[:rows], x[rows:])


def lanes_of(pair, part=0):
    return slice(part * WIDTH + pair * LANES, part * WIDTH + (pair + 1) * LANES)


DOC_LANES = slice(2 * WIDTH, PACK)


def near_window(index, own0, own1, low, high, lanes):
    def rim(ref, level):
        return ref[BLOCK * level : BLOCK * (level + 1), lanes]

    if index == 0:
        parts = [rim(low, 0), own0[0:192, lanes]]
    elif index == 1:
        parts = [own0[64:256, lanes], rim(high, 0)]
    elif index == 2:
        parts = [rim(low, 1), own1[:, lanes], rim(high, 1)]
    else:
        parts = [rim(low, 2), rim(high, 2)]
    return jnp.concatenate(parts, axis=0)


def far_window(refs, lanes):
    return jnp.concatenate([ref[:, lanes] for ref in refs], axis=0)


def fetch(sources, targets, sems):
    copies = [
        pltpu.make_async_copy(source, target, sems.at[i])
        for i, (source, target) in enumerate(zip(sources, targets))
    ]
    for copy in copies:
        copy.start()
    return copies


def coarsen_kernel(
    seg_hbm, k_hbm, v_hbm, up, down, far, third, own0, own1, qdoc, seg, k, v, sems
):
    copies = fetch((seg_hbm, k_hbm, v_hbm), (seg, k, v), sems)
    copies[0].wait()
    marks = jnp.where(seg[...] == iota((LANES, ROWS), 0), 1.0, 0.0).T.astype(BF16)

    def key_side(x):
        doc = iota(x.shape, 1) < DOCS
        return jnp.where(doc, (1.0 - x.astype(F32)) * BLOCKED, 0.0).astype(BF16)

    copies[1].wait()
    copies[2].wait()
    levels = [(k[...], v[...], key_side(marks))]
    qdoc[0:ROWS] = marks
    for level in range(1, LEVELS + 1):
        marks_c = dot(last_table(level), marks).astype(BF16)
        qdoc[AT[level] : AT[level] + COUNT[level]] = marks_c
        keys = dot(gather_table(level, 0.5**level), levels[0][0]).astype(BF16)
        values = dot(gather_table(level), levels[0][1]).astype(BF16)
        levels.append((keys, values, key_side(marks_c)))

    def put(ref, at, level, start, stop):
        for part, lanes in zip(
            levels[level], (slice(0, WIDTH), slice(WIDTH, 2 * WIDTH), DOC_LANES)
        ):
            ref[at : at + stop - start, lanes] = part[start:stop]

    for level in range(3):
        put(up, BLOCK * level, level, COUNT[level] - BLOCK, COUNT[level])
        put(down, BLOCK * level, level, 0, BLOCK)
    put(far, 0, 3, 0, COUNT[3])
    put(far, COUNT[3], 4, 0, COUNT[4])
    put(third, 0, 4, 0, COUNT[4])
    put(own0, 0, 0, 0, COUNT[0])
    put(own1, 0, 1, 0, COUNT[1])


def core_index():
    return lax.axis_index("ctx") % 2


def pair_kernel(far, far_partner, far3, far4):
    even = core_index() == 0
    for out, start, rows in ((far3, 0, 32), (far4, 32, 16)):
        own, other = far[start : start + rows], far_partner[start : start + rows]
        out[0:rows] = jnp.where(even, own, other)
        out[rows : 2 * rows] = jnp.where(even, other, own)


def prepare_kernel(q_hbm, d_hbm, w_hbm, q_out, grad_att, w, d_out, q, sems):
    copies = fetch((q_hbm, d_hbm, w_hbm), (q, d_out, w), sems)
    copies[0].wait()
    for level in range(LEVELS + 1):
        queries = q[...] if level == 0 else dot(gather_table(level, 0.5**level), q[...]).astype(BF16)
        q_out[AT[level] : AT[level] + COUNT[level]] = (queries * SCALE).astype(BF16)
    copies[1].wait()
    copies[2].wait()
    grad_att[...] = dot(d_out[...], w[...], 1, 1)


def attend(queries, query_docs, keys, key_docs, values):
    rows = queries.shape[0]
    scores = dot(
        jnp.concatenate([stacked(queries), query_docs], axis=1),
        jnp.concatenate([keys, key_docs], axis=1),
        1,
        1,
    )
    peak = jnp.maximum(jnp.max(scores, axis=1, keepdims=True), NEGATIVE)
    peak = peak.astype(BF16).astype(F32)
    p = jnp.exp(scores - peak).astype(BF16)
    ones = jnp.ones(values.shape, BF16)
    both = unstacked(dot(p, jnp.concatenate([values, ones], axis=1)), rows)
    wide_peak = jnp.where(head_lanes(rows), peak[:rows], peak[rows:])
    return p, jnp.concatenate([both, wide_peak], axis=1)


def docs_of(index, qdoc):
    level, start, rows, _ = GROUPS[index]
    docs = qdoc[AT[level] + start : AT[level] + start + rows]
    if index in NEAR:
        docs = docs + query_place(index)
    return jnp.concatenate([docs, docs], axis=0)


def near_kernel(q_all, qdoc, own0, own1, low, high, p_out, fine, coarse):
    for index in NEAR:
        level, start, rows, keys = GROUPS[index]
        at = AT[level] + start
        query_docs = docs_of(index, qdoc)
        key_docs = near_window(index, own0, own1, low, high, DOC_LANES) + key_place(index)
        for pair in range(PAIRS):
            window = [
                near_window(index, own0, own1, low, high, lanes_of(pair, part)) for part in (0, 1)
            ]
            p, stats = attend(
                q_all[at : at + rows, lanes_of(pair)], query_docs, window[0], key_docs, window[1]
            )
            p_out[pair, P_AT[index] : P_AT[index] + 2 * rows, 0:keys] = p
            if level == 0:
                fine[pair, at : at + rows] = stats
            else:
                coarse[pair, at - ROWS : at - ROWS + rows] = stats.astype(BF16)


def far_refs(refs):
    own3, got4, third, passed = refs
    return (
        (own3, passed.at[0:64]),
        (got4, passed.at[64:96], third, passed.at[96:112]),
    )


def block_at(block):
    x, y, core = block // 8, block // 2 % 4, block % 2
    return 16 * (16 * core + 4 * y + x)


def merge_kernel(q_all, qdoc, fine, coarse, grad_att, d_out, *refs):
    far = far_refs(refs[:4])
    attended_out, keep, give, p_out, g_out, d_side, d_w = refs[4:]
    docs = [(docs_of(index, qdoc), far_window(ref, DOC_LANES)) for index, ref in zip(FAR, far)]
    shape = (LANES, LANES)
    same_head = jnp.where(iota(shape, 0) // HEAD_DIM == iota(shape, 1) // HEAD_DIM, 1.0, 0.0)
    same_head = same_head.astype(BF16)
    spreads = [None] + [spread_table(level) for level in range(1, LEVELS + 1)]
    gathers = [None] + [gather_table(level) for level in range(1, LEVELS + 1)]
    for pair in range(PAIRS):
        cols = lanes_of(pair)
        packed = [None, coarse[pair, 0:128], coarse[pair, 128:192]]
        for index, ref, (query_docs, key_docs) in zip(FAR, far, docs):
            level, _, rows, keys = GROUPS[index]
            p, stats = attend(
                q_all[AT[level] : AT[level] + rows, cols],
                query_docs,
                far_window(ref, lanes_of(pair)),
                key_docs,
                far_window(ref, lanes_of(pair, 1)),
            )
            p_out[pair, P_AT[index] : P_AT[index] + 2 * rows, 0:keys] = p
            packed.append(stats.astype(BF16))
        wide = [fine[pair]] + [
            dot(spreads[level], packed[level]) for level in range(1, LEVELS + 1)
        ]
        levels = [[x[:, LANES * i : LANES * (i + 1)] for i in range(3)] for x in wide]
        top = functools.reduce(jnp.maximum, [x[2] for x in levels])
        weights = [jnp.exp(x[2] - top) for x in levels]
        norm = functools.reduce(
            jnp.add, [wt * x[1] * float(2**i) for i, (wt, x) in enumerate(zip(weights, levels))]
        )
        numer = functools.reduce(jnp.add, [wt * x[0] for wt, x in zip(weights, levels)])
        inverse = 1.0 / norm
        attended = (numer * inverse).astype(BF16)
        grad_w = dot(attended, d_out[...], 0, 0)
        for block in range(8):
            at = block_at(8 * pair + block)
            d_w[at : at + 16] = grad_w[16 * block : 16 * (block + 1)]
        attended_out[:, cols] = attended
        grad = grad_att[:, cols]
        high_part, low_part = split(grad * attended.astype(F32))
        delta = dot(high_part, same_head) + dot(low_part, same_head)
        for level in range(LEVELS + 1):
            share = weights[level] * inverse
            at, rows = AT[level], COUNT[level]
            if level == 0:
                grad_c, delta_c = share * grad, share * delta
            else:
                d_high, d_low = split(share * delta)
                terms = jnp.concatenate([(share * grad).astype(BF16), d_high, d_low], axis=1)
                summed = dot(gathers[level], terms)
                grad_c = summed[:, :LANES]
                delta_c = summed[:, LANES : 2 * LANES] + summed[:, 2 * LANES :]
            g_out[at : at + rows, cols] = grad_c.astype(BF16)
            d_high, d_low = split(delta_c * -float(2**level))
            upper = iota((rows, LANES), 1) % HEAD_DIM < HALF
            d_side[at : at + rows, cols] = jnp.where(
                upper, d_high.astype(F32), d_low.astype(F32)
            ).astype(BF16)
    core = core_index()
    keep[...] = d_w[pl.ds(pl.multiple_of(core * 256, 256), 256)]
    give[...] = d_w[pl.ds(pl.multiple_of((1 - core) * 256, 256), 256)].astype(BF16)


def attend_back(p, queries, grad, side, keys, values):
    rows = queries.shape[0]
    ones = jnp.where(iota(values.shape, 1) % HALF == 0, 1.0, 0.0).astype(BF16)
    grad = stacked(grad)
    product = dot(
        jnp.concatenate([grad, stacked(side)], axis=1),
        jnp.concatenate([values, ones], axis=1),
        1,
        1,
    )
    ds = (p.astype(F32) * product).astype(BF16)
    grad_q = unstacked(dot(ds, keys), rows) * SCALE
    return grad_q, dot(ds, stacked(queries), 0, 0), dot(p, grad, 0, 0)


def far_back_kernel(p_in, q_all, g_in, d_side, *refs):
    far = far_refs(refs[:4])
    d_q, to_3, to_4, to_third, to_partner = refs[-5:]
    to_far = (
        (to_3, to_partner.at[0:64]),
        (to_4, to_partner.at[64:96], to_third, to_partner.at[96:112]),
    )
    for pair in range(PAIRS):
        cols = lanes_of(pair)
        for index, ref, to in zip(FAR, far, to_far):
            level, _, rows, keys = GROUPS[index]
            at = AT[level]
            grad_q, grad_k, grad_v = attend_back(
                p_in[pair, P_AT[index] : P_AT[index] + 2 * rows, 0:keys],
                q_all[at : at + rows, cols],
                g_in[at : at + rows, cols],
                d_side[at : at + rows, cols],
                far_window(ref, cols),
                far_window(ref, lanes_of(pair, 1)),
            )
            d_q[at - AT[3] : at - AT[3] + rows, cols] = grad_q.astype(BF16)
            start = 0
            for out in to:
                stop = start + out.shape[0]
                out[:, cols] = grad_k[start:stop].astype(BF16)
                out[:, lanes_of(pair, 1)] = grad_v[start:stop].astype(BF16)
                start = stop


NEAR_PARTS = ((0,), (1, 2), (3,))


def near_back(pairs, p_in, q_all, g_in, d_side, own0, own1, low, high, d_far):
    spread = jnp.concatenate([spread_table(level, 0.5**level) for level in (1, 2, 3, 4)], axis=1)
    for pair in pairs:
        cols = lanes_of(pair)
        grads = []
        for index in NEAR:
            level, start, rows, keys = GROUPS[index]
            at = AT[level] + start
            grads.append(
                attend_back(
                    p_in[pair, P_AT[index] : P_AT[index] + 2 * rows, 0:keys],
                    q_all[at : at + rows, cols],
                    g_in[at : at + rows, cols],
                    d_side[at : at + rows, cols],
                    near_window(index, own0, own1, low, high, cols),
                    near_window(index, own0, own1, low, high, lanes_of(pair, 1)),
                )
            )
        coarse = [x[0].astype(BF16) for x in grads[2:]] + [d_far[:, cols]]
        whole = jnp.concatenate([x[0] for x in grads[:2]], axis=0)
        d_q = (whole + dot(spread, jnp.concatenate(coarse, axis=0))).astype(BF16)
        own, to_low, to_high = [], [], []
        for part, value in ((0, 0.5), (1, 1.0)):
            a, b, c, d = (x[1 + part] for x in grads)
            middle = jnp.concatenate([a[64:128], a[128:256] + b[0:128], b[128:192]], axis=0)
            own.append(middle + dot(spread_table(1, value), c[64:192].astype(BF16)))
            to_low.append(jnp.concatenate([a[:64], c[:64], d[:64]], axis=0).astype(BF16))
            to_high.append(jnp.concatenate([b[192:], c[192:], d[64:]], axis=0).astype(BF16))
        yield pair, d_q, own, to_low, to_high


def near_back_first_kernel(pairs, attended, w, *refs):
    inputs, outs = refs[:9], refs[9:]
    layer_out = None
    if attended is not None:
        layer_out, result, sem = outs[-3:]
        result[...] = dot(attended[...], w[...]).astype(BF16)
        copy = pltpu.make_async_copy(result, layer_out, sem)
        copy.start()
    d_q, own_k, own_v, to_low, to_high = outs[:5]
    for pair, dq, own, low, high in near_back(pairs, *inputs):
        at = slice((pair - pairs[0]) * LANES, (pair - pairs[0] + 1) * LANES)
        d_q[:, at], own_k[:, at], own_v[:, at] = dq, own[0], own[1]
        for part in range(2):
            to_low[part, :, at], to_high[part, :, at] = low[part], high[part]
    if attended is not None:
        copy.wait()


def near_back_a_kernel(attended, w, *refs):
    near_back_first_kernel(NEAR_PARTS[0], attended, w, *refs[:9], *refs[-8:])


def near_back_b_kernel(*refs):
    near_back_first_kernel(NEAR_PARTS[1], None, None, *refs[:9], *refs[-5:])


def near_back_c_kernel(*refs):
    inputs, earlier = refs[:9], (refs[9:12], refs[12:15])
    d_q_hbm, own_k, own_v, to_low, to_high, d_q, sems = refs[-7:]
    for pairs, (dq, low, high) in zip(NEAR_PARTS, earlier):
        cols = slice(pairs[0] * LANES, (pairs[-1] + 1) * LANES)
        d_q[:, cols] = dq[...]
        for part in range(2):
            lanes = slice(part * WIDTH + cols.start, part * WIDTH + cols.stop)
            to_low[:, lanes], to_high[:, lanes] = low[part], high[part]
    last = NEAR_PARTS[2][0] * LANES
    before = pltpu.make_async_copy(d_q.at[:, 0:last], d_q_hbm.at[:, 0:last], sems.at[0])
    before.start()
    for pair, dq, own, low, high in near_back(NEAR_PARTS[2], *inputs):
        d_q[:, lanes_of(pair)] = dq
        own_k[...], own_v[...] = own[0], own[1]
        after = pltpu.make_async_copy(
            d_q.at[:, lanes_of(pair)], d_q_hbm.at[:, lanes_of(pair)], sems.at[1]
        )
        after.start()
        for part in range(2):
            to_low[:, lanes_of(pair, part)] = low[part]
            to_high[:, lanes_of(pair, part)] = high[part]
    before.wait()
    after.wait()


def pass_on_kernel(got3, got4, third, own3, out):
    out[0:64] = got3[...]
    out[64:96] = got4[...]
    out[96:112] = third[...]
    own3[...] = jnp.where(core_index() == 0, got3[0:32], got3[32:64])


def far_sum_kernel(to_3, to_4, to_third, swapped, sum3, sum4, sum_third):
    even = core_index() == 0
    own3 = to_3[...].astype(F32)
    sum3[0:32] = (swapped[0:32].astype(F32) + jnp.where(even, own3, 0.0)).astype(BF16)
    sum3[32:64] = (swapped[32:64].astype(F32) + jnp.where(even, 0.0, own3)).astype(BF16)
    sum4[...] = (swapped[64:96].astype(F32) + to_4[...].astype(F32)).astype(BF16)
    sum_third[...] = (swapped[96:112].astype(F32) + to_third[...].astype(F32)).astype(BF16)


def core_rows(ref, core, rows):
    return ref[pl.ds(pl.multiple_of(core * rows, rows), rows)]


def far_split_kernel(back3, back4, give):
    other = 1 - core_index()
    give[0:32] = core_rows(back3, other, 32)
    give[32:48] = core_rows(back4, other, 16)


def halve_kernel(divisor, keep, got, *refs):
    keep_out, give_out, total = refs[-3:]
    total[...] = keep[...] + got[...].astype(F32)
    side = lax.axis_index("ctx") // divisor % 2
    half = total.shape[0] // 2
    keep_out[...] = total[pl.ds(pl.multiple_of(side * half, half), half)]
    give_out[...] = total[pl.ds(pl.multiple_of((1 - side) * half, half), half)].astype(BF16)


def copies_kernel(keep, got, *refs):
    total = keep[...] + got[...].astype(F32)
    for i in range(refs[-1].shape[0]):
        refs[-1][i] = total.astype(BF16)


def last_sum_kernel(parts, out):
    total = parts[0].astype(F32)
    for i in range(1, parts.shape[0]):
        total = total + parts[i].astype(F32)
    out[...] = total.astype(BF16)


def combine_kernel(*refs):
    own, (low, high) = (refs[0:3], refs[3:6]), refs[6:8]
    back3, back4, third, swapped = refs[8:12]
    d_k_hbm, d_v_hbm, d_k, d_v, sems = refs[12:]
    core = core_index()
    far3 = core_rows(back3, core, 32).astype(F32) + swapped[0:32].astype(F32)
    far4 = core_rows(back4, core, 16).astype(F32) + swapped[32:48].astype(F32)
    far4 = far4 + third[...].astype(F32)
    copies = []
    for part, out, out_hbm in ((0, d_k, d_k_hbm), (1, d_v, d_v_hbm)):
        lanes = slice(part * WIDTH, (part + 1) * WIDTH)
        table = jnp.concatenate(
            [spread_table(level, 1.0 if part else 0.5**level) for level in (1, 2, 3, 4)], axis=1
        )

        def rim(ref, level):
            return ref[BLOCK * level : BLOCK * (level + 1), lanes].astype(F32)

        coarse = jnp.concatenate(
            [
                rim(high, 1),
                rim(low, 1),
                rim(low, 2) + rim(high, 2),
                far3[:, lanes],
                far4[:, lanes],
            ],
            axis=0,
        ).astype(BF16)
        whole = jnp.concatenate([x[...] for x in own[part]], axis=1) + dot(table, coarse)
        out[0:64] = (whole[0:64] + rim(high, 0)).astype(BF16)
        out[64:192] = whole[64:192].astype(BF16)
        out[192:256] = (whole[192:256] + rim(low, 0)).astype(BF16)
        copies.append(pltpu.make_async_copy(out, out_hbm, sems.at[part]))
        copies[-1].start()
    for copy in copies:
        copy.wait()


def call(
    kernel, name, outs, args, scratch=(), in_hbm=0, microseconds=1.0, to_hbm=()
):
    vmem, hbm = pl.BlockSpec(memory_space=pltpu.VMEM), pl.BlockSpec(memory_space=pl.ANY)
    return pl.pallas_call(
        kernel,
        name=name,
        out_shape=[jax.ShapeDtypeStruct(shape, dtype) for shape, dtype in outs],
        in_specs=[vmem] * (len(args) - in_hbm) + [hbm] * in_hbm,
        out_specs=[hbm if i in to_hbm else vmem for i in range(len(outs))],
        scratch_shapes=scratch,
        cost_estimate=pl.CostEstimate(
            flops=int(microseconds * 1e9), bytes_accessed=1 << 20, transcendentals=0
        ),
        compiler_params=pltpu.CompilerParams(vmem_limit_bytes=VMEM_MIB * 1024 * 1024),
    )(*args)


def moved(x, route):
    count = lax.axis_size("ctx")
    return lax.ppermute(x, "ctx", [(i, route(i) % count) for i in range(count)])


def partner(i):
    return i ^ 1


def third(i):
    return i - 6 if i // 2 % 2 else i + 6


def route_3(i):
    return i - 2 if i % 2 else i + 2


def route_4(i):
    return i - 4 if i % 2 else i + 4


def back_3(i):
    return i + 2 if i % 2 else i - 2


def back_4(i):
    return i + 4 if i % 2 else i - 4


def body(queries, key_rows, value_rows, segment_ids, w_out, d_out):
    q, k, v, grad_out = queries[0], key_rows[0], value_rows[0], d_out[0]
    tokens, dma = (ROWS, WIDTH), pltpu.SemaphoreType.DMA
    up, down, far, third_rows, own0, own1, qdoc = call(
        coarsen_kernel,
        "coarsen",
        [((192, PACK), BF16), ((192, PACK), BF16), ((48, PACK), BF16), ((16, PACK), BF16)]
        + [((ROWS, PACK), BF16), ((128, PACK), BF16), ((ALL_ROWS, LANES), BF16)],
        [segment_ids, k, v],
        [pltpu.VMEM((1, ROWS), jnp.int32)] + [pltpu.VMEM(tokens, BF16)] * 2 + [dma((3,))],
        in_hbm=3,
    )
    far_partner = moved(far, partner)
    far3, far4 = call(
        pair_kernel, "pair", [((64, PACK), BF16), ((32, PACK), BF16)], [far, far_partner]
    )
    q_all, grad_att, w, grad_rows = call(
        prepare_kernel,
        "prepare",
        [((ALL_ROWS, WIDTH), BF16), (tokens, F32), ((WIDTH, WIDTH), BF16), (tokens, BF16)],
        [q, grad_out, w_out],
        [pltpu.VMEM(tokens, BF16), dma((3,))],
        in_hbm=3,
    )
    low = moved(up, lambda i: i + 1)
    high = moved(down, lambda i: i - 1)
    got3 = moved(far3, route_3)
    got4 = moved(far4, route_4)
    got_third = moved(third_rows, third)
    low, high, got3 = lax.optimization_barrier((low, high, got3))
    own3, passed = call(
        pass_on_kernel,
        "pass_on",
        [((32, PACK), BF16), ((112, PACK), BF16)],
        [got3, got4, got_third],
    )
    far = (own3, got4, got_third, moved(passed, partner))
    near = (own0, own1, low, high)
    p_near, fine, coarse = call(
        near_kernel,
        "near",
        [
            ((PAIRS, P_NEAR, 256), BF16),
            ((PAIRS, ROWS, 3 * LANES), F32),
            ((PAIRS, 192, 3 * LANES), BF16),
        ],
        [q_all, qdoc, *near],
        microseconds=50,
    )
    attended, keep, give, p_far, g, d_side = call(
        merge_kernel,
        "merge",
        [(tokens, BF16), ((256, WIDTH), F32), ((256, WIDTH), BF16)]
        + [((PAIRS, P_FAR, LANES), BF16)]
        + [((ALL_ROWS, WIDTH), BF16)] * 2,
        [q_all, qdoc, fine, coarse, grad_att, grad_rows, *far],
        [pltpu.VMEM((WIDTH, WIDTH), F32)],
        microseconds=6,
    )
    got_w = moved(give, partner)

    def halved(keep, got, divisor, route, *after):
        rows = keep.shape[0] // 2
        keep, give = call(
            functools.partial(halve_kernel, divisor),
            "halve_" + str(rows),
            [((rows, WIDTH), F32), ((rows, WIDTH), BF16)],
            [keep, got, *after],
            [pltpu.VMEM((2 * rows, WIDTH), F32)],
            in_hbm=len(after),
        )
        return keep, moved(give, route)

    keep, got_w = halved(keep, got_w, 4, lambda i: i ^ 6)
    d_far, *to_far, to_partner = call(
        far_back_kernel,
        "far_back",
        [((48, WIDTH), BF16), ((32, 2 * WIDTH), BF16), ((32, 2 * WIDTH), BF16)]
        + [((16, 2 * WIDTH), BF16), ((112, 2 * WIDTH), BF16)],
        [p_far, q_all, g, d_side, *far, keep],
        in_hbm=1,
    )
    swapped = moved(to_partner, partner)


    def part_outs(part):
        width = len(NEAR_PARTS[part]) * LANES
        return [((ROWS, width), BF16), ((ROWS, width), F32), ((ROWS, width), F32)] + [
            ((2, 192, width), BF16)
        ] * 2

    args = [p_near, q_all, g, d_side, *near, d_far]
    sum3, sum4, sum_third = call(
        far_sum_kernel,
        "far_sum",
        [((64, 2 * WIDTH), BF16), ((32, 2 * WIDTH), BF16), ((16, 2 * WIDTH), BF16)],
        [*to_far, swapped],
    )
    back3 = moved(sum3, back_3)
    back4 = moved(sum4, back_4)
    back_third = moved(sum_third, third)
    keep, got_w = halved(keep, got_w, 2, lambda i: i ^ 2, sum3)
    *part_a, layer_out = call(
        near_back_a_kernel,
        "near_back_a",
        part_outs(0) + [(tokens, BF16)],
        [attended, w, *args, keep],
        [pltpu.VMEM(tokens, BF16), dma(())],
        in_hbm=1,
        microseconds=3,
        to_hbm=(5,),
    )
    keep, got_w = halved(keep, got_w, 16, lambda i: i ^ 24, part_a[0])
    part_b = call(
        near_back_b_kernel,
        "near_back_b",
        part_outs(1),
        [*args, part_a[0], keep],
        in_hbm=2,
        microseconds=4,
    )
    keep, got_w = halved(keep, got_w, 8, lambda i: i ^ 8, part_b[0])
    give = call(far_split_kernel, "far_split", [((48, 2 * WIDTH), BF16)], [back3, back4])[0]
    swapped = moved(give, partner)
    d_q, own_k, own_v, to_low, to_high = call(
        near_back_c_kernel,
        "near_back_c",
        [(tokens, BF16), ((ROWS, LANES), F32), ((ROWS, LANES), F32)]
        + [((192, 2 * WIDTH), BF16)] * 2,
        [*args, part_a[0], *part_a[3:], part_b[0], *part_b[3:]]
        + [keep, give, back_third],
        [pltpu.VMEM(tokens, BF16), dma((2,))],
        in_hbm=3,
        microseconds=2,
        to_hbm=(0,),
    )
    low_back = moved(to_low, lambda i: i - 1)
    high_back = moved(to_high, lambda i: i + 1)
    copies = call(
        copies_kernel,
        "copies",
        [((lax.axis_size("dp"), 16, WIDTH), BF16)],
        [keep, got_w, to_low],
        in_hbm=1,
    )[0]
    copies = lax.all_to_all(copies, "dp", 0, 0, tiled=True)
    d_w = call(last_sum_kernel, "last_sum", [((16, WIDTH), BF16)], [copies])[0]
    d_k, d_v = call(
        combine_kernel,
        "combine",
        [(tokens, BF16)] * 2,
        [part_a[1], part_b[1], own_k, part_a[2], part_b[2], own_v, low_back, high_back]
        + [back3, back4, back_third, swapped],
        [pltpu.VMEM(tokens, BF16)] * 2 + [dma((2,))],
        to_hbm=(0, 1),
    )
    return layer_out[None], d_q[None], d_k[None], d_v[None], d_w


def solution(mesh):
    tokens = P("dp", "ctx", None)
    return jax.shard_map(
        body,
        mesh=mesh,
        in_specs=(tokens, tokens, tokens, P("dp", "ctx"), P(), tokens),
        out_specs=(tokens, tokens, tokens, tokens, P("ctx", None)),
        check_vma=False,
    )
```

```python
import functools

import jax
import jax.numpy as jnp
from jax import lax
from jax.experimental import pallas as pl
from jax.experimental.pallas import tpu as pltpu
from jax.sharding import PartitionSpec as P

HEAD_DIM = 64
BLOCK = 64
HALF = 32
LEVELS = 4
ROWS = 256
WIDTH = 512
PAIRS = 4
LANES = 128
DOCS = 4
NEGATIVE = -1e30
BLOCKED = -2e30
SCALE = HEAD_DIM**-0.5
PACK = 2 * WIDTH + LANES
COUNT = (256, 128, 64, 32, 16)
AT = (0, 256, 384, 448, 480)
ALL_ROWS = 496
F32 = jnp.float32
BF16 = jnp.bfloat16
VMEM_MIB = 20

GROUPS = (
    (0, 0, 128, 256),
    (0, 128, 128, 256),
    (1, 0, 128, 256),
    (2, 0, 64, 128),
    (3, 0, 32, 96),
    (4, 0, 16, 96),
)
NEAR = (0, 1, 2, 3)
FAR = (4, 5)
P_AT = {0: 0, 1: 256, 2: 512, 3: 768, 4: 0, 5: 64}
P_NEAR, P_FAR = 896, 96


def iota(shape, dim):
    return lax.broadcasted_iota(jnp.int32, shape, dim)


def gather_table(level, value=1.0):
    shape = (COUNT[level], ROWS)
    return jnp.where(iota(shape, 1) // 2**level == iota(shape, 0), value, 0.0).astype(BF16)


def spread_table(level, value=1.0):
    shape = (ROWS, COUNT[level])
    return jnp.where(iota(shape, 0) // 2**level == iota(shape, 1), value, 0.0).astype(BF16)


def last_table(level):
    shape = (COUNT[level], ROWS)
    last = iota(shape, 0) * 2**level + (2**level - 1)
    return jnp.where(iota(shape, 1) == last, 1.0, 0.0).astype(BF16)


def query_place(index):
    level, _, rows, _ = GROUPS[index]
    size = BLOCK if level == 0 else HALF
    shape = (rows, LANES)
    return jnp.where(iota(shape, 0) // size + 8 == iota(shape, 1), 1.0, 0.0).astype(BF16)


def key_place(index):
    level, _, _, keys = GROUPS[index]
    shape = (keys, LANES)
    row, place = iota(shape, 0), iota(shape, 1) - 8
    if level == 0:
        apart = row // BLOCK - place
        blocked = (apart < 0) | (apart > 2)
        places = 2
    elif level == 1:
        there, here = row // HALF, place + 2
        block_apart = jnp.abs(there // 2 - (place + 2) // 2)
        blocked = (block_apart > 1) | (jnp.abs(there - here) < 2)
        places = 4
    else:
        blocked = row // HALF == place + 1
        places = 2
    blocked = blocked & (place >= 0) & (place < places)
    return jnp.where(blocked, BLOCKED, 0.0).astype(BF16)


def dot(a, b, a_dim=1, b_dim=0):
    return lax.dot_general(a, b, (((a_dim,), (b_dim,)), ((), ())), preferred_element_type=F32)


def split(x):
    high = x.astype(BF16)
    return high, (x - high.astype(F32)).astype(BF16)


def head_lanes(rows, width=LANES):
    return iota((rows, width), 1) % LANES < HEAD_DIM


def stacked(x):
    first = head_lanes(x.shape[0]).astype(F32).astype(BF16)
    return jnp.concatenate([x * first, x * (1 - first)], axis=0)


def unstacked(x, rows):
    return jnp.where(head_lanes(rows, x.shape[1]), x[:rows], x[rows:])


def lanes_of(pair, part=0):
    return slice(part * WIDTH + pair * LANES, part * WIDTH + (pair + 1) * LANES)


DOC_LANES = slice(2 * WIDTH, PACK)


def near_window(index, own0, own1, low, high, lanes):
    def rim(ref, level):
        return ref[BLOCK * level : BLOCK * (level + 1), lanes]

    if index == 0:
        parts = [rim(low, 0), own0[0:192, lanes]]
    elif index == 1:
        parts = [own0[64:256, lanes], rim(high, 0)]
    elif index == 2:
        parts = [rim(low, 1), own1[:, lanes], rim(high, 1)]
    else:
        parts = [rim(low, 2), rim(high, 2)]
    return jnp.concatenate(parts, axis=0)


def far_window(refs, lanes):
    return jnp.concatenate([ref[:, lanes] for ref in refs], axis=0)


def fetch(sources, targets, sems):
    copies = [
        pltpu.make_async_copy(source, target, sems.at[i])
        for i, (source, target) in enumerate(zip(sources, targets))
    ]
    for copy in copies:
        copy.start()
    return copies


def coarsen_kernel(
    seg_hbm, k_hbm, v_hbm, up, down, far, third, own0, own1, qdoc, seg, k, v, sems
):
    copies = fetch((seg_hbm, k_hbm, v_hbm), (seg, k, v), sems)
    copies[0].wait()
    marks = jnp.where(seg[...] == iota((LANES, ROWS), 0), 1.0, 0.0).T.astype(BF16)

    def key_side(x):
        doc = iota(x.shape, 1) < DOCS
        return jnp.where(doc, (1.0 - x.astype(F32)) * BLOCKED, 0.0).astype(BF16)

    copies[1].wait()
    copies[2].wait()
    levels = [(k[...], v[...], key_side(marks))]
    qdoc[0:ROWS] = marks
    for level in range(1, LEVELS + 1):
        marks_c = dot(last_table(level), marks).astype(BF16)
        qdoc[AT[level] : AT[level] + COUNT[level]] = marks_c
        keys = dot(gather_table(level, 0.5**level), levels[0][0]).astype(BF16)
        values = dot(gather_table(level), levels[0][1]).astype(BF16)
        levels.append((keys, values, key_side(marks_c)))

    def put(ref, at, level, start, stop):
        for part, lanes in zip(
            levels[level], (slice(0, WIDTH), slice(WIDTH, 2 * WIDTH), DOC_LANES)
        ):
            ref[at : at + stop - start, lanes] = part[start:stop]

    for level in range(3):
        put(up, BLOCK * level, level, COUNT[level] - BLOCK, COUNT[level])
        put(down, BLOCK * level, level, 0, BLOCK)
    put(far, 0, 3, 0, COUNT[3])
    put(far, COUNT[3], 4, 0, COUNT[4])
    put(third, 0, 4, 0, COUNT[4])
    put(own0, 0, 0, 0, COUNT[0])
    put(own1, 0, 1, 0, COUNT[1])


def core_index():
    return lax.axis_index("ctx") % 2


def pair_kernel(far, far_partner, far3, far4):
    even = core_index() == 0
    for out, start, rows in ((far3, 0, 32), (far4, 32, 16)):
        own, other = far[start : start + rows], far_partner[start : start + rows]
        out[0:rows] = jnp.where(even, own, other)
        out[rows : 2 * rows] = jnp.where(even, other, own)


def prepare_kernel(q_hbm, d_hbm, w_hbm, q_out, grad_att, w, d_out, q, sems):
    copies = fetch((q_hbm, d_hbm, w_hbm), (q, d_out, w), sems)
    copies[0].wait()
    for level in range(LEVELS + 1):
        queries = q[...] if level == 0 else dot(gather_table(level, 0.5**level), q[...]).astype(BF16)
        q_out[AT[level] : AT[level] + COUNT[level]] = (queries * SCALE).astype(BF16)
    copies[1].wait()
    copies[2].wait()
    grad_att[...] = dot(d_out[...], w[...], 1, 1)


def attend(queries, query_docs, keys, key_docs, values):
    rows = queries.shape[0]
    scores = dot(
        jnp.concatenate([stacked(queries), query_docs], axis=1),
        jnp.concatenate([keys, key_docs], axis=1),
        1,
        1,
    )
    peak = jnp.maximum(jnp.max(scores, axis=1, keepdims=True), NEGATIVE)
    peak = peak.astype(BF16).astype(F32)
    p = jnp.exp(scores - peak).astype(BF16)
    ones = jnp.ones(values.shape, BF16)
    both = unstacked(dot(p, jnp.concatenate([values, ones], axis=1)), rows)
    wide_peak = jnp.where(head_lanes(rows), peak[:rows], peak[rows:])
    return p, jnp.concatenate([both, wide_peak], axis=1)


def docs_of(index, qdoc):
    level, start, rows, _ = GROUPS[index]
    docs = qdoc[AT[level] + start : AT[level] + start + rows]
    if index in NEAR:
        docs = docs + query_place(index)
    return jnp.concatenate([docs, docs], axis=0)


def near_kernel(q_all, qdoc, own0, own1, low, high, p_out, fine, coarse):
    for index in NEAR:
        level, start, rows, keys = GROUPS[index]
        at = AT[level] + start
        query_docs = docs_of(index, qdoc)
        key_docs = near_window(index, own0, own1, low, high, DOC_LANES) + key_place(index)
        for pair in range(PAIRS):
            window = [
                near_window(index, own0, own1, low, high, lanes_of(pair, part)) for part in (0, 1)
            ]
            p, stats = attend(
                q_all[at : at + rows, lanes_of(pair)], query_docs, window[0], key_docs, window[1]
            )
            p_out[pair, P_AT[index] : P_AT[index] + 2 * rows, 0:keys] = p
            if level == 0:
                fine[pair, at : at + rows] = stats
            else:
                coarse[pair, at - ROWS : at - ROWS + rows] = stats.astype(BF16)


def far_refs(refs):
    own3, got4, third, passed = refs
    return (
        (own3, passed.at[0:64]),
        (got4, passed.at[64:96], third, passed.at[96:112]),
    )


def block_at(block):
    x, y, core = block // 8, block // 2 % 4, block % 2
    return 16 * (16 * core + 4 * y + x)


def merge_kernel(q_all, qdoc, fine, coarse, grad_att, d_out, *refs):
    far = far_refs(refs[:4])
    attended_out, keep, give, p_out, g_out, d_side, d_w = refs[4:]
    docs = [(docs_of(index, qdoc), far_window(ref, DOC_LANES)) for index, ref in zip(FAR, far)]
    shape = (LANES, LANES)
    same_head = jnp.where(iota(shape, 0) // HEAD_DIM == iota(shape, 1) // HEAD_DIM, 1.0, 0.0)
    same_head = same_head.astype(BF16)
    spreads = [None] + [spread_table(level) for level in range(1, LEVELS + 1)]
    gathers = [None] + [gather_table(level) for level in range(1, LEVELS + 1)]
    for pair in range(PAIRS):
        cols = lanes_of(pair)
        packed = [None, coarse[pair, 0:128], coarse[pair, 128:192]]
        for index, ref, (query_docs, key_docs) in zip(FAR, far, docs):
            level, _, rows, keys = GROUPS[index]
            p, stats = attend(
                q_all[AT[level] : AT[level] + rows, cols],
                query_docs,
                far_window(ref, lanes_of(pair)),
                key_docs,
                far_window(ref, lanes_of(pair, 1)),
            )
            p_out[pair, P_AT[index] : P_AT[index] + 2 * rows, 0:keys] = p
            packed.append(stats.astype(BF16))
        wide = [fine[pair]] + [
            dot(spreads[level], packed[level]) for level in range(1, LEVELS + 1)
        ]
        levels = [[x[:, LANES * i : LANES * (i + 1)] for i in range(3)] for x in wide]
        top = functools.reduce(jnp.maximum, [x[2] for x in levels])
        weights = [jnp.exp(x[2] - top) for x in levels]
        norm = functools.reduce(
            jnp.add, [wt * x[1] * float(2**i) for i, (wt, x) in enumerate(zip(weights, levels))]
        )
        numer = functools.reduce(jnp.add, [wt * x[0] for wt, x in zip(weights, levels)])
        inverse = 1.0 / norm
        attended = (numer * inverse).astype(BF16)
        grad_w = dot(attended, d_out[...], 0, 0)
        for block in range(8):
            at = block_at(8 * pair + block)
            d_w[at : at + 16] = grad_w[16 * block : 16 * (block + 1)]
        attended_out[:, cols] = attended
        grad = grad_att[:, cols]
        high_part, low_part = split(grad * attended.astype(F32))
        delta = dot(high_part, same_head) + dot(low_part, same_head)
        for level in range(LEVELS + 1):
            share = weights[level] * inverse
            at, rows = AT[level], COUNT[level]
            if level == 0:
                grad_c, delta_c = share * grad, share * delta
            else:
                d_high, d_low = split(share * delta)
                terms = jnp.concatenate([(share * grad).astype(BF16), d_high, d_low], axis=1)
                summed = dot(gathers[level], terms)
                grad_c = summed[:, :LANES]
                delta_c = summed[:, LANES : 2 * LANES] + summed[:, 2 * LANES :]
            g_out[at : at + rows, cols] = grad_c.astype(BF16)
            d_high, d_low = split(delta_c * -float(2**level))
            upper = iota((rows, LANES), 1) % HEAD_DIM < HALF
            d_side[at : at + rows, cols] = jnp.where(
                upper, d_high.astype(F32), d_low.astype(F32)
            ).astype(BF16)
    core = core_index()
    keep[...] = d_w[pl.ds(pl.multiple_of(core * 256, 256), 256)]
    give[...] = d_w[pl.ds(pl.multiple_of((1 - core) * 256, 256), 256)].astype(BF16)


def attend_back(p, queries, grad, side, keys, values):
    rows = queries.shape[0]
    ones = jnp.where(iota(values.shape, 1) % HALF == 0, 1.0, 0.0).astype(BF16)
    grad = stacked(grad)
    product = dot(
        jnp.concatenate([grad, stacked(side)], axis=1),
        jnp.concatenate([values, ones], axis=1),
        1,
        1,
    )
    ds = (p.astype(F32) * product).astype(BF16)
    grad_q = unstacked(dot(ds, keys), rows) * SCALE
    return grad_q, dot(ds, stacked(queries), 0, 0), dot(p, grad, 0, 0)


PARTNER_ROWS = 112
MESSAGE_ROWS = 256 + 2 * PARTNER_ROWS


def far_back_kernel(p_in, q_all, g_in, d_side, own3, got4, third, passed, give, *refs):
    far = far_refs((own3, got4, third, passed))
    d_q, to_3, to_4, to_third, message = refs
    message[0:256] = give[...]
    to_far = ((to_3, (0, 64)), (to_4, (64, 96), to_third, (96, 112)))
    for pair in range(PAIRS):
        cols = lanes_of(pair)
        for index, ref, to in zip(FAR, far, to_far):
            level, _, rows, keys = GROUPS[index]
            at = AT[level]
            grad_q, grad_k, grad_v = attend_back(
                p_in[pair, P_AT[index] : P_AT[index] + 2 * rows, 0:keys],
                q_all[at : at + rows, cols],
                g_in[at : at + rows, cols],
                d_side[at : at + rows, cols],
                far_window(ref, cols),
                far_window(ref, lanes_of(pair, 1)),
            )
            d_q[at - AT[3] : at - AT[3] + rows, cols] = grad_q.astype(BF16)
            start = 0
            for out in to:
                partners = isinstance(out, tuple)
                stop = start + (out[1] - out[0] if partners else out.shape[0])
                for part, grad in enumerate((grad_k, grad_v)):
                    rows = grad[start:stop].astype(BF16)
                    if partners:
                        first = 256 + part * PARTNER_ROWS
                        message[first + out[0] : first + out[1], cols] = rows
                    else:
                        out[:, lanes_of(pair, part)] = rows
                start = stop


NEAR_PARTS = ((0,), (1,), (2,), (3,))


def near_back(pairs, p_in, q_all, g_in, d_side, own0, own1, low, high, d_far):
    spread = jnp.concatenate([spread_table(level, 0.5**level) for level in (1, 2, 3, 4)], axis=1)
    for pair in pairs:
        cols = lanes_of(pair)
        grads = []
        for index in NEAR:
            level, start, rows, keys = GROUPS[index]
            at = AT[level] + start
            grads.append(
                attend_back(
                    p_in[pair, P_AT[index] : P_AT[index] + 2 * rows, 0:keys],
                    q_all[at : at + rows, cols],
                    g_in[at : at + rows, cols],
                    d_side[at : at + rows, cols],
                    near_window(index, own0, own1, low, high, cols),
                    near_window(index, own0, own1, low, high, lanes_of(pair, 1)),
                )
            )
        coarse = [x[0].astype(BF16) for x in grads[2:]] + [d_far[:, cols]]
        whole = jnp.concatenate([x[0] for x in grads[:2]], axis=0)
        d_q = (whole + dot(spread, jnp.concatenate(coarse, axis=0))).astype(BF16)
        own, to_low, to_high = [], [], []
        for part, value in ((0, 0.5), (1, 1.0)):
            a, b, c, d = (x[1 + part] for x in grads)
            middle = jnp.concatenate([a[64:128], a[128:256] + b[0:128], b[128:192]], axis=0)
            own.append(middle + dot(spread_table(1, value), c[64:192].astype(BF16)))
            to_low.append(jnp.concatenate([a[:64], c[:64], d[:64]], axis=0).astype(BF16))
            to_high.append(jnp.concatenate([b[192:], c[192:], d[64:]], axis=0).astype(BF16))
        yield pair, d_q, own, to_low, to_high


def near_back_first_kernel(pairs, attended, w, *refs):
    inputs, outs = refs[:9], refs[9:]
    layer_out = None
    if attended is not None:
        layer_out, result, sem = outs[-3:]
        result[...] = dot(attended[...], w[...]).astype(BF16)
        copy = pltpu.make_async_copy(result, layer_out, sem)
        copy.start()
    d_q, own_k, own_v, to_low, to_high = outs[:5]
    for pair, dq, own, low, high in near_back(pairs, *inputs):
        at = slice((pair - pairs[0]) * LANES, (pair - pairs[0] + 1) * LANES)
        d_q[:, at], own_k[:, at], own_v[:, at] = dq, own[0], own[1]
        for part in range(2):
            to_low[part, :, at], to_high[part, :, at] = low[part], high[part]
    if attended is not None:
        copy.wait()


def near_back_a_kernel(attended, w, *refs):
    near_back_first_kernel(NEAR_PARTS[0], attended, w, *refs)


def near_back_more_kernel(pairs, *refs):
    near_back_first_kernel(pairs, None, None, *refs[:9], *refs[-5:])


def near_back_last_kernel(*refs):
    inputs, earlier = refs[:9], [refs[at : at + 3] for at in (9, 12, 15)]
    d_q_hbm, own_k, own_v, to_low, to_high, d_q, sems = refs[-7:]
    for pairs, (dq, low, high) in zip(NEAR_PARTS, earlier):
        cols = slice(pairs[0] * LANES, (pairs[-1] + 1) * LANES)
        d_q[:, cols] = dq[...]
        for part in range(2):
            lanes = slice(part * WIDTH + cols.start, part * WIDTH + cols.stop)
            to_low[:, lanes], to_high[:, lanes] = low[part], high[part]
    last = NEAR_PARTS[-1][0] * LANES
    before = pltpu.make_async_copy(d_q.at[:, 0:last], d_q_hbm.at[:, 0:last], sems.at[0])
    before.start()
    for pair, dq, own, low, high in near_back(NEAR_PARTS[-1], *inputs):
        d_q[:, lanes_of(pair)] = dq
        own_k[...], own_v[...] = own[0], own[1]
        after = pltpu.make_async_copy(
            d_q.at[:, lanes_of(pair)], d_q_hbm.at[:, lanes_of(pair)], sems.at[1]
        )
        after.start()
        for part in range(2):
            to_low[:, lanes_of(pair, part)] = low[part]
            to_high[:, lanes_of(pair, part)] = high[part]
    before.wait()
    after.wait()


def pass_on_kernel(got3, got4, third, own3, out):
    out[0:64] = got3[...]
    out[64:96] = got4[...]
    out[96:112] = third[...]
    own3[...] = jnp.where(core_index() == 0, got3[0:32], got3[32:64])


def partner_sum_kernel(to_3, to_4, to_third, keep, message, *refs):
    sum3, sum4, sum_third, keep_out, give_out, total = refs[-6:]
    even = core_index() == 0
    for part in range(2):
        lanes = slice(part * WIDTH, (part + 1) * WIDTH)
        at = 256 + part * PARTNER_ROWS
        own3 = to_3[:, lanes].astype(F32)

        def came(start, stop):
            return message[at + start : at + stop].astype(F32)

        sum3[0:32, lanes] = (came(0, 32) + jnp.where(even, own3, 0.0)).astype(BF16)
        sum3[32:64, lanes] = (came(32, 64) + jnp.where(even, 0.0, own3)).astype(BF16)
        sum4[:, lanes] = (came(64, 96) + to_4[:, lanes].astype(F32)).astype(BF16)
        sum_third[:, lanes] = (came(96, 112) + to_third[:, lanes].astype(F32)).astype(BF16)
    total[...] = keep[...] + message[0:256].astype(F32)
    halve(total, 4, keep_out, give_out)


def halve(total, divisor, keep, give):
    side = lax.axis_index("ctx") // divisor % 2
    half = total.shape[0] // 2
    keep[...] = total[pl.ds(pl.multiple_of(side * half, half), half)]
    give[...] = total[pl.ds(pl.multiple_of((1 - side) * half, half), half)].astype(BF16)


def core_rows(ref, core, rows):
    return ref[pl.ds(pl.multiple_of(core * rows, rows), rows)]


def far_split_kernel(back3, back4, give):
    other = 1 - core_index()
    give[0:32] = core_rows(back3, other, 32)
    give[32:48] = core_rows(back4, other, 16)


def halve_kernel(divisor, keep, got, *refs):
    keep_out, give_out, total = refs[-3:]
    total[...] = keep[...] + got[...].astype(F32)
    halve(total, divisor, keep_out, give_out)


def copies_kernel(keep, got, *refs):
    total = keep[...] + got[...].astype(F32)
    for i in range(refs[-1].shape[0]):
        refs[-1][i] = total.astype(BF16)


def last_sum_kernel(parts, _, out):
    total = parts[0].astype(F32)
    for i in range(1, parts.shape[0]):
        total = total + parts[i].astype(F32)
    out[...] = total.astype(BF16)


def combine_kernel(*refs):
    own, (low, high) = (refs[0:4], refs[4:8]), refs[8:10]
    back3, back4, third, swapped = refs[10:14]
    d_k_hbm, d_v_hbm, finished, d_k, d_v, sems = refs[14:]
    finished[...] = jnp.zeros(finished.shape, F32)
    core = core_index()
    far3 = core_rows(back3, core, 32).astype(F32) + swapped[0:32].astype(F32)
    far4 = core_rows(back4, core, 16).astype(F32) + swapped[32:48].astype(F32)
    far4 = far4 + third[...].astype(F32)
    copies = []
    for part, out, out_hbm in ((0, d_k, d_k_hbm), (1, d_v, d_v_hbm)):
        lanes = slice(part * WIDTH, (part + 1) * WIDTH)
        table = jnp.concatenate(
            [spread_table(level, 1.0 if part else 0.5**level) for level in (1, 2, 3, 4)], axis=1
        )

        def rim(ref, level):
            return ref[BLOCK * level : BLOCK * (level + 1), lanes].astype(F32)

        coarse = jnp.concatenate(
            [
                rim(high, 1),
                rim(low, 1),
                rim(low, 2) + rim(high, 2),
                far3[:, lanes],
                far4[:, lanes],
            ],
            axis=0,
        ).astype(BF16)
        whole = jnp.concatenate([x[...] for x in own[part]], axis=1) + dot(table, coarse)
        out[0:64] = (whole[0:64] + rim(high, 0)).astype(BF16)
        out[64:192] = whole[64:192].astype(BF16)
        out[192:256] = (whole[192:256] + rim(low, 0)).astype(BF16)
        copies.append(pltpu.make_async_copy(out, out_hbm, sems.at[part]))
        copies[-1].start()
    for copy in copies:
        copy.wait()


def call(
    kernel, name, outs, args, scratch=(), in_hbm=0, microseconds=1.0, to_hbm=()
):
    vmem, hbm = pl.BlockSpec(memory_space=pltpu.VMEM), pl.BlockSpec(memory_space=pl.ANY)
    return pl.pallas_call(
        kernel,
        name=name,
        out_shape=[jax.ShapeDtypeStruct(shape, dtype) for shape, dtype in outs],
        in_specs=[vmem] * (len(args) - in_hbm) + [hbm] * in_hbm,
        out_specs=[hbm if i in to_hbm else vmem for i in range(len(outs))],
        scratch_shapes=scratch,
        cost_estimate=pl.CostEstimate(
            flops=int(microseconds * 1e9), bytes_accessed=1 << 20, transcendentals=0
        ),
        compiler_params=pltpu.CompilerParams(vmem_limit_bytes=VMEM_MIB * 1024 * 1024),
    )(*args)


def moved(x, route):
    count = lax.axis_size("ctx")
    return lax.ppermute(x, "ctx", [(i, route(i) % count) for i in range(count)])


def partner(i):
    return i ^ 1


def third(i):
    return i - 6 if i // 2 % 2 else i + 6


def route_3(i):
    return i - 2 if i % 2 else i + 2


def route_4(i):
    return i - 4 if i % 2 else i + 4


def back_3(i):
    return i + 2 if i % 2 else i - 2


def back_4(i):
    return i + 4 if i % 2 else i - 4


def body(queries, key_rows, value_rows, segment_ids, w_out, d_out):
    q, k, v, grad_out = queries[0], key_rows[0], value_rows[0], d_out[0]
    tokens, dma = (ROWS, WIDTH), pltpu.SemaphoreType.DMA
    up, down, far, third_rows, own0, own1, qdoc = call(
        coarsen_kernel,
        "coarsen",
        [((192, PACK), BF16), ((192, PACK), BF16), ((48, PACK), BF16), ((16, PACK), BF16)]
        + [((ROWS, PACK), BF16), ((128, PACK), BF16), ((ALL_ROWS, LANES), BF16)],
        [segment_ids, k, v],
        [pltpu.VMEM((1, ROWS), jnp.int32)] + [pltpu.VMEM(tokens, BF16)] * 2 + [dma((3,))],
        in_hbm=3,
    )
    far_partner = moved(far, partner)
    far3, far4 = call(
        pair_kernel, "pair", [((64, PACK), BF16), ((32, PACK), BF16)], [far, far_partner]
    )
    q_all, grad_att, w, grad_rows = call(
        prepare_kernel,
        "prepare",
        [((ALL_ROWS, WIDTH), BF16), (tokens, F32), ((WIDTH, WIDTH), BF16), (tokens, BF16)],
        [q, grad_out, w_out],
        [pltpu.VMEM(tokens, BF16), dma((3,))],
        in_hbm=3,
    )
    low = moved(up, lambda i: i + 1)
    high = moved(down, lambda i: i - 1)
    got3 = moved(far3, route_3)
    got4 = moved(far4, route_4)
    got_third = moved(third_rows, third)
    low, high, got3 = lax.optimization_barrier((low, high, got3))
    own3, passed = call(
        pass_on_kernel,
        "pass_on",
        [((32, PACK), BF16), ((112, PACK), BF16)],
        [got3, got4, got_third],
    )
    far = (own3, got4, got_third, moved(passed, partner))
    near = (own0, own1, low, high)
    p_near, fine, coarse = call(
        near_kernel,
        "near",
        [
            ((PAIRS, P_NEAR, 256), BF16),
            ((PAIRS, ROWS, 3 * LANES), F32),
            ((PAIRS, 192, 3 * LANES), BF16),
        ],
        [q_all, qdoc, *near],
        microseconds=50,
    )
    attended, keep, give, p_far, g, d_side = call(
        merge_kernel,
        "merge",
        [(tokens, BF16), ((256, WIDTH), F32), ((256, WIDTH), BF16)]
        + [((PAIRS, P_FAR, LANES), BF16)]
        + [((ALL_ROWS, WIDTH), BF16)] * 2,
        [q_all, qdoc, fine, coarse, grad_att, grad_rows, *far],
        [pltpu.VMEM((WIDTH, WIDTH), F32)],
        microseconds=6,
    )
    def halved(keep, got, divisor, route, *after):
        rows = keep.shape[0] // 2
        keep, give = call(
            functools.partial(halve_kernel, divisor),
            "halve_" + str(rows),
            [((rows, WIDTH), F32), ((rows, WIDTH), BF16)],
            [keep, got, *after],
            [pltpu.VMEM((2 * rows, WIDTH), F32)],
            in_hbm=len(after),
        )
        return keep, moved(give, route)

    d_far, *to_far, message = call(
        far_back_kernel,
        "far_back",
        [((48, WIDTH), BF16), ((32, 2 * WIDTH), BF16), ((32, 2 * WIDTH), BF16)]
        + [((16, 2 * WIDTH), BF16), ((MESSAGE_ROWS, WIDTH), BF16)],
        [p_far, q_all, g, d_side, *far, give],
    )
    message = moved(message, partner)

    def part_outs(part):
        width = len(NEAR_PARTS[part]) * LANES
        return [((ROWS, width), BF16), ((ROWS, width), F32), ((ROWS, width), F32)] + [
            ((2, 192, width), BF16)
        ] * 2

    args = [p_near, q_all, g, d_side, *near, d_far]
    *part_a, layer_out = call(
        near_back_a_kernel,
        "near_back_a",
        part_outs(0) + [(tokens, BF16)],
        [attended, w, *args],
        [pltpu.VMEM(tokens, BF16), dma(())],
        microseconds=3,
        to_hbm=(5,),
    )
    sum3, sum4, sum_third, keep, give = call(
        partner_sum_kernel,
        "partner_sum",
        [((64, 2 * WIDTH), BF16), ((32, 2 * WIDTH), BF16), ((16, 2 * WIDTH), BF16)]
        + [((128, WIDTH), F32), ((128, WIDTH), BF16)],
        [*to_far, keep, message, part_a[0]],
        [pltpu.VMEM((256, WIDTH), F32)],
        in_hbm=1,
    )
    got_w = moved(give, lambda i: i ^ 6)
    back3 = moved(sum3, back_3)
    back4 = moved(sum4, back_4)
    keep, got_w = halved(keep, got_w, 2, lambda i: i ^ 2)
    part_b = call(
        functools.partial(near_back_more_kernel, NEAR_PARTS[1]),
        "near_back_b",
        part_outs(1),
        [*args, part_a[0], keep],
        in_hbm=2,
        microseconds=3,
    )
    keep, got_w = halved(keep, got_w, 16, lambda i: i ^ 24, part_b[0])
    part_c = call(
        functools.partial(near_back_more_kernel, NEAR_PARTS[2]),
        "near_back_c",
        part_outs(2),
        [*args, part_b[0], keep],
        in_hbm=2,
        microseconds=3,
    )
    keep, got_w = halved(keep, got_w, 8, lambda i: i ^ 8, part_c[0])
    give = call(far_split_kernel, "far_split", [((48, 2 * WIDTH), BF16)], [back3, back4])[0]
    swapped = moved(give, partner)
    d_q, own_k, own_v, to_low, to_high = call(
        near_back_last_kernel,
        "near_back_d",
        [(tokens, BF16), ((ROWS, LANES), F32), ((ROWS, LANES), F32)]
        + [((192, 2 * WIDTH), BF16)] * 2,
        [*args, *(x for part in (part_a, part_b, part_c) for x in (part[0], *part[3:]))]
        + [keep, give],
        [pltpu.VMEM(tokens, BF16), dma((2,))],
        in_hbm=2,
        microseconds=3,
        to_hbm=(0,),
    )
    to_low, to_high, got_w = lax.optimization_barrier((to_low, to_high, got_w))
    low_back = moved(to_low, lambda i: i - 1)
    high_back = moved(to_high, lambda i: i + 1)
    copies = call(
        copies_kernel,
        "copies",
        [((lax.axis_size("dp"), 16, WIDTH), BF16)],
        [keep, got_w],
    )[0]
    sum_third, copies = lax.optimization_barrier((sum_third, copies))
    copies = lax.all_to_all(copies, "dp", 0, 0, tiled=True)
    back_third = moved(sum_third, third)
    d_k, d_v, finished = call(
        combine_kernel,
        "combine",
        [(tokens, BF16)] * 2 + [((8, LANES), F32)],
        [part_a[1], part_b[1], part_c[1], own_k, part_a[2], part_b[2], part_c[2], own_v]
        + [low_back, high_back, back3, back4, back_third, swapped],
        [pltpu.VMEM(tokens, BF16)] * 2 + [dma((2,))],
        to_hbm=(0, 1),
    )
    d_w = call(last_sum_kernel, "last_sum", [((16, WIDTH), BF16)], [copies, finished], in_hbm=1)[0]
    return layer_out[None], d_q[None], d_k[None], d_v[None], d_w


def solution(mesh):
    tokens = P("dp", "ctx", None)
    return jax.shard_map(
        body,
        mesh=mesh,
        in_specs=(tokens, tokens, tokens, P("dp", "ctx"), P(), tokens),
        out_specs=(tokens, tokens, tokens, tokens, P("ctx", None)),
        check_vma=False,
    )
```

```python
import functools

import jax
import jax.numpy as jnp
from jax import lax
from jax.experimental import pallas as pl
from jax.experimental.pallas import tpu as pltpu
from jax.sharding import PartitionSpec as P

HEAD_DIM = 64
BLOCK = 64
HALF = 32
LEVELS = 4
ROWS = 256
WIDTH = 512
PAIRS = 4
LANES = 128
DOCS = 4
NEGATIVE = -1e30
BLOCKED = -2e30
SCALE = HEAD_DIM**-0.5
PACK = 2 * WIDTH + LANES
COUNT = (256, 128, 64, 32, 16)
AT = (0, 256, 384, 448, 480)
ALL_ROWS = 496
F32 = jnp.float32
BF16 = jnp.bfloat16
VMEM_MIB = 20

GROUPS = (
    (0, 0, 128, 256),
    (0, 128, 128, 256),
    (1, 0, 128, 256),
    (2, 0, 64, 128),
    (3, 0, 32, 96),
    (4, 0, 16, 96),
)
NEAR = (0, 1, 2, 3)
FAR = (4, 5)
P_AT = {0: 0, 1: 256, 2: 512, 3: 768, 4: 0, 5: 64}
P_NEAR, P_FAR = 896, 96


def iota(shape, dim):
    return lax.broadcasted_iota(jnp.int32, shape, dim)


def gather_table(level, value=1.0):
    shape = (COUNT[level], ROWS)
    return jnp.where(iota(shape, 1) // 2**level == iota(shape, 0), value, 0.0).astype(BF16)


def spread_table(level, value=1.0):
    shape = (ROWS, COUNT[level])
    return jnp.where(iota(shape, 0) // 2**level == iota(shape, 1), value, 0.0).astype(BF16)


def last_table(level):
    shape = (COUNT[level], ROWS)
    last = iota(shape, 0) * 2**level + (2**level - 1)
    return jnp.where(iota(shape, 1) == last, 1.0, 0.0).astype(BF16)


def query_place(index):
    level, _, rows, _ = GROUPS[index]
    size = BLOCK if level == 0 else HALF
    shape = (rows, LANES)
    return jnp.where(iota(shape, 0) // size + 8 == iota(shape, 1), 1.0, 0.0).astype(BF16)


def key_place(index):
    level, _, _, keys = GROUPS[index]
    shape = (keys, LANES)
    row, place = iota(shape, 0), iota(shape, 1) - 8
    if level == 0:
        apart = row // BLOCK - place
        blocked = (apart < 0) | (apart > 2)
        places = 2
    elif level == 1:
        there, here = row // HALF, place + 2
        block_apart = jnp.abs(there // 2 - (place + 2) // 2)
        blocked = (block_apart > 1) | (jnp.abs(there - here) < 2)
        places = 4
    else:
        blocked = row // HALF == place + 1
        places = 2
    blocked = blocked & (place >= 0) & (place < places)
    return jnp.where(blocked, BLOCKED, 0.0).astype(BF16)


def dot(a, b, a_dim=1, b_dim=0):
    return lax.dot_general(a, b, (((a_dim,), (b_dim,)), ((), ())), preferred_element_type=F32)


def split(x):
    high = x.astype(BF16)
    return high, (x - high.astype(F32)).astype(BF16)


def head_lanes(rows, width=LANES):
    return iota((rows, width), 1) % LANES < HEAD_DIM


def stacked(x):
    first = head_lanes(x.shape[0]).astype(F32).astype(BF16)
    return jnp.concatenate([x * first, x * (1 - first)], axis=0)


def unstacked(x, rows):
    return jnp.where(head_lanes(rows, x.shape[1]), x[:rows], x[rows:])


def lanes_of(pair, part=0):
    return slice(part * WIDTH + pair * LANES, part * WIDTH + (pair + 1) * LANES)


DOC_LANES = slice(2 * WIDTH, PACK)


def near_window(index, own0, own1, low, high, lanes):
    def rim(ref, level):
        return ref[BLOCK * level : BLOCK * (level + 1), lanes]

    if index == 0:
        parts = [rim(low, 0), own0[0:192, lanes]]
    elif index == 1:
        parts = [own0[64:256, lanes], rim(high, 0)]
    elif index == 2:
        parts = [rim(low, 1), own1[:, lanes], rim(high, 1)]
    else:
        parts = [rim(low, 2), rim(high, 2)]
    return jnp.concatenate(parts, axis=0)


def far_window(refs, lanes):
    return jnp.concatenate([ref[:, lanes] for ref in refs], axis=0)


def fetch(sources, targets, sems):
    copies = [
        pltpu.make_async_copy(source, target, sems.at[i])
        for i, (source, target) in enumerate(zip(sources, targets))
    ]
    for copy in copies:
        copy.start()
    return copies


def documents_kernel(seg_hbm, qdoc, seg, sem):
    copy = pltpu.make_async_copy(seg_hbm, seg, sem)
    copy.start()
    copy.wait()
    marks = jnp.where(seg[...] == iota((LANES, ROWS), 0), 1.0, 0.0).T.astype(BF16)
    qdoc[0:ROWS] = marks
    for level in range(1, LEVELS + 1):
        marks_c = dot(last_table(level), marks).astype(BF16)
        qdoc[AT[level] : AT[level] + COUNT[level]] = marks_c


def coarsen_kernel(qdoc, k_hbm, v_hbm, up, down, far, third, own0, own1, k, v, sems):
    copies = fetch((k_hbm, v_hbm), (k, v), sems)
    doc = iota((ALL_ROWS, LANES), 1) < DOCS
    docs = jnp.where(doc, (1.0 - qdoc[...].astype(F32)) * BLOCKED, 0.0).astype(BF16)
    copies[0].wait()
    copies[1].wait()
    levels = [(k[...], v[...], docs[0:ROWS])]
    for level in range(1, LEVELS + 1):
        keys = dot(gather_table(level, 0.5**level), levels[0][0]).astype(BF16)
        values = dot(gather_table(level), levels[0][1]).astype(BF16)
        levels.append((keys, values, docs[AT[level] : AT[level] + COUNT[level]]))

    def put(ref, at, level, start, stop):
        for part, lanes in zip(
            levels[level], (slice(0, WIDTH), slice(WIDTH, 2 * WIDTH), DOC_LANES)
        ):
            ref[at : at + stop - start, lanes] = part[start:stop]

    for level in range(3):
        put(up, BLOCK * level, level, COUNT[level] - BLOCK, COUNT[level])
        put(down, BLOCK * level, level, 0, BLOCK)
    put(far, 0, 3, 0, COUNT[3])
    put(far, COUNT[3], 4, 0, COUNT[4])
    put(third, 0, 4, 0, COUNT[4])
    put(own0, 0, 0, 0, COUNT[0])
    put(own1, 0, 1, 0, COUNT[1])


def core_index():
    return lax.axis_index("ctx") % 2


def pair_kernel(far, far_partner, far3, far4):
    even = core_index() == 0
    for out, start, rows in ((far3, 0, 32), (far4, 32, 16)):
        own, other = far[start : start + rows], far_partner[start : start + rows]
        out[0:rows] = jnp.where(even, own, other)
        out[rows : 2 * rows] = jnp.where(even, other, own)


def prepare_kernel(q_hbm, d_hbm, w_hbm, q_out, grad_att, w, d_out, q, sems):
    copies = fetch((q_hbm, d_hbm, w_hbm), (q, d_out, w), sems)
    copies[0].wait()
    for level in range(LEVELS + 1):
        queries = q[...] if level == 0 else dot(gather_table(level, 0.5**level), q[...]).astype(BF16)
        q_out[AT[level] : AT[level] + COUNT[level]] = (queries * SCALE).astype(BF16)
    copies[1].wait()
    copies[2].wait()
    grad_att[...] = dot(d_out[...], w[...], 1, 1)


def attend(queries, query_docs, keys, key_docs, values):
    rows = queries.shape[0]
    scores = dot(
        jnp.concatenate([stacked(queries), query_docs], axis=1),
        jnp.concatenate([keys, key_docs], axis=1),
        1,
        1,
    )
    peak = jnp.maximum(jnp.max(scores, axis=1, keepdims=True), NEGATIVE)
    peak = peak.astype(BF16).astype(F32)
    p = jnp.exp(scores - peak).astype(BF16)
    ones = jnp.ones(values.shape, BF16)
    both = dot(p, jnp.concatenate([values, ones], axis=1))
    return p, unstacked(both[:, :LANES], rows), both[:, LANES:], peak


def with_stats(stats, pair, sums, peak):
    rows = sums.shape[0] // 2
    lane = iota((rows, LANES), 1)
    result = []
    for old, new in zip(stats, (sums, peak)):
        old = jnp.where(lane == 2 * pair, new[:rows], old)
        result.append(jnp.where(lane == 2 * pair + 1, new[rows:], old))
    return result


def no_stats(rows):
    return [jnp.zeros((rows, LANES), F32)] * 2


def head_spread(pair):
    shape = (2 * LANES, LANES)
    head = iota(shape, 0) % LANES
    return jnp.where(head == 2 * pair + iota(shape, 1) // HEAD_DIM, 1.0, 0.0).astype(BF16)


def head_sum(pair):
    shape = (2 * LANES, LANES)
    head = 2 * pair + iota(shape, 0) % LANES // HEAD_DIM
    return jnp.where(head == iota(shape, 1), 1.0, 0.0).astype(BF16)


def both_parts(x):
    return jnp.concatenate(split(x), axis=1)


def docs_of(index, qdoc):
    level, start, rows, _ = GROUPS[index]
    docs = qdoc[AT[level] + start : AT[level] + start + rows]
    if index in NEAR:
        docs = docs + query_place(index)
    return jnp.concatenate([docs, docs], axis=0)


def near_kernel(q_all, qdoc, own0, own1, low, high, p_out, fine, fine_stats, coarse, coarse_stats):
    for index in NEAR:
        level, start, rows, keys = GROUPS[index]
        at = AT[level] + start
        query_docs = docs_of(index, qdoc)
        key_docs = near_window(index, own0, own1, low, high, DOC_LANES) + key_place(index)
        stats = no_stats(rows)
        for pair in range(PAIRS):
            window = [
                near_window(index, own0, own1, low, high, lanes_of(pair, part)) for part in (0, 1)
            ]
            p, numer, sums, peak = attend(
                q_all[at : at + rows, lanes_of(pair)], query_docs, window[0], key_docs, window[1]
            )
            stats = with_stats(stats, pair, sums, peak)
            p_out[pair, P_AT[index] : P_AT[index] + 2 * rows, 0:keys] = p
            if level == 0:
                fine[at : at + rows, lanes_of(pair)] = numer
            else:
                coarse[at - ROWS : at - ROWS + rows, lanes_of(pair)] = numer.astype(BF16)
        if level == 0:
            fine_stats[at : at + rows] = jnp.concatenate(stats, axis=1)
        else:
            coarse_stats[at - ROWS : at - ROWS + rows] = jnp.concatenate(stats, axis=1).astype(BF16)


def far_refs(refs):
    own3, got4, third, passed = refs
    return (
        (own3, passed.at[0:64]),
        (got4, passed.at[64:96], third, passed.at[96:112]),
    )


def block_at(block):
    x, y, core = block // 8, block // 2 % 4, block % 2
    return 16 * (16 * core + 4 * y + x)


def merge_kernel(
    q_all, qdoc, fine, fine_stats, coarse, coarse_stats, grad_att, d_out, *refs
):
    far = far_refs(refs[:4])
    attended_out, keep, give, p_out, g_out, d_side, d_w = refs[4:]
    spreads = [None] + [spread_table(level) for level in range(1, LEVELS + 1)]
    gathers = [None] + [gather_table(level) for level in range(1, LEVELS + 1)]
    numers, stats = [None, coarse[0:128], coarse[128:192]], [None, coarse_stats[0:128]]
    stats.append(coarse_stats[128:192])
    for index, ref in zip(FAR, far):
        level, _, rows, keys = GROUPS[index]
        query_docs, key_docs = docs_of(index, qdoc), far_window(ref, DOC_LANES)
        own_stats, own_numers = no_stats(rows), []
        for pair in range(PAIRS):
            p, numer, sums, peak = attend(
                q_all[AT[level] : AT[level] + rows, lanes_of(pair)],
                query_docs,
                far_window(ref, lanes_of(pair)),
                key_docs,
                far_window(ref, lanes_of(pair, 1)),
            )
            own_stats = with_stats(own_stats, pair, sums, peak)
            own_numers.append(numer.astype(BF16))
            p_out[pair, P_AT[index] : P_AT[index] + 2 * rows, 0:keys] = p
        numers.append(jnp.concatenate(own_numers, axis=1))
        stats.append(jnp.concatenate(own_stats, axis=1).astype(BF16))
    wide = [fine_stats[...]] + [
        dot(spreads[level], stats[level]) for level in range(1, LEVELS + 1)
    ]
    sums, peaks = [x[:, :LANES] for x in wide], [x[:, LANES:] for x in wide]
    top = functools.reduce(jnp.maximum, peaks)
    weights = [jnp.exp(x - top) for x in peaks]
    norm = functools.reduce(
        jnp.add, [wt * x * float(2**i) for i, (wt, x) in enumerate(zip(weights, sums))]
    )
    inverse = 1.0 / jnp.where(iota(norm.shape, 1) < 2 * PAIRS, norm, 1.0)
    shares = [wt * inverse for wt in weights]
    share_parts = [both_parts(x) for x in shares]
    delta = jnp.zeros((ROWS, LANES), F32)
    for pair in range(PAIRS):
        cols = lanes_of(pair)
        to_lanes = head_spread(pair)
        wide_shares = [dot(x, to_lanes) for x in share_parts]
        numer = wide_shares[0] * fine[:, cols]
        for level in range(1, LEVELS + 1):
            numer = numer + wide_shares[level] * dot(spreads[level], numers[level][:, cols])
        attended = numer.astype(BF16)
        attended_out[:, cols] = attended
        grad_w = dot(attended, d_out[...], 0, 0)
        for block in range(8):
            at = block_at(8 * pair + block)
            d_w[at : at + 16] = grad_w[16 * block : 16 * (block + 1)]
        grad = grad_att[:, cols]
        delta = delta + dot(both_parts(grad * attended.astype(F32)), head_sum(pair))
        for level in range(LEVELS + 1):
            rows = (wide_shares[level] * grad).astype(BF16)
            if level > 0:
                rows = dot(gathers[level], rows).astype(BF16)
            g_out[AT[level] : AT[level] + COUNT[level], cols] = rows
    core = core_index()
    keep[...] = d_w[pl.ds(pl.multiple_of(core * 256, 256), 256)]
    give[...] = d_w[pl.ds(pl.multiple_of((1 - core) * 256, 256), 256)].astype(BF16)
    shape = (2 * LANES, LANES)
    part, head = iota(shape, 0) // LANES, iota(shape, 0) % LANES
    place = jnp.where((head < 8) & (iota(shape, 1) == 8 * part + head), 1.0, 0.0).astype(BF16)
    for level in range(LEVELS + 1):
        delta_c = shares[level] * delta
        if level > 0:
            summed = dot(gathers[level], both_parts(delta_c))
            delta_c = summed[:, :LANES] + summed[:, LANES:]
        terms = dot(both_parts(delta_c * -float(2**level)), place)
        d_side[AT[level] : AT[level] + COUNT[level]] = terms.astype(BF16)


def attend_back(pair, p, queries, grad, side, keys, values):
    rows = queries.shape[0]
    ones = jnp.where(iota(values.shape, 1) < 16, 1.0, 0.0).astype(BF16)
    grad = stacked(grad)
    lane = iota(side.shape, 1)
    sides = [
        side * jnp.where((lane < 16) & (lane % 8 == 2 * pair + i), 1.0, 0.0).astype(BF16)
        for i in (0, 1)
    ]
    product = dot(
        jnp.concatenate([grad, jnp.concatenate(sides, axis=0)], axis=1),
        jnp.concatenate([values, ones], axis=1),
        1,
        1,
    )
    ds = (p.astype(F32) * product).astype(BF16)
    grad_q = unstacked(dot(ds, keys), rows) * SCALE
    return grad_q, dot(ds, stacked(queries), 0, 0), dot(p, grad, 0, 0)


PARTNER_ROWS = 112
MESSAGE_ROWS = 256 + 2 * PARTNER_ROWS


def far_back_kernel(p_in, q_all, g_in, d_side, own3, got4, third, passed, give, *refs):
    far = far_refs((own3, got4, third, passed))
    d_q, to_3, to_4, to_third, message = refs
    message[0:256] = give[...]
    to_far = ((to_3, (0, 64)), (to_4, (64, 96), to_third, (96, 112)))
    for pair in range(PAIRS):
        cols = lanes_of(pair)
        for index, ref, to in zip(FAR, far, to_far):
            level, _, rows, keys = GROUPS[index]
            at = AT[level]
            grad_q, grad_k, grad_v = attend_back(
                pair,
                p_in[pair, P_AT[index] : P_AT[index] + 2 * rows, 0:keys],
                q_all[at : at + rows, cols],
                g_in[at : at + rows, cols],
                d_side[at : at + rows],
                far_window(ref, cols),
                far_window(ref, lanes_of(pair, 1)),
            )
            d_q[at - AT[3] : at - AT[3] + rows, cols] = grad_q.astype(BF16)
            start = 0
            for out in to:
                partners = isinstance(out, tuple)
                stop = start + (out[1] - out[0] if partners else out.shape[0])
                for part, grad in enumerate((grad_k, grad_v)):
                    rows = grad[start:stop].astype(BF16)
                    if partners:
                        first = 256 + part * PARTNER_ROWS
                        message[first + out[0] : first + out[1], cols] = rows
                    else:
                        out[:, lanes_of(pair, part)] = rows
                start = stop


NEAR_PARTS = ((0,), (1,), (2,), (3,))


def near_back(pairs, p_in, q_all, g_in, d_side, own0, own1, low, high, d_far):
    spread = jnp.concatenate([spread_table(level, 0.5**level) for level in (1, 2, 3, 4)], axis=1)
    for pair in pairs:
        cols = lanes_of(pair)
        grads = []
        for index in NEAR:
            level, start, rows, keys = GROUPS[index]
            at = AT[level] + start
            grads.append(
                attend_back(
                    pair,
                    p_in[pair, P_AT[index] : P_AT[index] + 2 * rows, 0:keys],
                    q_all[at : at + rows, cols],
                    g_in[at : at + rows, cols],
                    d_side[at : at + rows],
                    near_window(index, own0, own1, low, high, cols),
                    near_window(index, own0, own1, low, high, lanes_of(pair, 1)),
                )
            )
        coarse = [x[0].astype(BF16) for x in grads[2:]] + [d_far[:, cols]]
        whole = jnp.concatenate([x[0] for x in grads[:2]], axis=0)
        d_q = (whole + dot(spread, jnp.concatenate(coarse, axis=0))).astype(BF16)
        own, to_low, to_high = [], [], []
        for part, value in ((0, 0.5), (1, 1.0)):
            a, b, c, d = (x[1 + part] for x in grads)
            middle = jnp.concatenate([a[64:128], a[128:256] + b[0:128], b[128:192]], axis=0)
            own.append(middle + dot(spread_table(1, value), c[64:192].astype(BF16)))
            to_low.append(jnp.concatenate([a[:64], c[:64], d[:64]], axis=0).astype(BF16))
            to_high.append(jnp.concatenate([b[192:], c[192:], d[64:]], axis=0).astype(BF16))
        yield pair, d_q, own, to_low, to_high


def near_back_first_kernel(pairs, attended, w, *refs):
    inputs, outs = refs[:9], refs[9:]
    layer_out = None
    if attended is not None:
        layer_out, result, sem = outs[-3:]
        result[...] = dot(attended[...], w[...]).astype(BF16)
        copy = pltpu.make_async_copy(result, layer_out, sem)
        copy.start()
    d_q, own_k, own_v, to_low, to_high = outs[:5]
    for pair, dq, own, low, high in near_back(pairs, *inputs):
        at = slice((pair - pairs[0]) * LANES, (pair - pairs[0] + 1) * LANES)
        d_q[:, at], own_k[:, at], own_v[:, at] = dq, own[0], own[1]
        for part in range(2):
            to_low[part, :, at], to_high[part, :, at] = low[part], high[part]
    if attended is not None:
        copy.wait()


def near_back_a_kernel(attended, w, *refs):
    near_back_first_kernel(NEAR_PARTS[0], attended, w, *refs)


def near_back_more_kernel(pairs, *refs):
    near_back_first_kernel(pairs, None, None, *refs[:9], *refs[-5:])


def near_back_last_kernel(*refs):
    inputs, earlier = refs[:9], [refs[at : at + 3] for at in (9, 12, 15)]
    d_q_hbm, own_k, own_v, to_low, to_high, d_q, sems = refs[-7:]
    for pairs, (dq, low, high) in zip(NEAR_PARTS, earlier):
        cols = slice(pairs[0] * LANES, (pairs[-1] + 1) * LANES)
        d_q[:, cols] = dq[...]
        for part in range(2):
            lanes = slice(part * WIDTH + cols.start, part * WIDTH + cols.stop)
            to_low[:, lanes], to_high[:, lanes] = low[part], high[part]
    last = NEAR_PARTS[-1][0] * LANES
    before = pltpu.make_async_copy(d_q.at[:, 0:last], d_q_hbm.at[:, 0:last], sems.at[0])
    before.start()
    for pair, dq, own, low, high in near_back(NEAR_PARTS[-1], *inputs):
        d_q[:, lanes_of(pair)] = dq
        own_k[...], own_v[...] = own[0], own[1]
        after = pltpu.make_async_copy(
            d_q.at[:, lanes_of(pair)], d_q_hbm.at[:, lanes_of(pair)], sems.at[1]
        )
        after.start()
        for part in range(2):
            to_low[:, lanes_of(pair, part)] = low[part]
            to_high[:, lanes_of(pair, part)] = high[part]
    before.wait()
    after.wait()


def pass_on_kernel(got3, got4, third, own3, out):
    out[0:64] = got3[...]
    out[64:96] = got4[...]
    out[96:112] = third[...]
    own3[...] = jnp.where(core_index() == 0, got3[0:32], got3[32:64])


def partner_sum_kernel(to_3, to_4, to_third, keep, message, *refs):
    sum3, sum4, sum_third, keep_out, give_out, total = refs[-6:]
    even = core_index() == 0
    for part in range(2):
        lanes = slice(part * WIDTH, (part + 1) * WIDTH)
        at = 256 + part * PARTNER_ROWS
        own3 = to_3[:, lanes].astype(F32)

        def came(start, stop):
            return message[at + start : at + stop].astype(F32)

        sum3[0:32, lanes] = (came(0, 32) + jnp.where(even, own3, 0.0)).astype(BF16)
        sum3[32:64, lanes] = (came(32, 64) + jnp.where(even, 0.0, own3)).astype(BF16)
        sum4[:, lanes] = (came(64, 96) + to_4[:, lanes].astype(F32)).astype(BF16)
        sum_third[:, lanes] = (came(96, 112) + to_third[:, lanes].astype(F32)).astype(BF16)
    total[...] = keep[...] + message[0:256].astype(F32)
    halve(total, 4, keep_out, give_out)


def halve(total, divisor, keep, give):
    side = lax.axis_index("ctx") // divisor % 2
    half = total.shape[0] // 2
    keep[...] = total[pl.ds(pl.multiple_of(side * half, half), half)]
    give[...] = total[pl.ds(pl.multiple_of((1 - side) * half, half), half)].astype(BF16)


def core_rows(ref, core, rows):
    return ref[pl.ds(pl.multiple_of(core * rows, rows), rows)]


def far_split_kernel(back3, back4, give):
    other = 1 - core_index()
    give[0:32] = core_rows(back3, other, 32)
    give[32:48] = core_rows(back4, other, 16)


def halve_kernel(divisor, keep, got, *refs):
    keep_out, give_out, total = refs[-3:]
    total[...] = keep[...] + got[...].astype(F32)
    halve(total, divisor, keep_out, give_out)


def copies_kernel(keep, got, *refs):
    total = keep[...] + got[...].astype(F32)
    for i in range(refs[-1].shape[0]):
        refs[-1][i] = total.astype(BF16)


def last_sum_kernel(parts, _, out):
    total = parts[0].astype(F32)
    for i in range(1, parts.shape[0]):
        total = total + parts[i].astype(F32)
    out[...] = total.astype(BF16)


def combine_kernel(*refs):
    own, (low, high) = (refs[0:4], refs[4:8]), refs[8:10]
    back3, back4, third, swapped = refs[10:14]
    d_k_hbm, d_v_hbm, finished, d_k, d_v, sems = refs[14:]
    finished[...] = jnp.zeros(finished.shape, F32)
    core = core_index()
    far3 = core_rows(back3, core, 32).astype(F32) + swapped[0:32].astype(F32)
    far4 = core_rows(back4, core, 16).astype(F32) + swapped[32:48].astype(F32)
    far4 = far4 + third[...].astype(F32)
    copies = []
    for part, out, out_hbm in ((0, d_k, d_k_hbm), (1, d_v, d_v_hbm)):
        lanes = slice(part * WIDTH, (part + 1) * WIDTH)
        table = jnp.concatenate(
            [spread_table(level, 1.0 if part else 0.5**level) for level in (1, 2, 3, 4)], axis=1
        )

        def rim(ref, level):
            return ref[BLOCK * level : BLOCK * (level + 1), lanes].astype(F32)

        coarse = jnp.concatenate(
            [
                rim(high, 1),
                rim(low, 1),
                rim(low, 2) + rim(high, 2),
                far3[:, lanes],
                far4[:, lanes],
            ],
            axis=0,
        ).astype(BF16)
        whole = jnp.concatenate([x[...] for x in own[part]], axis=1) + dot(table, coarse)
        out[0:64] = (whole[0:64] + rim(high, 0)).astype(BF16)
        out[64:192] = whole[64:192].astype(BF16)
        out[192:256] = (whole[192:256] + rim(low, 0)).astype(BF16)
        copies.append(pltpu.make_async_copy(out, out_hbm, sems.at[part]))
        copies[-1].start()
    for copy in copies:
        copy.wait()


def call(
    kernel, name, outs, args, scratch=(), in_hbm=0, microseconds=1.0, to_hbm=()
):
    vmem, hbm = pl.BlockSpec(memory_space=pltpu.VMEM), pl.BlockSpec(memory_space=pl.ANY)
    return pl.pallas_call(
        kernel,
        name=name,
        out_shape=[jax.ShapeDtypeStruct(shape, dtype) for shape, dtype in outs],
        in_specs=[vmem] * (len(args) - in_hbm) + [hbm] * in_hbm,
        out_specs=[hbm if i in to_hbm else vmem for i in range(len(outs))],
        scratch_shapes=scratch,
        cost_estimate=pl.CostEstimate(
            flops=int(microseconds * 1e9), bytes_accessed=1 << 20, transcendentals=0
        ),
        compiler_params=pltpu.CompilerParams(vmem_limit_bytes=VMEM_MIB * 1024 * 1024),
    )(*args)


def moved(x, route):
    count = lax.axis_size("ctx")
    return lax.ppermute(x, "ctx", [(i, route(i) % count) for i in range(count)])


def partner(i):
    return i ^ 1


def third(i):
    return i - 6 if i // 2 % 2 else i + 6


def route_3(i):
    return i - 2 if i % 2 else i + 2


def route_4(i):
    return i - 4 if i % 2 else i + 4


def back_3(i):
    return i + 2 if i % 2 else i - 2


def back_4(i):
    return i + 4 if i % 2 else i - 4


def body(queries, key_rows, value_rows, segment_ids, w_out, d_out):
    q, k, v, grad_out = queries[0], key_rows[0], value_rows[0], d_out[0]
    tokens, dma = (ROWS, WIDTH), pltpu.SemaphoreType.DMA
    qdoc = call(
        documents_kernel,
        "documents",
        [((ALL_ROWS, LANES), BF16)],
        [segment_ids],
        [pltpu.VMEM((1, ROWS), jnp.int32), dma(())],
        in_hbm=1,
    )[0]
    up, down, far, third_rows, own0, own1 = call(
        coarsen_kernel,
        "coarsen",
        [((192, PACK), BF16), ((192, PACK), BF16), ((48, PACK), BF16), ((16, PACK), BF16)]
        + [((ROWS, PACK), BF16), ((128, PACK), BF16)],
        [qdoc, k, v],
        [pltpu.VMEM(tokens, BF16)] * 2 + [dma((2,))],
        in_hbm=2,
    )
    far_partner = moved(far, partner)
    far3, far4 = call(
        pair_kernel, "pair", [((64, PACK), BF16), ((32, PACK), BF16)], [far, far_partner]
    )
    q_all, grad_att, w, grad_rows = call(
        prepare_kernel,
        "prepare",
        [((ALL_ROWS, WIDTH), BF16), (tokens, F32), ((WIDTH, WIDTH), BF16), (tokens, BF16)],
        [q, grad_out, w_out],
        [pltpu.VMEM(tokens, BF16), dma((3,))],
        in_hbm=3,
    )
    low = moved(up, lambda i: i + 1)
    high = moved(down, lambda i: i - 1)
    got3 = moved(far3, route_3)
    got4 = moved(far4, route_4)
    got_third = moved(third_rows, third)
    low, high, got3 = lax.optimization_barrier((low, high, got3))
    own3, passed = call(
        pass_on_kernel,
        "pass_on",
        [((32, PACK), BF16), ((112, PACK), BF16)],
        [got3, got4, got_third],
    )
    far = (own3, got4, got_third, moved(passed, partner))
    near = (own0, own1, low, high)
    p_near, *near_sums = call(
        near_kernel,
        "near",
        [((PAIRS, P_NEAR, 256), BF16), (tokens, F32), ((ROWS, 2 * LANES), F32)]
        + [((192, WIDTH), BF16), ((192, 2 * LANES), BF16)],
        [q_all, qdoc, *near],
        microseconds=50,
    )
    attended, keep, give, p_far, g, d_side = call(
        merge_kernel,
        "merge",
        [(tokens, BF16), ((256, WIDTH), F32), ((256, WIDTH), BF16)]
        + [((PAIRS, P_FAR, LANES), BF16)]
        + [((ALL_ROWS, WIDTH), BF16), ((ALL_ROWS, LANES), BF16)],
        [q_all, qdoc, *near_sums, grad_att, grad_rows, *far],
        [pltpu.VMEM((WIDTH, WIDTH), F32)],
        microseconds=6,
    )

    def halved(keep, got, divisor, route, *after):
        rows = keep.shape[0] // 2
        keep, give = call(
            functools.partial(halve_kernel, divisor),
            "halve_" + str(rows),
            [((rows, WIDTH), F32), ((rows, WIDTH), BF16)],
            [keep, got, *after],
            [pltpu.VMEM((2 * rows, WIDTH), F32)],
            in_hbm=len(after),
        )
        return keep, moved(give, route)

    d_far, *to_far, message = call(
        far_back_kernel,
        "far_back",
        [((48, WIDTH), BF16), ((32, 2 * WIDTH), BF16), ((32, 2 * WIDTH), BF16)]
        + [((16, 2 * WIDTH), BF16), ((MESSAGE_ROWS, WIDTH), BF16)],
        [p_far, q_all, g, d_side, *far, give],
    )
    message = moved(message, partner)

    def part_outs(part):
        width = len(NEAR_PARTS[part]) * LANES
        return [((ROWS, width), BF16), ((ROWS, width), F32), ((ROWS, width), F32)] + [
            ((2, 192, width), BF16)
        ] * 2

    args = [p_near, q_all, g, d_side, *near, d_far]
    *part_a, layer_out = call(
        near_back_a_kernel,
        "near_back_a",
        part_outs(0) + [(tokens, BF16)],
        [attended, w, *args],
        [pltpu.VMEM(tokens, BF16), dma(())],
        microseconds=3,
        to_hbm=(5,),
    )
    sum3, sum4, sum_third, keep, give = call(
        partner_sum_kernel,
        "partner_sum",
        [((64, 2 * WIDTH), BF16), ((32, 2 * WIDTH), BF16), ((16, 2 * WIDTH), BF16)]
        + [((128, WIDTH), F32), ((128, WIDTH), BF16)],
        [*to_far, keep, message, part_a[0]],
        [pltpu.VMEM((256, WIDTH), F32)],
        in_hbm=1,
    )
    got_w = moved(give, lambda i: i ^ 6)
    back3 = moved(sum3, back_3)
    back4 = moved(sum4, back_4)
    keep, got_w = halved(keep, got_w, 2, lambda i: i ^ 2)
    part_b = call(
        functools.partial(near_back_more_kernel, NEAR_PARTS[1]),
        "near_back_b",
        part_outs(1),
        [*args, part_a[0], keep],
        in_hbm=2,
        microseconds=3,
    )
    keep, got_w = halved(keep, got_w, 16, lambda i: i ^ 24, part_b[0])
    part_c = call(
        functools.partial(near_back_more_kernel, NEAR_PARTS[2]),
        "near_back_c",
        part_outs(2),
        [*args, part_b[0], keep],
        in_hbm=2,
        microseconds=3,
    )
    keep, got_w = halved(keep, got_w, 8, lambda i: i ^ 8, part_c[0])
    give = call(far_split_kernel, "far_split", [((48, 2 * WIDTH), BF16)], [back3, back4])[0]
    swapped = moved(give, partner)
    d_q, own_k, own_v, to_low, to_high = call(
        near_back_last_kernel,
        "near_back_d",
        [(tokens, BF16), ((ROWS, LANES), F32), ((ROWS, LANES), F32)]
        + [((192, 2 * WIDTH), BF16)] * 2,
        [*args, *(x for part in (part_a, part_b, part_c) for x in (part[0], *part[3:]))]
        + [keep, give],
        [pltpu.VMEM(tokens, BF16), dma((2,))],
        in_hbm=2,
        microseconds=3,
        to_hbm=(0,),
    )
    to_low, to_high, got_w = lax.optimization_barrier((to_low, to_high, got_w))
    low_back = moved(to_low, lambda i: i - 1)
    high_back = moved(to_high, lambda i: i + 1)
    copies = call(
        copies_kernel,
        "copies",
        [((lax.axis_size("dp"), 16, WIDTH), BF16)],
        [keep, got_w],
    )[0]
    sum_third, copies = lax.optimization_barrier((sum_third, copies))
    copies = lax.all_to_all(copies, "dp", 0, 0, tiled=True)
    back_third = moved(sum_third, third)
    d_k, d_v, finished = call(
        combine_kernel,
        "combine",
        [(tokens, BF16)] * 2 + [((8, LANES), F32)],
        [part_a[1], part_b[1], part_c[1], own_k, part_a[2], part_b[2], part_c[2], own_v]
        + [low_back, high_back, back3, back4, back_third, swapped],
        [pltpu.VMEM(tokens, BF16)] * 2 + [dma((2,))],
        to_hbm=(0, 1),
    )
    d_w = call(last_sum_kernel, "last_sum", [((16, WIDTH), BF16)], [copies, finished], in_hbm=1)[0]
    return layer_out[None], d_q[None], d_k[None], d_v[None], d_w


def solution(mesh):
    tokens = P("dp", "ctx", None)
    return jax.shard_map(
        body,
        mesh=mesh,
        in_specs=(tokens, tokens, tokens, P("dp", "ctx"), P(), tokens),
        out_specs=(tokens, tokens, tokens, tokens, P("ctx", None)),
        check_vma=False,
    )
```

```python
import functools

import jax
import jax.numpy as jnp
from jax import lax
from jax.experimental import pallas as pl
from jax.experimental.pallas import tpu as pltpu
from jax.sharding import PartitionSpec as P

HEAD_DIM = 64
BLOCK = 64
HALF = 32
LEVELS = 4
ROWS = 256
WIDTH = 512
PAIRS = 4
LANES = 128
DOCS = 4
NEGATIVE = -1e30
BLOCKED = -2e30
SCALE = HEAD_DIM**-0.5
PACK = 2 * WIDTH + LANES
COUNT = (256, 128, 64, 32, 16)
AT = (0, 256, 384, 448, 480)
ALL_ROWS = 496
F32 = jnp.float32
BF16 = jnp.bfloat16
VMEM_MIB = 20

GROUPS = (
    (0, 0, 128, 256),
    (0, 128, 128, 256),
    (1, 0, 128, 256),
    (2, 0, 64, 128),
    (3, 0, 32, 96),
    (4, 0, 16, 96),
)
NEAR = (0, 1, 2, 3)
FAR = (4, 5)
P_AT = {0: 0, 1: 256, 2: 512, 3: 768, 4: 0, 5: 64}
P_NEAR, P_FAR = 896, 96


def iota(shape, dim):
    return lax.broadcasted_iota(jnp.int32, shape, dim)


def gather_table(level, value=1.0):
    shape = (COUNT[level], ROWS)
    return jnp.where(iota(shape, 1) // 2**level == iota(shape, 0), value, 0.0).astype(BF16)


def spread_table(level, value=1.0):
    shape = (ROWS, COUNT[level])
    return jnp.where(iota(shape, 0) // 2**level == iota(shape, 1), value, 0.0).astype(BF16)


def last_table(level):
    shape = (COUNT[level], ROWS)
    last = iota(shape, 0) * 2**level + (2**level - 1)
    return jnp.where(iota(shape, 1) == last, 1.0, 0.0).astype(BF16)


def query_place(index):
    level, _, rows, _ = GROUPS[index]
    size = BLOCK if level == 0 else HALF
    shape = (rows, LANES)
    return jnp.where(iota(shape, 0) // size + 8 == iota(shape, 1), 1.0, 0.0).astype(BF16)


def key_place(index):
    level, _, _, keys = GROUPS[index]
    shape = (keys, LANES)
    row, place = iota(shape, 0), iota(shape, 1) - 8
    if level == 0:
        apart = row // BLOCK - place
        blocked = (apart < 0) | (apart > 2)
        places = 2
    elif level == 1:
        there, here = row // HALF, place + 2
        block_apart = jnp.abs(there // 2 - (place + 2) // 2)
        blocked = (block_apart > 1) | (jnp.abs(there - here) < 2)
        places = 4
    else:
        blocked = row // HALF == place + 1
        places = 2
    blocked = blocked & (place >= 0) & (place < places)
    return jnp.where(blocked, BLOCKED, 0.0).astype(BF16)


def dot(a, b, a_dim=1, b_dim=0):
    return lax.dot_general(a, b, (((a_dim,), (b_dim,)), ((), ())), preferred_element_type=F32)


def split(x):
    high = x.astype(BF16)
    return high, (x - high.astype(F32)).astype(BF16)


def head_lanes(rows, width=LANES):
    return iota((rows, width), 1) % LANES < HEAD_DIM


def stacked(x):
    first = head_lanes(x.shape[0]).astype(F32).astype(BF16)
    return jnp.concatenate([x * first, x * (1 - first)], axis=0)


def unstacked(x, rows):
    return jnp.where(head_lanes(rows, x.shape[1]), x[:rows], x[rows:])


def lanes_of(pair, part=0):
    return slice(part * WIDTH + pair * LANES, part * WIDTH + (pair + 1) * LANES)


DOC_LANES = slice(2 * WIDTH, PACK)


def near_window(index, own0, own1, low, high, lanes):
    def rim(ref, level):
        return ref[BLOCK * level : BLOCK * (level + 1), lanes]

    if index == 0:
        parts = [rim(low, 0), own0[0:192, lanes]]
    elif index == 1:
        parts = [own0[64:256, lanes], rim(high, 0)]
    elif index == 2:
        parts = [rim(low, 1), own1[:, lanes], rim(high, 1)]
    else:
        parts = [rim(low, 2), rim(high, 2)]
    return jnp.concatenate(parts, axis=0)


def far_window(refs, lanes):
    return jnp.concatenate([ref[:, lanes] for ref in refs], axis=0)


def fetch(sources, targets, sems):
    copies = [
        pltpu.make_async_copy(source, target, sems.at[i])
        for i, (source, target) in enumerate(zip(sources, targets))
    ]
    for copy in copies:
        copy.start()
    return copies


def documents_kernel(seg_hbm, qdoc, seg, sem):
    copy = pltpu.make_async_copy(seg_hbm, seg, sem)
    copy.start()
    copy.wait()
    marks = jnp.where(seg[...] == iota((LANES, ROWS), 0), 1.0, 0.0).T.astype(BF16)
    qdoc[0:ROWS] = marks
    for level in range(1, LEVELS + 1):
        marks_c = dot(last_table(level), marks).astype(BF16)
        qdoc[AT[level] : AT[level] + COUNT[level]] = marks_c


def coarsen_kernel(qdoc, k_hbm, v_hbm, up, down, far, third, own0, own1, k, v, sems):
    copies = fetch((k_hbm, v_hbm), (k, v), sems)
    doc = iota((ALL_ROWS, LANES), 1) < DOCS
    docs = jnp.where(doc, (1.0 - qdoc[...].astype(F32)) * BLOCKED, 0.0).astype(BF16)
    copies[0].wait()
    copies[1].wait()
    levels = [(k[...], v[...], docs[0:ROWS])]
    for level in range(1, LEVELS + 1):
        keys = dot(gather_table(level, 0.5**level), levels[0][0]).astype(BF16)
        values = dot(gather_table(level), levels[0][1]).astype(BF16)
        levels.append((keys, values, docs[AT[level] : AT[level] + COUNT[level]]))

    def put(ref, at, level, start, stop):
        for part, lanes in zip(
            levels[level], (slice(0, WIDTH), slice(WIDTH, 2 * WIDTH), DOC_LANES)
        ):
            ref[at : at + stop - start, lanes] = part[start:stop]

    for level in range(3):
        put(up, BLOCK * level, level, COUNT[level] - BLOCK, COUNT[level])
        put(down, BLOCK * level, level, 0, BLOCK)
    put(far, 0, 3, 0, COUNT[3])
    put(far, COUNT[3], 4, 0, COUNT[4])
    put(third, 0, 4, 0, COUNT[4])
    put(own0, 0, 0, 0, COUNT[0])
    put(own1, 0, 1, 0, COUNT[1])


def core_index():
    return lax.axis_index("ctx") % 2


def pair_kernel(far, far_partner, far3, far4):
    even = core_index() == 0
    for out, start, rows in ((far3, 0, 32), (far4, 32, 16)):
        own, other = far[start : start + rows], far_partner[start : start + rows]
        out[0:rows] = jnp.where(even, own, other)
        out[rows : 2 * rows] = jnp.where(even, other, own)


def prepare_kernel(q_hbm, d_hbm, w_hbm, q_out, grad_att, w, d_out, q, sems):
    copies = fetch((q_hbm, d_hbm, w_hbm), (q, d_out, w), sems)
    copies[0].wait()
    for level in range(LEVELS + 1):
        queries = q[...] if level == 0 else dot(gather_table(level, 0.5**level), q[...]).astype(BF16)
        q_out[AT[level] : AT[level] + COUNT[level]] = (queries * SCALE).astype(BF16)
    copies[1].wait()
    copies[2].wait()
    grad_att[...] = dot(d_out[...], w[...], 1, 1)


def attend(queries, query_docs, keys, key_docs, values):
    rows = queries.shape[0]
    scores = dot(
        jnp.concatenate([stacked(queries), query_docs], axis=1),
        jnp.concatenate([keys, key_docs], axis=1),
        1,
        1,
    )
    peak = jnp.maximum(jnp.max(scores, axis=1, keepdims=True), NEGATIVE)
    peak = peak.astype(BF16).astype(F32)
    p = jnp.exp(scores - peak).astype(BF16)
    ones = jnp.ones(values.shape, BF16)
    both = dot(p, jnp.concatenate([values, ones], axis=1))
    return p, unstacked(both[:, :LANES], rows), both[:, LANES:], peak


def with_stats(stats, pair, sums, peak):
    rows = sums.shape[0] // 2
    lane = iota((rows, LANES), 1)
    result = []
    for old, new in zip(stats, (sums, peak)):
        old = jnp.where(lane == 2 * pair, new[:rows], old)
        result.append(jnp.where(lane == 2 * pair + 1, new[rows:], old))
    return result


def no_stats(rows):
    return [jnp.zeros((rows, LANES), F32)] * 2


def head_spread(pair):
    shape = (2 * LANES, LANES)
    head = iota(shape, 0) % LANES
    return jnp.where(head == 2 * pair + iota(shape, 1) // HEAD_DIM, 1.0, 0.0).astype(BF16)


def head_sum(pair):
    shape = (2 * LANES, LANES)
    head = 2 * pair + iota(shape, 0) % LANES // HEAD_DIM
    return jnp.where(head == iota(shape, 1), 1.0, 0.0).astype(BF16)


def both_parts(x):
    return jnp.concatenate(split(x), axis=1)


def docs_of(index, qdoc):
    level, start, rows, _ = GROUPS[index]
    docs = qdoc[AT[level] + start : AT[level] + start + rows]
    if index in NEAR:
        docs = docs + query_place(index)
    return jnp.concatenate([docs, docs], axis=0)


def near_kernel(q_all, qdoc, own0, own1, low, high, p_out, fine, fine_stats, coarse, coarse_stats):
    for index in NEAR:
        level, start, rows, keys = GROUPS[index]
        at = AT[level] + start
        query_docs = docs_of(index, qdoc)
        key_docs = near_window(index, own0, own1, low, high, DOC_LANES) + key_place(index)
        stats = no_stats(rows)
        for pair in range(PAIRS):
            window = [
                near_window(index, own0, own1, low, high, lanes_of(pair, part)) for part in (0, 1)
            ]
            p, numer, sums, peak = attend(
                q_all[at : at + rows, lanes_of(pair)], query_docs, window[0], key_docs, window[1]
            )
            stats = with_stats(stats, pair, sums, peak)
            p_out[pair, P_AT[index] : P_AT[index] + 2 * rows, 0:keys] = p
            if level == 0:
                fine[at : at + rows, lanes_of(pair)] = numer
            else:
                coarse[at - ROWS : at - ROWS + rows, lanes_of(pair)] = numer.astype(BF16)
        if level == 0:
            fine_stats[at : at + rows] = jnp.concatenate(stats, axis=1)
        else:
            coarse_stats[at - ROWS : at - ROWS + rows] = jnp.concatenate(stats, axis=1).astype(BF16)


def far_refs(refs):
    own3, got4, third, passed = refs
    return (
        (own3, passed.at[0:64]),
        (got4, passed.at[64:96], third, passed.at[96:112]),
    )


def block_at(block):
    x, y, core = block // 8, block // 2 % 4, block % 2
    return 16 * (16 * core + 4 * y + x)


def merge_kernel(
    q_all, qdoc, fine, fine_stats, coarse, coarse_stats, grad_att, d_out, *refs
):
    far = far_refs(refs[:4])
    attended_out, keep, give, p_out, g_out, d_side, d_w = refs[4:]
    spreads = [None] + [spread_table(level) for level in range(1, LEVELS + 1)]
    gathers = [None] + [gather_table(level) for level in range(1, LEVELS + 1)]
    numers, stats = [None, coarse[0:128], coarse[128:192]], [None, coarse_stats[0:128]]
    stats.append(coarse_stats[128:192])
    for index, ref in zip(FAR, far):
        level, _, rows, keys = GROUPS[index]
        query_docs, key_docs = docs_of(index, qdoc), far_window(ref, DOC_LANES)
        own_stats, own_numers = no_stats(rows), []
        for pair in range(PAIRS):
            p, numer, sums, peak = attend(
                q_all[AT[level] : AT[level] + rows, lanes_of(pair)],
                query_docs,
                far_window(ref, lanes_of(pair)),
                key_docs,
                far_window(ref, lanes_of(pair, 1)),
            )
            own_stats = with_stats(own_stats, pair, sums, peak)
            own_numers.append(numer.astype(BF16))
            p_out[pair, P_AT[index] : P_AT[index] + 2 * rows, 0:keys] = p
        numers.append(jnp.concatenate(own_numers, axis=1))
        stats.append(jnp.concatenate(own_stats, axis=1).astype(BF16))
    wide = [fine_stats[...]] + [
        dot(spreads[level], stats[level]) for level in range(1, LEVELS + 1)
    ]
    sums, peaks = [x[:, :LANES] for x in wide], [x[:, LANES:] for x in wide]
    top = functools.reduce(jnp.maximum, peaks)
    weights = [jnp.exp(x - top) for x in peaks]
    norm = functools.reduce(
        jnp.add, [wt * x * float(2**i) for i, (wt, x) in enumerate(zip(weights, sums))]
    )
    inverse = 1.0 / jnp.where(iota(norm.shape, 1) < 2 * PAIRS, norm, 1.0)
    shares = [wt * inverse for wt in weights]
    share_parts = [both_parts(x) for x in shares]
    delta = jnp.zeros((ROWS, LANES), F32)
    for pair in range(PAIRS):
        cols = lanes_of(pair)
        to_lanes = head_spread(pair)
        wide_shares = [dot(x, to_lanes) for x in share_parts]
        numer = wide_shares[0] * fine[:, cols]
        for level in range(1, LEVELS + 1):
            numer = numer + wide_shares[level] * dot(spreads[level], numers[level][:, cols])
        attended = numer.astype(BF16)
        attended_out[:, cols] = attended
        grad_w = dot(attended, d_out[...], 0, 0)
        for block in range(8):
            at = block_at(8 * pair + block)
            d_w[at : at + 16] = grad_w[16 * block : 16 * (block + 1)]
        grad = grad_att[:, cols]
        delta = delta + dot(both_parts(grad * attended.astype(F32)), head_sum(pair))
        for level in range(LEVELS + 1):
            rows = (wide_shares[level] * grad).astype(BF16)
            if level > 0:
                rows = dot(gathers[level], rows).astype(BF16)
            g_out[AT[level] : AT[level] + COUNT[level], cols] = rows
    core = core_index()
    keep[...] = d_w[pl.ds(pl.multiple_of(core * 256, 256), 256)]
    give[...] = d_w[pl.ds(pl.multiple_of((1 - core) * 256, 256), 256)].astype(BF16)
    shape = (2 * LANES, LANES)
    part, head = iota(shape, 0) // LANES, iota(shape, 0) % LANES
    place = jnp.where((head < 8) & (iota(shape, 1) == 8 * part + head), 1.0, 0.0).astype(BF16)
    for level in range(LEVELS + 1):
        delta_c = shares[level] * delta
        if level > 0:
            summed = dot(gathers[level], both_parts(delta_c))
            delta_c = summed[:, :LANES] + summed[:, LANES:]
        terms = dot(both_parts(delta_c * -float(2**level)), place)
        d_side[AT[level] : AT[level] + COUNT[level]] = terms.astype(BF16)


def attend_back(pair, p, queries, grad, side, keys, values):
    rows = queries.shape[0]
    ones = jnp.where(iota(values.shape, 1) < 16, 1.0, 0.0).astype(BF16)
    grad = stacked(grad)
    lane = iota(side.shape, 1)
    sides = [
        side * jnp.where((lane < 16) & (lane % 8 == 2 * pair + i), 1.0, 0.0).astype(BF16)
        for i in (0, 1)
    ]
    product = dot(
        jnp.concatenate([grad, jnp.concatenate(sides, axis=0)], axis=1),
        jnp.concatenate([values, ones], axis=1),
        1,
        1,
    )
    ds = (p.astype(F32) * product).astype(BF16)
    grad_q = unstacked(dot(ds, keys), rows) * SCALE
    return grad_q, dot(ds, stacked(queries), 0, 0), dot(p, grad, 0, 0)


PARTNER_ROWS = 112
MESSAGE_ROWS = 256 + 2 * PARTNER_ROWS


def far_back_kernel(p_in, q_all, g_in, d_side, own3, got4, third, passed, give, *refs):
    far = far_refs((own3, got4, third, passed))
    d_q, to_3, to_4, to_third, message = refs
    message[0:256] = give[...]
    to_far = ((to_3, (0, 64)), (to_4, (64, 96), to_third, (96, 112)))
    for pair in range(PAIRS):
        cols = lanes_of(pair)
        for index, ref, to in zip(FAR, far, to_far):
            level, _, rows, keys = GROUPS[index]
            at = AT[level]
            grad_q, grad_k, grad_v = attend_back(
                pair,
                p_in[pair, P_AT[index] : P_AT[index] + 2 * rows, 0:keys],
                q_all[at : at + rows, cols],
                g_in[at : at + rows, cols],
                d_side[at : at + rows],
                far_window(ref, cols),
                far_window(ref, lanes_of(pair, 1)),
            )
            d_q[at - AT[3] : at - AT[3] + rows, cols] = grad_q.astype(BF16)
            start = 0
            for out in to:
                partners = isinstance(out, tuple)
                stop = start + (out[1] - out[0] if partners else out.shape[0])
                for part, grad in enumerate((grad_k, grad_v)):
                    rows = grad[start:stop].astype(BF16)
                    if partners:
                        first = 256 + part * PARTNER_ROWS
                        message[first + out[0] : first + out[1], cols] = rows
                    else:
                        out[:, lanes_of(pair, part)] = rows
                start = stop


NEAR_PARTS = ((0,), (1,), (2,), (3,))


def near_back(pairs, p_in, q_all, g_in, d_side, own0, own1, low, high, d_far):
    spread = jnp.concatenate([spread_table(level, 0.5**level) for level in (1, 2, 3, 4)], axis=1)
    for pair in pairs:
        cols = lanes_of(pair)
        grads = []
        for index in NEAR:
            level, start, rows, keys = GROUPS[index]
            at = AT[level] + start
            grads.append(
                attend_back(
                    pair,
                    p_in[pair, P_AT[index] : P_AT[index] + 2 * rows, 0:keys],
                    q_all[at : at + rows, cols],
                    g_in[at : at + rows, cols],
                    d_side[at : at + rows],
                    near_window(index, own0, own1, low, high, cols),
                    near_window(index, own0, own1, low, high, lanes_of(pair, 1)),
                )
            )
        coarse = [x[0].astype(BF16) for x in grads[2:]] + [d_far[:, cols]]
        whole = jnp.concatenate([x[0] for x in grads[:2]], axis=0)
        d_q = (whole + dot(spread, jnp.concatenate(coarse, axis=0))).astype(BF16)
        own, to_low, to_high = [], [], []
        for part, value in ((0, 0.5), (1, 1.0)):
            a, b, c, d = (x[1 + part] for x in grads)
            middle = jnp.concatenate([a[64:128], a[128:256] + b[0:128], b[128:192]], axis=0)
            near = dot(spread_table(1, value), c[64:192].astype(BF16))
            own.append((middle + near).astype(BF16))
            to_low.append(jnp.concatenate([a[:64], c[:64], d[:64]], axis=0).astype(BF16))
            to_high.append(jnp.concatenate([b[192:], c[192:], d[64:]], axis=0).astype(BF16))
        yield pair, d_q, own, to_low, to_high


def near_back_kernel(pairs, *refs):
    inputs, outs = refs[:9], refs[-5:]
    d_q, own_k, own_v, to_low, to_high = outs
    for pair, dq, own, low, high in near_back(pairs, *inputs):
        at = slice((pair - pairs[0]) * LANES, (pair - pairs[0] + 1) * LANES)
        d_q[:, at], own_k[:, at], own_v[:, at] = dq, own[0], own[1]
        for part in range(2):
            to_low[part, :, at], to_high[part, :, at] = low[part], high[part]


def near_back_last_kernel(*refs):
    inputs, earlier = refs[:9], [refs[at : at + 2] for at in (9, 11, 13)]
    d_q, own_k, own_v, to_low, to_high = refs[-5:]
    for pairs, (low, high) in zip(NEAR_PARTS, earlier):
        for part in range(2):
            lanes = slice(
                part * WIDTH + pairs[0] * LANES, part * WIDTH + (pairs[-1] + 1) * LANES
            )
            to_low[:, lanes], to_high[:, lanes] = low[part], high[part]
    for pair, dq, own, low, high in near_back(NEAR_PARTS[-1], *inputs):
        d_q[...], own_k[...], own_v[...] = dq, own[0], own[1]
        for part in range(2):
            to_low[:, lanes_of(pair, part)] = low[part]
            to_high[:, lanes_of(pair, part)] = high[part]


def pass_on_kernel(got3, got4, third, own3, out):
    out[0:64] = got3[...]
    out[64:96] = got4[...]
    out[96:112] = third[...]
    own3[...] = jnp.where(core_index() == 0, got3[0:32], got3[32:64])


def partner_sum_kernel(to_3, to_4, to_third, keep, message, *refs):
    sum3, sum4, sum_third, keep_out, give_out, total = refs[-6:]
    even = core_index() == 0
    for part in range(2):
        lanes = slice(part * WIDTH, (part + 1) * WIDTH)
        at = 256 + part * PARTNER_ROWS
        own3 = to_3[:, lanes].astype(F32)

        def came(start, stop):
            return message[at + start : at + stop].astype(F32)

        sum3[0:32, lanes] = (came(0, 32) + jnp.where(even, own3, 0.0)).astype(BF16)
        sum3[32:64, lanes] = (came(32, 64) + jnp.where(even, 0.0, own3)).astype(BF16)
        sum4[:, lanes] = (came(64, 96) + to_4[:, lanes].astype(F32)).astype(BF16)
        sum_third[:, lanes] = (came(96, 112) + to_third[:, lanes].astype(F32)).astype(BF16)
    total[...] = keep[...] + message[0:256].astype(F32)
    halve(total, 4, keep_out, give_out)


def halve(total, divisor, keep, give):
    side = lax.axis_index("ctx") // divisor % 2
    half = total.shape[0] // 2
    keep[...] = total[pl.ds(pl.multiple_of(side * half, half), half)]
    give[...] = total[pl.ds(pl.multiple_of((1 - side) * half, half), half)].astype(BF16)


def core_rows(ref, core, rows):
    return ref[pl.ds(pl.multiple_of(core * rows, rows), rows)]


def far_split_kernel(back3, back4, give):
    other = 1 - core_index()
    give[0:32] = core_rows(back3, other, 32)
    give[32:48] = core_rows(back4, other, 16)


def halve_kernel(divisor, keep, got, *refs):
    keep_out, give_out, total = refs[-3:]
    total[...] = keep[...] + got[...].astype(F32)
    halve(total, divisor, keep_out, give_out)


def copies_kernel(keep, got, *refs):
    total = keep[...] + got[...].astype(F32)
    for i in range(refs[-1].shape[0]):
        refs[-1][i] = total.astype(BF16)


def last_sum_kernel(parts, _, out):
    total = parts[0].astype(F32)
    for i in range(1, parts.shape[0]):
        total = total + parts[i].astype(F32)
    out[...] = total.astype(BF16)


def project_kernel(attended, w, _, layer_hbm, finished, layer_out, sem):
    finished[...] = jnp.zeros(finished.shape, F32)
    layer_out[...] = dot(attended[...], w[...]).astype(BF16)
    copy = pltpu.make_async_copy(layer_out, layer_hbm, sem)
    copy.start()
    copy.wait()


def combine_kernel(*refs):
    own, (low, high), grads_q = (refs[0:4], refs[4:8]), refs[8:10], refs[14:18]
    back3, back4, third, swapped = refs[10:14]
    d_k_hbm, d_v_hbm, d_q_hbm, finished, d_k, d_v, d_q, sems = refs[18:]
    finished[...] = jnp.zeros(finished.shape, F32)
    for pair, ref in enumerate(grads_q):
        d_q[:, lanes_of(pair)] = ref[...]
    copies = [pltpu.make_async_copy(d_q, d_q_hbm, sems.at[2])]
    copies[0].start()
    core = core_index()
    far3 = core_rows(back3, core, 32).astype(F32) + swapped[0:32].astype(F32)
    far4 = core_rows(back4, core, 16).astype(F32) + swapped[32:48].astype(F32)
    far4 = far4 + third[...].astype(F32)
    for part, out, out_hbm in ((0, d_k, d_k_hbm), (1, d_v, d_v_hbm)):
        lanes = slice(part * WIDTH, (part + 1) * WIDTH)
        table = jnp.concatenate(
            [spread_table(level, 1.0 if part else 0.5**level) for level in (1, 2, 3, 4)], axis=1
        )

        def rim(ref, level):
            return ref[BLOCK * level : BLOCK * (level + 1), lanes].astype(F32)

        coarse = jnp.concatenate(
            [
                rim(high, 1),
                rim(low, 1),
                rim(low, 2) + rim(high, 2),
                far3[:, lanes],
                far4[:, lanes],
            ],
            axis=0,
        ).astype(BF16)
        whole = jnp.concatenate([x[...] for x in own[part]], axis=1).astype(F32)
        whole = whole + dot(table, coarse)
        out[0:64] = (whole[0:64] + rim(high, 0)).astype(BF16)
        out[64:192] = whole[64:192].astype(BF16)
        out[192:256] = (whole[192:256] + rim(low, 0)).astype(BF16)
        copies.append(pltpu.make_async_copy(out, out_hbm, sems.at[part]))
        copies[-1].start()
    for copy in copies:
        copy.wait()


def call(
    kernel, name, outs, args, scratch=(), in_hbm=0, microseconds=1.0, to_hbm=()
):
    vmem, hbm = pl.BlockSpec(memory_space=pltpu.VMEM), pl.BlockSpec(memory_space=pl.ANY)
    return pl.pallas_call(
        kernel,
        name=name,
        out_shape=[jax.ShapeDtypeStruct(shape, dtype) for shape, dtype in outs],
        in_specs=[vmem] * (len(args) - in_hbm) + [hbm] * in_hbm,
        out_specs=[hbm if i in to_hbm else vmem for i in range(len(outs))],
        scratch_shapes=scratch,
        cost_estimate=pl.CostEstimate(
            flops=int(microseconds * 1e9), bytes_accessed=1 << 20, transcendentals=0
        ),
        compiler_params=pltpu.CompilerParams(vmem_limit_bytes=VMEM_MIB * 1024 * 1024),
    )(*args)


def moved(x, route):
    count = lax.axis_size("ctx")
    return lax.ppermute(x, "ctx", [(i, route(i) % count) for i in range(count)])


def partner(i):
    return i ^ 1


def third(i):
    return i - 6 if i // 2 % 2 else i + 6


def route_3(i):
    return i - 2 if i % 2 else i + 2


def route_4(i):
    return i - 4 if i % 2 else i + 4


def back_3(i):
    return i + 2 if i % 2 else i - 2


def back_4(i):
    return i + 4 if i % 2 else i - 4


def body(queries, key_rows, value_rows, segment_ids, w_out, d_out):
    q, k, v, grad_out = queries[0], key_rows[0], value_rows[0], d_out[0]
    tokens, dma = (ROWS, WIDTH), pltpu.SemaphoreType.DMA
    qdoc = call(
        documents_kernel,
        "documents",
        [((ALL_ROWS, LANES), BF16)],
        [segment_ids],
        [pltpu.VMEM((1, ROWS), jnp.int32), dma(())],
        in_hbm=1,
    )[0]
    up, down, far, third_rows, own0, own1 = call(
        coarsen_kernel,
        "coarsen",
        [((192, PACK), BF16), ((192, PACK), BF16), ((48, PACK), BF16), ((16, PACK), BF16)]
        + [((ROWS, PACK), BF16), ((128, PACK), BF16)],
        [qdoc, k, v],
        [pltpu.VMEM(tokens, BF16)] * 2 + [dma((2,))],
        in_hbm=2,
    )
    far_partner = moved(far, partner)
    far3, far4 = call(
        pair_kernel, "pair", [((64, PACK), BF16), ((32, PACK), BF16)], [far, far_partner]
    )
    q_all, grad_att, w, grad_rows = call(
        prepare_kernel,
        "prepare",
        [((ALL_ROWS, WIDTH), BF16), (tokens, F32), ((WIDTH, WIDTH), BF16), (tokens, BF16)],
        [q, grad_out, w_out],
        [pltpu.VMEM(tokens, BF16), dma((3,))],
        in_hbm=3,
    )
    low = moved(up, lambda i: i + 1)
    high = moved(down, lambda i: i - 1)
    got3 = moved(far3, route_3)
    got4 = moved(far4, route_4)
    got_third = moved(third_rows, third)
    low, high, got3 = lax.optimization_barrier((low, high, got3))
    own3, passed = call(
        pass_on_kernel,
        "pass_on",
        [((32, PACK), BF16), ((112, PACK), BF16)],
        [got3, got4, got_third],
    )
    far = (own3, got4, got_third, moved(passed, partner))
    near = (own0, own1, low, high)
    p_near, *near_sums = call(
        near_kernel,
        "near",
        [((PAIRS, P_NEAR, 256), BF16), (tokens, F32), ((ROWS, 2 * LANES), F32)]
        + [((192, WIDTH), BF16), ((192, 2 * LANES), BF16)],
        [q_all, qdoc, *near],
        microseconds=50,
    )
    attended, keep, give, p_far, g, d_side = call(
        merge_kernel,
        "merge",
        [(tokens, BF16), ((256, WIDTH), F32), ((256, WIDTH), BF16)]
        + [((PAIRS, P_FAR, LANES), BF16)]
        + [((ALL_ROWS, WIDTH), BF16), ((ALL_ROWS, LANES), BF16)],
        [q_all, qdoc, *near_sums, grad_att, grad_rows, *far],
        [pltpu.VMEM((WIDTH, WIDTH), F32)],
        microseconds=6,
    )

    def halved(keep, got, divisor, route, *after):
        rows = keep.shape[0] // 2
        keep, give = call(
            functools.partial(halve_kernel, divisor),
            "halve_" + str(rows),
            [((rows, WIDTH), F32), ((rows, WIDTH), BF16)],
            [keep, got, *after],
            [pltpu.VMEM((2 * rows, WIDTH), F32)],
            in_hbm=len(after),
        )
        return keep, moved(give, route)

    d_far, *to_far, message = call(
        far_back_kernel,
        "far_back",
        [((48, WIDTH), BF16), ((32, 2 * WIDTH), BF16), ((32, 2 * WIDTH), BF16)]
        + [((16, 2 * WIDTH), BF16), ((MESSAGE_ROWS, WIDTH), BF16)],
        [p_far, q_all, g, d_side, *far, give],
    )
    message = moved(message, partner)

    def part_outs(part):
        width = len(NEAR_PARTS[part]) * LANES
        return [((ROWS, width), BF16)] * 3 + [((2, 192, width), BF16)] * 2

    args = [p_near, q_all, g, d_side, *near, d_far]
    part_a = call(
        functools.partial(near_back_kernel, NEAR_PARTS[0]),
        "near_back_a",
        part_outs(0),
        args,
        microseconds=3,
    )
    sum3, sum4, sum_third, keep, give = call(
        partner_sum_kernel,
        "partner_sum",
        [((64, 2 * WIDTH), BF16), ((32, 2 * WIDTH), BF16), ((16, 2 * WIDTH), BF16)]
        + [((128, WIDTH), F32), ((128, WIDTH), BF16)],
        [*to_far, keep, message, part_a[0]],
        [pltpu.VMEM((256, WIDTH), F32)],
        in_hbm=1,
    )
    got_w = moved(give, lambda i: i ^ 6)
    back3 = moved(sum3, back_3)
    back4 = moved(sum4, back_4)
    layer_out, projected = call(
        project_kernel,
        "project",
        [(tokens, BF16), ((8, LANES), F32)],
        [attended, w, sum3],
        [pltpu.VMEM(tokens, BF16), dma(())],
        in_hbm=1,
        to_hbm=(0,),
    )
    keep, got_w = halved(keep, got_w, 2, lambda i: i ^ 2, projected)
    part_b = call(
        functools.partial(near_back_kernel, NEAR_PARTS[1]),
        "near_back_b",
        part_outs(1),
        [*args, part_a[0], keep],
        in_hbm=2,
        microseconds=3,
    )
    keep, got_w = halved(keep, got_w, 16, lambda i: i ^ 24, part_b[0])
    part_c = call(
        functools.partial(near_back_kernel, NEAR_PARTS[2]),
        "near_back_c",
        part_outs(2),
        [*args, part_b[0], keep],
        in_hbm=2,
        microseconds=3,
    )
    keep, got_w = halved(keep, got_w, 8, lambda i: i ^ 8, part_c[0])
    give = call(far_split_kernel, "far_split", [((48, 2 * WIDTH), BF16)], [back3, back4])[0]
    swapped = moved(give, partner)
    d_q, own_k, own_v, to_low, to_high = call(
        near_back_last_kernel,
        "near_back_d",
        part_outs(3)[:3] + [((192, 2 * WIDTH), BF16)] * 2,
        [*args, *part_a[3:], *part_b[3:], *part_c[3:], keep, give],
        in_hbm=2,
        microseconds=3,
    )
    to_low, to_high, got_w = lax.optimization_barrier((to_low, to_high, got_w))
    low_back = moved(to_low, lambda i: i - 1)
    high_back = moved(to_high, lambda i: i + 1)
    copies = call(
        copies_kernel,
        "copies",
        [((lax.axis_size("dp"), 16, WIDTH), BF16)],
        [keep, got_w],
    )[0]
    sum_third, copies = lax.optimization_barrier((sum_third, copies))
    copies = lax.all_to_all(copies, "dp", 0, 0, tiled=True)
    back_third = moved(sum_third, third)
    d_k, d_v, d_q, finished = call(
        combine_kernel,
        "combine",
        [(tokens, BF16)] * 3 + [((8, LANES), F32)],
        [part_a[1], part_b[1], part_c[1], own_k, part_a[2], part_b[2], part_c[2], own_v]
        + [low_back, high_back, back3, back4, back_third, swapped]
        + [part_a[0], part_b[0], part_c[0], d_q],
        [pltpu.VMEM(tokens, BF16)] * 3 + [dma((3,))],
        to_hbm=(0, 1, 2),
    )
    d_w = call(last_sum_kernel, "last_sum", [((16, WIDTH), BF16)], [copies, finished], in_hbm=1)[0]
    return layer_out[None], d_q[None], d_k[None], d_v[None], d_w


def solution(mesh):
    tokens = P("dp", "ctx", None)
    return jax.shard_map(
        body,
        mesh=mesh,
        in_specs=(tokens, tokens, tokens, P("dp", "ctx"), P(), tokens),
        out_specs=(tokens, tokens, tokens, tokens, P("ctx", None)),
        check_vma=False,
    )
```

```python
import functools

import jax
import jax.numpy as jnp
from jax import lax
from jax.experimental import pallas as pl
from jax.experimental.pallas import tpu as pltpu
from jax.sharding import PartitionSpec as P

HEAD_DIM = 64
BLOCK = 64
HALF = 32
LEVELS = 4
ROWS = 256
WIDTH = 512
PAIRS = 4
LANES = 128
DOCS = 4
NEGATIVE = -1e30
BLOCKED = -2e30
SCALE = HEAD_DIM**-0.5
PACK = 2 * WIDTH + LANES
COUNT = (256, 128, 64, 32, 16)
AT = (0, 256, 384, 448, 480)
ALL_ROWS = 496
F32 = jnp.float32
BF16 = jnp.bfloat16
VMEM_MIB = 20

GROUPS = (
    (0, 0, 128, 256),
    (0, 128, 128, 256),
    (1, 0, 128, 256),
    (2, 0, 64, 128),
    (3, 0, 32, 96),
    (4, 0, 16, 96),
)
NEAR = (0, 1, 2, 3)
FAR = (4, 5)
P_AT = {0: 0, 1: 256, 2: 512, 3: 768, 4: 0, 5: 64}
P_NEAR, P_FAR = 896, 96


def iota(shape, dim):
    return lax.broadcasted_iota(jnp.int32, shape, dim)


def gather_table(level, value=1.0):
    shape = (COUNT[level], ROWS)
    return jnp.where(iota(shape, 1) // 2**level == iota(shape, 0), value, 0.0).astype(BF16)


def spread_table(level, value=1.0):
    shape = (ROWS, COUNT[level])
    return jnp.where(iota(shape, 0) // 2**level == iota(shape, 1), value, 0.0).astype(BF16)


def last_table(level):
    shape = (COUNT[level], ROWS)
    last = iota(shape, 0) * 2**level + (2**level - 1)
    return jnp.where(iota(shape, 1) == last, 1.0, 0.0).astype(BF16)


def query_place(index):
    level, _, rows, _ = GROUPS[index]
    size = BLOCK if level == 0 else HALF
    shape = (rows, LANES)
    return jnp.where(iota(shape, 0) // size + 8 == iota(shape, 1), 1.0, 0.0).astype(BF16)


def key_place(index):
    level, _, _, keys = GROUPS[index]
    shape = (keys, LANES)
    row, place = iota(shape, 0), iota(shape, 1) - 8
    if level == 0:
        apart = row // BLOCK - place
        blocked = (apart < 0) | (apart > 2)
        places = 2
    elif level == 1:
        there, here = row // HALF, place + 2
        block_apart = jnp.abs(there // 2 - (place + 2) // 2)
        blocked = (block_apart > 1) | (jnp.abs(there - here) < 2)
        places = 4
    else:
        blocked = row // HALF == place + 1
        places = 2
    blocked = blocked & (place >= 0) & (place < places)
    return jnp.where(blocked, BLOCKED, 0.0).astype(BF16)


def dot(a, b, a_dim=1, b_dim=0):
    return lax.dot_general(a, b, (((a_dim,), (b_dim,)), ((), ())), preferred_element_type=F32)


def split(x):
    high = x.astype(BF16)
    return high, (x - high.astype(F32)).astype(BF16)


def head_lanes(rows, width=LANES):
    return iota((rows, width), 1) % LANES < HEAD_DIM


def stacked(x):
    first = head_lanes(x.shape[0]).astype(F32).astype(BF16)
    return jnp.concatenate([x * first, x * (1 - first)], axis=0)


def unstacked(x, rows):
    return jnp.where(head_lanes(rows, x.shape[1]), x[:rows], x[rows:])


def lanes_of(pair, part=0):
    return slice(part * WIDTH + pair * LANES, part * WIDTH + (pair + 1) * LANES)


DOC_LANES = slice(2 * WIDTH, PACK)


def near_window(index, own0, own1, low, high, lanes):
    def rim(ref, level):
        return ref[BLOCK * level : BLOCK * (level + 1), lanes]

    if index == 0:
        parts = [rim(low, 0), own0[0:192, lanes]]
    elif index == 1:
        parts = [own0[64:256, lanes], rim(high, 0)]
    elif index == 2:
        parts = [rim(low, 1), own1[:, lanes], rim(high, 1)]
    else:
        parts = [rim(low, 2), rim(high, 2)]
    return jnp.concatenate(parts, axis=0)


def far_window(refs, lanes):
    return jnp.concatenate([ref[:, lanes] for ref in refs], axis=0)


def fetch(sources, targets, sems):
    copies = [
        pltpu.make_async_copy(source, target, sems.at[i])
        for i, (source, target) in enumerate(zip(sources, targets))
    ]
    for copy in copies:
        copy.start()
    return copies


def documents_kernel(seg_hbm, qdoc, seg, sem):
    copy = pltpu.make_async_copy(seg_hbm, seg, sem)
    copy.start()
    copy.wait()
    marks = jnp.where(seg[...] == iota((LANES, ROWS), 0), 1.0, 0.0).T.astype(BF16)
    qdoc[0:ROWS] = marks
    for level in range(1, LEVELS + 1):
        marks_c = dot(last_table(level), marks).astype(BF16)
        qdoc[AT[level] : AT[level] + COUNT[level]] = marks_c


def coarsen_kernel(qdoc, k_hbm, v_hbm, up, down, far, third, own0, own1, k, v, sems):
    copies = fetch((k_hbm, v_hbm), (k, v), sems)
    doc = iota((ALL_ROWS, LANES), 1) < DOCS
    docs = jnp.where(doc, (1.0 - qdoc[...].astype(F32)) * BLOCKED, 0.0).astype(BF16)
    copies[0].wait()
    copies[1].wait()
    levels = [(k[...], v[...], docs[0:ROWS])]
    for level in range(1, LEVELS + 1):
        keys = dot(gather_table(level, 0.5**level), levels[0][0]).astype(BF16)
        values = dot(gather_table(level), levels[0][1]).astype(BF16)
        levels.append((keys, values, docs[AT[level] : AT[level] + COUNT[level]]))

    def put(ref, at, level, start, stop):
        for part, lanes in zip(
            levels[level], (slice(0, WIDTH), slice(WIDTH, 2 * WIDTH), DOC_LANES)
        ):
            ref[at : at + stop - start, lanes] = part[start:stop]

    for level in range(3):
        put(up, BLOCK * level, level, COUNT[level] - BLOCK, COUNT[level])
        put(down, BLOCK * level, level, 0, BLOCK)
    put(far, 0, 3, 0, COUNT[3])
    put(far, COUNT[3], 4, 0, COUNT[4])
    put(third, 0, 4, 0, COUNT[4])
    put(own0, 0, 0, 0, COUNT[0])
    put(own1, 0, 1, 0, COUNT[1])


def core_index():
    return lax.axis_index("ctx") % 2


def pair_kernel(far, far_partner, far3, far4):
    even = core_index() == 0
    for out, start, rows in ((far3, 0, 32), (far4, 32, 16)):
        own, other = far[start : start + rows], far_partner[start : start + rows]
        out[0:rows] = jnp.where(even, own, other)
        out[rows : 2 * rows] = jnp.where(even, other, own)


def prepare_kernel(q_hbm, d_hbm, w_hbm, q_out, grad_att, w, d_out, q, sems):
    copies = fetch((q_hbm, d_hbm, w_hbm), (q, d_out, w), sems)
    copies[0].wait()
    for level in range(LEVELS + 1):
        queries = q[...] if level == 0 else dot(gather_table(level, 0.5**level), q[...]).astype(BF16)
        q_out[AT[level] : AT[level] + COUNT[level]] = (queries * SCALE).astype(BF16)
    copies[1].wait()
    copies[2].wait()
    grad_att[...] = dot(d_out[...], w[...], 1, 1)


def attend(queries, query_docs, keys, key_docs, values):
    rows = queries.shape[0]
    scores = dot(
        jnp.concatenate([stacked(queries), query_docs], axis=1),
        jnp.concatenate([keys, key_docs], axis=1),
        1,
        1,
    )
    peak = jnp.maximum(jnp.max(scores, axis=1, keepdims=True), NEGATIVE)
    peak = peak.astype(BF16).astype(F32)
    p = jnp.exp(scores - peak).astype(BF16)
    ones = jnp.ones(values.shape, BF16)
    both = dot(p, jnp.concatenate([values, ones], axis=1))
    return p, unstacked(both[:, :LANES], rows), both[:, LANES:], peak


def with_stats(stats, pair, sums, peak):
    rows = sums.shape[0] // 2
    lane = iota((rows, LANES), 1)
    result = []
    for old, new in zip(stats, (sums, peak)):
        old = jnp.where(lane == 2 * pair, new[:rows], old)
        result.append(jnp.where(lane == 2 * pair + 1, new[rows:], old))
    return result


def no_stats(rows):
    return [jnp.zeros((rows, LANES), F32)] * 2


def head_spread(pair):
    shape = (2 * LANES, LANES)
    head = iota(shape, 0) % LANES
    return jnp.where(head == 2 * pair + iota(shape, 1) // HEAD_DIM, 1.0, 0.0).astype(BF16)


def head_sum(pair):
    shape = (2 * LANES, LANES)
    head = 2 * pair + iota(shape, 0) % LANES // HEAD_DIM
    return jnp.where(head == iota(shape, 1), 1.0, 0.0).astype(BF16)


def both_parts(x):
    return jnp.concatenate(split(x), axis=1)


def docs_of(index, qdoc):
    level, start, rows, _ = GROUPS[index]
    docs = qdoc[AT[level] + start : AT[level] + start + rows]
    if index in NEAR:
        docs = docs + query_place(index)
    return jnp.concatenate([docs, docs], axis=0)


def near_kernel(q_all, qdoc, own0, own1, low, high, p_out, fine, fine_stats, coarse, coarse_stats):
    for index in NEAR:
        level, start, rows, keys = GROUPS[index]
        at = AT[level] + start
        query_docs = docs_of(index, qdoc)
        key_docs = near_window(index, own0, own1, low, high, DOC_LANES) + key_place(index)
        stats = no_stats(rows)
        for pair in range(PAIRS):
            window = [
                near_window(index, own0, own1, low, high, lanes_of(pair, part)) for part in (0, 1)
            ]
            p, numer, sums, peak = attend(
                q_all[at : at + rows, lanes_of(pair)], query_docs, window[0], key_docs, window[1]
            )
            stats = with_stats(stats, pair, sums, peak)
            p_out[pair, P_AT[index] : P_AT[index] + 2 * rows, 0:keys] = p
            if level == 0:
                fine[at : at + rows, lanes_of(pair)] = numer
            else:
                coarse[at - ROWS : at - ROWS + rows, lanes_of(pair)] = numer.astype(BF16)
        if level == 0:
            fine_stats[at : at + rows] = jnp.concatenate(stats, axis=1)
        else:
            coarse_stats[at - ROWS : at - ROWS + rows] = jnp.concatenate(stats, axis=1).astype(BF16)


def far_refs(refs):
    own3, got4, third, passed = refs
    return (
        (own3, passed.at[0:64]),
        (got4, passed.at[64:96], third, passed.at[96:112]),
    )


def block_at(block):
    x, y, core = block // 8, block // 2 % 4, block % 2
    return 16 * (16 * core + 4 * x + y)


def merge_kernel(
    q_all, qdoc, fine, fine_stats, coarse, coarse_stats, grad_att, d_out, *refs
):
    far = far_refs(refs[:4])
    attended_out, keep, give, p_out, g_out, d_side, d_w = refs[4:]
    spreads = [None] + [spread_table(level) for level in range(1, LEVELS + 1)]
    gathers = [None] + [gather_table(level) for level in range(1, LEVELS + 1)]
    numers, stats = [None, coarse[0:128], coarse[128:192]], [None, coarse_stats[0:128]]
    stats.append(coarse_stats[128:192])
    for index, ref in zip(FAR, far):
        level, _, rows, keys = GROUPS[index]
        query_docs, key_docs = docs_of(index, qdoc), far_window(ref, DOC_LANES)
        own_stats, own_numers = no_stats(rows), []
        for pair in range(PAIRS):
            p, numer, sums, peak = attend(
                q_all[AT[level] : AT[level] + rows, lanes_of(pair)],
                query_docs,
                far_window(ref, lanes_of(pair)),
                key_docs,
                far_window(ref, lanes_of(pair, 1)),
            )
            own_stats = with_stats(own_stats, pair, sums, peak)
            own_numers.append(numer.astype(BF16))
            p_out[pair, P_AT[index] : P_AT[index] + 2 * rows, 0:keys] = p
        numers.append(jnp.concatenate(own_numers, axis=1))
        stats.append(jnp.concatenate(own_stats, axis=1).astype(BF16))
    wide = [fine_stats[...]] + [
        dot(spreads[level], stats[level]) for level in range(1, LEVELS + 1)
    ]
    sums, peaks = [x[:, :LANES] for x in wide], [x[:, LANES:] for x in wide]
    top = functools.reduce(jnp.maximum, peaks)
    weights = [jnp.exp(x - top) for x in peaks]
    norm = functools.reduce(
        jnp.add, [wt * x * float(2**i) for i, (wt, x) in enumerate(zip(weights, sums))]
    )
    inverse = 1.0 / jnp.where(iota(norm.shape, 1) < 2 * PAIRS, norm, 1.0)
    shares = [wt * inverse for wt in weights]
    share_parts = [both_parts(x) for x in shares]
    delta = jnp.zeros((ROWS, LANES), F32)
    for pair in range(PAIRS):
        cols = lanes_of(pair)
        to_lanes = head_spread(pair)
        wide_shares = [dot(x, to_lanes) for x in share_parts]
        numer = wide_shares[0] * fine[:, cols]
        for level in range(1, LEVELS + 1):
            numer = numer + wide_shares[level] * dot(spreads[level], numers[level][:, cols])
        attended = numer.astype(BF16)
        attended_out[:, cols] = attended
        grad_w = dot(attended, d_out[...], 0, 0)
        for block in range(8):
            at = block_at(8 * pair + block)
            d_w[at : at + 16] = grad_w[16 * block : 16 * (block + 1)]
        grad = grad_att[:, cols]
        delta = delta + dot(both_parts(grad * attended.astype(F32)), head_sum(pair))
        for level in range(LEVELS + 1):
            rows = (wide_shares[level] * grad).astype(BF16)
            if level > 0:
                rows = dot(gathers[level], rows).astype(BF16)
            g_out[AT[level] : AT[level] + COUNT[level], cols] = rows
    core = core_index()
    keep[...] = d_w[pl.ds(pl.multiple_of(core * 256, 256), 256)]
    give[...] = d_w[pl.ds(pl.multiple_of((1 - core) * 256, 256), 256)].astype(BF16)
    shape = (2 * LANES, LANES)
    part, head = iota(shape, 0) // LANES, iota(shape, 0) % LANES
    place = jnp.where((head < 8) & (iota(shape, 1) == 8 * part + head), 1.0, 0.0).astype(BF16)
    for level in range(LEVELS + 1):
        delta_c = shares[level] * delta
        if level > 0:
            summed = dot(gathers[level], both_parts(delta_c))
            delta_c = summed[:, :LANES] + summed[:, LANES:]
        terms = dot(both_parts(delta_c * -float(2**level)), place)
        d_side[AT[level] : AT[level] + COUNT[level]] = terms.astype(BF16)


def attend_back(pair, p, queries, grad, side, keys, values):
    rows = queries.shape[0]
    ones = jnp.where(iota(values.shape, 1) < 16, 1.0, 0.0).astype(BF16)
    grad = stacked(grad)
    lane = iota(side.shape, 1)
    sides = [
        side * jnp.where((lane < 16) & (lane % 8 == 2 * pair + i), 1.0, 0.0).astype(BF16)
        for i in (0, 1)
    ]
    product = dot(
        jnp.concatenate([grad, jnp.concatenate(sides, axis=0)], axis=1),
        jnp.concatenate([values, ones], axis=1),
        1,
        1,
    )
    ds = (p.astype(F32) * product).astype(BF16)
    grad_q = unstacked(dot(ds, keys), rows) * SCALE
    return grad_q, dot(ds, stacked(queries), 0, 0), dot(p, grad, 0, 0)


PARTNER_ROWS = 112
MESSAGE_ROWS = 256 + 2 * PARTNER_ROWS


def far_back_kernel(p_in, q_all, g_in, d_side, own3, got4, third, passed, give, *refs):
    far = far_refs((own3, got4, third, passed))
    d_q, to_3, to_4, to_third, message = refs
    message[0:256] = give[...]
    to_far = ((to_3, (0, 64)), (to_4, (64, 96), to_third, (96, 112)))
    for pair in range(PAIRS):
        cols = lanes_of(pair)
        for index, ref, to in zip(FAR, far, to_far):
            level, _, rows, keys = GROUPS[index]
            at = AT[level]
            grad_q, grad_k, grad_v = attend_back(
                pair,
                p_in[pair, P_AT[index] : P_AT[index] + 2 * rows, 0:keys],
                q_all[at : at + rows, cols],
                g_in[at : at + rows, cols],
                d_side[at : at + rows],
                far_window(ref, cols),
                far_window(ref, lanes_of(pair, 1)),
            )
            d_q[at - AT[3] : at - AT[3] + rows, cols] = grad_q.astype(BF16)
            start = 0
            for out in to:
                partners = isinstance(out, tuple)
                stop = start + (out[1] - out[0] if partners else out.shape[0])
                for part, grad in enumerate((grad_k, grad_v)):
                    rows = grad[start:stop].astype(BF16)
                    if partners:
                        first = 256 + part * PARTNER_ROWS
                        message[first + out[0] : first + out[1], cols] = rows
                    else:
                        out[:, lanes_of(pair, part)] = rows
                start = stop


NEAR_PARTS = ((0,), (1,), (2,), (3,))


def near_back(pairs, p_in, q_all, g_in, d_side, own0, own1, low, high, d_far):
    spread = jnp.concatenate([spread_table(level, 0.5**level) for level in (1, 2, 3, 4)], axis=1)
    for pair in pairs:
        cols = lanes_of(pair)
        grads = []
        for index in NEAR:
            level, start, rows, keys = GROUPS[index]
            at = AT[level] + start
            grads.append(
                attend_back(
                    pair,
                    p_in[pair, P_AT[index] : P_AT[index] + 2 * rows, 0:keys],
                    q_all[at : at + rows, cols],
                    g_in[at : at + rows, cols],
                    d_side[at : at + rows],
                    near_window(index, own0, own1, low, high, cols),
                    near_window(index, own0, own1, low, high, lanes_of(pair, 1)),
                )
            )
        coarse = [x[0].astype(BF16) for x in grads[2:]] + [d_far[:, cols]]
        whole = jnp.concatenate([x[0] for x in grads[:2]], axis=0)
        d_q = (whole + dot(spread, jnp.concatenate(coarse, axis=0))).astype(BF16)
        own, to_low, to_high = [], [], []
        for part, value in ((0, 0.5), (1, 1.0)):
            a, b, c, d = (x[1 + part] for x in grads)
            middle = jnp.concatenate([a[64:128], a[128:256] + b[0:128], b[128:192]], axis=0)
            near = dot(spread_table(1, value), c[64:192].astype(BF16))
            own.append((middle + near).astype(BF16))
            to_low.append(jnp.concatenate([a[:64], c[:64], d[:64]], axis=0).astype(BF16))
            to_high.append(jnp.concatenate([b[192:], c[192:], d[64:]], axis=0).astype(BF16))
        yield pair, d_q, own, to_low, to_high


def near_back_kernel(pairs, *refs):
    inputs, outs = refs[:9], refs[-5:]
    d_q, own_k, own_v, to_low, to_high = outs
    for pair, dq, own, low, high in near_back(pairs, *inputs):
        at = slice((pair - pairs[0]) * LANES, (pair - pairs[0] + 1) * LANES)
        d_q[:, at], own_k[:, at], own_v[:, at] = dq, own[0], own[1]
        for part in range(2):
            to_low[part, :, at], to_high[part, :, at] = low[part], high[part]


def near_back_last_kernel(*refs):
    inputs, earlier = refs[:9], [refs[at : at + 2] for at in (9, 11, 13)]
    d_q, own_k, own_v, to_low, to_high = refs[-5:]
    for pairs, (low, high) in zip(NEAR_PARTS, earlier):
        for part in range(2):
            lanes = slice(
                part * WIDTH + pairs[0] * LANES, part * WIDTH + (pairs[-1] + 1) * LANES
            )
            to_low[:, lanes], to_high[:, lanes] = low[part], high[part]
    for pair, dq, own, low, high in near_back(NEAR_PARTS[-1], *inputs):
        d_q[...], own_k[...], own_v[...] = dq, own[0], own[1]
        for part in range(2):
            to_low[:, lanes_of(pair, part)] = low[part]
            to_high[:, lanes_of(pair, part)] = high[part]


def pass_on_kernel(got3, got4, third, own3, out):
    out[0:64] = got3[...]
    out[64:96] = got4[...]
    out[96:112] = third[...]
    own3[...] = jnp.where(core_index() == 0, got3[0:32], got3[32:64])


def partner_sum_kernel(to_3, to_4, to_third, keep, message, *refs):
    sum3, sum4, sum_third, keep_out, give_out, total = refs[-6:]
    even = core_index() == 0
    for part in range(2):
        lanes = slice(part * WIDTH, (part + 1) * WIDTH)
        at = 256 + part * PARTNER_ROWS
        own3 = to_3[:, lanes].astype(F32)

        def came(start, stop):
            return message[at + start : at + stop].astype(F32)

        sum3[0:32, lanes] = (came(0, 32) + jnp.where(even, own3, 0.0)).astype(BF16)
        sum3[32:64, lanes] = (came(32, 64) + jnp.where(even, 0.0, own3)).astype(BF16)
        sum4[:, lanes] = (came(64, 96) + to_4[:, lanes].astype(F32)).astype(BF16)
        sum_third[:, lanes] = (came(96, 112) + to_third[:, lanes].astype(F32)).astype(BF16)
    total[...] = keep[...] + message[0:256].astype(F32)
    halve(total, 16, keep_out, give_out)


def halve(total, divisor, keep, give):
    side = lax.axis_index("ctx") // divisor % 2
    half = total.shape[0] // 2
    keep[...] = total[pl.ds(pl.multiple_of(side * half, half), half)]
    give[...] = total[pl.ds(pl.multiple_of((1 - side) * half, half), half)].astype(BF16)


def core_rows(ref, core, rows):
    return ref[pl.ds(pl.multiple_of(core * rows, rows), rows)]


def far_split_kernel(back3, back4, give):
    other = 1 - core_index()
    give[0:32] = core_rows(back3, other, 32)
    give[32:48] = core_rows(back4, other, 16)


def halve_kernel(divisor, keep, got, *refs):
    keep_out, give_out, total = refs[-3:]
    total[...] = keep[...] + got[...].astype(F32)
    halve(total, divisor, keep_out, give_out)


def copies_kernel(keep, got, *refs):
    total = keep[...] + got[...].astype(F32)
    for i in range(refs[-1].shape[0]):
        refs[-1][i] = total.astype(BF16)


def last_sum_kernel(parts, _, out):
    total = parts[0].astype(F32)
    for i in range(1, parts.shape[0]):
        total = total + parts[i].astype(F32)
    out[...] = total.astype(BF16)


def project_kernel(attended, w, _, layer_hbm, finished, layer_out, sem):
    finished[...] = jnp.zeros(finished.shape, F32)
    layer_out[...] = dot(attended[...], w[...]).astype(BF16)
    copy = pltpu.make_async_copy(layer_out, layer_hbm, sem)
    copy.start()
    copy.wait()


def combine_kernel(*refs):
    own, (low, high), grads_q = (refs[0:4], refs[4:8]), refs[8:10], refs[14:18]
    back3, back4, third, swapped = refs[10:14]
    d_k_hbm, d_v_hbm, d_q_hbm, finished, d_k, d_v, d_q, sems = refs[18:]
    finished[...] = jnp.zeros(finished.shape, F32)
    for pair, ref in enumerate(grads_q):
        d_q[:, lanes_of(pair)] = ref[...]
    copies = [pltpu.make_async_copy(d_q, d_q_hbm, sems.at[2])]
    copies[0].start()
    core = core_index()
    far3 = core_rows(back3, core, 32).astype(F32) + swapped[0:32].astype(F32)
    far4 = core_rows(back4, core, 16).astype(F32) + swapped[32:48].astype(F32)
    far4 = far4 + third[...].astype(F32)
    for part, out, out_hbm in ((0, d_k, d_k_hbm), (1, d_v, d_v_hbm)):
        lanes = slice(part * WIDTH, (part + 1) * WIDTH)
        table = jnp.concatenate(
            [spread_table(level, 1.0 if part else 0.5**level) for level in (1, 2, 3, 4)], axis=1
        )

        def rim(ref, level):
            return ref[BLOCK * level : BLOCK * (level + 1), lanes].astype(F32)

        coarse = jnp.concatenate(
            [
                rim(high, 1),
                rim(low, 1),
                rim(low, 2) + rim(high, 2),
                far3[:, lanes],
                far4[:, lanes],
            ],
            axis=0,
        ).astype(BF16)
        whole = jnp.concatenate([x[...] for x in own[part]], axis=1).astype(F32)
        whole = whole + dot(table, coarse)
        out[0:64] = (whole[0:64] + rim(high, 0)).astype(BF16)
        out[64:192] = whole[64:192].astype(BF16)
        out[192:256] = (whole[192:256] + rim(low, 0)).astype(BF16)
        copies.append(pltpu.make_async_copy(out, out_hbm, sems.at[part]))
        copies[-1].start()
    for copy in copies:
        copy.wait()


def call(
    kernel, name, outs, args, scratch=(), in_hbm=0, microseconds=1.0, to_hbm=()
):
    vmem, hbm = pl.BlockSpec(memory_space=pltpu.VMEM), pl.BlockSpec(memory_space=pl.ANY)
    return pl.pallas_call(
        kernel,
        name=name,
        out_shape=[jax.ShapeDtypeStruct(shape, dtype) for shape, dtype in outs],
        in_specs=[vmem] * (len(args) - in_hbm) + [hbm] * in_hbm,
        out_specs=[hbm if i in to_hbm else vmem for i in range(len(outs))],
        scratch_shapes=scratch,
        cost_estimate=pl.CostEstimate(
            flops=int(microseconds * 1e9), bytes_accessed=1 << 20, transcendentals=0
        ),
        compiler_params=pltpu.CompilerParams(vmem_limit_bytes=VMEM_MIB * 1024 * 1024),
    )(*args)


def moved(x, route):
    count = lax.axis_size("ctx")
    return lax.ppermute(x, "ctx", [(i, route(i) % count) for i in range(count)])


def partner(i):
    return i ^ 1


def third(i):
    return i - 6 if i // 2 % 2 else i + 6


def route_3(i):
    return i - 2 if i % 2 else i + 2


def route_4(i):
    return i - 4 if i % 2 else i + 4


def back_3(i):
    return i + 2 if i % 2 else i - 2


def back_4(i):
    return i + 4 if i % 2 else i - 4


def body(queries, key_rows, value_rows, segment_ids, w_out, d_out):
    q, k, v, grad_out = queries[0], key_rows[0], value_rows[0], d_out[0]
    tokens, dma = (ROWS, WIDTH), pltpu.SemaphoreType.DMA
    qdoc = call(
        documents_kernel,
        "documents",
        [((ALL_ROWS, LANES), BF16)],
        [segment_ids],
        [pltpu.VMEM((1, ROWS), jnp.int32), dma(())],
        in_hbm=1,
    )[0]
    up, down, far, third_rows, own0, own1 = call(
        coarsen_kernel,
        "coarsen",
        [((192, PACK), BF16), ((192, PACK), BF16), ((48, PACK), BF16), ((16, PACK), BF16)]
        + [((ROWS, PACK), BF16), ((128, PACK), BF16)],
        [qdoc, k, v],
        [pltpu.VMEM(tokens, BF16)] * 2 + [dma((2,))],
        in_hbm=2,
    )
    far_partner = moved(far, partner)
    far3, far4 = call(
        pair_kernel, "pair", [((64, PACK), BF16), ((32, PACK), BF16)], [far, far_partner]
    )
    q_all, grad_att, w, grad_rows = call(
        prepare_kernel,
        "prepare",
        [((ALL_ROWS, WIDTH), BF16), (tokens, F32), ((WIDTH, WIDTH), BF16), (tokens, BF16)],
        [q, grad_out, w_out],
        [pltpu.VMEM(tokens, BF16), dma((3,))],
        in_hbm=3,
    )
    low = moved(up, lambda i: i + 1)
    high = moved(down, lambda i: i - 1)
    got3 = moved(far3, route_3)
    got4 = moved(far4, route_4)
    got_third = moved(third_rows, third)
    low, high, got3 = lax.optimization_barrier((low, high, got3))
    own3, passed = call(
        pass_on_kernel,
        "pass_on",
        [((32, PACK), BF16), ((112, PACK), BF16)],
        [got3, got4, got_third],
    )
    far = (own3, got4, got_third, moved(passed, partner))
    near = (own0, own1, low, high)
    p_near, *near_sums = call(
        near_kernel,
        "near",
        [((PAIRS, P_NEAR, 256), BF16), (tokens, F32), ((ROWS, 2 * LANES), F32)]
        + [((192, WIDTH), BF16), ((192, 2 * LANES), BF16)],
        [q_all, qdoc, *near],
        microseconds=50,
    )
    attended, keep, give, p_far, g, d_side = call(
        merge_kernel,
        "merge",
        [(tokens, BF16), ((256, WIDTH), F32), ((256, WIDTH), BF16)]
        + [((PAIRS, P_FAR, LANES), BF16)]
        + [((ALL_ROWS, WIDTH), BF16), ((ALL_ROWS, LANES), BF16)],
        [q_all, qdoc, *near_sums, grad_att, grad_rows, *far],
        [pltpu.VMEM((WIDTH, WIDTH), F32)],
        microseconds=6,
    )

    def halved(keep, got, divisor, route, *after):
        rows = keep.shape[0] // 2
        keep, give = call(
            functools.partial(halve_kernel, divisor),
            "halve_" + str(rows),
            [((rows, WIDTH), F32), ((rows, WIDTH), BF16)],
            [keep, got, *after],
            [pltpu.VMEM((2 * rows, WIDTH), F32)],
            in_hbm=len(after),
        )
        return keep, moved(give, route)

    d_far, *to_far, message = call(
        far_back_kernel,
        "far_back",
        [((48, WIDTH), BF16), ((32, 2 * WIDTH), BF16), ((32, 2 * WIDTH), BF16)]
        + [((16, 2 * WIDTH), BF16), ((MESSAGE_ROWS, WIDTH), BF16)],
        [p_far, q_all, g, d_side, *far, give],
    )
    message = moved(message, partner)

    def part_outs(part):
        width = len(NEAR_PARTS[part]) * LANES
        return [((ROWS, width), BF16)] * 3 + [((2, 192, width), BF16)] * 2

    args = [p_near, q_all, g, d_side, *near, d_far]
    part_a = call(
        functools.partial(near_back_kernel, NEAR_PARTS[0]),
        "near_back_a",
        part_outs(0),
        args,
        microseconds=3,
    )
    sum3, sum4, sum_third, keep, give = call(
        partner_sum_kernel,
        "partner_sum",
        [((64, 2 * WIDTH), BF16), ((32, 2 * WIDTH), BF16), ((16, 2 * WIDTH), BF16)]
        + [((128, WIDTH), F32), ((128, WIDTH), BF16)],
        [*to_far, keep, message, part_a[0]],
        [pltpu.VMEM((256, WIDTH), F32)],
        in_hbm=1,
    )
    got_w = moved(give, lambda i: i ^ 24)
    back3 = moved(sum3, back_3)
    back4 = moved(sum4, back_4)
    layer_out, projected = call(
        project_kernel,
        "project",
        [(tokens, BF16), ((8, LANES), F32)],
        [attended, w, sum3],
        [pltpu.VMEM(tokens, BF16), dma(())],
        in_hbm=1,
        to_hbm=(0,),
    )
    keep, got_w = halved(keep, got_w, 8, lambda i: i ^ 8, projected)
    part_b = call(
        functools.partial(near_back_kernel, NEAR_PARTS[1]),
        "near_back_b",
        part_outs(1),
        [*args, part_a[0], keep],
        in_hbm=2,
        microseconds=3,
    )
    keep, got_w = halved(keep, got_w, 4, lambda i: i ^ 6, part_b[0])
    part_c = call(
        functools.partial(near_back_kernel, NEAR_PARTS[2]),
        "near_back_c",
        part_outs(2),
        [*args, part_b[0], keep],
        in_hbm=2,
        microseconds=3,
    )
    keep, got_w = halved(keep, got_w, 2, lambda i: i ^ 2, part_c[0])
    give = call(far_split_kernel, "far_split", [((48, 2 * WIDTH), BF16)], [back3, back4])[0]
    swapped = moved(give, partner)
    d_q, own_k, own_v, to_low, to_high = call(
        near_back_last_kernel,
        "near_back_d",
        part_outs(3)[:3] + [((192, 2 * WIDTH), BF16)] * 2,
        [*args, *part_a[3:], *part_b[3:], *part_c[3:], keep, give],
        in_hbm=2,
        microseconds=3,
    )
    to_low, to_high, got_w = lax.optimization_barrier((to_low, to_high, got_w))
    low_back = moved(to_low, lambda i: i - 1)
    high_back = moved(to_high, lambda i: i + 1)
    copies = call(
        copies_kernel,
        "copies",
        [((lax.axis_size("dp"), 16, WIDTH), BF16)],
        [keep, got_w],
    )[0]
    sum_third, copies = lax.optimization_barrier((sum_third, copies))
    copies = lax.all_to_all(copies, "dp", 0, 0, tiled=True)
    back_third = moved(sum_third, third)
    d_k, d_v, d_q, finished = call(
        combine_kernel,
        "combine",
        [(tokens, BF16)] * 3 + [((8, LANES), F32)],
        [part_a[1], part_b[1], part_c[1], own_k, part_a[2], part_b[2], part_c[2], own_v]
        + [low_back, high_back, back3, back4, back_third, swapped]
        + [part_a[0], part_b[0], part_c[0], d_q],
        [pltpu.VMEM(tokens, BF16)] * 3 + [dma((3,))],
        to_hbm=(0, 1, 2),
    )
    d_w = call(last_sum_kernel, "last_sum", [((16, WIDTH), BF16)], [copies, finished], in_hbm=1)[0]
    return layer_out[None], d_q[None], d_k[None], d_v[None], d_w


def solution(mesh):
    tokens = P("dp", "ctx", None)
    return jax.shard_map(
        body,
        mesh=mesh,
        in_specs=(tokens, tokens, tokens, P("dp", "ctx"), P(), tokens),
        out_specs=(tokens, tokens, tokens, tokens, P("ctx", None)),
        check_vma=False,
    )
```

```python
import functools

import jax
import jax.numpy as jnp
from jax import lax
from jax.experimental import pallas as pl
from jax.experimental.pallas import tpu as pltpu
from jax.sharding import PartitionSpec as P

HEAD_DIM = 64
BLOCK = 64
HALF = 32
LEVELS = 4
ROWS = 256
WIDTH = 512
PAIRS = 4
LANES = 128
DOCS = 4
NEGATIVE = -1e30
BLOCKED = -2e30
SCALE = HEAD_DIM**-0.5
PACK = 2 * WIDTH + LANES
COUNT = (256, 128, 64, 32, 16)
AT = (0, 256, 384, 448, 480)
ALL_ROWS = 496
F32 = jnp.float32
BF16 = jnp.bfloat16
VMEM_MIB = 20

GROUPS = (
    (0, 0, 128, 256),
    (0, 128, 128, 256),
    (1, 0, 128, 256),
    (2, 0, 64, 128),
    (3, 0, 32, 96),
    (4, 0, 16, 96),
)
NEAR = (0, 1, 2, 3)
FAR = (4, 5)
P_AT = {0: 0, 1: 256, 2: 512, 3: 768, 4: 0, 5: 64}
P_NEAR, P_FAR = 896, 96


def iota(shape, dim):
    return lax.broadcasted_iota(jnp.int32, shape, dim)


def gather_table(level, value=1.0):
    shape = (COUNT[level], ROWS)
    return jnp.where(iota(shape, 1) // 2**level == iota(shape, 0), value, 0.0).astype(BF16)


def spread_table(level, value=1.0):
    shape = (ROWS, COUNT[level])
    return jnp.where(iota(shape, 0) // 2**level == iota(shape, 1), value, 0.0).astype(BF16)


def last_table(level):
    shape = (COUNT[level], ROWS)
    last = iota(shape, 0) * 2**level + (2**level - 1)
    return jnp.where(iota(shape, 1) == last, 1.0, 0.0).astype(BF16)


def query_place(index):
    level, _, rows, _ = GROUPS[index]
    size = BLOCK if level == 0 else HALF
    shape = (rows, LANES)
    return jnp.where(iota(shape, 0) // size + 8 == iota(shape, 1), 1.0, 0.0).astype(BF16)


def key_place(index):
    level, _, _, keys = GROUPS[index]
    shape = (keys, LANES)
    row, place = iota(shape, 0), iota(shape, 1) - 8
    if level == 0:
        apart = row // BLOCK - place
        blocked = (apart < 0) | (apart > 2)
        places = 2
    elif level == 1:
        there, here = row // HALF, place + 2
        block_apart = jnp.abs(there // 2 - (place + 2) // 2)
        blocked = (block_apart > 1) | (jnp.abs(there - here) < 2)
        places = 4
    else:
        blocked = row // HALF == place + 1
        places = 2
    blocked = blocked & (place >= 0) & (place < places)
    return jnp.where(blocked, BLOCKED, 0.0).astype(BF16)


def dot(a, b, a_dim=1, b_dim=0):
    return lax.dot_general(a, b, (((a_dim,), (b_dim,)), ((), ())), preferred_element_type=F32)


def split(x):
    high = x.astype(BF16)
    return high, (x - high.astype(F32)).astype(BF16)


def head_lanes(rows, width=LANES):
    return iota((rows, width), 1) % LANES < HEAD_DIM


def stacked(x):
    first = head_lanes(x.shape[0]).astype(F32).astype(BF16)
    return jnp.concatenate([x * first, x * (1 - first)], axis=0)


def unstacked(x, rows):
    return jnp.where(head_lanes(rows, x.shape[1]), x[:rows], x[rows:])


def lanes_of(pair, part=0):
    return slice(part * WIDTH + pair * LANES, part * WIDTH + (pair + 1) * LANES)


DOC_LANES = slice(2 * WIDTH, PACK)


def near_window(index, own0, own1, low, high, lanes):
    def rim(ref, level):
        return ref[BLOCK * level : BLOCK * (level + 1), lanes]

    if index == 0:
        parts = [rim(low, 0), own0[0:192, lanes]]
    elif index == 1:
        parts = [own0[64:256, lanes], rim(high, 0)]
    elif index == 2:
        parts = [rim(low, 1), own1[:, lanes], rim(high, 1)]
    else:
        parts = [rim(low, 2), rim(high, 2)]
    return jnp.concatenate(parts, axis=0)


def far_window(refs, lanes):
    return jnp.concatenate([ref[:, lanes] for ref in refs], axis=0)


def fetch(sources, targets, sems):
    copies = [
        pltpu.make_async_copy(source, target, sems.at[i])
        for i, (source, target) in enumerate(zip(sources, targets))
    ]
    for copy in copies:
        copy.start()
    return copies


def documents_kernel(seg_hbm, qdoc, seg, sem):
    copy = pltpu.make_async_copy(seg_hbm, seg, sem)
    copy.start()
    copy.wait()
    marks = jnp.where(seg[...] == iota((LANES, ROWS), 0), 1.0, 0.0).T.astype(BF16)
    qdoc[0:ROWS] = marks
    for level in range(1, LEVELS + 1):
        marks_c = dot(last_table(level), marks).astype(BF16)
        qdoc[AT[level] : AT[level] + COUNT[level]] = marks_c


def coarsen_kernel(qdoc, k_hbm, v_hbm, up, down, far, third, own0, own1, k, v, sems):
    copies = fetch((k_hbm, v_hbm), (k, v), sems)
    doc = iota((ALL_ROWS, LANES), 1) < DOCS
    docs = jnp.where(doc, (1.0 - qdoc[...].astype(F32)) * BLOCKED, 0.0).astype(BF16)
    copies[0].wait()
    copies[1].wait()
    levels = [(k[...], v[...], docs[0:ROWS])]
    for level in range(1, LEVELS + 1):
        keys = dot(gather_table(level, 0.5**level), levels[0][0]).astype(BF16)
        values = dot(gather_table(level), levels[0][1]).astype(BF16)
        levels.append((keys, values, docs[AT[level] : AT[level] + COUNT[level]]))

    def put(ref, at, level, start, stop):
        for part, lanes in zip(
            levels[level], (slice(0, WIDTH), slice(WIDTH, 2 * WIDTH), DOC_LANES)
        ):
            ref[at : at + stop - start, lanes] = part[start:stop]

    for level in range(3):
        put(up, BLOCK * level, level, COUNT[level] - BLOCK, COUNT[level])
        put(down, BLOCK * level, level, 0, BLOCK)
    put(far, 0, 3, 0, COUNT[3])
    put(far, COUNT[3], 4, 0, COUNT[4])
    put(third, 0, 4, 0, COUNT[4])
    put(own0, 0, 0, 0, COUNT[0])
    put(own1, 0, 1, 0, COUNT[1])


def core_index():
    return lax.axis_index("ctx") % 2


def pair_kernel(far, far_partner, far3, far4):
    even = core_index() == 0
    for out, start, rows in ((far3, 0, 32), (far4, 32, 16)):
        own, other = far[start : start + rows], far_partner[start : start + rows]
        out[0:rows] = jnp.where(even, own, other)
        out[rows : 2 * rows] = jnp.where(even, other, own)


def prepare_kernel(q_hbm, d_hbm, w_hbm, q_out, grad_att, w, d_out, q, sems):
    copies = fetch((q_hbm, d_hbm, w_hbm), (q, d_out, w), sems)
    copies[0].wait()
    for level in range(LEVELS + 1):
        queries = q[...] if level == 0 else dot(gather_table(level, 0.5**level), q[...]).astype(BF16)
        q_out[AT[level] : AT[level] + COUNT[level]] = (queries * SCALE).astype(BF16)
    copies[1].wait()
    copies[2].wait()
    grad_att[...] = dot(d_out[...], w[...], 1, 1)


def attend(queries, query_docs, keys, key_docs, values):
    rows = queries.shape[0]
    scores = dot(
        jnp.concatenate([stacked(queries), query_docs], axis=1),
        jnp.concatenate([keys, key_docs], axis=1),
        1,
        1,
    )
    peak = jnp.maximum(jnp.max(scores, axis=1, keepdims=True), NEGATIVE)
    peak = peak.astype(BF16).astype(F32)
    p = jnp.exp(scores - peak).astype(BF16)
    ones = jnp.ones(values.shape, BF16)
    both = dot(p, jnp.concatenate([values, ones], axis=1))
    return p, unstacked(both[:, :LANES], rows), both[:, LANES:], peak


def with_stats(stats, pair, sums, peak):
    rows = sums.shape[0] // 2
    lane = iota((rows, LANES), 1)
    result = []
    for old, new in zip(stats, (sums, peak)):
        old = jnp.where(lane == 2 * pair, new[:rows], old)
        result.append(jnp.where(lane == 2 * pair + 1, new[rows:], old))
    return result


def no_stats(rows):
    return [jnp.zeros((rows, LANES), F32)] * 2


def head_spread(pair):
    shape = (2 * LANES, LANES)
    head = iota(shape, 0) % LANES
    return jnp.where(head == 2 * pair + iota(shape, 1) // HEAD_DIM, 1.0, 0.0).astype(BF16)


def head_sum(pair):
    shape = (2 * LANES, LANES)
    head = 2 * pair + iota(shape, 0) % LANES // HEAD_DIM
    return jnp.where(head == iota(shape, 1), 1.0, 0.0).astype(BF16)


def both_parts(x):
    return jnp.concatenate(split(x), axis=1)


def docs_of(index, qdoc):
    level, start, rows, _ = GROUPS[index]
    docs = qdoc[AT[level] + start : AT[level] + start + rows]
    if index in NEAR:
        docs = docs + query_place(index)
    return jnp.concatenate([docs, docs], axis=0)


def near_kernel(q_all, qdoc, own0, own1, low, high, p_out, fine, fine_stats, coarse, coarse_stats):
    for index in NEAR:
        level, start, rows, keys = GROUPS[index]
        at = AT[level] + start
        query_docs = docs_of(index, qdoc)
        key_docs = near_window(index, own0, own1, low, high, DOC_LANES) + key_place(index)
        stats = no_stats(rows)
        for pair in range(PAIRS):
            window = [
                near_window(index, own0, own1, low, high, lanes_of(pair, part)) for part in (0, 1)
            ]
            p, numer, sums, peak = attend(
                q_all[at : at + rows, lanes_of(pair)], query_docs, window[0], key_docs, window[1]
            )
            stats = with_stats(stats, pair, sums, peak)
            p_out[pair, P_AT[index] : P_AT[index] + 2 * rows, 0:keys] = p
            if level == 0:
                fine[at : at + rows, lanes_of(pair)] = numer
            else:
                coarse[at - ROWS : at - ROWS + rows, lanes_of(pair)] = numer.astype(BF16)
        if level == 0:
            fine_stats[at : at + rows] = jnp.concatenate(stats, axis=1)
        else:
            coarse_stats[at - ROWS : at - ROWS + rows] = jnp.concatenate(stats, axis=1).astype(BF16)


def far_refs(refs):
    own3, got4, third, passed = refs
    return (
        (own3, passed.at[0:64]),
        (got4, passed.at[64:96], third, passed.at[96:112]),
    )


def block_at(block):
    x, y, core = block // 8, block // 2 % 4, block % 2
    return 16 * (16 * core + 4 * x + y)


def merge_kernel(
    q_all, qdoc, fine, fine_stats, coarse, coarse_stats, grad_att, d_out, *refs
):
    far = far_refs(refs[:4])
    attended_out, keep, give, p_out, g_out, d_side, d_w = refs[4:]
    spreads = [None] + [spread_table(level) for level in range(1, LEVELS + 1)]
    gathers = [None] + [gather_table(level) for level in range(1, LEVELS + 1)]
    numers, stats = [None, coarse[0:128], coarse[128:192]], [None, coarse_stats[0:128]]
    stats.append(coarse_stats[128:192])
    for index, ref in zip(FAR, far):
        level, _, rows, keys = GROUPS[index]
        query_docs, key_docs = docs_of(index, qdoc), far_window(ref, DOC_LANES)
        own_stats, own_numers = no_stats(rows), []
        for pair in range(PAIRS):
            p, numer, sums, peak = attend(
                q_all[AT[level] : AT[level] + rows, lanes_of(pair)],
                query_docs,
                far_window(ref, lanes_of(pair)),
                key_docs,
                far_window(ref, lanes_of(pair, 1)),
            )
            own_stats = with_stats(own_stats, pair, sums, peak)
            own_numers.append(numer.astype(BF16))
            p_out[pair, P_AT[index] : P_AT[index] + 2 * rows, 0:keys] = p
        numers.append(jnp.concatenate(own_numers, axis=1))
        stats.append(jnp.concatenate(own_stats, axis=1).astype(BF16))
    wide = [fine_stats[...]] + [
        dot(spreads[level], stats[level]) for level in range(1, LEVELS + 1)
    ]
    sums, peaks = [x[:, :LANES] for x in wide], [x[:, LANES:] for x in wide]
    top = functools.reduce(jnp.maximum, peaks)
    weights = [jnp.exp(x - top) for x in peaks]
    norm = functools.reduce(
        jnp.add, [wt * x * float(2**i) for i, (wt, x) in enumerate(zip(weights, sums))]
    )
    inverse = 1.0 / jnp.where(iota(norm.shape, 1) < 2 * PAIRS, norm, 1.0)
    shares = [wt * inverse for wt in weights]
    share_parts = [both_parts(x) for x in shares]
    delta = jnp.zeros((ROWS, LANES), F32)
    for pair in range(PAIRS):
        cols = lanes_of(pair)
        to_lanes = head_spread(pair)
        wide_shares = [dot(x, to_lanes) for x in share_parts]
        numer = wide_shares[0] * fine[:, cols]
        for level in range(1, LEVELS + 1):
            numer = numer + wide_shares[level] * dot(spreads[level], numers[level][:, cols])
        attended = numer.astype(BF16)
        attended_out[:, cols] = attended
        grad_w = dot(attended, d_out[...], 0, 0)
        for block in range(8):
            at = block_at(8 * pair + block)
            d_w[at : at + 16] = grad_w[16 * block : 16 * (block + 1)]
        grad = grad_att[:, cols]
        delta = delta + dot(both_parts(grad * attended.astype(F32)), head_sum(pair))
        for level in range(LEVELS + 1):
            rows = (wide_shares[level] * grad).astype(BF16)
            if level > 0:
                rows = dot(gathers[level], rows).astype(BF16)
            g_out[AT[level] : AT[level] + COUNT[level], cols] = rows
    core = core_index()
    keep[...] = d_w[pl.ds(pl.multiple_of(core * 256, 256), 256)]
    give[...] = d_w[pl.ds(pl.multiple_of((1 - core) * 256, 256), 256)].astype(BF16)
    shape = (2 * LANES, LANES)
    part, head = iota(shape, 0) // LANES, iota(shape, 0) % LANES
    place = jnp.where((head < 8) & (iota(shape, 1) == 8 * part + head), 1.0, 0.0).astype(BF16)
    for level in range(LEVELS + 1):
        delta_c = shares[level] * delta
        if level > 0:
            summed = dot(gathers[level], both_parts(delta_c))
            delta_c = summed[:, :LANES] + summed[:, LANES:]
        terms = dot(both_parts(delta_c * -float(2**level)), place)
        d_side[AT[level] : AT[level] + COUNT[level]] = terms.astype(BF16)


def attend_back(pair, p, queries, grad, side, keys, values):
    rows = queries.shape[0]
    ones = jnp.where(iota(values.shape, 1) < 16, 1.0, 0.0).astype(BF16)
    grad = stacked(grad)
    lane = iota(side.shape, 1)
    sides = [
        side * jnp.where((lane < 16) & (lane % 8 == 2 * pair + i), 1.0, 0.0).astype(BF16)
        for i in (0, 1)
    ]
    product = dot(
        jnp.concatenate([grad, jnp.concatenate(sides, axis=0)], axis=1),
        jnp.concatenate([values, ones], axis=1),
        1,
        1,
    )
    ds = (p.astype(F32) * product).astype(BF16)
    grad_q = unstacked(dot(ds, keys), rows) * SCALE
    return grad_q, dot(ds, stacked(queries), 0, 0), dot(p, grad, 0, 0)


PARTNER_ROWS = 112
MESSAGE_ROWS = 256 + 2 * PARTNER_ROWS


def far_back_kernel(p_in, q_all, g_in, d_side, own3, got4, third, passed, give, *refs):
    far = far_refs((own3, got4, third, passed))
    d_q, to_3, to_4, to_third, message = refs
    message[0:256] = give[...]
    to_far = ((to_3, (0, 64)), (to_4, (64, 96), to_third, (96, 112)))
    for pair in range(PAIRS):
        cols = lanes_of(pair)
        for index, ref, to in zip(FAR, far, to_far):
            level, _, rows, keys = GROUPS[index]
            at = AT[level]
            grad_q, grad_k, grad_v = attend_back(
                pair,
                p_in[pair, P_AT[index] : P_AT[index] + 2 * rows, 0:keys],
                q_all[at : at + rows, cols],
                g_in[at : at + rows, cols],
                d_side[at : at + rows],
                far_window(ref, cols),
                far_window(ref, lanes_of(pair, 1)),
            )
            d_q[at - AT[3] : at - AT[3] + rows, cols] = grad_q.astype(BF16)
            start = 0
            for out in to:
                partners = isinstance(out, tuple)
                stop = start + (out[1] - out[0] if partners else out.shape[0])
                for part, grad in enumerate((grad_k, grad_v)):
                    rows = grad[start:stop].astype(BF16)
                    if partners:
                        first = 256 + part * PARTNER_ROWS
                        message[first + out[0] : first + out[1], cols] = rows
                    else:
                        out[:, lanes_of(pair, part)] = rows
                start = stop


NEAR_PARTS = ((0,), (1,), (2,), (3,))


def near_back(pairs, p_in, q_all, g_in, d_side, own0, own1, low, high, d_far):
    spread = jnp.concatenate([spread_table(level, 0.5**level) for level in (1, 2, 3, 4)], axis=1)
    for pair in pairs:
        cols = lanes_of(pair)
        grads = []
        for index in NEAR:
            level, start, rows, keys = GROUPS[index]
            at = AT[level] + start
            grads.append(
                attend_back(
                    pair,
                    p_in[pair, P_AT[index] : P_AT[index] + 2 * rows, 0:keys],
                    q_all[at : at + rows, cols],
                    g_in[at : at + rows, cols],
                    d_side[at : at + rows],
                    near_window(index, own0, own1, low, high, cols),
                    near_window(index, own0, own1, low, high, lanes_of(pair, 1)),
                )
            )
        coarse = [x[0].astype(BF16) for x in grads[2:]] + [d_far[:, cols]]
        whole = jnp.concatenate([x[0] for x in grads[:2]], axis=0)
        d_q = (whole + dot(spread, jnp.concatenate(coarse, axis=0))).astype(BF16)
        own, to_low, to_high = [], [], []
        for part, value in ((0, 0.5), (1, 1.0)):
            a, b, c, d = (x[1 + part] for x in grads)
            middle = jnp.concatenate([a[64:128], a[128:256] + b[0:128], b[128:192]], axis=0)
            near = dot(spread_table(1, value), c[64:192].astype(BF16))
            own.append((middle + near).astype(BF16))
            to_low.append(jnp.concatenate([a[:64], c[:64], d[:64]], axis=0).astype(BF16))
            to_high.append(jnp.concatenate([b[192:], c[192:], d[64:]], axis=0).astype(BF16))
        yield pair, d_q, own, to_low, to_high


def near_back_kernel(pairs, *refs):
    inputs, outs = refs[:9], refs[-5:]
    d_q, own_k, own_v, to_low, to_high = outs
    for pair, dq, own, low, high in near_back(pairs, *inputs):
        at = slice((pair - pairs[0]) * LANES, (pair - pairs[0] + 1) * LANES)
        d_q[:, at], own_k[:, at], own_v[:, at] = dq, own[0], own[1]
        for part in range(2):
            to_low[part, :, at], to_high[part, :, at] = low[part], high[part]


def near_back_last_kernel(*refs):
    inputs, earlier = refs[:9], [refs[at : at + 2] for at in (9, 11, 13)]
    d_q, own_k, own_v, to_low, to_high = refs[-5:]
    for pairs, (low, high) in zip(NEAR_PARTS, earlier):
        for part in range(2):
            lanes = slice(
                part * WIDTH + pairs[0] * LANES, part * WIDTH + (pairs[-1] + 1) * LANES
            )
            to_low[:, lanes], to_high[:, lanes] = low[part], high[part]
    for pair, dq, own, low, high in near_back(NEAR_PARTS[-1], *inputs):
        d_q[...], own_k[...], own_v[...] = dq, own[0], own[1]
        for part in range(2):
            to_low[:, lanes_of(pair, part)] = low[part]
            to_high[:, lanes_of(pair, part)] = high[part]


def pass_on_kernel(got3, got4, third, own3, out):
    out[0:64] = got3[...]
    out[64:96] = got4[...]
    out[96:112] = third[...]
    own3[...] = jnp.where(core_index() == 0, got3[0:32], got3[32:64])


def partner_sum_kernel(to_3, to_4, to_third, keep, message, *refs):
    sum3, sum4, sum_third, keep_out, give_out, total = refs[-6:]
    even = core_index() == 0
    for part in range(2):
        lanes = slice(part * WIDTH, (part + 1) * WIDTH)
        at = 256 + part * PARTNER_ROWS
        own3 = to_3[:, lanes].astype(F32)

        def came(start, stop):
            return message[at + start : at + stop].astype(F32)

        sum3[0:32, lanes] = (came(0, 32) + jnp.where(even, own3, 0.0)).astype(BF16)
        sum3[32:64, lanes] = (came(32, 64) + jnp.where(even, 0.0, own3)).astype(BF16)
        sum4[:, lanes] = (came(64, 96) + to_4[:, lanes].astype(F32)).astype(BF16)
        sum_third[:, lanes] = (came(96, 112) + to_third[:, lanes].astype(F32)).astype(BF16)
    total[...] = keep[...] + message[0:256].astype(F32)
    halve(total, 16, keep_out, give_out)


def halve(total, divisor, keep, give):
    side = lax.axis_index("ctx") // divisor % 2
    half = total.shape[0] // 2
    keep[...] = total[pl.ds(pl.multiple_of(side * half, half), half)]
    give[...] = total[pl.ds(pl.multiple_of((1 - side) * half, half), half)].astype(BF16)


def core_rows(ref, core, rows):
    return ref[pl.ds(pl.multiple_of(core * rows, rows), rows)]


def far_split_kernel(back, give):
    give[...] = core_rows(back, 1 - core_index(), give.shape[0])


def halve_kernel(divisor, keep, got, *refs):
    keep_out, give_out, total = refs[-3:]
    total[...] = keep[...] + got[...].astype(F32)
    halve(total, divisor, keep_out, give_out)


def copies_kernel(keep, got, *refs):
    total = keep[...] + got[...].astype(F32)
    for i in range(refs[-1].shape[0]):
        refs[-1][i] = total.astype(BF16)


def last_sum_kernel(parts, _, out):
    total = parts[0].astype(F32)
    for i in range(1, parts.shape[0]):
        total = total + parts[i].astype(F32)
    out[...] = total.astype(BF16)


def project_kernel(attended, w, _, layer_hbm, finished, layer_out, sem):
    finished[...] = jnp.zeros(finished.shape, F32)
    layer_out[...] = dot(attended[...], w[...]).astype(BF16)
    copy = pltpu.make_async_copy(layer_out, layer_hbm, sem)
    copy.start()
    copy.wait()


def combine_kernel(*refs):
    own, (low, high), grads_q = (refs[0:4], refs[4:8]), refs[8:10], refs[15:19]
    back3, back4, third, swapped3, swapped4 = refs[10:15]
    d_k_hbm, d_v_hbm, d_q_hbm, finished, d_k, d_v, d_q, sems = refs[19:]
    finished[...] = jnp.zeros(finished.shape, F32)
    for pair, ref in enumerate(grads_q):
        d_q[:, lanes_of(pair)] = ref[...]
    copies = [pltpu.make_async_copy(d_q, d_q_hbm, sems.at[2])]
    copies[0].start()
    core = core_index()
    far3 = core_rows(back3, core, 32).astype(F32) + swapped3[...].astype(F32)
    far4 = core_rows(back4, core, 16).astype(F32) + swapped4[...].astype(F32)
    far4 = far4 + third[...].astype(F32)
    for part, out, out_hbm in ((0, d_k, d_k_hbm), (1, d_v, d_v_hbm)):
        lanes = slice(part * WIDTH, (part + 1) * WIDTH)
        table = jnp.concatenate(
            [spread_table(level, 1.0 if part else 0.5**level) for level in (1, 2, 3, 4)], axis=1
        )

        def rim(ref, level):
            return ref[BLOCK * level : BLOCK * (level + 1), lanes].astype(F32)

        coarse = jnp.concatenate(
            [
                rim(high, 1),
                rim(low, 1),
                rim(low, 2) + rim(high, 2),
                far3[:, lanes],
                far4[:, lanes],
            ],
            axis=0,
        ).astype(BF16)
        whole = jnp.concatenate([x[...] for x in own[part]], axis=1).astype(F32)
        whole = whole + dot(table, coarse)
        out[0:64] = (whole[0:64] + rim(high, 0)).astype(BF16)
        out[64:192] = whole[64:192].astype(BF16)
        out[192:256] = (whole[192:256] + rim(low, 0)).astype(BF16)
        copies.append(pltpu.make_async_copy(out, out_hbm, sems.at[part]))
        copies[-1].start()
    for copy in copies:
        copy.wait()


def call(
    kernel, name, outs, args, scratch=(), in_hbm=0, microseconds=1.0, to_hbm=()
):
    vmem, hbm = pl.BlockSpec(memory_space=pltpu.VMEM), pl.BlockSpec(memory_space=pl.ANY)
    return pl.pallas_call(
        kernel,
        name=name,
        out_shape=[jax.ShapeDtypeStruct(shape, dtype) for shape, dtype in outs],
        in_specs=[vmem] * (len(args) - in_hbm) + [hbm] * in_hbm,
        out_specs=[hbm if i in to_hbm else vmem for i in range(len(outs))],
        scratch_shapes=scratch,
        cost_estimate=pl.CostEstimate(
            flops=int(microseconds * 1e9), bytes_accessed=1 << 20, transcendentals=0
        ),
        compiler_params=pltpu.CompilerParams(vmem_limit_bytes=VMEM_MIB * 1024 * 1024),
    )(*args)


def moved(x, route):
    count = lax.axis_size("ctx")
    return lax.ppermute(x, "ctx", [(i, route(i) % count) for i in range(count)])


def partner(i):
    return i ^ 1


def third(i):
    return i - 6 if i // 2 % 2 else i + 6


def route_3(i):
    return i - 2 if i % 2 else i + 2


def route_4(i):
    return i - 4 if i % 2 else i + 4


def back_3(i):
    return i + 2 if i % 2 else i - 2


def back_4(i):
    return i + 4 if i % 2 else i - 4


def body(queries, key_rows, value_rows, segment_ids, w_out, d_out):
    q, k, v, grad_out = queries[0], key_rows[0], value_rows[0], d_out[0]
    tokens, dma = (ROWS, WIDTH), pltpu.SemaphoreType.DMA
    qdoc = call(
        documents_kernel,
        "documents",
        [((ALL_ROWS, LANES), BF16)],
        [segment_ids],
        [pltpu.VMEM((1, ROWS), jnp.int32), dma(())],
        in_hbm=1,
    )[0]
    up, down, far, third_rows, own0, own1 = call(
        coarsen_kernel,
        "coarsen",
        [((192, PACK), BF16), ((192, PACK), BF16), ((48, PACK), BF16), ((16, PACK), BF16)]
        + [((ROWS, PACK), BF16), ((128, PACK), BF16)],
        [qdoc, k, v],
        [pltpu.VMEM(tokens, BF16)] * 2 + [dma((2,))],
        in_hbm=2,
    )
    far_partner = moved(far, partner)
    far3, far4 = call(
        pair_kernel, "pair", [((64, PACK), BF16), ((32, PACK), BF16)], [far, far_partner]
    )
    q_all, grad_att, w, grad_rows = call(
        prepare_kernel,
        "prepare",
        [((ALL_ROWS, WIDTH), BF16), (tokens, F32), ((WIDTH, WIDTH), BF16), (tokens, BF16)],
        [q, grad_out, w_out],
        [pltpu.VMEM(tokens, BF16), dma((3,))],
        in_hbm=3,
    )
    low = moved(up, lambda i: i + 1)
    high = moved(down, lambda i: i - 1)
    got3 = moved(far3, route_3)
    got4 = moved(far4, route_4)
    got_third = moved(third_rows, third)
    low, high, got3 = lax.optimization_barrier((low, high, got3))
    own3, passed = call(
        pass_on_kernel,
        "pass_on",
        [((32, PACK), BF16), ((112, PACK), BF16)],
        [got3, got4, got_third],
    )
    far = (own3, got4, got_third, moved(passed, partner))
    near = (own0, own1, low, high)
    p_near, *near_sums = call(
        near_kernel,
        "near",
        [((PAIRS, P_NEAR, 256), BF16), (tokens, F32), ((ROWS, 2 * LANES), F32)]
        + [((192, WIDTH), BF16), ((192, 2 * LANES), BF16)],
        [q_all, qdoc, *near],
        microseconds=50,
    )
    attended, keep, give, p_far, g, d_side = call(
        merge_kernel,
        "merge",
        [(tokens, BF16), ((256, WIDTH), F32), ((256, WIDTH), BF16)]
        + [((PAIRS, P_FAR, LANES), BF16)]
        + [((ALL_ROWS, WIDTH), BF16), ((ALL_ROWS, LANES), BF16)],
        [q_all, qdoc, *near_sums, grad_att, grad_rows, *far],
        [pltpu.VMEM((WIDTH, WIDTH), F32)],
        microseconds=6,
    )

    def halved(keep, got, divisor, route, *after):
        rows = keep.shape[0] // 2
        keep, give = call(
            functools.partial(halve_kernel, divisor),
            "halve_" + str(rows),
            [((rows, WIDTH), F32), ((rows, WIDTH), BF16)],
            [keep, got, *after],
            [pltpu.VMEM((2 * rows, WIDTH), F32)],
            in_hbm=len(after),
        )
        return keep, moved(give, route)

    d_far, *to_far, message = call(
        far_back_kernel,
        "far_back",
        [((48, WIDTH), BF16), ((32, 2 * WIDTH), BF16), ((32, 2 * WIDTH), BF16)]
        + [((16, 2 * WIDTH), BF16), ((MESSAGE_ROWS, WIDTH), BF16)],
        [p_far, q_all, g, d_side, *far, give],
    )
    message = moved(message, partner)

    def part_outs(part):
        width = len(NEAR_PARTS[part]) * LANES
        return [((ROWS, width), BF16)] * 3 + [((2, 192, width), BF16)] * 2

    args = [p_near, q_all, g, d_side, *near, d_far]
    part_a = call(
        functools.partial(near_back_kernel, NEAR_PARTS[0]),
        "near_back_a",
        part_outs(0),
        args,
        microseconds=3,
    )
    sum3, sum4, sum_third, keep, give = call(
        partner_sum_kernel,
        "partner_sum",
        [((64, 2 * WIDTH), BF16), ((32, 2 * WIDTH), BF16), ((16, 2 * WIDTH), BF16)]
        + [((128, WIDTH), F32), ((128, WIDTH), BF16)],
        [*to_far, keep, message, part_a[0]],
        [pltpu.VMEM((256, WIDTH), F32)],
        in_hbm=1,
    )
    got_w = moved(give, lambda i: i ^ 24)
    back3 = moved(sum3, back_3)
    layer_out, projected = call(
        project_kernel,
        "project",
        [(tokens, BF16), ((8, LANES), F32)],
        [attended, w, sum3],
        [pltpu.VMEM(tokens, BF16), dma(())],
        in_hbm=1,
        to_hbm=(0,),
    )
    keep, got_w = halved(keep, got_w, 8, lambda i: i ^ 8, projected)
    part_b = call(
        functools.partial(near_back_kernel, NEAR_PARTS[1]),
        "near_back_b",
        part_outs(1),
        [*args, part_a[0], keep],
        in_hbm=2,
        microseconds=3,
    )
    keep, got_w = halved(keep, got_w, 4, lambda i: i ^ 6, part_b[0])
    part_c = call(
        functools.partial(near_back_kernel, NEAR_PARTS[2]),
        "near_back_c",
        part_outs(2),
        [*args, part_b[0], keep],
        in_hbm=2,
        microseconds=3,
    )
    keep, got_w = halved(keep, got_w, 2, lambda i: i ^ 2, part_c[0])
    give = call(far_split_kernel, "split_3", [((32, 2 * WIDTH), BF16)], [back3])[0]
    swapped3 = moved(give, partner)
    d_q, own_k, own_v, to_low, to_high = call(
        near_back_last_kernel,
        "near_back_d",
        part_outs(3)[:3] + [((192, 2 * WIDTH), BF16)] * 2,
        [*args, *part_a[3:], *part_b[3:], *part_c[3:], keep, give],
        in_hbm=2,
        microseconds=3,
    )
    to_low, to_high, got_w = lax.optimization_barrier((to_low, to_high, got_w))
    low_back = moved(to_low, lambda i: i - 1)
    high_back = moved(to_high, lambda i: i + 1)
    copies = call(
        copies_kernel,
        "copies",
        [((lax.axis_size("dp"), 16, WIDTH), BF16)],
        [keep, got_w],
    )[0]
    sum4, sum_third, copies = lax.optimization_barrier((sum4, sum_third, copies))
    copies = lax.all_to_all(copies, "dp", 0, 0, tiled=True)
    back4 = moved(sum4, back_4)
    back_third = moved(sum_third, third)
    give = call(far_split_kernel, "split_4", [((16, 2 * WIDTH), BF16)], [back4])[0]
    swapped4 = moved(give, partner)
    d_k, d_v, d_q, finished = call(
        combine_kernel,
        "combine",
        [(tokens, BF16)] * 3 + [((8, LANES), F32)],
        [part_a[1], part_b[1], part_c[1], own_k, part_a[2], part_b[2], part_c[2], own_v]
        + [low_back, high_back, back3, back4, back_third, swapped3, swapped4]
        + [part_a[0], part_b[0], part_c[0], d_q],
        [pltpu.VMEM(tokens, BF16)] * 3 + [dma((3,))],
        to_hbm=(0, 1, 2),
    )
    d_w = call(last_sum_kernel, "last_sum", [((16, WIDTH), BF16)], [copies, finished], in_hbm=1)[0]
    return layer_out[None], d_q[None], d_k[None], d_v[None], d_w


def solution(mesh):
    tokens = P("dp", "ctx", None)
    return jax.shard_map(
        body,
        mesh=mesh,
        in_specs=(tokens, tokens, tokens, P("dp", "ctx"), P(), tokens),
        out_specs=(tokens, tokens, tokens, tokens, P("ctx", None)),
        check_vma=False,
    )
```

```python
import functools

import jax
import jax.numpy as jnp
from jax import lax
from jax.experimental import pallas as pl
from jax.experimental.pallas import tpu as pltpu
from jax.sharding import PartitionSpec as P

HEAD_DIM = 64
BLOCK = 64
HALF = 32
LEVELS = 4
ROWS = 256
WIDTH = 512
PAIRS = 4
LANES = 128
DOCS = 4
NEGATIVE = -1e30
BLOCKED = -2e30
SCALE = HEAD_DIM**-0.5
PACK = 2 * WIDTH + LANES
COUNT = (256, 128, 64, 32, 16)
AT = (0, 256, 384, 448, 480)
ALL_ROWS = 496
F32 = jnp.float32
BF16 = jnp.bfloat16
VMEM_MIB = 20

GROUPS = (
    (0, 0, 128, 256),
    (0, 128, 128, 256),
    (1, 0, 128, 256),
    (2, 0, 64, 128),
    (3, 0, 32, 96),
    (4, 0, 16, 96),
)
NEAR = (0, 1, 2, 3)
FAR = (4, 5)
P_AT = {0: 0, 1: 256, 2: 512, 3: 768, 4: 0, 5: 64}
P_NEAR, P_FAR = 896, 96


def iota(shape, dim):
    return lax.broadcasted_iota(jnp.int32, shape, dim)


def gather_table(level, value=1.0):
    shape = (COUNT[level], ROWS)
    return jnp.where(iota(shape, 1) // 2**level == iota(shape, 0), value, 0.0).astype(BF16)


def spread_table(level, value=1.0):
    shape = (ROWS, COUNT[level])
    return jnp.where(iota(shape, 0) // 2**level == iota(shape, 1), value, 0.0).astype(BF16)


def last_table(level):
    shape = (COUNT[level], ROWS)
    last = iota(shape, 0) * 2**level + (2**level - 1)
    return jnp.where(iota(shape, 1) == last, 1.0, 0.0).astype(BF16)


def query_place(index):
    level, _, rows, _ = GROUPS[index]
    size = BLOCK if level == 0 else HALF
    shape = (rows, LANES)
    return jnp.where(iota(shape, 0) // size + 8 == iota(shape, 1), 1.0, 0.0).astype(BF16)


def key_place(index):
    level, _, _, keys = GROUPS[index]
    shape = (keys, LANES)
    row, place = iota(shape, 0), iota(shape, 1) - 8
    if level == 0:
        apart = row // BLOCK - place
        blocked = (apart < 0) | (apart > 2)
        places = 2
    elif level == 1:
        there, here = row // HALF, place + 2
        block_apart = jnp.abs(there // 2 - (place + 2) // 2)
        blocked = (block_apart > 1) | (jnp.abs(there - here) < 2)
        places = 4
    else:
        blocked = row // HALF == place + 1
        places = 2
    blocked = blocked & (place >= 0) & (place < places)
    return jnp.where(blocked, BLOCKED, 0.0).astype(BF16)


def dot(a, b, a_dim=1, b_dim=0):
    return lax.dot_general(a, b, (((a_dim,), (b_dim,)), ((), ())), preferred_element_type=F32)


def split(x):
    high = x.astype(BF16)
    return high, (x - high.astype(F32)).astype(BF16)


def head_lanes(rows, width=LANES):
    return iota((rows, width), 1) % LANES < HEAD_DIM


def stacked(x):
    first = head_lanes(x.shape[0]).astype(F32).astype(BF16)
    return jnp.concatenate([x * first, x * (1 - first)], axis=0)


def unstacked(x, rows):
    return jnp.where(head_lanes(rows, x.shape[1]), x[:rows], x[rows:])


def lanes_of(pair, part=0):
    return slice(part * WIDTH + pair * LANES, part * WIDTH + (pair + 1) * LANES)


DOC_LANES = slice(2 * WIDTH, PACK)


def near_window(index, own0, own1, low, high, lanes):
    def rim(ref, level):
        return ref[BLOCK * level : BLOCK * (level + 1), lanes]

    if index == 0:
        parts = [rim(low, 0), own0[0:192, lanes]]
    elif index == 1:
        parts = [own0[64:256, lanes], rim(high, 0)]
    elif index == 2:
        parts = [rim(low, 1), own1[:, lanes], rim(high, 1)]
    else:
        parts = [rim(low, 2), rim(high, 2)]
    return jnp.concatenate(parts, axis=0)


def far_window(refs, lanes):
    return jnp.concatenate([ref[:, lanes] for ref in refs], axis=0)


def fetch(sources, targets, sems):
    copies = [
        pltpu.make_async_copy(source, target, sems.at[i])
        for i, (source, target) in enumerate(zip(sources, targets))
    ]
    for copy in copies:
        copy.start()
    return copies


def documents_kernel(seg_hbm, qdoc, seg, sem):
    copy = pltpu.make_async_copy(seg_hbm, seg, sem)
    copy.start()
    copy.wait()
    marks = jnp.where(seg[...] == iota((LANES, ROWS), 0), 1.0, 0.0).T.astype(BF16)
    qdoc[0:ROWS] = marks
    for level in range(1, LEVELS + 1):
        marks_c = dot(last_table(level), marks).astype(BF16)
        qdoc[AT[level] : AT[level] + COUNT[level]] = marks_c


def coarsen_kernel(qdoc, k_hbm, v_hbm, up, down, far, third, own0, own1, k, v, sems):
    copies = fetch((k_hbm, v_hbm), (k, v), sems)
    doc = iota((ALL_ROWS, LANES), 1) < DOCS
    docs = jnp.where(doc, (1.0 - qdoc[...].astype(F32)) * BLOCKED, 0.0).astype(BF16)
    copies[0].wait()
    copies[1].wait()
    levels = [(k[...], v[...], docs[0:ROWS])]
    for level in range(1, LEVELS + 1):
        keys = dot(gather_table(level, 0.5**level), levels[0][0]).astype(BF16)
        values = dot(gather_table(level), levels[0][1]).astype(BF16)
        levels.append((keys, values, docs[AT[level] : AT[level] + COUNT[level]]))

    def put(ref, at, level, start, stop):
        for part, lanes in zip(
            levels[level], (slice(0, WIDTH), slice(WIDTH, 2 * WIDTH), DOC_LANES)
        ):
            ref[at : at + stop - start, lanes] = part[start:stop]

    for level in range(3):
        put(up, BLOCK * level, level, COUNT[level] - BLOCK, COUNT[level])
        put(down, BLOCK * level, level, 0, BLOCK)
    put(far, 0, 3, 0, COUNT[3])
    put(far, COUNT[3], 4, 0, COUNT[4])
    put(third, 0, 4, 0, COUNT[4])
    put(own0, 0, 0, 0, COUNT[0])
    put(own1, 0, 1, 0, COUNT[1])


def core_index():
    return lax.axis_index("ctx") % 2


def pair_kernel(far, far_partner, far3, far4):
    even = core_index() == 0
    for out, start, rows in ((far3, 0, 32), (far4, 32, 16)):
        own, other = far[start : start + rows], far_partner[start : start + rows]
        out[0:rows] = jnp.where(even, own, other)
        out[rows : 2 * rows] = jnp.where(even, other, own)


def prepare_kernel(q_hbm, d_hbm, w_hbm, q_out, grad_att, w, d_out, q, sems):
    copies = fetch((q_hbm, d_hbm, w_hbm), (q, d_out, w), sems)
    copies[0].wait()
    for level in range(LEVELS + 1):
        queries = q[...] if level == 0 else dot(gather_table(level, 0.5**level), q[...]).astype(BF16)
        q_out[AT[level] : AT[level] + COUNT[level]] = (queries * SCALE).astype(BF16)
    copies[1].wait()
    copies[2].wait()
    grad_att[...] = dot(d_out[...], w[...], 1, 1)


def attend(queries, query_docs, keys, key_docs, values):
    rows = queries.shape[0]
    scores = dot(
        jnp.concatenate([stacked(queries), query_docs], axis=1),
        jnp.concatenate([keys, key_docs], axis=1),
        1,
        1,
    )
    peak = jnp.maximum(jnp.max(scores, axis=1, keepdims=True), NEGATIVE)
    peak = peak.astype(BF16).astype(F32)
    p = jnp.exp(scores - peak).astype(BF16)
    ones = jnp.ones(values.shape, BF16)
    both = dot(p, jnp.concatenate([values, ones], axis=1))
    return p, unstacked(both[:, :LANES], rows), both[:, LANES:], peak


def with_stats(stats, pair, sums, peak):
    rows = sums.shape[0] // 2
    lane = iota((rows, LANES), 1)
    result = []
    for old, new in zip(stats, (sums, peak)):
        old = jnp.where(lane == 2 * pair, new[:rows], old)
        result.append(jnp.where(lane == 2 * pair + 1, new[rows:], old))
    return result


def no_stats(rows):
    return [jnp.zeros((rows, LANES), F32)] * 2


def head_spread(pair):
    shape = (2 * LANES, LANES)
    head = iota(shape, 0) % LANES
    return jnp.where(head == 2 * pair + iota(shape, 1) // HEAD_DIM, 1.0, 0.0).astype(BF16)


def head_sum(pair):
    shape = (2 * LANES, LANES)
    head = 2 * pair + iota(shape, 0) % LANES // HEAD_DIM
    return jnp.where(head == iota(shape, 1), 1.0, 0.0).astype(BF16)


def both_parts(x):
    return jnp.concatenate(split(x), axis=1)


def docs_of(index, qdoc):
    level, start, rows, _ = GROUPS[index]
    docs = qdoc[AT[level] + start : AT[level] + start + rows]
    if index in NEAR:
        docs = docs + query_place(index)
    return jnp.concatenate([docs, docs], axis=0)


def near_kernel(q_all, qdoc, own0, own1, low, high, p_out, fine, fine_stats, coarse, coarse_stats):
    for index in NEAR:
        level, start, rows, keys = GROUPS[index]
        at = AT[level] + start
        query_docs = docs_of(index, qdoc)
        key_docs = near_window(index, own0, own1, low, high, DOC_LANES) + key_place(index)
        stats = no_stats(rows)
        for pair in range(PAIRS):
            window = [
                near_window(index, own0, own1, low, high, lanes_of(pair, part)) for part in (0, 1)
            ]
            p, numer, sums, peak = attend(
                q_all[at : at + rows, lanes_of(pair)], query_docs, window[0], key_docs, window[1]
            )
            stats = with_stats(stats, pair, sums, peak)
            p_out[pair, P_AT[index] : P_AT[index] + 2 * rows, 0:keys] = p
            if level == 0:
                fine[at : at + rows, lanes_of(pair)] = numer
            else:
                coarse[at - ROWS : at - ROWS + rows, lanes_of(pair)] = numer.astype(BF16)
        if level == 0:
            fine_stats[at : at + rows] = jnp.concatenate(stats, axis=1)
        else:
            coarse_stats[at - ROWS : at - ROWS + rows] = jnp.concatenate(stats, axis=1).astype(BF16)


def far_refs(refs):
    own3, got4, third, passed = refs
    return (
        (own3, passed.at[0:64]),
        (got4, passed.at[64:96], third, passed.at[96:112]),
    )


def block_at(block):
    x, y, core = block // 8, block // 2 % 4, block % 2
    return 16 * (16 * core + 4 * (0, 2, 3, 1)[x] + y)


def merge_kernel(
    q_all, qdoc, fine, fine_stats, coarse, coarse_stats, grad_att, d_out, *refs
):
    far = far_refs(refs[:4])
    attended_out, keep, give, p_out, g_out, d_side, d_w = refs[4:]
    spreads = [None] + [spread_table(level) for level in range(1, LEVELS + 1)]
    gathers = [None] + [gather_table(level) for level in range(1, LEVELS + 1)]
    numers, stats = [None, coarse[0:128], coarse[128:192]], [None, coarse_stats[0:128]]
    stats.append(coarse_stats[128:192])
    for index, ref in zip(FAR, far):
        level, _, rows, keys = GROUPS[index]
        query_docs, key_docs = docs_of(index, qdoc), far_window(ref, DOC_LANES)
        own_stats, own_numers = no_stats(rows), []
        for pair in range(PAIRS):
            p, numer, sums, peak = attend(
                q_all[AT[level] : AT[level] + rows, lanes_of(pair)],
                query_docs,
                far_window(ref, lanes_of(pair)),
                key_docs,
                far_window(ref, lanes_of(pair, 1)),
            )
            own_stats = with_stats(own_stats, pair, sums, peak)
            own_numers.append(numer.astype(BF16))
            p_out[pair, P_AT[index] : P_AT[index] + 2 * rows, 0:keys] = p
        numers.append(jnp.concatenate(own_numers, axis=1))
        stats.append(jnp.concatenate(own_stats, axis=1).astype(BF16))
    wide = [fine_stats[...]] + [
        dot(spreads[level], stats[level]) for level in range(1, LEVELS + 1)
    ]
    sums, peaks = [x[:, :LANES] for x in wide], [x[:, LANES:] for x in wide]
    top = functools.reduce(jnp.maximum, peaks)
    weights = [jnp.exp(x - top) for x in peaks]
    norm = functools.reduce(
        jnp.add, [wt * x * float(2**i) for i, (wt, x) in enumerate(zip(weights, sums))]
    )
    inverse = 1.0 / jnp.where(iota(norm.shape, 1) < 2 * PAIRS, norm, 1.0)
    shares = [wt * inverse for wt in weights]
    share_parts = [both_parts(x) for x in shares]
    delta = jnp.zeros((ROWS, LANES), F32)
    for pair in range(PAIRS):
        cols = lanes_of(pair)
        to_lanes = head_spread(pair)
        wide_shares = [dot(x, to_lanes) for x in share_parts]
        numer = wide_shares[0] * fine[:, cols]
        for level in range(1, LEVELS + 1):
            numer = numer + wide_shares[level] * dot(spreads[level], numers[level][:, cols])
        attended = numer.astype(BF16)
        attended_out[:, cols] = attended
        grad_w = dot(attended, d_out[...], 0, 0)
        for block in range(8):
            at = block_at(8 * pair + block)
            d_w[at : at + 16] = grad_w[16 * block : 16 * (block + 1)]
        grad = grad_att[:, cols]
        delta = delta + dot(both_parts(grad * attended.astype(F32)), head_sum(pair))
        for level in range(LEVELS + 1):
            rows = (wide_shares[level] * grad).astype(BF16)
            if level > 0:
                rows = dot(gathers[level], rows).astype(BF16)
            g_out[AT[level] : AT[level] + COUNT[level], cols] = rows
    core = core_index()
    keep[...] = d_w[pl.ds(pl.multiple_of(core * 256, 256), 256)]
    give[...] = d_w[pl.ds(pl.multiple_of((1 - core) * 256, 256), 256)].astype(BF16)
    shape = (2 * LANES, LANES)
    part, head = iota(shape, 0) // LANES, iota(shape, 0) % LANES
    place = jnp.where((head < 8) & (iota(shape, 1) == 8 * part + head), 1.0, 0.0).astype(BF16)
    for level in range(LEVELS + 1):
        delta_c = shares[level] * delta
        if level > 0:
            summed = dot(gathers[level], both_parts(delta_c))
            delta_c = summed[:, :LANES] + summed[:, LANES:]
        terms = dot(both_parts(delta_c * -float(2**level)), place)
        d_side[AT[level] : AT[level] + COUNT[level]] = terms.astype(BF16)


def attend_back(pair, p, queries, grad, side, keys, values):
    rows = queries.shape[0]
    ones = jnp.where(iota(values.shape, 1) < 16, 1.0, 0.0).astype(BF16)
    grad = stacked(grad)
    lane = iota(side.shape, 1)
    sides = [
        side * jnp.where((lane < 16) & (lane % 8 == 2 * pair + i), 1.0, 0.0).astype(BF16)
        for i in (0, 1)
    ]
    product = dot(
        jnp.concatenate([grad, jnp.concatenate(sides, axis=0)], axis=1),
        jnp.concatenate([values, ones], axis=1),
        1,
        1,
    )
    ds = (p.astype(F32) * product).astype(BF16)
    grad_q = unstacked(dot(ds, keys), rows) * SCALE
    return grad_q, dot(ds, stacked(queries), 0, 0), dot(p, grad, 0, 0)


PARTNER_ROWS = 112
MESSAGE_ROWS = 256 + 2 * PARTNER_ROWS


def far_back_kernel(p_in, q_all, g_in, d_side, own3, got4, third, passed, give, *refs):
    far = far_refs((own3, got4, third, passed))
    d_q, to_3, to_4, to_third, message = refs
    message[0:256] = give[...]
    to_far = ((to_3, (0, 64)), (to_4, (64, 96), to_third, (96, 112)))
    for pair in range(PAIRS):
        cols = lanes_of(pair)
        for index, ref, to in zip(FAR, far, to_far):
            level, _, rows, keys = GROUPS[index]
            at = AT[level]
            grad_q, grad_k, grad_v = attend_back(
                pair,
                p_in[pair, P_AT[index] : P_AT[index] + 2 * rows, 0:keys],
                q_all[at : at + rows, cols],
                g_in[at : at + rows, cols],
                d_side[at : at + rows],
                far_window(ref, cols),
                far_window(ref, lanes_of(pair, 1)),
            )
            d_q[at - AT[3] : at - AT[3] + rows, cols] = grad_q.astype(BF16)
            start = 0
            for out in to:
                partners = isinstance(out, tuple)
                stop = start + (out[1] - out[0] if partners else out.shape[0])
                for part, grad in enumerate((grad_k, grad_v)):
                    rows = grad[start:stop].astype(BF16)
                    if partners:
                        first = 256 + part * PARTNER_ROWS
                        message[first + out[0] : first + out[1], cols] = rows
                    else:
                        out[:, lanes_of(pair, part)] = rows
                start = stop


NEAR_PARTS = ((0,), (1,), (2,), (3,))


def near_back(pairs, p_in, q_all, g_in, d_side, own0, own1, low, high, d_far):
    spread = jnp.concatenate([spread_table(level, 0.5**level) for level in (1, 2, 3, 4)], axis=1)
    for pair in pairs:
        cols = lanes_of(pair)
        grads = []
        for index in NEAR:
            level, start, rows, keys = GROUPS[index]
            at = AT[level] + start
            grads.append(
                attend_back(
                    pair,
                    p_in[pair, P_AT[index] : P_AT[index] + 2 * rows, 0:keys],
                    q_all[at : at + rows, cols],
                    g_in[at : at + rows, cols],
                    d_side[at : at + rows],
                    near_window(index, own0, own1, low, high, cols),
                    near_window(index, own0, own1, low, high, lanes_of(pair, 1)),
                )
            )
        coarse = [x[0].astype(BF16) for x in grads[2:]] + [d_far[:, cols]]
        whole = jnp.concatenate([x[0] for x in grads[:2]], axis=0)
        d_q = (whole + dot(spread, jnp.concatenate(coarse, axis=0))).astype(BF16)
        own, to_low, to_high = [], [], []
        for part, value in ((0, 0.5), (1, 1.0)):
            a, b, c, d = (x[1 + part] for x in grads)
            middle = jnp.concatenate([a[64:128], a[128:256] + b[0:128], b[128:192]], axis=0)
            near = dot(spread_table(1, value), c[64:192].astype(BF16))
            own.append((middle + near).astype(BF16))
            to_low.append(jnp.concatenate([a[:64], c[:64], d[:64]], axis=0).astype(BF16))
            to_high.append(jnp.concatenate([b[192:], c[192:], d[64:]], axis=0).astype(BF16))
        yield pair, d_q, own, to_low, to_high


def near_back_kernel(pairs, *refs):
    inputs, outs = refs[:9], refs[-5:]
    d_q, own_k, own_v, to_low, to_high = outs
    for pair, dq, own, low, high in near_back(pairs, *inputs):
        at = slice((pair - pairs[0]) * LANES, (pair - pairs[0] + 1) * LANES)
        d_q[:, at], own_k[:, at], own_v[:, at] = dq, own[0], own[1]
        for part in range(2):
            to_low[part, :, at], to_high[part, :, at] = low[part], high[part]


def near_back_last_kernel(*refs):
    inputs, earlier = refs[:9], [refs[at : at + 2] for at in (9, 11, 13)]
    d_q, own_k, own_v, to_low, to_high = refs[-5:]
    for pairs, (low, high) in zip(NEAR_PARTS, earlier):
        for part in range(2):
            lanes = slice(
                part * WIDTH + pairs[0] * LANES, part * WIDTH + (pairs[-1] + 1) * LANES
            )
            to_low[:, lanes], to_high[:, lanes] = low[part], high[part]
    for pair, dq, own, low, high in near_back(NEAR_PARTS[-1], *inputs):
        d_q[...], own_k[...], own_v[...] = dq, own[0], own[1]
        for part in range(2):
            to_low[:, lanes_of(pair, part)] = low[part]
            to_high[:, lanes_of(pair, part)] = high[part]


def pass_on_kernel(got3, got4, third, own3, out):
    out[0:64] = got3[...]
    out[64:96] = got4[...]
    out[96:112] = third[...]
    own3[...] = jnp.where(core_index() == 0, got3[0:32], got3[32:64])


def partner_sum_kernel(to_3, to_4, to_third, keep, message, *refs):
    sum3, sum4, sum_third, keep_out, give_out, total = refs[-6:]
    even = core_index() == 0
    for part in range(2):
        lanes = slice(part * WIDTH, (part + 1) * WIDTH)
        at = 256 + part * PARTNER_ROWS
        own3 = to_3[:, lanes].astype(F32)

        def came(start, stop):
            return message[at + start : at + stop].astype(F32)

        sum3[0:32, lanes] = (came(0, 32) + jnp.where(even, own3, 0.0)).astype(BF16)
        sum3[32:64, lanes] = (came(32, 64) + jnp.where(even, 0.0, own3)).astype(BF16)
        sum4[:, lanes] = (came(64, 96) + to_4[:, lanes].astype(F32)).astype(BF16)
        sum_third[:, lanes] = (came(96, 112) + to_third[:, lanes].astype(F32)).astype(BF16)
    total[...] = keep[...] + message[0:256].astype(F32)
    halve(total, (8, 16), keep_out, give_out)


def halve(total, divisors, keep, give):
    index = lax.axis_index("ctx")
    side = sum(index // divisor for divisor in divisors) % 2
    half = total.shape[0] // 2
    keep[...] = total[pl.ds(pl.multiple_of(side * half, half), half)]
    give[...] = total[pl.ds(pl.multiple_of((1 - side) * half, half), half)].astype(BF16)


def core_rows(ref, core, rows):
    return ref[pl.ds(pl.multiple_of(core * rows, rows), rows)]


def far_split_kernel(back3, back4, give):
    other = 1 - core_index()
    give[0:32] = core_rows(back3, other, 32)
    give[32:48] = core_rows(back4, other, 16)


def halve_kernel(divisor, keep, got, *refs):
    keep_out, give_out, total = refs[-3:]
    total[...] = keep[...] + got[...].astype(F32)
    halve(total, (divisor,), keep_out, give_out)


def copies_kernel(keep, got, *refs):
    total = keep[...] + got[...].astype(F32)
    for i in range(refs[-1].shape[0]):
        refs[-1][i] = total.astype(BF16)


def last_sum_kernel(parts, _, out):
    total = parts[0].astype(F32)
    for i in range(1, parts.shape[0]):
        total = total + parts[i].astype(F32)
    out[...] = total.astype(BF16)


def project_kernel(attended, w, _, layer_hbm, finished, layer_out, sem):
    finished[...] = jnp.zeros(finished.shape, F32)
    layer_out[...] = dot(attended[...], w[...]).astype(BF16)
    copy = pltpu.make_async_copy(layer_out, layer_hbm, sem)
    copy.start()
    copy.wait()


def combine_kernel(*refs):
    own, (low, high), grads_q = (refs[0:4], refs[4:8]), refs[8:10], refs[14:18]
    back3, back4, third, swapped = refs[10:14]
    d_k_hbm, d_v_hbm, d_q_hbm, finished, d_k, d_v, d_q, sems = refs[18:]
    finished[...] = jnp.zeros(finished.shape, F32)
    for pair, ref in enumerate(grads_q):
        d_q[:, lanes_of(pair)] = ref[...]
    copies = [pltpu.make_async_copy(d_q, d_q_hbm, sems.at[2])]
    copies[0].start()
    core = core_index()
    far3 = core_rows(back3, core, 32).astype(F32) + swapped[0:32].astype(F32)
    far4 = core_rows(back4, core, 16).astype(F32) + swapped[32:48].astype(F32)
    far4 = far4 + third[...].astype(F32)
    for part, out, out_hbm in ((0, d_k, d_k_hbm), (1, d_v, d_v_hbm)):
        lanes = slice(part * WIDTH, (part + 1) * WIDTH)
        table = jnp.concatenate(
            [spread_table(level, 1.0 if part else 0.5**level) for level in (1, 2, 3, 4)], axis=1
        )

        def rim(ref, level):
            return ref[BLOCK * level : BLOCK * (level + 1), lanes].astype(F32)

        coarse = jnp.concatenate(
            [
                rim(high, 1),
                rim(low, 1),
                rim(low, 2) + rim(high, 2),
                far3[:, lanes],
                far4[:, lanes],
            ],
            axis=0,
        ).astype(BF16)
        whole = jnp.concatenate([x[...] for x in own[part]], axis=1).astype(F32)
        whole = whole + dot(table, coarse)
        out[0:64] = (whole[0:64] + rim(high, 0)).astype(BF16)
        out[64:192] = whole[64:192].astype(BF16)
        out[192:256] = (whole[192:256] + rim(low, 0)).astype(BF16)
        copies.append(pltpu.make_async_copy(out, out_hbm, sems.at[part]))
        copies[-1].start()
    for copy in copies:
        copy.wait()


def call(
    kernel, name, outs, args, scratch=(), in_hbm=0, microseconds=1.0, to_hbm=()
):
    vmem, hbm = pl.BlockSpec(memory_space=pltpu.VMEM), pl.BlockSpec(memory_space=pl.ANY)
    return pl.pallas_call(
        kernel,
        name=name,
        out_shape=[jax.ShapeDtypeStruct(shape, dtype) for shape, dtype in outs],
        in_specs=[vmem] * (len(args) - in_hbm) + [hbm] * in_hbm,
        out_specs=[hbm if i in to_hbm else vmem for i in range(len(outs))],
        scratch_shapes=scratch,
        cost_estimate=pl.CostEstimate(
            flops=int(microseconds * 1e9), bytes_accessed=1 << 20, transcendentals=0
        ),
        compiler_params=pltpu.CompilerParams(vmem_limit_bytes=VMEM_MIB * 1024 * 1024),
    )(*args)


def moved(x, route):
    count = lax.axis_size("ctx")
    return lax.ppermute(x, "ctx", [(i, route(i) % count) for i in range(count)])


def partner(i):
    return i ^ 1


def third(i):
    return i - 6 if i // 2 % 2 else i + 6


def route_3(i):
    return i - 2 if i % 2 else i + 2


def route_4(i):
    return i - 4 if i % 2 else i + 4


def back_3(i):
    return i + 2 if i % 2 else i - 2


def back_4(i):
    return i + 4 if i % 2 else i - 4


def body(queries, key_rows, value_rows, segment_ids, w_out, d_out):
    q, k, v, grad_out = queries[0], key_rows[0], value_rows[0], d_out[0]
    tokens, dma = (ROWS, WIDTH), pltpu.SemaphoreType.DMA
    qdoc = call(
        documents_kernel,
        "documents",
        [((ALL_ROWS, LANES), BF16)],
        [segment_ids],
        [pltpu.VMEM((1, ROWS), jnp.int32), dma(())],
        in_hbm=1,
    )[0]
    up, down, far, third_rows, own0, own1 = call(
        coarsen_kernel,
        "coarsen",
        [((192, PACK), BF16), ((192, PACK), BF16), ((48, PACK), BF16), ((16, PACK), BF16)]
        + [((ROWS, PACK), BF16), ((128, PACK), BF16)],
        [qdoc, k, v],
        [pltpu.VMEM(tokens, BF16)] * 2 + [dma((2,))],
        in_hbm=2,
    )
    far_partner = moved(far, partner)
    far3, far4 = call(
        pair_kernel, "pair", [((64, PACK), BF16), ((32, PACK), BF16)], [far, far_partner]
    )
    q_all, grad_att, w, grad_rows = call(
        prepare_kernel,
        "prepare",
        [((ALL_ROWS, WIDTH), BF16), (tokens, F32), ((WIDTH, WIDTH), BF16), (tokens, BF16)],
        [q, grad_out, w_out],
        [pltpu.VMEM(tokens, BF16), dma((3,))],
        in_hbm=3,
    )
    low = moved(up, lambda i: i + 1)
    high = moved(down, lambda i: i - 1)
    got3 = moved(far3, route_3)
    got4 = moved(far4, route_4)
    got_third = moved(third_rows, third)
    low, high, got3 = lax.optimization_barrier((low, high, got3))
    own3, passed = call(
        pass_on_kernel,
        "pass_on",
        [((32, PACK), BF16), ((112, PACK), BF16)],
        [got3, got4, got_third],
    )
    far = (own3, got4, got_third, moved(passed, partner))
    near = (own0, own1, low, high)
    p_near, *near_sums = call(
        near_kernel,
        "near",
        [((PAIRS, P_NEAR, 256), BF16), (tokens, F32), ((ROWS, 2 * LANES), F32)]
        + [((192, WIDTH), BF16), ((192, 2 * LANES), BF16)],
        [q_all, qdoc, *near],
        microseconds=50,
    )
    attended, keep, give, p_far, g, d_side = call(
        merge_kernel,
        "merge",
        [(tokens, BF16), ((256, WIDTH), F32), ((256, WIDTH), BF16)]
        + [((PAIRS, P_FAR, LANES), BF16)]
        + [((ALL_ROWS, WIDTH), BF16), ((ALL_ROWS, LANES), BF16)],
        [q_all, qdoc, *near_sums, grad_att, grad_rows, *far],
        [pltpu.VMEM((WIDTH, WIDTH), F32)],
        microseconds=6,
    )

    def halved(keep, got, divisor, route, *after):
        rows = keep.shape[0] // 2
        keep, give = call(
            functools.partial(halve_kernel, divisor),
            "halve_" + str(rows),
            [((rows, WIDTH), F32), ((rows, WIDTH), BF16)],
            [keep, got, *after],
            [pltpu.VMEM((2 * rows, WIDTH), F32)],
            in_hbm=len(after),
        )
        return keep, moved(give, route)

    d_far, *to_far, message = call(
        far_back_kernel,
        "far_back",
        [((48, WIDTH), BF16), ((32, 2 * WIDTH), BF16), ((32, 2 * WIDTH), BF16)]
        + [((16, 2 * WIDTH), BF16), ((MESSAGE_ROWS, WIDTH), BF16)],
        [p_far, q_all, g, d_side, *far, give],
    )
    message = moved(message, partner)

    def part_outs(part):
        width = len(NEAR_PARTS[part]) * LANES
        return [((ROWS, width), BF16)] * 3 + [((2, 192, width), BF16)] * 2

    args = [p_near, q_all, g, d_side, *near, d_far]
    part_a = call(
        functools.partial(near_back_kernel, NEAR_PARTS[0]),
        "near_back_a",
        part_outs(0),
        args,
        microseconds=3,
    )
    sum3, sum4, sum_third, keep, give = call(
        partner_sum_kernel,
        "partner_sum",
        [((64, 2 * WIDTH), BF16), ((32, 2 * WIDTH), BF16), ((16, 2 * WIDTH), BF16)]
        + [((128, WIDTH), F32), ((128, WIDTH), BF16)],
        [*to_far, keep, message, part_a[0]],
        [pltpu.VMEM((256, WIDTH), F32)],
        in_hbm=1,
    )
    got_w = moved(give, lambda i: i ^ 8)
    back3 = moved(sum3, back_3)
    back4 = moved(sum4, back_4)
    layer_out, projected = call(
        project_kernel,
        "project",
        [(tokens, BF16), ((8, LANES), F32)],
        [attended, w, sum3],
        [pltpu.VMEM(tokens, BF16), dma(())],
        in_hbm=1,
        to_hbm=(0,),
    )
    keep, got_w = halved(keep, got_w, 16, lambda i: i ^ 24, projected)
    part_b = call(
        functools.partial(near_back_kernel, NEAR_PARTS[1]),
        "near_back_b",
        part_outs(1),
        [*args, part_a[0], keep],
        in_hbm=2,
        microseconds=3,
    )
    keep, got_w = halved(keep, got_w, 4, lambda i: i ^ 6, part_b[0])
    part_c = call(
        functools.partial(near_back_kernel, NEAR_PARTS[2]),
        "near_back_c",
        part_outs(2),
        [*args, part_b[0], keep],
        in_hbm=2,
        microseconds=3,
    )
    keep, got_w = halved(keep, got_w, 2, lambda i: i ^ 2, part_c[0])
    give = call(far_split_kernel, "far_split", [((48, 2 * WIDTH), BF16)], [back3, back4])[0]
    swapped = moved(give, partner)
    d_q, own_k, own_v, to_low, to_high = call(
        near_back_last_kernel,
        "near_back_d",
        part_outs(3)[:3] + [((192, 2 * WIDTH), BF16)] * 2,
        [*args, *part_a[3:], *part_b[3:], *part_c[3:], keep, give],
        in_hbm=2,
        microseconds=3,
    )
    to_low, to_high, got_w = lax.optimization_barrier((to_low, to_high, got_w))
    low_back = moved(to_low, lambda i: i - 1)
    high_back = moved(to_high, lambda i: i + 1)
    copies = call(
        copies_kernel,
        "copies",
        [((lax.axis_size("dp"), 16, WIDTH), BF16)],
        [keep, got_w],
    )[0]
    sum_third, copies = lax.optimization_barrier((sum_third, copies))
    copies = lax.all_to_all(copies, "dp", 0, 0, tiled=True)
    back_third = moved(sum_third, third)
    d_k, d_v, d_q, finished = call(
        combine_kernel,
        "combine",
        [(tokens, BF16)] * 3 + [((8, LANES), F32)],
        [part_a[1], part_b[1], part_c[1], own_k, part_a[2], part_b[2], part_c[2], own_v]
        + [low_back, high_back, back3, back4, back_third, swapped]
        + [part_a[0], part_b[0], part_c[0], d_q],
        [pltpu.VMEM(tokens, BF16)] * 3 + [dma((3,))],
        to_hbm=(0, 1, 2),
    )
    d_w = call(last_sum_kernel, "last_sum", [((16, WIDTH), BF16)], [copies, finished], in_hbm=1)[0]
    return layer_out[None], d_q[None], d_k[None], d_v[None], d_w


def solution(mesh):
    tokens = P("dp", "ctx", None)
    return jax.shard_map(
        body,
        mesh=mesh,
        in_specs=(tokens, tokens, tokens, P("dp", "ctx"), P(), tokens),
        out_specs=(tokens, tokens, tokens, tokens, P("ctx", None)),
        check_vma=False,
    )
```

```python
import functools

import jax
import jax.numpy as jnp
from jax import lax
from jax.experimental import pallas as pl
from jax.experimental.pallas import tpu as pltpu
from jax.sharding import PartitionSpec as P

HEAD_DIM = 64
BLOCK = 64
HALF = 32
LEVELS = 4
ROWS = 256
WIDTH = 512
PAIRS = 4
LANES = 128
DOCS = 4
NEGATIVE = -1e30
BLOCKED = -2e30
SCALE = HEAD_DIM**-0.5
PACK = 2 * WIDTH + LANES
COUNT = (256, 128, 64, 32, 16)
AT = (0, 256, 384, 448, 480)
ALL_ROWS = 496
F32 = jnp.float32
BF16 = jnp.bfloat16
VMEM_MIB = 20

GROUPS = (
    (0, 0, 128, 256),
    (0, 128, 128, 256),
    (1, 0, 128, 256),
    (2, 0, 64, 128),
    (3, 0, 32, 96),
    (4, 0, 16, 96),
)
NEAR = (0, 1, 2, 3)
FAR = (4, 5)
P_AT = {0: 0, 1: 256, 2: 512, 3: 768, 4: 0, 5: 64}
P_NEAR, P_FAR = 896, 96


def iota(shape, dim):
    return lax.broadcasted_iota(jnp.int32, shape, dim)


def gather_table(level, value=1.0):
    shape = (COUNT[level], ROWS)
    return jnp.where(iota(shape, 1) // 2**level == iota(shape, 0), value, 0.0).astype(BF16)


def spread_table(level, value=1.0):
    shape = (ROWS, COUNT[level])
    return jnp.where(iota(shape, 0) // 2**level == iota(shape, 1), value, 0.0).astype(BF16)


def last_table(level):
    shape = (COUNT[level], ROWS)
    last = iota(shape, 0) * 2**level + (2**level - 1)
    return jnp.where(iota(shape, 1) == last, 1.0, 0.0).astype(BF16)


def query_place(index):
    level, _, rows, _ = GROUPS[index]
    size = BLOCK if level == 0 else HALF
    shape = (rows, LANES)
    return jnp.where(iota(shape, 0) // size + 8 == iota(shape, 1), 1.0, 0.0).astype(BF16)


def key_place(index):
    level, _, _, keys = GROUPS[index]
    shape = (keys, LANES)
    row, place = iota(shape, 0), iota(shape, 1) - 8
    if level == 0:
        apart = row // BLOCK - place
        blocked = (apart < 0) | (apart > 2)
        places = 2
    elif level == 1:
        there, here = row // HALF, place + 2
        block_apart = jnp.abs(there // 2 - (place + 2) // 2)
        blocked = (block_apart > 1) | (jnp.abs(there - here) < 2)
        places = 4
    else:
        blocked = row // HALF == place + 1
        places = 2
    blocked = blocked & (place >= 0) & (place < places)
    return jnp.where(blocked, BLOCKED, 0.0).astype(BF16)


def dot(a, b, a_dim=1, b_dim=0):
    return lax.dot_general(a, b, (((a_dim,), (b_dim,)), ((), ())), preferred_element_type=F32)


def split(x):
    high = x.astype(BF16)
    return high, (x - high.astype(F32)).astype(BF16)


def head_lanes(rows, width=LANES):
    return iota((rows, width), 1) % LANES < HEAD_DIM


def stacked(x):
    first = head_lanes(x.shape[0]).astype(F32).astype(BF16)
    return jnp.concatenate([x * first, x * (1 - first)], axis=0)


def unstacked(x, rows):
    return jnp.where(head_lanes(rows, x.shape[1]), x[:rows], x[rows:])


def lanes_of(pair, part=0):
    return slice(part * WIDTH + pair * LANES, part * WIDTH + (pair + 1) * LANES)


DOC_LANES = slice(2 * WIDTH, PACK)


def near_window(index, own0, own1, low, high, lanes):
    def rim(ref, level):
        return ref[BLOCK * level : BLOCK * (level + 1), lanes]

    if index == 0:
        parts = [rim(low, 0), own0[0:192, lanes]]
    elif index == 1:
        parts = [own0[64:256, lanes], rim(high, 0)]
    elif index == 2:
        parts = [rim(low, 1), own1[:, lanes], rim(high, 1)]
    else:
        parts = [rim(low, 2), rim(high, 2)]
    return jnp.concatenate(parts, axis=0)


def far_window(refs, lanes):
    return jnp.concatenate([ref[:, lanes] for ref in refs], axis=0)


def fetch(sources, targets, sems):
    copies = [
        pltpu.make_async_copy(source, target, sems.at[i])
        for i, (source, target) in enumerate(zip(sources, targets))
    ]
    for copy in copies:
        copy.start()
    return copies


def documents_kernel(seg_hbm, qdoc, seg, sem):
    copy = pltpu.make_async_copy(seg_hbm, seg, sem)
    copy.start()
    copy.wait()
    marks = jnp.where(seg[...] == iota((LANES, ROWS), 0), 1.0, 0.0).T.astype(BF16)
    qdoc[0:ROWS] = marks
    for level in range(1, LEVELS + 1):
        marks_c = dot(last_table(level), marks).astype(BF16)
        qdoc[AT[level] : AT[level] + COUNT[level]] = marks_c


def coarsen_kernel(qdoc, k_hbm, v_hbm, up, down, far, third, own0, own1, k, v, sems):
    copies = fetch((k_hbm, v_hbm), (k, v), sems)
    doc = iota((ALL_ROWS, LANES), 1) < DOCS
    docs = jnp.where(doc, (1.0 - qdoc[...].astype(F32)) * BLOCKED, 0.0).astype(BF16)
    copies[0].wait()
    copies[1].wait()
    levels = [(k[...], v[...], docs[0:ROWS])]
    for level in range(1, LEVELS + 1):
        keys = dot(gather_table(level, 0.5**level), levels[0][0]).astype(BF16)
        values = dot(gather_table(level), levels[0][1]).astype(BF16)
        levels.append((keys, values, docs[AT[level] : AT[level] + COUNT[level]]))

    def put(ref, at, level, start, stop):
        for part, lanes in zip(
            levels[level], (slice(0, WIDTH), slice(WIDTH, 2 * WIDTH), DOC_LANES)
        ):
            ref[at : at + stop - start, lanes] = part[start:stop]

    for level in range(3):
        put(up, BLOCK * level, level, COUNT[level] - BLOCK, COUNT[level])
        put(down, BLOCK * level, level, 0, BLOCK)
    put(far, 0, 3, 0, COUNT[3])
    put(far, COUNT[3], 4, 0, COUNT[4])
    put(third, 0, 4, 0, COUNT[4])
    put(own0, 0, 0, 0, COUNT[0])
    put(own1, 0, 1, 0, COUNT[1])


def core_index():
    return lax.axis_index("ctx") % 2


def pair_kernel(far, far_partner, far3, far4):
    even = core_index() == 0
    for out, start, rows in ((far3, 0, 32), (far4, 32, 16)):
        own, other = far[start : start + rows], far_partner[start : start + rows]
        out[0:rows] = jnp.where(even, own, other)
        out[rows : 2 * rows] = jnp.where(even, other, own)


def prepare_kernel(q_hbm, d_hbm, w_hbm, q_out, grad_att, w, d_out, q, sems):
    copies = fetch((q_hbm, d_hbm, w_hbm), (q, d_out, w), sems)
    copies[0].wait()
    for level in range(LEVELS + 1):
        queries = q[...] if level == 0 else dot(gather_table(level, 0.5**level), q[...]).astype(BF16)
        q_out[AT[level] : AT[level] + COUNT[level]] = (queries * SCALE).astype(BF16)
    copies[1].wait()
    copies[2].wait()
    grad_att[...] = dot(d_out[...], w[...], 1, 1)


def attend(queries, query_docs, keys, key_docs, values):
    rows = queries.shape[0]
    scores = dot(
        jnp.concatenate([stacked(queries), query_docs], axis=1),
        jnp.concatenate([keys, key_docs], axis=1),
        1,
        1,
    )
    peak = jnp.maximum(jnp.max(scores, axis=1, keepdims=True), NEGATIVE)
    peak = peak.astype(BF16).astype(F32)
    p = jnp.exp(scores - peak).astype(BF16)
    ones = jnp.ones(values.shape, BF16)
    both = dot(p, jnp.concatenate([values, ones], axis=1))
    return p, unstacked(both[:, :LANES], rows), both[:, LANES:], peak


def with_stats(stats, pair, sums, peak):
    rows = sums.shape[0] // 2
    lane = iota((rows, LANES), 1)
    result = []
    for old, new in zip(stats, (sums, peak)):
        old = jnp.where(lane == 2 * pair, new[:rows], old)
        result.append(jnp.where(lane == 2 * pair + 1, new[rows:], old))
    return result


def no_stats(rows):
    return [jnp.zeros((rows, LANES), F32)] * 2


def head_spread(pair):
    shape = (2 * LANES, LANES)
    head = iota(shape, 0) % LANES
    return jnp.where(head == 2 * pair + iota(shape, 1) // HEAD_DIM, 1.0, 0.0).astype(BF16)


def head_sum(pair):
    shape = (2 * LANES, LANES)
    head = 2 * pair + iota(shape, 0) % LANES // HEAD_DIM
    return jnp.where(head == iota(shape, 1), 1.0, 0.0).astype(BF16)


def both_parts(x):
    return jnp.concatenate(split(x), axis=1)


def docs_of(index, qdoc):
    level, start, rows, _ = GROUPS[index]
    docs = qdoc[AT[level] + start : AT[level] + start + rows]
    if index in NEAR:
        docs = docs + query_place(index)
    return jnp.concatenate([docs, docs], axis=0)


def near_kernel(q_all, qdoc, own0, own1, low, high, p_out, fine, fine_stats, coarse, coarse_stats):
    for index in NEAR:
        level, start, rows, keys = GROUPS[index]
        at = AT[level] + start
        query_docs = docs_of(index, qdoc)
        key_docs = near_window(index, own0, own1, low, high, DOC_LANES) + key_place(index)
        stats = no_stats(rows)
        for pair in range(PAIRS):
            window = [
                near_window(index, own0, own1, low, high, lanes_of(pair, part)) for part in (0, 1)
            ]
            p, numer, sums, peak = attend(
                q_all[at : at + rows, lanes_of(pair)], query_docs, window[0], key_docs, window[1]
            )
            stats = with_stats(stats, pair, sums, peak)
            p_out[pair, P_AT[index] : P_AT[index] + 2 * rows, 0:keys] = p
            if level == 0:
                fine[at : at + rows, lanes_of(pair)] = numer
            else:
                coarse[at - ROWS : at - ROWS + rows, lanes_of(pair)] = numer.astype(BF16)
        if level == 0:
            fine_stats[at : at + rows] = jnp.concatenate(stats, axis=1)
        else:
            coarse_stats[at - ROWS : at - ROWS + rows] = jnp.concatenate(stats, axis=1).astype(BF16)


def far_refs(refs):
    own3, got4, third, passed = refs
    return (
        (own3, passed.at[0:64]),
        (got4, passed.at[64:96], third, passed.at[96:112]),
    )


def block_at(block):
    x, y, core = block // 8, block // 2 % 4, block % 2
    return 16 * (16 * core + 4 * ((0, 2, 3, 1), (0, 1, 3, 2))[core][x] + y)


def merge_kernel(
    q_all, qdoc, fine, fine_stats, coarse, coarse_stats, grad_att, d_out, *refs
):
    far = far_refs(refs[:4])
    attended_out, keep, give, p_out, g_out, d_side, d_w = refs[4:]
    spreads = [None] + [spread_table(level) for level in range(1, LEVELS + 1)]
    gathers = [None] + [gather_table(level) for level in range(1, LEVELS + 1)]
    numers, stats = [None, coarse[0:128], coarse[128:192]], [None, coarse_stats[0:128]]
    stats.append(coarse_stats[128:192])
    for index, ref in zip(FAR, far):
        level, _, rows, keys = GROUPS[index]
        query_docs, key_docs = docs_of(index, qdoc), far_window(ref, DOC_LANES)
        own_stats, own_numers = no_stats(rows), []
        for pair in range(PAIRS):
            p, numer, sums, peak = attend(
                q_all[AT[level] : AT[level] + rows, lanes_of(pair)],
                query_docs,
                far_window(ref, lanes_of(pair)),
                key_docs,
                far_window(ref, lanes_of(pair, 1)),
            )
            own_stats = with_stats(own_stats, pair, sums, peak)
            own_numers.append(numer.astype(BF16))
            p_out[pair, P_AT[index] : P_AT[index] + 2 * rows, 0:keys] = p
        numers.append(jnp.concatenate(own_numers, axis=1))
        stats.append(jnp.concatenate(own_stats, axis=1).astype(BF16))
    wide = [fine_stats[...]] + [
        dot(spreads[level], stats[level]) for level in range(1, LEVELS + 1)
    ]
    sums, peaks = [x[:, :LANES] for x in wide], [x[:, LANES:] for x in wide]
    top = functools.reduce(jnp.maximum, peaks)
    weights = [jnp.exp(x - top) for x in peaks]
    norm = functools.reduce(
        jnp.add, [wt * x * float(2**i) for i, (wt, x) in enumerate(zip(weights, sums))]
    )
    inverse = 1.0 / jnp.where(iota(norm.shape, 1) < 2 * PAIRS, norm, 1.0)
    shares = [wt * inverse for wt in weights]
    share_parts = [both_parts(x) for x in shares]
    delta = jnp.zeros((ROWS, LANES), F32)
    for pair in range(PAIRS):
        cols = lanes_of(pair)
        to_lanes = head_spread(pair)
        wide_shares = [dot(x, to_lanes) for x in share_parts]
        numer = wide_shares[0] * fine[:, cols]
        for level in range(1, LEVELS + 1):
            numer = numer + wide_shares[level] * dot(spreads[level], numers[level][:, cols])
        attended = numer.astype(BF16)
        attended_out[:, cols] = attended
        grad_w = dot(attended, d_out[...], 0, 0)
        for block in range(8):
            at = block_at(8 * pair + block)
            d_w[at : at + 16] = grad_w[16 * block : 16 * (block + 1)]
        grad = grad_att[:, cols]
        delta = delta + dot(both_parts(grad * attended.astype(F32)), head_sum(pair))
        for level in range(LEVELS + 1):
            rows = (wide_shares[level] * grad).astype(BF16)
            if level > 0:
                rows = dot(gathers[level], rows).astype(BF16)
            g_out[AT[level] : AT[level] + COUNT[level], cols] = rows
    core = core_index()
    keep[...] = d_w[pl.ds(pl.multiple_of(core * 256, 256), 256)]
    give[...] = d_w[pl.ds(pl.multiple_of((1 - core) * 256, 256), 256)].astype(BF16)
    shape = (2 * LANES, LANES)
    part, head = iota(shape, 0) // LANES, iota(shape, 0) % LANES
    place = jnp.where((head < 8) & (iota(shape, 1) == 8 * part + head), 1.0, 0.0).astype(BF16)
    for level in range(LEVELS + 1):
        delta_c = shares[level] * delta
        if level > 0:
            summed = dot(gathers[level], both_parts(delta_c))
            delta_c = summed[:, :LANES] + summed[:, LANES:]
        terms = dot(both_parts(delta_c * -float(2**level)), place)
        d_side[AT[level] : AT[level] + COUNT[level]] = terms.astype(BF16)


def attend_back(pair, p, queries, grad, side, keys, values):
    rows = queries.shape[0]
    ones = jnp.where(iota(values.shape, 1) < 16, 1.0, 0.0).astype(BF16)
    grad = stacked(grad)
    lane = iota(side.shape, 1)
    sides = [
        side * jnp.where((lane < 16) & (lane % 8 == 2 * pair + i), 1.0, 0.0).astype(BF16)
        for i in (0, 1)
    ]
    product = dot(
        jnp.concatenate([grad, jnp.concatenate(sides, axis=0)], axis=1),
        jnp.concatenate([values, ones], axis=1),
        1,
        1,
    )
    ds = (p.astype(F32) * product).astype(BF16)
    grad_q = unstacked(dot(ds, keys), rows) * SCALE
    return grad_q, dot(ds, stacked(queries), 0, 0), dot(p, grad, 0, 0)


PARTNER_ROWS = 112
MESSAGE_ROWS = 256 + 2 * PARTNER_ROWS


def far_back_kernel(p_in, q_all, g_in, d_side, own3, got4, third, passed, give, *refs):
    far = far_refs((own3, got4, third, passed))
    d_q, to_3, to_4, to_third, message = refs
    message[0:256] = give[...]
    to_far = ((to_3, (0, 64)), (to_4, (64, 96), to_third, (96, 112)))
    for pair in range(PAIRS):
        cols = lanes_of(pair)
        for index, ref, to in zip(FAR, far, to_far):
            level, _, rows, keys = GROUPS[index]
            at = AT[level]
            grad_q, grad_k, grad_v = attend_back(
                pair,
                p_in[pair, P_AT[index] : P_AT[index] + 2 * rows, 0:keys],
                q_all[at : at + rows, cols],
                g_in[at : at + rows, cols],
                d_side[at : at + rows],
                far_window(ref, cols),
                far_window(ref, lanes_of(pair, 1)),
            )
            d_q[at - AT[3] : at - AT[3] + rows, cols] = grad_q.astype(BF16)
            start = 0
            for out in to:
                partners = isinstance(out, tuple)
                stop = start + (out[1] - out[0] if partners else out.shape[0])
                for part, grad in enumerate((grad_k, grad_v)):
                    rows = grad[start:stop].astype(BF16)
                    if partners:
                        first = 256 + part * PARTNER_ROWS
                        message[first + out[0] : first + out[1], cols] = rows
                    else:
                        out[:, lanes_of(pair, part)] = rows
                start = stop


NEAR_PARTS = ((0,), (1,), (2,), (3,))


def near_back(pairs, p_in, q_all, g_in, d_side, own0, own1, low, high, d_far):
    spread = jnp.concatenate([spread_table(level, 0.5**level) for level in (1, 2, 3, 4)], axis=1)
    for pair in pairs:
        cols = lanes_of(pair)
        grads = []
        for index in NEAR:
            level, start, rows, keys = GROUPS[index]
            at = AT[level] + start
            grads.append(
                attend_back(
                    pair,
                    p_in[pair, P_AT[index] : P_AT[index] + 2 * rows, 0:keys],
                    q_all[at : at + rows, cols],
                    g_in[at : at + rows, cols],
                    d_side[at : at + rows],
                    near_window(index, own0, own1, low, high, cols),
                    near_window(index, own0, own1, low, high, lanes_of(pair, 1)),
                )
            )
        coarse = [x[0].astype(BF16) for x in grads[2:]] + [d_far[:, cols]]
        whole = jnp.concatenate([x[0] for x in grads[:2]], axis=0)
        d_q = (whole + dot(spread, jnp.concatenate(coarse, axis=0))).astype(BF16)
        own, to_low, to_high = [], [], []
        for part, value in ((0, 0.5), (1, 1.0)):
            a, b, c, d = (x[1 + part] for x in grads)
            middle = jnp.concatenate([a[64:128], a[128:256] + b[0:128], b[128:192]], axis=0)
            near = dot(spread_table(1, value), c[64:192].astype(BF16))
            own.append((middle + near).astype(BF16))
            to_low.append(jnp.concatenate([a[:64], c[:64], d[:64]], axis=0).astype(BF16))
            to_high.append(jnp.concatenate([b[192:], c[192:], d[64:]], axis=0).astype(BF16))
        yield pair, d_q, own, to_low, to_high


def near_back_kernel(pairs, *refs):
    inputs, outs = refs[:9], refs[-5:]
    d_q, own_k, own_v, to_low, to_high = outs
    for pair, dq, own, low, high in near_back(pairs, *inputs):
        at = slice((pair - pairs[0]) * LANES, (pair - pairs[0] + 1) * LANES)
        d_q[:, at], own_k[:, at], own_v[:, at] = dq, own[0], own[1]
        for part in range(2):
            to_low[part, :, at], to_high[part, :, at] = low[part], high[part]


def near_back_last_kernel(*refs):
    inputs, earlier = refs[:9], [refs[at : at + 2] for at in (9, 11, 13)]
    d_q, own_k, own_v, to_low, to_high = refs[-5:]
    for pairs, (low, high) in zip(NEAR_PARTS, earlier):
        for part in range(2):
            lanes = slice(
                part * WIDTH + pairs[0] * LANES, part * WIDTH + (pairs[-1] + 1) * LANES
            )
            to_low[:, lanes], to_high[:, lanes] = low[part], high[part]
    for pair, dq, own, low, high in near_back(NEAR_PARTS[-1], *inputs):
        d_q[...], own_k[...], own_v[...] = dq, own[0], own[1]
        for part in range(2):
            to_low[:, lanes_of(pair, part)] = low[part]
            to_high[:, lanes_of(pair, part)] = high[part]


def pass_on_kernel(got3, got4, third, own3, out):
    out[0:64] = got3[...]
    out[64:96] = got4[...]
    out[96:112] = third[...]
    own3[...] = jnp.where(core_index() == 0, got3[0:32], got3[32:64])


def partner_sum_kernel(to_3, to_4, to_third, keep, message, *refs):
    sum3, sum4, sum_third, keep_out, give_out, total = refs[-6:]
    even = core_index() == 0
    for part in range(2):
        lanes = slice(part * WIDTH, (part + 1) * WIDTH)
        at = 256 + part * PARTNER_ROWS
        own3 = to_3[:, lanes].astype(F32)

        def came(start, stop):
            return message[at + start : at + stop].astype(F32)

        sum3[0:32, lanes] = (came(0, 32) + jnp.where(even, own3, 0.0)).astype(BF16)
        sum3[32:64, lanes] = (came(32, 64) + jnp.where(even, 0.0, own3)).astype(BF16)
        sum4[:, lanes] = (came(64, 96) + to_4[:, lanes].astype(F32)).astype(BF16)
        sum_third[:, lanes] = (came(96, 112) + to_third[:, lanes].astype(F32)).astype(BF16)
    total[...] = keep[...] + message[0:256].astype(F32)
    halve(total, ((8, 16), (16,)), keep_out, give_out)


def halve(total, divisors, keep, give):
    index = lax.axis_index("ctx")
    sides = [sum(index // divisor for divisor in chosen) % 2 for chosen in divisors]
    side = sides[0] * (1 - index % 2) + sides[1] * (index % 2)
    half = total.shape[0] // 2
    keep[...] = total[pl.ds(pl.multiple_of(side * half, half), half)]
    give[...] = total[pl.ds(pl.multiple_of((1 - side) * half, half), half)].astype(BF16)


def core_rows(ref, core, rows):
    return ref[pl.ds(pl.multiple_of(core * rows, rows), rows)]


def far_split_kernel(back3, back4, give):
    other = 1 - core_index()
    give[0:32] = core_rows(back3, other, 32)
    give[32:48] = core_rows(back4, other, 16)


def halve_kernel(divisor, keep, got, *refs):
    keep_out, give_out, total = refs[-3:]
    total[...] = keep[...] + got[...].astype(F32)
    halve(total, divisor, keep_out, give_out)


def copies_kernel(keep, got, *refs):
    total = keep[...] + got[...].astype(F32)
    for i in range(refs[-1].shape[0]):
        refs[-1][i] = total.astype(BF16)


def last_sum_kernel(parts, _, out):
    total = parts[0].astype(F32)
    for i in range(1, parts.shape[0]):
        total = total + parts[i].astype(F32)
    out[...] = total.astype(BF16)


def project_kernel(attended, w, _, layer_hbm, finished, layer_out, sem):
    finished[...] = jnp.zeros(finished.shape, F32)
    layer_out[...] = dot(attended[...], w[...]).astype(BF16)
    copy = pltpu.make_async_copy(layer_out, layer_hbm, sem)
    copy.start()
    copy.wait()


def combine_kernel(*refs):
    own, (low, high), grads_q = (refs[0:4], refs[4:8]), refs[8:10], refs[14:18]
    back3, back4, third, swapped = refs[10:14]
    d_k_hbm, d_v_hbm, d_q_hbm, finished, d_k, d_v, d_q, sems = refs[18:]
    finished[...] = jnp.zeros(finished.shape, F32)
    for pair, ref in enumerate(grads_q):
        d_q[:, lanes_of(pair)] = ref[...]
    copies = [pltpu.make_async_copy(d_q, d_q_hbm, sems.at[2])]
    copies[0].start()
    core = core_index()
    far3 = core_rows(back3, core, 32).astype(F32) + swapped[0:32].astype(F32)
    far4 = core_rows(back4, core, 16).astype(F32) + swapped[32:48].astype(F32)
    far4 = far4 + third[...].astype(F32)
    for part, out, out_hbm in ((0, d_k, d_k_hbm), (1, d_v, d_v_hbm)):
        lanes = slice(part * WIDTH, (part + 1) * WIDTH)
        table = jnp.concatenate(
            [spread_table(level, 1.0 if part else 0.5**level) for level in (1, 2, 3, 4)], axis=1
        )

        def rim(ref, level):
            return ref[BLOCK * level : BLOCK * (level + 1), lanes].astype(F32)

        coarse = jnp.concatenate(
            [
                rim(high, 1),
                rim(low, 1),
                rim(low, 2) + rim(high, 2),
                far3[:, lanes],
                far4[:, lanes],
            ],
            axis=0,
        ).astype(BF16)
        whole = jnp.concatenate([x[...] for x in own[part]], axis=1).astype(F32)
        whole = whole + dot(table, coarse)
        out[0:64] = (whole[0:64] + rim(high, 0)).astype(BF16)
        out[64:192] = whole[64:192].astype(BF16)
        out[192:256] = (whole[192:256] + rim(low, 0)).astype(BF16)
        copies.append(pltpu.make_async_copy(out, out_hbm, sems.at[part]))
        copies[-1].start()
    for copy in copies:
        copy.wait()


def call(
    kernel, name, outs, args, scratch=(), in_hbm=0, microseconds=1.0, to_hbm=()
):
    vmem, hbm = pl.BlockSpec(memory_space=pltpu.VMEM), pl.BlockSpec(memory_space=pl.ANY)
    return pl.pallas_call(
        kernel,
        name=name,
        out_shape=[jax.ShapeDtypeStruct(shape, dtype) for shape, dtype in outs],
        in_specs=[vmem] * (len(args) - in_hbm) + [hbm] * in_hbm,
        out_specs=[hbm if i in to_hbm else vmem for i in range(len(outs))],
        scratch_shapes=scratch,
        cost_estimate=pl.CostEstimate(
            flops=int(microseconds * 1e9), bytes_accessed=1 << 20, transcendentals=0
        ),
        compiler_params=pltpu.CompilerParams(vmem_limit_bytes=VMEM_MIB * 1024 * 1024),
    )(*args)


def moved(x, route):
    count = lax.axis_size("ctx")
    return lax.ppermute(x, "ctx", [(i, route(i) % count) for i in range(count)])


def partner(i):
    return i ^ 1


def third(i):
    return i - 6 if i // 2 % 2 else i + 6


def route_3(i):
    return i - 2 if i % 2 else i + 2


def route_4(i):
    return i - 4 if i % 2 else i + 4


def back_3(i):
    return i + 2 if i % 2 else i - 2


def back_4(i):
    return i + 4 if i % 2 else i - 4


def body(queries, key_rows, value_rows, segment_ids, w_out, d_out):
    q, k, v, grad_out = queries[0], key_rows[0], value_rows[0], d_out[0]
    tokens, dma = (ROWS, WIDTH), pltpu.SemaphoreType.DMA
    qdoc = call(
        documents_kernel,
        "documents",
        [((ALL_ROWS, LANES), BF16)],
        [segment_ids],
        [pltpu.VMEM((1, ROWS), jnp.int32), dma(())],
        in_hbm=1,
    )[0]
    up, down, far, third_rows, own0, own1 = call(
        coarsen_kernel,
        "coarsen",
        [((192, PACK), BF16), ((192, PACK), BF16), ((48, PACK), BF16), ((16, PACK), BF16)]
        + [((ROWS, PACK), BF16), ((128, PACK), BF16)],
        [qdoc, k, v],
        [pltpu.VMEM(tokens, BF16)] * 2 + [dma((2,))],
        in_hbm=2,
    )
    far_partner = moved(far, partner)
    far3, far4 = call(
        pair_kernel, "pair", [((64, PACK), BF16), ((32, PACK), BF16)], [far, far_partner]
    )
    q_all, grad_att, w, grad_rows = call(
        prepare_kernel,
        "prepare",
        [((ALL_ROWS, WIDTH), BF16), (tokens, F32), ((WIDTH, WIDTH), BF16), (tokens, BF16)],
        [q, grad_out, w_out],
        [pltpu.VMEM(tokens, BF16), dma((3,))],
        in_hbm=3,
    )
    low = moved(up, lambda i: i + 1)
    high = moved(down, lambda i: i - 1)
    got3 = moved(far3, route_3)
    got4 = moved(far4, route_4)
    got_third = moved(third_rows, third)
    low, high, got3 = lax.optimization_barrier((low, high, got3))
    own3, passed = call(
        pass_on_kernel,
        "pass_on",
        [((32, PACK), BF16), ((112, PACK), BF16)],
        [got3, got4, got_third],
    )
    far = (own3, got4, got_third, moved(passed, partner))
    near = (own0, own1, low, high)
    p_near, *near_sums = call(
        near_kernel,
        "near",
        [((PAIRS, P_NEAR, 256), BF16), (tokens, F32), ((ROWS, 2 * LANES), F32)]
        + [((192, WIDTH), BF16), ((192, 2 * LANES), BF16)],
        [q_all, qdoc, *near],
        microseconds=50,
    )
    attended, keep, give, p_far, g, d_side = call(
        merge_kernel,
        "merge",
        [(tokens, BF16), ((256, WIDTH), F32), ((256, WIDTH), BF16)]
        + [((PAIRS, P_FAR, LANES), BF16)]
        + [((ALL_ROWS, WIDTH), BF16), ((ALL_ROWS, LANES), BF16)],
        [q_all, qdoc, *near_sums, grad_att, grad_rows, *far],
        [pltpu.VMEM((WIDTH, WIDTH), F32)],
        microseconds=6,
    )

    def halved(keep, got, divisor, route, *after):
        rows = keep.shape[0] // 2
        keep, give = call(
            functools.partial(halve_kernel, divisor),
            "halve_" + str(rows),
            [((rows, WIDTH), F32), ((rows, WIDTH), BF16)],
            [keep, got, *after],
            [pltpu.VMEM((2 * rows, WIDTH), F32)],
            in_hbm=len(after),
        )
        return keep, moved(give, route)

    d_far, *to_far, message = call(
        far_back_kernel,
        "far_back",
        [((48, WIDTH), BF16), ((32, 2 * WIDTH), BF16), ((32, 2 * WIDTH), BF16)]
        + [((16, 2 * WIDTH), BF16), ((MESSAGE_ROWS, WIDTH), BF16)],
        [p_far, q_all, g, d_side, *far, give],
    )
    message = moved(message, partner)

    def part_outs(part):
        width = len(NEAR_PARTS[part]) * LANES
        return [((ROWS, width), BF16)] * 3 + [((2, 192, width), BF16)] * 2

    args = [p_near, q_all, g, d_side, *near, d_far]
    part_a = call(
        functools.partial(near_back_kernel, NEAR_PARTS[0]),
        "near_back_a",
        part_outs(0),
        args,
        microseconds=3,
    )
    sum3, sum4, sum_third, keep, give = call(
        partner_sum_kernel,
        "partner_sum",
        [((64, 2 * WIDTH), BF16), ((32, 2 * WIDTH), BF16), ((16, 2 * WIDTH), BF16)]
        + [((128, WIDTH), F32), ((128, WIDTH), BF16)],
        [*to_far, keep, message, part_a[0]],
        [pltpu.VMEM((256, WIDTH), F32)],
        in_hbm=1,
    )
    got_w = moved(give, lambda i: i ^ (24 if i % 2 else 8))
    back3 = moved(sum3, back_3)
    back4 = moved(sum4, back_4)
    layer_out, projected = call(
        project_kernel,
        "project",
        [(tokens, BF16), ((8, LANES), F32)],
        [attended, w, sum3],
        [pltpu.VMEM(tokens, BF16), dma(())],
        in_hbm=1,
        to_hbm=(0,),
    )
    keep, got_w = halved(keep, got_w, ((16,), (8, 16)), lambda i: i ^ (8 if i % 2 else 24), projected)
    part_b = call(
        functools.partial(near_back_kernel, NEAR_PARTS[1]),
        "near_back_b",
        part_outs(1),
        [*args, part_a[0], keep],
        in_hbm=2,
        microseconds=3,
    )
    keep, got_w = halved(keep, got_w, ((4,), (4,)), lambda i: i ^ 6, part_b[0])
    part_c = call(
        functools.partial(near_back_kernel, NEAR_PARTS[2]),
        "near_back_c",
        part_outs(2),
        [*args, part_b[0], keep],
        in_hbm=2,
        microseconds=3,
    )
    keep, got_w = halved(keep, got_w, ((2,), (2,)), lambda i: i ^ 2, part_c[0])
    give = call(far_split_kernel, "far_split", [((48, 2 * WIDTH), BF16)], [back3, back4])[0]
    swapped = moved(give, partner)
    d_q, own_k, own_v, to_low, to_high = call(
        near_back_last_kernel,
        "near_back_d",
        part_outs(3)[:3] + [((192, 2 * WIDTH), BF16)] * 2,
        [*args, *part_a[3:], *part_b[3:], *part_c[3:], keep, give],
        in_hbm=2,
        microseconds=3,
    )
    to_low, to_high, got_w = lax.optimization_barrier((to_low, to_high, got_w))
    low_back = moved(to_low, lambda i: i - 1)
    high_back = moved(to_high, lambda i: i + 1)
    copies = call(
        copies_kernel,
        "copies",
        [((lax.axis_size("dp"), 16, WIDTH), BF16)],
        [keep, got_w],
    )[0]
    sum_third, copies = lax.optimization_barrier((sum_third, copies))
    copies = lax.all_to_all(copies, "dp", 0, 0, tiled=True)
    back_third = moved(sum_third, third)
    d_k, d_v, d_q, finished = call(
        combine_kernel,
        "combine",
        [(tokens, BF16)] * 3 + [((8, LANES), F32)],
        [part_a[1], part_b[1], part_c[1], own_k, part_a[2], part_b[2], part_c[2], own_v]
        + [low_back, high_back, back3, back4, back_third, swapped]
        + [part_a[0], part_b[0], part_c[0], d_q],
        [pltpu.VMEM(tokens, BF16)] * 3 + [dma((3,))],
        to_hbm=(0, 1, 2),
    )
    d_w = call(last_sum_kernel, "last_sum", [((16, WIDTH), BF16)], [copies, finished], in_hbm=1)[0]
    return layer_out[None], d_q[None], d_k[None], d_v[None], d_w


def solution(mesh):
    tokens = P("dp", "ctx", None)
    return jax.shard_map(
        body,
        mesh=mesh,
        in_specs=(tokens, tokens, tokens, P("dp", "ctx"), P(), tokens),
        out_specs=(tokens, tokens, tokens, tokens, P("ctx", None)),
        check_vma=False,
    )
```
